32 devices in a mesh: section: 2 (over core), seq: 8 (over z, y), head: 2 (over x).
Axes of the slice: x: 2, y: 2, z: 4, core: 2. Of those that a mesh axis runs over, the one named last changes fastest.
Arguments:
- boundary_in: float32 [2, 2, 2048, 768], P('section', None, ('seq', 'head')), may hold values from -6 to 6
- short_items: int32 [1, 3], replicated, may hold values from 1 to 4, 8 in all within a row
- norm_gains: float32 [2, 2, 768], P('section'), may hold values from 0.5 to 1.5
- norm_biases: float32 [2, 2, 768], P('section'), may hold values from -1.2 to 1.2
- projection_in: float32 [2, 768, 3, 768], P('section', None, None, 'head'), may hold values from -0.21875 to 0.21875
- head_bias: float32 [2, 2, 768], P('section', None, 'head'), may hold values from -1.2 to 1.2
- projection_out: float32 [2, 768, 768], P('section', 'head'), may hold values from -1.75 to 1.75
- residual_bias: float32 [2, 2, 768], P('section'), may hold values from -1.2 to 1.2
- up_weight: float32 [2, 768, 3072], P('section', None, 'head'), may hold values from -0.21875 to 0.21875
- up_bias: float32 [2, 3072], P('section', 'head'), may hold values from -1.2 to 1.2
- down_weight: float32 [2, 3072, 768], P('section', 'head'), may hold values from -0.109375 to 0.109375
- memory_tokens: float32 [2, 16, 768], P('section', 'head'), may hold values from -6 to 6
- query_memory: float32 [2, 768, 384], P('section'), may hold values from -0.21875 to 0.21875
- key_memory: float32 [2, 768, 384], P('section'), may hold values from -0.21875 to 0.21875
- value_memory: float32 [2, 768, 768], P('section', None, 'head'), may hold values from -1.75 to 1.75
Outputs:
- boundary_out: float32 [2, 2, 2048, 768], P('section', None, ('seq', 'head'))
- grad_norm_gains: float32 [2, 2, 768], P('section')
- grad_norm_biases: float32 [2, 2, 768], P('section')
- grad_projection_in: float32 [2, 768, 3, 768], P('section', None, None, 'head')
- grad_head_bias: float32 [2, 2, 768], P('section', None, 'head')
- grad_projection_out: float32 [2, 768, 768], P('section', 'head')
- grad_residual_bias: float32 [2, 2, 768], P('section')
- grad_up_weight: float32 [2, 768, 3072], P('section', None, 'head')
- grad_up_bias: float32 [2, 3072], P('section', 'head')
- grad_down_weight: float32 [2, 3072, 768], P('section', 'head')
- grad_memory_tokens: float32 [2, 16, 768], P('section', 'head')
- grad_query_memory: float32 [2, 768, 384], P('section')
- grad_key_memory: float32 [2, 768, 384], P('section')
- grad_value_memory: float32 [2, 768, 768], P('section', None, 'head')
The draws below stay inside these ranges and needn't reach their ends.
Inputs may be any that keep to these rules, and one draw needn't show every extreme that they name: `short_items`: each row lists, in order along the segments, the segment counts of one micro-batch's items; every row sums to 8.
All inputs are finite; a program needn't handle non-finite values.
Results may differ from the reference program's by a relative error of at most 0.0003.
Values sent between devices are 32-bit elements; how exact they have to be, the bound alone decides.
A program may use at most 320 MiB of HBM per device.

```python
import math
from functools import partial
import jax
import jax.numpy as jnp
import numpy as np
from jax import lax

D = 768
HEADS = 12
HEAD_DIM = 64
FF = 3072
DK = 384
NMEM = 16
SEG = 256
MICRO = 2
PIECES = 3
LAYERS = 2
TOKENS = 2048
N_SEQ = 8


def levels(key, extent, pieces, least, largest):
    loudness, own = 1.0, jax.random.fold_in(key, 6)
    for dim, blocks in pieces:
        steps = jnp.exp(jax.random.uniform(jax.random.fold_in(own, dim), (blocks,), jnp.float32, least / len(pieces), largest / len(pieces)))
        loudness = loudness * jnp.repeat(steps, extent[dim] // blocks).reshape([-1 if axis == dim else 1 for axis in range(len(extent))])
    return loudness


def length_profile(amount, total, bound, skew):
    portions = [(1 << 20) // math.isqrt(grade ** skew) + 1 for grade in range(2, amount + 1)]
    rest, given = total - bound - (amount - 1), [1] * (amount - 1)
    while rest > 0:
        movable = [i for i in range(amount - 1) if given[i] < bound]
        whole, left = sum([portions[i] for i in movable]), rest
        for i in movable:
            more = min(bound - given[i], max(1, left * portions[i] // whole), rest)
            given[i] = given[i] + more
            rest = rest - more
    return np.array([bound] + given)


def uneven_parts(rng, count, total, reach, slope):
    if count == 2:
        one = jax.random.randint(rng, (), max(1, total - reach), min(reach, total - 1) + 1)
        return jnp.stack([one, total - one])
    tallies = jnp.asarray(length_profile(count, total, reach, slope), jnp.int32)
    twos = (count - 1) // 2
    source_of, sink = tallies[1:1 + 2 * twos:2], tallies[2:2 + 2 * twos:2]
    margin = jnp.minimum(source_of - 1, reach - sink)
    shifted = jax.random.randint(jax.random.fold_in(rng, 1), (twos,), 0, 1 << 20) % (margin + 1)
    tallies = tallies.at[1:1 + 2 * twos:2].set(source_of - shifted).at[2:2 + 2 * twos:2].set(sink + shifted)
    return tallies[jax.random.permutation(jax.random.fold_in(rng, 2), count)]


def noise(own_key, dims, deviation, bound, pieces=(), dtype=jnp.bfloat16):
    entries = jax.random.normal(own_key, dims, jnp.float32) * deviation
    if len(pieces) > 0:
        entries = levels(own_key, dims, pieces, -0.22, 0.18) * entries
    return jnp.clip(entries, min=-bound, max=bound).astype(dtype)


def setup_inputs(seed: int = 0) -> dict:
    key_list = jax.random.split(jax.random.key(seed), 16)
    boundary_in = noise(key_list[0], (2, MICRO, TOKENS, D), 1.0, 6.0, ((0, 2), (2, 16)), jnp.float32)
    short_items = jax.vmap(lambda own: uneven_parts(own, PIECES, N_SEQ, N_SEQ // 2, 0))(jax.random.split(key_list[1], (MICRO - 1))).reshape((MICRO - 1, PIECES)).astype(jnp.int32)
    norm_gains = jnp.clip(1.0 + 0.1 * jax.random.normal(key_list[2], (LAYERS, 2, D), jnp.float32), 0.5, 1.5)
    norm_biases = noise(key_list[3], (LAYERS, 2, D), 0.2, 1.2, ((0, 2),), jnp.float32)
    projection_in = noise(key_list[4], (LAYERS, D, 3, D), D ** -0.5, 0.21875, ((0, 2), (3, 2)), jnp.float32)
    head_bias = noise(key_list[5], (LAYERS, 2, D), 0.2, 1.2, ((0, 2), (2, 2)), jnp.float32)
    projection_out = noise(key_list[6], (LAYERS, D, D), (D // 64) ** -0.5, 1.75, ((0, 2), (1, 2)), jnp.float32)
    residual_bias = noise(key_list[7], (LAYERS, 2, D), 0.2, 1.2, ((0, 2),), jnp.float32)
    up_weight = noise(key_list[8], (LAYERS, D, FF), D ** -0.5, 0.21875, ((0, 2), (2, 2)), jnp.float32)
    up_bias = noise(key_list[9], (LAYERS, FF), 0.2, 1.2, ((0, 2), (1, 2)), jnp.float32)
    down_weight = noise(key_list[10], (LAYERS, FF, D), FF ** -0.5, 0.109375, ((0, 2), (1, 2)), jnp.float32)
    memory_tokens = noise(key_list[11], (LAYERS, NMEM, D), 1.0, 6.0, ((0, 2), (1, 2)), jnp.float32)
    query_memory = noise(key_list[12], (LAYERS, D, DK), D ** -0.5, 0.21875, ((0, 2),), jnp.float32)
    key_memory = noise(key_list[13], (LAYERS, D, DK), D ** -0.5, 0.21875, ((0, 2),), jnp.float32)
    value_memory = noise(key_list[14], (LAYERS, D, D), (D // 64) ** -0.5, 1.75, ((0, 2), (2, 2)), jnp.float32)
    return {"boundary_in": boundary_in, "short_items": short_items, "norm_gains": norm_gains, "norm_biases": norm_biases, "projection_in": projection_in, "head_bias": head_bias, "projection_out": projection_out, "residual_bias": residual_bias, "up_weight": up_weight, "up_bias": up_bias, "down_weight": down_weight, "memory_tokens": memory_tokens, "query_memory": query_memory, "key_memory": key_memory, "value_memory": value_memory}


@jax.custom_vjp
def low(v):
    return lax.optimization_barrier(v.astype(jnp.bfloat16)).astype(jnp.float32)

@jax.custom_vjp
def low_back(v):
    return v

def low_keep(v):
    return (low(v), None)

def low_pass(kept, grad):
    return (grad,)

def back_keep(v):
    return (v, None)

def back_low(kept, grad):
    return (low(grad),)
low.defvjp(low_keep, low_pass)
low_back.defvjp(back_keep, back_low)
EPSILON = 1e-05
HIGHEST_PRECISION = lax.Precision.HIGHEST

def matmul(left_mat, right_mat):
    return jnp.dot(left_mat, right_mat, precision=HIGHEST_PRECISION, preferred_element_type=jnp.float32)

def normalize(values_in, gain_row, bias_row):
    centred = values_in - lax.optimization_barrier(jnp.mean(values_in, axis=-1, keepdims=True))
    spread = lax.optimization_barrier(jnp.mean(centred * centred, axis=-1, keepdims=True))
    return centred * lax.rsqrt(spread + EPSILON) * gain_row + bias_row

def features(projected):
    halves = jnp.concatenate([jax.nn.softplus(projected), jax.nn.softplus(-projected)], axis=-1)
    return jnp.concatenate([halves * jnp.roll(halves, rolled_by, axis=-1) for rolled_by in (1, 2, 3)], axis=-1)

def gelu_tanh(values_in):
    return jax.nn.gelu(values_in, approximate=True)

def block(all_rows, layer_params):
    norm_gains, norm_biases, projection_in, head_bias, projection_out, residual_bias, up_weight, up_bias, down_weight = layer_params[:9]
    row_count = all_rows.shape[0]
    normed = normalize(all_rows, norm_gains[0], norm_biases[0])
    projected = jnp.einsum('rd,dte->rte', normed, projection_in, precision=HIGHEST_PRECISION)
    query_heads = (projected[:, 0] + head_bias[0]).reshape(row_count, HEADS, HEAD_DIM)
    key_heads = projected[:, 1].reshape(row_count, HEADS, HEAD_DIM)
    value_heads = (projected[:, 2] + head_bias[1]).reshape(row_count, HEADS, HEAD_DIM)
    scores = jnp.einsum('qhe,khe->hqk', query_heads, key_heads, precision=HIGHEST_PRECISION) / math.sqrt(HEAD_DIM)
    places = jnp.arange(row_count)
    scores = jnp.where((places[:, None] >= places[None, :])[None], scores, -1e+30)
    soft_weights = jax.nn.softmax(scores, axis=-1)
    attended = jnp.einsum('hqk,khe->qhe', soft_weights, value_heads, precision=HIGHEST_PRECISION).reshape(row_count, D)
    hidden = all_rows + matmul(attended, projection_out) + residual_bias[0]
    mixed_rows = normalize(hidden, norm_gains[1], norm_biases[1])
    inner_act = gelu_tanh(matmul(mixed_rows, up_weight) + up_bias)
    return hidden + matmul(inner_act, down_weight) + residual_bias[1]

def segment_step(layer_params, carried, step_inputs):
    memory_a, memory_z = carried
    seg_rows, item_flag = step_inputs
    keep_share = 1.0 - item_flag
    result = block(jnp.concatenate([seg_rows, layer_params[9]], axis=0), layer_params)
    seg_out = result[:SEG]
    mem_out = result[SEG:]
    key_feats = features(matmul(mem_out, layer_params[11]))
    value_rows = matmul(mem_out, layer_params[12])
    state_a = keep_share * memory_a
    state_z = keep_share * memory_z
    query_feats = features(matmul(seg_out, layer_params[10]))
    numerator = matmul(query_feats, state_a.T)
    denominator = matmul(query_feats, state_z[:, None]) + 1.0
    next_state = (state_a + matmul(value_rows.T, key_feats), state_z + lax.optimization_barrier(jnp.sum(key_feats, axis=0)))
    return (next_state, seg_out + numerator / denominator)

def item_starts(short_items):
    positions = jnp.arange(N_SEQ).astype(jnp.int32)
    flag_rows = [(positions == 0).astype(jnp.float32)]
    for micro_number in range(MICRO - 1):
        counts = short_items[micro_number].astype(jnp.int32)
        bounds = jnp.cumsum(counts) - counts
        flag_rows.append(jnp.any(positions[:, None] == bounds[None, :], axis=1).astype(jnp.float32))
    return jnp.stack(flag_rows)

def forward(layer_input, starts, params):
    current = layer_input
    for layer_number in range(LAYERS):
        layer_params = tuple((weight_array[layer_number] for weight_array in params))
        step_fn = jax.checkpoint(partial(segment_step, layer_params))
        outputs = []
        for micro_number in range(MICRO):
            segments = current[micro_number].reshape(N_SEQ, SEG, D)
            initial = (jnp.zeros((D, 6 * DK), jnp.float32), jnp.zeros((6 * DK,), jnp.float32))
            _, layer_out = lax.scan(step_fn, initial, (segments, starts[micro_number]))
            outputs.append(layer_out.reshape(N_SEQ * SEG, D))
        current = jnp.stack(outputs)
    return current

def reference(boundary_in, short_items, norm_gains, norm_biases, projection_in, head_bias, projection_out, residual_bias, up_weight, up_bias, down_weight, memory_tokens, query_memory, key_memory, value_memory):
    starts = item_starts(short_items)
    params = (norm_gains, norm_biases, projection_in, head_bias, projection_out, residual_bias, up_weight, up_bias, down_weight, memory_tokens, query_memory, key_memory, value_memory)

    def run(layer_input, *weights):
        return forward(layer_input, starts, weights)
    final_out, pull_back = jax.vjp(run, boundary_in[0], *params)
    grads = pull_back(boundary_in[1])
    boundary_out = jnp.stack([grads[0], final_out])
    return (boundary_out, grads[1], grads[2], grads[3], grads[4], grads[5], grads[6], grads[7], grads[8], grads[9], grads[10], grads[11], grads[12], grads[13])
```

```python
import math

import jax
import jax.numpy as jnp
from jax import lax
from jax.sharding import PartitionSpec as P

HEAD_DIM = 64
EPSILON = 1e-05
SCALE = 1.0 / math.sqrt(HEAD_DIM)


def mm(left, right, dims=((1,), (0,))):
    return lax.dot_general(
        left, right, (dims, ((), ())), precision=lax.Precision.HIGH, preferred_element_type=jnp.float32
    )


def mm_nt(left, right):
    return mm(left, right, ((1,), (1,)))


def mm_tn(left, right):
    return mm(left, right, ((0,), (0,)))


def unit_rows(rows):
    centred = rows - jnp.mean(rows, axis=-1, keepdims=True)
    inverse = lax.rsqrt(jnp.mean(centred * centred, axis=-1, keepdims=True) + EPSILON)
    return centred * inverse, inverse


def unit_rows_back(d_unit, unit, inverse):
    return inverse * (
        d_unit
        - jnp.mean(d_unit, axis=-1, keepdims=True)
        - unit * jnp.mean(d_unit * unit, axis=-1, keepdims=True)
    )


def features(projected):
    halves = jnp.concatenate([jax.nn.softplus(projected), jax.nn.softplus(-projected)], axis=-1)
    return jnp.concatenate(
        [halves * jnp.roll(halves, rolled_by, axis=-1) for rolled_by in (1, 2, 3)], axis=-1
    )


def gelu_tanh(values_in):
    return jax.nn.gelu(values_in, approximate=True)


def swap(value):
    return lax.ppermute(value, "head", [(0, 1), (1, 0)])


def head_sum(value):
    if lax.axis_size("head") == 2:
        return value + swap(value)
    return lax.psum(value, "head")


def head_sum_rows(rows, share):
    count = lax.axis_size("head")
    segment = count * share
    if count == 2:
        other = swap(rows)
        return rows + jnp.concatenate(
            [other[share:segment], other[:share], other[segment:]], axis=0
        )
    turn = lax.axis_index("head") * share
    total = lax.psum(
        jnp.concatenate([jnp.roll(rows[:segment], turn, axis=0), rows[segment:]], axis=0), "head"
    )
    return jnp.concatenate([jnp.roll(total[:segment], -turn, axis=0), total[segment:]], axis=0)


def head_rows(local):
    count = lax.axis_size("head")
    if count == 2:
        return jnp.concatenate([local, swap(local)], axis=0)
    gathered = lax.all_gather(local, "head", axis=0, tiled=True)
    return jnp.roll(gathered, -lax.axis_index("head") * local.shape[0], axis=0)


def head_scatter(rows):
    count = lax.axis_size("head")
    share = rows.shape[0] // count
    if count == 2:
        return rows[:share] + swap(rows[share:])
    placed = jnp.roll(rows, lax.axis_index("head") * share, axis=0)
    return lax.psum_scatter(placed, "head", scatter_dimension=0, tiled=True)


def head_columns(values):
    count = lax.axis_size("head")
    share = values.shape[1] // count
    place = lax.axis_index("head")
    if count == 2:
        own = lax.dynamic_slice_in_dim(values, place * share, share, 1)
        other = lax.dynamic_slice_in_dim(values, (1 - place) * share, share, 1)
        return own + swap(other)
    return lax.psum_scatter(values, "head", scatter_dimension=1, tiled=True)


def heads_of(part):
    return part.reshape(part.shape[0], -1, HEAD_DIM).transpose(1, 0, 2)


def rows_of(part):
    return part.transpose(1, 0, 2).reshape(part.shape[1], -1)


def bmm(left, right, left_dim, right_dim):
    return lax.dot_general(
        left,
        right,
        (((left_dim,), (right_dim,)), ((0,), (0,))),
        precision=lax.Precision.HIGH,
        preferred_element_type=jnp.float32,
    )


def layer_forward(local, params, mask, allowed):
    width = local.shape[1]
    local_count = local.shape[0]
    segment = lax.axis_size("head") * local_count
    rows = jnp.concatenate([head_rows(local), params["memory"]], axis=0)
    unit_one, inverse_one = unit_rows(rows)
    normed = unit_one * params["gains"][0] + params["biases"][0]
    projected = mm(normed, params["proj_in"]) + params["in_bias"]
    share = projected.shape[1] // 3
    query, key, value = (heads_of(projected[:, i * share : (i + 1) * share]) for i in range(3))
    scores = jnp.where(allowed, bmm(query, key, 2, 2) * SCALE, -1e30)
    row_top = jnp.max(scores, axis=-1, keepdims=True)
    exponent = jnp.exp(scores - row_top)
    soft = exponent / jnp.sum(exponent, axis=-1, keepdims=True)
    attended = rows_of(bmm(soft, value, 2, 1))
    hidden = rows + head_sum_rows(mm(attended, params["proj_out"]), local_count) + params["residual"][0]
    unit_two, inverse_two = unit_rows(hidden)
    mixed = unit_two * params["gains"][1] + params["biases"][1]
    inner_pre = mm(mixed, params["up"]) + params["up_bias"]
    inner_act = gelu_tanh(inner_pre)
    partial = mm(inner_act, params["down"])
    out_local = head_scatter(partial[:segment]) + hidden[:local_count] + params["residual"][1]
    out_mem = head_sum(partial[segment:]) + hidden[segment:] + params["residual"][1]
    key_proj = mm(out_mem, params["key_mem"])
    values = mm(out_mem, params["value_mem"])
    gathered = lax.all_gather(jnp.concatenate([key_proj, values], axis=1), "seq", axis=0, tiled=True)
    dk = key_proj.shape[1]
    keys_all = gathered[:, :dk]
    values_all = lax.all_gather(gathered[:, dk:], "head", axis=1, tiled=True)
    key_feats = features(keys_all)
    query_proj = mm(out_local, params["query_mem"])
    query_feats = features(query_proj)
    weights = mask * mm_nt(query_feats, key_feats)
    denominator = jnp.sum(weights, axis=1, keepdims=True) + 1.0
    read = mm(weights, values_all) / denominator
    return dict(
        unit_one=unit_one,
        inverse_one=inverse_one,
        projected=projected,
        attended=attended,
        soft=soft,
        unit_two=unit_two,
        inverse_two=inverse_two,
        inner_pre=inner_pre,
        out_local=out_local,
        out_mem=out_mem,
        keys_all=keys_all,
        values_all=values_all,
        query_proj=query_proj,
        weights=weights,
        denominator=denominator,
        read=read,
        output=out_local + read,
    )


def layer_backward(grad, record, params, mask):
    head_count = lax.axis_size("head")
    seq_count = lax.axis_size("seq")
    width = grad.shape[1]
    local_count = grad.shape[0]
    segment = head_count * local_count
    denominator = record["denominator"]
    d_numer = grad / denominator
    d_denom = -jnp.sum(grad * record["read"], axis=1, keepdims=True) / denominator
    d_weights = mask * (mm_nt(d_numer, record["values_all"]) + d_denom)
    key_feats, keys_back = jax.vjp(features, record["keys_all"])
    query_feats, query_back = jax.vjp(features, record["query_proj"])
    d_query_proj = query_back(mm(d_weights, key_feats))[0]
    d_keys = keys_back(mm_tn(d_weights, query_feats))[0]
    d_values = mm_tn(record["weights"], d_numer)
    d_memory = lax.psum_scatter(
        jnp.concatenate([d_keys, d_values], axis=1), "seq", scatter_dimension=0, tiled=True
    )
    dk = d_keys.shape[1]
    d_key_proj = d_memory[:, :dk]
    d_value = head_columns(d_memory[:, dk:])
    d_mem = head_sum(mm_nt(d_key_proj, params["key_mem"]) + mm_nt(d_value, params["value_mem"]))
    d_local = grad + mm_nt(d_query_proj, params["query_mem"])
    d_result = jnp.concatenate([head_rows(d_local), d_mem], axis=0)
    inner_act, gelu_back = jax.vjp(gelu_tanh, record["inner_pre"])
    grad_down = mm_tn(inner_act, d_result)
    d_pre = gelu_back(mm_nt(d_result, params["down"]))[0]
    gains, biases = params["gains"], params["biases"]
    mixed = record["unit_two"] * gains[1] + biases[1]
    grad_up = mm_tn(mixed, d_pre)
    d_mixed = head_sum_rows(mm_nt(d_pre, params["up"]), local_count)
    d_hidden = d_result + unit_rows_back(d_mixed * gains[1], record["unit_two"], record["inverse_two"])
    grad_out = mm_tn(record["attended"], d_hidden)
    d_attended = mm_nt(d_hidden, params["proj_out"])
    share = d_attended.shape[1]
    query, key, value = (
        heads_of(record["projected"][:, i * share : (i + 1) * share]) for i in range(3)
    )
    soft = record["soft"]
    d_heads = heads_of(d_attended)
    inner_dot = jnp.sum(d_heads * heads_of(record["attended"]), axis=-1, keepdims=True)
    d_scores = soft * (bmm(d_heads, value, 2, 2) - inner_dot) * SCALE
    d_projected = jnp.concatenate(
        [
            rows_of(bmm(d_scores, key, 2, 1)),
            rows_of(bmm(d_scores, query, 1, 1)),
            rows_of(bmm(soft, d_heads, 1, 1)),
        ],
        axis=1,
    )
    normed = record["unit_one"] * gains[0] + biases[0]
    grad_in = mm_tn(normed, d_projected)
    columns = jnp.sum(d_projected, axis=0)
    grad_head_bias = jnp.stack([columns[:share], columns[2 * share :]])
    d_normed_all = mm_nt(d_projected, params["proj_in"])
    d_normed = head_scatter(d_normed_all[:segment])
    d_normed_mem = lax.psum_scatter(
        d_normed_all[segment:], "head", scatter_dimension=0, tiled=True
    )
    mem_count = d_normed_mem.shape[0]
    own_mem = segment + lax.axis_index("head") * mem_count

    def own(values):
        return jnp.concatenate(
            [values[:local_count], lax.dynamic_slice_in_dim(values, own_mem, mem_count, 0)], axis=0
        )

    d_normed_own = jnp.concatenate([d_normed, d_normed_mem], axis=0)
    unit_own = own(record["unit_one"])
    d_rows = own(d_hidden) + unit_rows_back(
        d_normed_own * gains[0], unit_own, own(record["inverse_one"])
    )
    part = 1.0 / head_count
    sharded = (
        grad_in,
        grad_head_bias,
        grad_out,
        grad_up,
        jnp.sum(d_pre, axis=0),
        grad_down,
        d_rows[local_count:],
        mm_tn(record["out_mem"], d_value),
    )
    shared = (
        jnp.stack(
            [
                jnp.sum(d_normed_own * unit_own, axis=0),
                part * jnp.sum(d_mixed * record["unit_two"], axis=0),
            ]
        ),
        jnp.stack([jnp.sum(d_normed_own, axis=0), part * jnp.sum(d_mixed, axis=0)]),
        part * jnp.stack([jnp.sum(d_hidden, axis=0), jnp.sum(d_result, axis=0)]),
        mm_tn(record["out_local"], d_query_proj),
        mm_tn(record["out_mem"], d_key_proj),
    )
    return (d_rows[:local_count], sharded, shared)


def passed_along(value, axis, steps):
    count = lax.axis_size(axis)
    first, last = (max(0, -steps), min(count, count - steps))
    return lax.ppermute(value, axis, [(source, source + steps) for source in range(first, last)])


def shards(
    boundary_in,
    short_items,
    norm_gains,
    norm_biases,
    projection_in,
    head_bias,
    projection_out,
    residual_bias,
    up_weight,
    up_bias,
    down_weight,
    memory_tokens,
    query_memory,
    key_memory,
    value_memory,
):
    section = lax.axis_index("section")
    sections = lax.axis_size("section")
    head_count = lax.axis_size("head")
    head_place = lax.axis_index("head")
    seq_count = lax.axis_size("seq")
    seq_place = lax.axis_index("seq")
    micro_total = boundary_in.shape[1]
    local_count = boundary_in.shape[2]
    width = boundary_in.shape[3]
    segment = head_count * local_count
    head_width = projection_in.shape[3]
    memory_all = lax.all_gather(memory_tokens[0], "head", axis=0, tiled=True)
    mem_count = memory_all.shape[0]
    params = dict(
        gains=norm_gains[0],
        biases=norm_biases[0],
        proj_in=projection_in[0].reshape(width, 3 * head_width),
        in_bias=jnp.concatenate(
            [head_bias[0, 0], jnp.zeros((head_width,), jnp.float32), head_bias[0, 1]]
        ),
        proj_out=projection_out[0],
        residual=residual_bias[0],
        up=up_weight[0],
        up_bias=up_bias[0],
        down=down_weight[0],
        memory=memory_all,
        query_mem=query_memory[0],
        key_mem=key_memory[0],
        value_mem=value_memory[0],
    )
    ordinal = jnp.arange(segment)
    places = jnp.concatenate(
        [(ordinal + head_place * local_count) % segment, segment + jnp.arange(mem_count)]
    )
    allowed = (places[:, None] >= places[None, :])[None]

    positions = jnp.arange(seq_count)
    masks = []
    for micro in range(micro_total):
        if micro == 0:
            item = jnp.zeros((seq_count,), jnp.int32)
        else:
            ends = jnp.cumsum(short_items[micro - 1])
            item = jnp.sum((positions[:, None] >= ends[None, :]).astype(jnp.int32), axis=1)
        own_item = jnp.sum(jnp.where(positions == seq_place, item, 0))
        seen = jnp.logical_and(positions < seq_place, item == own_item).astype(jnp.float32)
        masks.append(jnp.repeat(seen, mem_count)[None, :])
    masks = jnp.stack(masks)

    tick_total = micro_total + sections - 1
    received = jnp.zeros_like(boundary_in[0, 0])
    records = []
    for tick in range(tick_total):
        micro = jnp.clip(tick - section, 0, micro_total - 1)
        local = jnp.where(section == 0, boundary_in[0, min(tick, micro_total - 1)], received)
        records.append(layer_forward(local, params, masks[micro], allowed))
        if tick + 1 < tick_total:
            received = passed_along(records[-1]["output"], "section", 1)
    back_received = jnp.zeros_like(boundary_in[0, 0])
    grads_input = []
    total = None
    for tick in range(tick_total):
        raw = tick - (sections - 1 - section)
        valid = jnp.logical_and(raw >= 0, raw < micro_total)
        micro = jnp.clip(raw, 0, micro_total - 1)
        grad = jnp.where(
            section == sections - 1, boundary_in[0, min(tick, micro_total - 1)], back_received
        )
        record = jax.tree.map(
            lambda *kinds: lax.select_n(section, *kinds),
            *[
                records[min(max(tick - (sections - 1 - place), 0), micro_total - 1) + place]
                for place in range(sections)
            ],
        )
        grad_x, sharded, shared = layer_backward(grad, record, params, masks[micro])
        fresh = jax.tree.map(lambda part: jnp.where(valid, part, 0.0), (sharded, shared))
        total = fresh if total is None else jax.tree.map(jnp.add, total, fresh)
        grads_input.append(grad_x)
        if tick + 1 < tick_total:
            back_received = passed_along(grad_x, "section", -1)
    sharded, shared = total
    grad_in, grad_heads_bias, grad_out, grad_up, grad_up_b, grad_down, grad_mem, grad_value = lax.psum(
        sharded, "seq"
    )
    grad_gains, grad_biases, grad_residual, grad_query, grad_key = lax.psum(shared, ("seq", "head"))
    finished_grads = jnp.stack(
        [grads_input[micro + sections - 1] for micro in range(micro_total)]
    )
    finished_outputs = jnp.stack(
        [records[micro + sections - 1]["output"] for micro in range(micro_total)]
    )
    boundary_out = jnp.where(section == 0, finished_grads, finished_outputs)[None]
    return (
        boundary_out,
        grad_gains[None],
        grad_biases[None],
        grad_in.reshape(projection_in.shape),
        grad_heads_bias[None],
        grad_out[None],
        grad_residual[None],
        grad_up[None],
        grad_up_b[None],
        grad_down[None],
        grad_mem[None],
        grad_query[None],
        grad_key[None],
        grad_value[None],
    )


def solution(mesh):
    return jax.shard_map(
        shards,
        mesh=mesh,
        in_specs=(
            P("section", None, ("seq", "head"), None),
            P(),
            P("section", None, None),
            P("section", None, None),
            P("section", None, None, "head"),
            P("section", None, "head"),
            P("section", "head", None),
            P("section", None, None),
            P("section", None, "head"),
            P("section", "head"),
            P("section", "head", None),
            P("section", "head", None),
            P("section", None, None),
            P("section", None, None),
            P("section", None, "head"),
        ),
        out_specs=(
            P("section", None, ("seq", "head"), None),
            P("section", None, None),
            P("section", None, None),
            P("section", None, None, "head"),
            P("section", None, "head"),
            P("section", "head", None),
            P("section", None, None),
            P("section", None, "head"),
            P("section", "head"),
            P("section", "head", None),
            P("section", "head", None),
            P("section", None, None),
            P("section", None, None),
            P("section", None, "head"),
        ),
        check_vma=False,
    )
```

```python
import functools
import math

import jax
import jax.numpy as jnp
from jax import lax
from jax.experimental import pallas as pl
from jax.experimental.pallas import tpu as pltpu
from jax.sharding import PartitionSpec as P

HEAD_DIM = 64
EPSILON = 1e-05
SCALE = 1.0 / math.sqrt(HEAD_DIM)
MESH = pl.DeviceIdType.MESH
VMEM = pl.BlockSpec(memory_space=pltpu.VMEM)
HBM = pl.BlockSpec(memory_space=pltpu.HBM)


def mm(left, right, dims=((1,), (0,))):
    return lax.dot_general(
        left, right, (dims, ((), ())), precision=lax.Precision.HIGH, preferred_element_type=jnp.float32
    )


def mm_nt(left, right):
    return mm(left, right, ((1,), (1,)))


def mm_tn(left, right):
    return mm(left, right, ((0,), (0,)))


def unit_rows(rows):
    centred = rows - jnp.mean(rows, axis=-1, keepdims=True)
    inverse = lax.rsqrt(jnp.mean(centred * centred, axis=-1, keepdims=True) + EPSILON)
    return centred * inverse, inverse


def unit_rows_back(d_unit, unit, inverse):
    return inverse * (
        d_unit
        - jnp.mean(d_unit, axis=-1, keepdims=True)
        - unit * jnp.mean(d_unit * unit, axis=-1, keepdims=True)
    )


def features(projected):
    halves = jnp.concatenate([jax.nn.softplus(projected), jax.nn.softplus(-projected)], axis=-1)
    return jnp.concatenate(
        [halves * jnp.roll(halves, rolled_by, axis=-1) for rolled_by in (1, 2, 3)], axis=-1
    )


def gelu_tanh(values_in):
    return jax.nn.gelu(values_in, approximate=True)


def barrier_with(pairs, wait_count):
    barrier = pltpu.get_barrier_semaphore()
    for condition, device in pairs:

        @pl.when(condition)
        def _(device=device):
            pl.semaphore_signal(barrier, inc=1, device_id=device, device_id_type=MESH)

    @pl.when(wait_count > 0)
    def _():
        pl.semaphore_wait(barrier, wait_count)


def runs_in(active):
    section = lax.axis_index("section")
    if len(active) == 1:
        return section == active[0]
    return section >= 0


def gather_kernel(active, block, keys, values, send_k, send_v, recv_k, recv_v):
    seq = lax.axis_index("seq")
    head = lax.axis_index("head")
    seqs, heads = lax.axis_size("seq"), lax.axis_size("head")
    mem = block.shape[0]
    dk = keys.shape[1]
    dv = values.shape[1] // heads
    keys[...] = jnp.zeros_like(keys)
    values[...] = jnp.zeros_like(values)

    def key_copy(source, target):
        return pltpu.make_async_remote_copy(
            src_ref=block.at[:, pl.ds(0, dk)],
            dst_ref=keys.at[pl.ds(pl.multiple_of(source * mem, mem), mem)],
            send_sem=send_k.at[target],
            recv_sem=recv_k.at[source],
            device_id={"seq": target},
            device_id_type=MESH,
        )

    def value_copy(source, source_head, target, target_head):
        return pltpu.make_async_remote_copy(
            src_ref=block.at[:, pl.ds(dk, dv)],
            dst_ref=values.at[
                pl.ds(pl.multiple_of(source * mem, mem), mem),
                pl.ds(pl.multiple_of(source_head * dv, 128), dv),
            ],
            send_sem=send_v.at[target, target_head],
            recv_sem=recv_v.at[source, source_head],
            device_id={"seq": target, "head": target_head},
            device_id_type=MESH,
        )

    @pl.when(runs_in(active))
    def _():
        barrier_with(
            [
                (other < seq, {"seq": other, "head": place})
                for other in range(seqs)
                for place in range(heads)
            ],
            (seqs - 1 - seq) * heads,
        )
        for other in range(seqs):

            @pl.when(other > seq)
            def _(other=other):
                key_copy(seq, other).start()
                for place in range(heads):
                    value_copy(seq, head, other, place).start()

        for other in range(seqs):

            @pl.when(other < seq)
            def _(other=other):
                key_copy(other, other).wait_recv()
                for place in range(heads):
                    value_copy(other, place, other, place).wait_recv()

        for other in range(seqs):

            @pl.when(other > seq)
            def _(other=other):
                key_copy(seq, other).wait_send()
                for place in range(heads):
                    value_copy(seq, head, other, place).wait_send()


def gather_memory(key_proj, values, active, number):
    seqs, heads = lax.axis_size("seq"), lax.axis_size("head")
    mem, dk = key_proj.shape
    dv = values.shape[1]
    if heads != 2:
        return (
            lax.all_gather(key_proj, "seq", axis=0, tiled=True),
            lax.all_gather(
                lax.all_gather(values, "seq", axis=0, tiled=True), "head", axis=1, tiled=True
            ),
        )
    return pl.pallas_call(
        functools.partial(gather_kernel, active),
        out_shape=(
            jax.ShapeDtypeStruct((seqs * mem, dk), jnp.float32),
            jax.ShapeDtypeStruct((seqs * mem, heads * dv), jnp.float32),
        ),
        in_specs=[VMEM],
        out_specs=(VMEM, VMEM),
        scratch_shapes=[
            pltpu.SemaphoreType.DMA((seqs,)),
            pltpu.SemaphoreType.DMA((seqs, heads)),
            pltpu.SemaphoreType.DMA((seqs,)),
            pltpu.SemaphoreType.DMA((seqs, heads)),
        ],
        compiler_params=pltpu.CompilerParams(collective_id=number, has_side_effects=True),
    )(jnp.concatenate([key_proj, values], axis=1))


def scatter_kernel(active, d_keys, d_values, out_k, out_v, from_k, from_v, send_k, send_v, recv_k, recv_v):
    seq = lax.axis_index("seq")
    head = lax.axis_index("head")
    seqs, heads = lax.axis_size("seq"), lax.axis_size("head")
    mem, dk = out_k.shape
    dv = out_v.shape[1]
    from_k[...] = jnp.zeros_like(from_k)
    from_v[...] = jnp.zeros_like(from_v)

    def key_copy(source, target):
        return pltpu.make_async_remote_copy(
            src_ref=d_keys.at[pl.ds(pl.multiple_of(target * mem, mem), mem)],
            dst_ref=from_k.at[source],
            send_sem=send_k.at[target],
            recv_sem=recv_k.at[source],
            device_id={"seq": target},
            device_id_type=MESH,
        )

    def value_copy(source, source_head, target, target_head):
        return pltpu.make_async_remote_copy(
            src_ref=d_values.at[
                pl.ds(pl.multiple_of(target * mem, mem), mem),
                pl.ds(pl.multiple_of(target_head * dv, 128), dv),
            ],
            dst_ref=from_v.at[source, source_head],
            send_sem=send_v.at[target, target_head],
            recv_sem=recv_v.at[source, source_head],
            device_id={"seq": target, "head": target_head},
            device_id_type=MESH,
        )

    @pl.when(runs_in(active))
    def _():
        barrier_with(
            [
                (other > seq, {"seq": other, "head": place})
                for other in range(seqs)
                for place in range(heads)
            ],
            seq * heads,
        )
        for other in range(seqs):

            @pl.when(other < seq)
            def _(other=other):
                key_copy(seq, other).start()
                for place in range(heads):
                    value_copy(seq, head, other, place).start()

        for other in range(seqs):

            @pl.when(other > seq)
            def _(other=other):
                key_copy(other, other).wait_recv()
                for place in range(heads):
                    value_copy(other, place, other, place).wait_recv()

        for other in range(seqs):

            @pl.when(other < seq)
            def _(other=other):
                key_copy(seq, other).wait_send()
                for place in range(heads):
                    value_copy(seq, head, other, place).wait_send()

    out_k[...] = jnp.sum(from_k[...], axis=0)
    out_v[...] = jnp.sum(from_v[...], axis=(0, 1))


def scatter_memory(d_keys, d_values, active, number):
    seqs, heads = lax.axis_size("seq"), lax.axis_size("head")
    mem = d_keys.shape[0] // seqs
    dk = d_keys.shape[1]
    dv = d_values.shape[1] // heads
    if heads != 2:
        d_values = lax.psum_scatter(d_values, "head", scatter_dimension=1, tiled=True)
        return (
            lax.psum_scatter(d_keys, "seq", scatter_dimension=0, tiled=True),
            lax.psum_scatter(d_values, "seq", scatter_dimension=0, tiled=True),
        )
    return pl.pallas_call(
        functools.partial(scatter_kernel, active),
        out_shape=(
            jax.ShapeDtypeStruct((mem, dk), jnp.float32),
            jax.ShapeDtypeStruct((mem, dv), jnp.float32),
        ),
        in_specs=[VMEM, VMEM],
        out_specs=(VMEM, VMEM),
        scratch_shapes=[
            pltpu.VMEM((seqs, mem, dk), jnp.float32),
            pltpu.VMEM((seqs, heads, mem, dv), jnp.float32),
            pltpu.SemaphoreType.DMA((seqs,)),
            pltpu.SemaphoreType.DMA((seqs, heads)),
            pltpu.SemaphoreType.DMA((seqs,)),
            pltpu.SemaphoreType.DMA((seqs, heads)),
        ],
        compiler_params=pltpu.CompilerParams(collective_id=number, has_side_effects=True),
    )(d_keys, d_values)


def ring_kernel(active, lanes, count, aliased, *refs):
    arrays = refs[:count]
    refs = refs[count + (count if aliased else 0) :]
    sums = refs[:count]
    held = refs[count : 2 * count]
    send, recv, local = refs[2 * count :]
    seqs = lax.axis_size("seq")
    along = seqs // lanes
    seq = lax.axis_index("seq")
    z, y = seq // lanes, lax.rem(seq, lanes)
    place = y * along + jnp.where(lax.rem(y, 2) == 0, z, along - 1 - z)

    def device(spot):
        row = spot // along
        column = lax.rem(spot, along)
        column = jnp.where(lax.rem(row, 2) == 0, column, along - 1 - column)
        return {"seq": column * lanes + row}

    targets = (device(lax.rem(place + 1, seqs)), device(lax.rem(place + seqs - 1, seqs)))
    signs = (1, -1)

    def block(ref, way, spot):
        rows = ref.shape[0] // seqs
        half = rows // 2
        spot = lax.rem(spot + 2 * seqs, seqs)
        return ref.at[pl.ds(pl.multiple_of(spot * rows + way * half, half), half)]

    def copy(source, target, way, index, step):
        return pltpu.make_async_remote_copy(
            src_ref=source,
            dst_ref=target,
            send_sem=send.at[step, way, index],
            recv_sem=recv.at[step, way, index],
            device_id=targets[way],
            device_id_type=MESH,
        )

    ways = [(index, way) for index in range(count) for way in range(2)]
    last = seqs - 2

    @pl.when(runs_in(active))
    def _():
        barrier_with([(place >= 0, targets[0]), (place >= 0, targets[1])], place * 0 + 2)
        for index, way in ways:
            copy(block(arrays[index], way, place), held[index].at[way, 0], way, index, 0).start()

        def forward(step, carry):
            for index, way in ways:
                got = held[index].at[way, step - 1]
                copy(got, got, way, index, step - 1).wait_recv()
                got[...] += block(arrays[index], way, place - signs[way] * step)[...]
                copy(got, held[index].at[way, step], way, index, step).start()
            return carry

        lax.fori_loop(1, seqs - 1, forward, 0)
        for index, way in ways:
            got = held[index].at[way, last]
            copy(got, got, way, index, last).wait_recv()
            spot = place + signs[way]
            got[...] += block(arrays[index], way, spot)[...]
            home = block(sums[index], way, spot)
            copy(got, home, way, index, seqs - 1).start()
            pltpu.make_async_copy(got, home, local.at[way, index]).start()

        def onward(step, carry):
            for index, way in ways:
                got = block(sums[index], way, place - signs[way] * (step - 1))
                copy(got, got, way, index, seqs - 1 + step - 1).wait_recv()
                copy(got, got, way, index, seqs - 1 + step).start()
            return carry

        lax.fori_loop(1, seqs - 1, onward, 0)
        for index, way in ways:
            got = block(sums[index], way, place - signs[way] * last)
            copy(got, got, way, index, 2 * seqs - 3).wait_recv()
            own = held[index].at[way, last]
            pltpu.make_async_copy(
                own, block(sums[index], way, place + signs[way]), local.at[way, index]
            ).wait()

        def sent(step, carry):
            for index, way in ways:
                own = held[index].at[way, 0]
                copy(own, own, way, index, step).wait_send()
            return carry

        lax.fori_loop(0, 2 * seqs - 2, sent, 0)


def ring_sum(arrays, before, active, lanes, number):
    seqs = lax.axis_size("seq")
    count = len(arrays)
    aliased = before is not None
    if lax.axis_size("head") != 2:
        sums = tuple(lax.psum(a, "seq") for a in arrays)
        if not aliased:
            return sums
        return tuple(jnp.where(runs_in(active), a, b) for a, b in zip(sums, before))
    shapes = tuple(jax.ShapeDtypeStruct(a.shape, a.dtype) for a in arrays)
    nbytes = sum(a.size * 4 for a in arrays)
    return pl.pallas_call(
        functools.partial(ring_kernel, active, lanes, count, aliased),
        out_shape=shapes,
        in_specs=[VMEM] * count + ([HBM] * count if aliased else []),
        out_specs=(HBM,) * count,
        input_output_aliases={count + i: i for i in range(count)} if aliased else {},
        scratch_shapes=[
            pltpu.VMEM((2, seqs - 1, a.shape[0] // (2 * seqs), a.shape[1]), jnp.float32)
            for a in arrays
        ]
        + [
            pltpu.SemaphoreType.DMA((2 * seqs - 2, 2, count)),
            pltpu.SemaphoreType.DMA((2 * seqs - 2, 2, count)),
            pltpu.SemaphoreType.DMA((2, count)),
        ],
        compiler_params=pltpu.CompilerParams(
            collective_id=number, has_side_effects=True, vmem_limit_bytes=48 << 20
        ),
        cost_estimate=pl.CostEstimate(flops=0, bytes_accessed=20 * nbytes, transcendentals=0),
    )(*arrays, *(before or ()))


def swap(value, active):
    pairs = [(2 * s + h, 2 * s + 1 - h) for s in active for h in range(2)]
    return lax.ppermute(value, ("section", "head"), pairs)


def head_sum(value, active):
    if lax.axis_size("head") == 2:
        return value + swap(value, active)
    return lax.psum(value, "head")


def head_sum_rows(rows, share, active):
    count = lax.axis_size("head")
    segment = count * share
    if count == 2:
        other = swap(rows, active)
        return rows + jnp.concatenate(
            [other[share:segment], other[:share], other[segment:]], axis=0
        )
    turn = lax.axis_index("head") * share
    total = lax.psum(
        jnp.concatenate([jnp.roll(rows[:segment], turn, axis=0), rows[segment:]], axis=0), "head"
    )
    return jnp.concatenate([jnp.roll(total[:segment], -turn, axis=0), total[segment:]], axis=0)


def head_rows(local, active):
    count = lax.axis_size("head")
    if count == 2:
        return jnp.concatenate([local, swap(local, active)], axis=0)
    gathered = lax.all_gather(local, "head", axis=0, tiled=True)
    return jnp.roll(gathered, -lax.axis_index("head") * local.shape[0], axis=0)


def head_scatter(rows, active):
    count = lax.axis_size("head")
    share = rows.shape[0] // count
    if count == 2:
        return rows[:share] + swap(rows[share:], active)
    placed = jnp.roll(rows, lax.axis_index("head") * share, axis=0)
    return lax.psum_scatter(placed, "head", scatter_dimension=0, tiled=True)


def heads_of(part):
    return part.reshape(part.shape[0], -1, HEAD_DIM).transpose(1, 0, 2)


def rows_of(part):
    return part.transpose(1, 0, 2).reshape(part.shape[1], -1)


def bmm(left, right, left_dim, right_dim):
    return lax.dot_general(
        left,
        right,
        (((left_dim,), (right_dim,)), ((0,), (0,))),
        precision=lax.Precision.HIGH,
        preferred_element_type=jnp.float32,
    )


def layer_forward(local, params, mask, allowed, active, tick):
    width = local.shape[1]
    local_count = local.shape[0]
    segment = lax.axis_size("head") * local_count
    rows = jnp.concatenate([head_rows(local, active), params["memory"]], axis=0)
    unit_one, inverse_one = unit_rows(rows)
    normed = unit_one * params["gains"][0] + params["biases"][0]
    projected = mm(normed, params["proj_in"]) + params["in_bias"]
    share = projected.shape[1] // 3
    query, key, value = (heads_of(projected[:, i * share : (i + 1) * share]) for i in range(3))
    scores = jnp.where(allowed, bmm(query, key, 2, 2) * SCALE, -1e30)
    row_top = jnp.max(scores, axis=-1, keepdims=True)
    exponent = jnp.exp(scores - row_top)
    soft = exponent / jnp.sum(exponent, axis=-1, keepdims=True)
    attended = rows_of(bmm(soft, value, 2, 1))
    hidden = rows + head_sum_rows(mm(attended, params["proj_out"]), local_count, active) + params["residual"][0]
    unit_two, inverse_two = unit_rows(hidden)
    mixed = unit_two * params["gains"][1] + params["biases"][1]
    inner_pre = mm(mixed, params["up"]) + params["up_bias"]
    inner_act = gelu_tanh(inner_pre)
    partial = mm(inner_act, params["down"])
    out_local = head_scatter(partial[:segment], active) + hidden[:local_count] + params["residual"][1]
    out_mem = head_sum(partial[segment:], active) + hidden[segment:] + params["residual"][1]
    key_proj = mm(out_mem, params["key_mem"])
    values = mm(out_mem, params["value_mem"])
    keys_all, values_all = gather_memory(key_proj, values, active, tick)
    key_feats = features(keys_all)
    query_proj = mm(out_local, params["query_mem"])
    query_feats = features(query_proj)
    weights = mask * mm_nt(query_feats, key_feats)
    denominator = jnp.sum(weights, axis=1, keepdims=True) + 1.0
    read = mm(weights, values_all) / denominator
    return dict(
        unit_one=unit_one,
        inverse_one=inverse_one,
        projected=projected,
        attended=attended,
        soft=soft,
        unit_two=unit_two,
        inverse_two=inverse_two,
        inner_pre=inner_pre,
        out_local=out_local,
        out_mem=out_mem,
        keys_all=keys_all,
        values_all=values_all,
        query_proj=query_proj,
        weights=weights,
        denominator=denominator,
        read=read,
        output=out_local + read,
    )


def layer_backward(grad, record, params, mask, active, tick):
    head_count = lax.axis_size("head")
    rows_total = record["unit_one"].shape[0]
    local_count = grad.shape[0]
    segment = head_count * local_count
    denominator = record["denominator"]
    d_numer = grad / denominator
    d_denom = -jnp.sum(grad * record["read"], axis=1, keepdims=True) / denominator
    d_weights = mask * (mm_nt(d_numer, record["values_all"]) + d_denom)
    key_feats, keys_back = jax.vjp(features, record["keys_all"])
    query_feats, query_back = jax.vjp(features, record["query_proj"])
    d_query_proj = query_back(mm(d_weights, key_feats))[0]
    d_keys = keys_back(mm_tn(d_weights, query_feats))[0]
    d_values = mm_tn(record["weights"], d_numer)
    d_key_proj, d_value = scatter_memory(d_keys, d_values, active, tick)
    d_mem = head_sum(mm_nt(d_key_proj, params["key_mem"]) + mm_nt(d_value, params["value_mem"]), active)
    d_local = grad + mm_nt(d_query_proj, params["query_mem"])
    d_result = jnp.concatenate([head_rows(d_local, active), d_mem], axis=0)
    inner_act, gelu_back = jax.vjp(gelu_tanh, record["inner_pre"])
    grad_down = mm_tn(inner_act, d_result)
    d_pre = gelu_back(mm_nt(d_result, params["down"]))[0]
    gains, biases = params["gains"], params["biases"]
    mixed = record["unit_two"] * gains[1] + biases[1]
    grad_up = mm_tn(mixed, d_pre)
    d_mixed = head_sum_rows(mm_nt(d_pre, params["up"]), local_count, active)
    d_hidden = d_result + unit_rows_back(d_mixed * gains[1], record["unit_two"], record["inverse_two"])
    grad_out = mm_tn(record["attended"], d_hidden)
    d_attended = mm_nt(d_hidden, params["proj_out"])
    share = d_attended.shape[1]
    query, key, value = (
        heads_of(record["projected"][:, i * share : (i + 1) * share]) for i in range(3)
    )
    soft = record["soft"]
    d_heads = heads_of(d_attended)
    inner_dot = jnp.sum(d_heads * heads_of(record["attended"]), axis=-1, keepdims=True)
    d_scores = soft * (bmm(d_heads, value, 2, 2) - inner_dot) * SCALE
    d_projected = jnp.concatenate(
        [
            rows_of(bmm(d_scores, key, 2, 1)),
            rows_of(bmm(d_scores, query, 1, 1)),
            rows_of(bmm(soft, d_heads, 1, 1)),
        ],
        axis=1,
    )
    normed = record["unit_one"] * gains[0] + biases[0]
    grad_in = mm_tn(normed, d_projected)
    columns = jnp.sum(d_projected, axis=0)
    grad_head_bias = jnp.stack([columns[:share], columns[2 * share :]])
    d_normed_all = mm_nt(d_projected, params["proj_in"])
    d_normed = head_scatter(d_normed_all[:segment], active)
    mem_count = (rows_total - segment) // head_count
    own_mem = lax.axis_index("head") * mem_count
    d_normed_mem = lax.dynamic_slice_in_dim(
        head_sum(d_normed_all[segment:], active), own_mem, mem_count, 0
    )
    own_mem = segment + own_mem

    def own(values):
        return jnp.concatenate(
            [values[:local_count], lax.dynamic_slice_in_dim(values, own_mem, mem_count, 0)], axis=0
        )

    d_normed_own = jnp.concatenate([d_normed, d_normed_mem], axis=0)
    unit_own = own(record["unit_one"])
    d_rows = own(d_hidden) + unit_rows_back(
        d_normed_own * gains[0], unit_own, own(record["inverse_one"])
    )
    part = 1.0 / head_count
    sharded = (
        grad_in,
        grad_head_bias,
        grad_out,
        grad_up,
        jnp.sum(d_pre, axis=0),
        grad_down,
        d_rows[local_count:],
        mm_tn(record["out_mem"], d_value),
    )
    shared = (
        jnp.stack(
            [
                jnp.sum(d_normed_own * unit_own, axis=0),
                part * jnp.sum(d_mixed * record["unit_two"], axis=0),
            ]
        ),
        jnp.stack([jnp.sum(d_normed_own, axis=0), part * jnp.sum(d_mixed, axis=0)]),
        part * jnp.stack([jnp.sum(d_hidden, axis=0), jnp.sum(d_result, axis=0)]),
        mm_tn(record["out_local"], d_query_proj),
        mm_tn(record["out_mem"], d_key_proj),
    )
    return (d_rows[:local_count], sharded, shared)


def passed_along(value, axis, steps):
    count = lax.axis_size(axis)
    first, last = (max(0, -steps), min(count, count - steps))
    return lax.ppermute(value, axis, [(source, source + steps) for source in range(first, last)])


def pack_gradients(sharded, shared, active):
    grad_in, grad_heads_bias, grad_out, grad_up, grad_up_b, grad_down, grad_mem, grad_value = sharded
    gains, biases, residual, grad_query, grad_key = shared
    first = lax.axis_index("head") == 0
    few = (gains, biases, residual)
    few_flat = jnp.concatenate([part.reshape(-1) for part in few]).reshape(-1, 128)
    few_flat = head_sum(few_flat, active)
    if lax.axis_size("head") == 2:
        own_whole = jnp.where(first, grad_query, grad_key)
        own_whole = own_whole + swap(jnp.where(first, grad_key, grad_query), active)
    else:
        own_whole = lax.psum(jnp.concatenate([grad_query, grad_key], axis=0), "head")
    rest = (grad_heads_bias, grad_up_b, grad_mem)
    small = jnp.concatenate([few_flat] + [part.reshape(-1, 128) for part in rest], axis=0)
    unit = 16 * lax.axis_size("seq")
    small_rows = small.shape[0]
    small = jnp.pad(small, ((0, -small_rows % unit), (0, 0)))
    arrays = (grad_down, grad_up, grad_out, grad_in, grad_value, own_whole, small)

    def unpack(finished):
        down, up, out, proj_in, value, whole, small = finished
        if lax.axis_size("head") == 2:
            other = swap(whole, range(lax.axis_size("section")))
            query, key = jnp.where(first, whole, other), jnp.where(first, other, whole)
        else:
            query, key = jnp.split(whole, 2, axis=0)
        parts, at = [], 0
        for part in few + rest:
            rows = part.size // 128
            parts.append(small[at : at + rows].reshape(part.shape))
            at += rows
        gains, biases, residual, heads_bias, up_b, mem = parts
        return (
            proj_in, heads_bias, out, up, up_b, down, mem, value, gains, biases, residual, query, key
        )

    return arrays, unpack


def shards(
    boundary_in,
    short_items,
    norm_gains,
    norm_biases,
    projection_in,
    head_bias,
    projection_out,
    residual_bias,
    up_weight,
    up_bias,
    down_weight,
    memory_tokens,
    query_memory,
    key_memory,
    value_memory,
):
    section = lax.axis_index("section")
    sections = lax.axis_size("section")
    head_count = lax.axis_size("head")
    head_place = lax.axis_index("head")
    seq_count = lax.axis_size("seq")
    seq_place = lax.axis_index("seq")
    micro_total = boundary_in.shape[1]
    local_count = boundary_in.shape[2]
    width = boundary_in.shape[3]
    segment = head_count * local_count
    head_width = projection_in.shape[3]
    memory_all = lax.all_gather(memory_tokens[0], "head", axis=0, tiled=True)
    mem_count = memory_all.shape[0]
    params = dict(
        gains=norm_gains[0],
        biases=norm_biases[0],
        proj_in=projection_in[0].reshape(width, 3 * head_width),
        in_bias=jnp.concatenate(
            [head_bias[0, 0], jnp.zeros((head_width,), jnp.float32), head_bias[0, 1]]
        ),
        proj_out=projection_out[0],
        residual=residual_bias[0],
        up=up_weight[0],
        up_bias=up_bias[0],
        down=down_weight[0],
        memory=memory_all,
        query_mem=query_memory[0],
        key_mem=key_memory[0],
        value_mem=value_memory[0],
    )
    ordinal = jnp.arange(segment)
    places = jnp.concatenate(
        [(ordinal + head_place * local_count) % segment, segment + jnp.arange(mem_count)]
    )
    allowed = (places[:, None] >= places[None, :])[None]

    positions = jnp.arange(seq_count)
    masks = []
    for micro in range(micro_total):
        if micro == 0:
            item = jnp.zeros((seq_count,), jnp.int32)
        else:
            ends = jnp.cumsum(short_items[micro - 1])
            item = jnp.sum((positions[:, None] >= ends[None, :]).astype(jnp.int32), axis=1)
        own_item = jnp.sum(jnp.where(positions == seq_place, item, 0))
        seen = jnp.logical_and(positions < seq_place, item == own_item).astype(jnp.float32)
        masks.append(jnp.repeat(seen, mem_count)[None, :])
    masks = jnp.stack(masks)

    tick_total = micro_total + sections - 1
    received = jnp.zeros_like(boundary_in[0, 0])
    records = []
    for tick in range(tick_total):
        micro = jnp.clip(tick - section, 0, micro_total - 1)
        local = jnp.where(section == 0, boundary_in[0, min(tick, micro_total - 1)], received)
        active = [place for place in range(sections) if 0 <= tick - place < micro_total]
        records.append(layer_forward(local, params, masks[micro], allowed, active, tick))
        if tick + 1 < tick_total:
            received = passed_along(records[-1]["output"], "section", 1)
    back_received = jnp.zeros_like(boundary_in[0, 0])
    grads_input = []
    total = None
    finished = None
    for tick in range(tick_total):
        raw = tick - (sections - 1 - section)
        valid = jnp.logical_and(raw >= 0, raw < micro_total)
        micro = jnp.clip(raw, 0, micro_total - 1)
        grad = jnp.where(
            section == sections - 1, boundary_in[0, min(tick, micro_total - 1)], back_received
        )
        record = jax.tree.map(
            lambda *kinds: lax.select_n(section, *kinds),
            *[
                records[min(max(tick - (sections - 1 - place), 0), micro_total - 1) + place]
                for place in range(sections)
            ],
        )
        active = [
            place for place in range(sections) if 0 <= tick - (sections - 1 - place) < micro_total
        ]
        grad_x, sharded, shared = layer_backward(
            grad, record, params, masks[micro], active, tick_total + tick
        )
        fresh = jax.tree.map(lambda part: jnp.where(valid, part, 0.0), (sharded, shared))
        total = fresh if total is None else jax.tree.map(jnp.add, total, fresh)
        grads_input.append(grad_x)
        if tick + 1 < tick_total:
            back_received = passed_along(grad_x, "section", -1)
        if tick >= micro_total - 1:
            done = sections - 1 - (tick - (micro_total - 1))
            arrays, unpack = pack_gradients(*total, [done])
            finished = ring_sum(arrays, finished, [done], head_count, 2 * tick_total + done)
            if tick + 1 < tick_total:
                back_received, finished = lax.optimization_barrier((back_received, finished))
    (
        grad_in,
        grad_heads_bias,
        grad_out,
        grad_up,
        grad_up_b,
        grad_down,
        grad_mem,
        grad_value,
        grad_gains,
        grad_biases,
        grad_residual,
        grad_query,
        grad_key,
    ) = unpack(finished)
    finished_grads = jnp.stack(
        [grads_input[micro + sections - 1] for micro in range(micro_total)]
    )
    finished_outputs = jnp.stack(
        [records[micro + sections - 1]["output"] for micro in range(micro_total)]
    )
    boundary_out = jnp.where(section == 0, finished_grads, finished_outputs)[None]
    return (
        boundary_out,
        grad_gains[None],
        grad_biases[None],
        grad_in.reshape(projection_in.shape),
        grad_heads_bias[None],
        grad_out[None],
        grad_residual[None],
        grad_up[None],
        grad_up_b[None],
        grad_down[None],
        grad_mem[None],
        grad_query[None],
        grad_key[None],
        grad_value[None],
    )


def solution(mesh):
    return jax.shard_map(
        shards,
        mesh=mesh,
        in_specs=(
            P("section", None, ("seq", "head"), None),
            P(),
            P("section", None, None),
            P("section", None, None),
            P("section", None, None, "head"),
            P("section", None, "head"),
            P("section", "head", None),
            P("section", None, None),
            P("section", None, "head"),
            P("section", "head"),
            P("section", "head", None),
            P("section", "head", None),
            P("section", None, None),
            P("section", None, None),
            P("section", None, "head"),
        ),
        out_specs=(
            P("section", None, ("seq", "head"), None),
            P("section", None, None),
            P("section", None, None),
            P("section", None, None, "head"),
            P("section", None, "head"),
            P("section", "head", None),
            P("section", None, None),
            P("section", None, "head"),
            P("section", "head"),
            P("section", "head", None),
            P("section", "head", None),
            P("section", None, None),
            P("section", None, None),
            P("section", None, "head"),
        ),
        check_vma=False,
    )
```

```python
import functools
import math

import jax
import jax.numpy as jnp
from jax import lax
from jax.experimental import pallas as pl
from jax.experimental.pallas import tpu as pltpu
from jax.sharding import PartitionSpec as P

HEAD_DIM = 64
EPSILON = 1e-05
SCALE = 1.0 / math.sqrt(HEAD_DIM)
MESH = pl.DeviceIdType.MESH
VMEM = pl.BlockSpec(memory_space=pltpu.VMEM)
HBM = pl.BlockSpec(memory_space=pltpu.HBM)
SMEM = pl.BlockSpec(memory_space=pltpu.SMEM)
SHARED_ROWS = 36


def mm(left, right, dims=((1,), (0,))):
    return lax.dot_general(
        left, right, (dims, ((), ())), precision=lax.Precision.HIGH, preferred_element_type=jnp.float32
    )


def mm_nt(left, right):
    return mm(left, right, ((1,), (1,)))


def mm_tn(left, right):
    return mm(left, right, ((0,), (0,)))


def unit_rows(rows):
    centred = rows - jnp.mean(rows, axis=-1, keepdims=True)
    inverse = lax.rsqrt(jnp.mean(centred * centred, axis=-1, keepdims=True) + EPSILON)
    return centred * inverse, inverse


def unit_rows_back(d_unit, unit, inverse):
    return inverse * (
        d_unit
        - jnp.mean(d_unit, axis=-1, keepdims=True)
        - unit * jnp.mean(d_unit * unit, axis=-1, keepdims=True)
    )


def features(projected):
    halves = jnp.concatenate([jax.nn.softplus(projected), jax.nn.softplus(-projected)], axis=-1)
    return jnp.concatenate(
        [halves * jnp.roll(halves, rolled_by, axis=-1) for rolled_by in (1, 2, 3)], axis=-1
    )


def gelu_tanh(values_in):
    return jax.nn.gelu(values_in, approximate=True)


def head_sum_rows(rows, share):
    segment = lax.axis_size("head") * share
    turn = lax.axis_index("head") * share
    total = lax.psum(
        jnp.concatenate([jnp.roll(rows[:segment], turn, axis=0), rows[segment:]], axis=0), "head"
    )
    return jnp.concatenate([jnp.roll(total[:segment], -turn, axis=0), total[segment:]], axis=0)


def head_rows(local):
    gathered = lax.all_gather(local, "head", axis=0, tiled=True)
    return jnp.roll(gathered, -lax.axis_index("head") * local.shape[0], axis=0)


def head_scatter(rows):
    share = rows.shape[0] // lax.axis_size("head")
    placed = jnp.roll(rows, lax.axis_index("head") * share, axis=0)
    return lax.psum_scatter(placed, "head", scatter_dimension=0, tiled=True)


def heads_of(part):
    return part.reshape(part.shape[0], -1, HEAD_DIM).transpose(1, 0, 2)


def rows_of(part):
    return part.transpose(1, 0, 2).reshape(part.shape[1], -1)


def bmm(left, right, left_dim, right_dim):
    return lax.dot_general(
        left,
        right,
        (((left_dim,), (right_dim,)), ((0,), (0,))),
        precision=lax.Precision.HIGH,
        preferred_element_type=jnp.float32,
    )


def layer_forward(local, params, mask, allowed):
    width = local.shape[1]
    local_count = local.shape[0]
    segment = lax.axis_size("head") * local_count
    rows = jnp.concatenate([head_rows(local), params["memory"]], axis=0)
    unit_one, inverse_one = unit_rows(rows)
    normed = unit_one * params["gains"][0] + params["biases"][0]
    projected = mm(normed, params["proj_in"]) + params["in_bias"]
    share = projected.shape[1] // 3
    query, key, value = (heads_of(projected[:, i * share : (i + 1) * share]) for i in range(3))
    scores = jnp.where(allowed, bmm(query, key, 2, 2) * SCALE, -1e30)
    row_top = jnp.max(scores, axis=-1, keepdims=True)
    exponent = jnp.exp(scores - row_top)
    soft = exponent / jnp.sum(exponent, axis=-1, keepdims=True)
    attended = rows_of(bmm(soft, value, 2, 1))
    hidden = rows + head_sum_rows(mm(attended, params["proj_out"]), local_count) + params["residual"][0]
    unit_two, inverse_two = unit_rows(hidden)
    mixed = unit_two * params["gains"][1] + params["biases"][1]
    inner_pre = mm(mixed, params["up"]) + params["up_bias"]
    inner_act = gelu_tanh(inner_pre)
    partial = mm(inner_act, params["down"])
    out_local = head_scatter(partial[:segment]) + hidden[:local_count] + params["residual"][1]
    out_mem = lax.psum(partial[segment:], "head") + hidden[segment:] + params["residual"][1]
    key_proj = mm(out_mem, params["key_mem"])
    values = mm(out_mem, params["value_mem"])
    gathered = lax.all_gather(jnp.concatenate([key_proj, values], axis=1), "seq", axis=0, tiled=True)
    dk = key_proj.shape[1]
    keys_all = gathered[:, :dk]
    values_all = lax.all_gather(gathered[:, dk:], "head", axis=1, tiled=True)
    key_feats = features(keys_all)
    query_proj = mm(out_local, params["query_mem"])
    query_feats = features(query_proj)
    weights = mask * mm_nt(query_feats, key_feats)
    denominator = jnp.sum(weights, axis=1, keepdims=True) + 1.0
    read = mm(weights, values_all) / denominator
    return dict(
        unit_one=unit_one,
        inverse_one=inverse_one,
        projected=projected,
        attended=attended,
        soft=soft,
        unit_two=unit_two,
        inverse_two=inverse_two,
        inner_pre=inner_pre,
        out_local=out_local,
        out_mem=out_mem,
        keys_all=keys_all,
        values_all=values_all,
        query_proj=query_proj,
        weights=weights,
        denominator=denominator,
        read=read,
        output=out_local + read,
    )


def layer_backward(grad, record, params, mask):
    head_count = lax.axis_size("head")
    seq_count = lax.axis_size("seq")
    width = grad.shape[1]
    local_count = grad.shape[0]
    segment = head_count * local_count
    denominator = record["denominator"]
    d_numer = grad / denominator
    d_denom = -jnp.sum(grad * record["read"], axis=1, keepdims=True) / denominator
    d_weights = mask * (mm_nt(d_numer, record["values_all"]) + d_denom)
    key_feats, keys_back = jax.vjp(features, record["keys_all"])
    query_feats, query_back = jax.vjp(features, record["query_proj"])
    d_query_proj = query_back(mm(d_weights, key_feats))[0]
    d_keys = keys_back(mm_tn(d_weights, query_feats))[0]
    d_values = mm_tn(record["weights"], d_numer)
    d_memory = lax.psum_scatter(
        jnp.concatenate([d_keys, d_values], axis=1), "seq", scatter_dimension=0, tiled=True
    )
    dk = d_keys.shape[1]
    d_key_proj = d_memory[:, :dk]
    d_value = lax.psum_scatter(
        d_memory[:, dk:], "head", scatter_dimension=1, tiled=True
    )
    d_mem = lax.psum(
        mm_nt(d_key_proj, params["key_mem"]) + mm_nt(d_value, params["value_mem"]), "head"
    )
    d_local = grad + mm_nt(d_query_proj, params["query_mem"])
    d_result = jnp.concatenate([head_rows(d_local), d_mem], axis=0)
    inner_act, gelu_back = jax.vjp(gelu_tanh, record["inner_pre"])
    grad_down = mm_tn(inner_act, d_result)
    d_pre = gelu_back(mm_nt(d_result, params["down"]))[0]
    gains, biases = params["gains"], params["biases"]
    mixed = record["unit_two"] * gains[1] + biases[1]
    grad_up = mm_tn(mixed, d_pre)
    d_mixed = head_sum_rows(mm_nt(d_pre, params["up"]), local_count)
    d_hidden = d_result + unit_rows_back(d_mixed * gains[1], record["unit_two"], record["inverse_two"])
    grad_out = mm_tn(record["attended"], d_hidden)
    d_attended = mm_nt(d_hidden, params["proj_out"])
    share = d_attended.shape[1]
    query, key, value = (
        heads_of(record["projected"][:, i * share : (i + 1) * share]) for i in range(3)
    )
    soft = record["soft"]
    d_heads = heads_of(d_attended)
    inner_dot = jnp.sum(d_heads * heads_of(record["attended"]), axis=-1, keepdims=True)
    d_scores = soft * (bmm(d_heads, value, 2, 2) - inner_dot) * SCALE
    d_projected = jnp.concatenate(
        [
            rows_of(bmm(d_scores, key, 2, 1)),
            rows_of(bmm(d_scores, query, 1, 1)),
            rows_of(bmm(soft, d_heads, 1, 1)),
        ],
        axis=1,
    )
    normed = record["unit_one"] * gains[0] + biases[0]
    grad_in = mm_tn(normed, d_projected)
    columns = jnp.sum(d_projected, axis=0)
    grad_head_bias = jnp.stack([columns[:share], columns[2 * share :]])
    d_normed_all = mm_nt(d_projected, params["proj_in"])
    d_normed = head_scatter(d_normed_all[:segment])
    d_normed_mem = lax.psum_scatter(
        d_normed_all[segment:], "head", scatter_dimension=0, tiled=True
    )
    mem_count = d_normed_mem.shape[0]
    own_mem = segment + lax.axis_index("head") * mem_count

    def own(values):
        return jnp.concatenate(
            [values[:local_count], lax.dynamic_slice_in_dim(values, own_mem, mem_count, 0)], axis=0
        )

    d_normed_own = jnp.concatenate([d_normed, d_normed_mem], axis=0)
    unit_own = own(record["unit_one"])
    d_rows = own(d_hidden) + unit_rows_back(
        d_normed_own * gains[0], unit_own, own(record["inverse_one"])
    )
    part = 1.0 / head_count
    sharded = (
        grad_in,
        grad_head_bias,
        grad_out,
        grad_up,
        jnp.sum(d_pre, axis=0),
        grad_down,
        d_rows[local_count:],
        mm_tn(record["out_mem"], d_value),
    )
    shared = (
        jnp.stack(
            [
                jnp.sum(d_normed_own * unit_own, axis=0),
                part * jnp.sum(d_mixed * record["unit_two"], axis=0),
            ]
        ),
        jnp.stack([jnp.sum(d_normed_own, axis=0), part * jnp.sum(d_mixed, axis=0)]),
        part * jnp.stack([jnp.sum(d_hidden, axis=0), jnp.sum(d_result, axis=0)]),
        mm_tn(record["out_local"], d_query_proj),
        mm_tn(record["out_mem"], d_key_proj),
    )
    return (d_rows[:local_count], sharded, shared)


def passed_along(value, axis, steps):
    count = lax.axis_size(axis)
    first, last = (max(0, -steps), min(count, count - steps))
    return lax.ppermute(value, axis, [(source, source + steps) for source in range(first, last)])


def shards(
    boundary_in,
    short_items,
    norm_gains,
    norm_biases,
    projection_in,
    head_bias,
    projection_out,
    residual_bias,
    up_weight,
    up_bias,
    down_weight,
    memory_tokens,
    query_memory,
    key_memory,
    value_memory,
):
    section = lax.axis_index("section")
    sections = lax.axis_size("section")
    head_count = lax.axis_size("head")
    head_place = lax.axis_index("head")
    seq_count = lax.axis_size("seq")
    seq_place = lax.axis_index("seq")
    micro_total = boundary_in.shape[1]
    local_count = boundary_in.shape[2]
    width = boundary_in.shape[3]
    segment = head_count * local_count
    head_width = projection_in.shape[3]
    memory_all = lax.all_gather(memory_tokens[0], "head", axis=0, tiled=True)
    mem_count = memory_all.shape[0]
    params = dict(
        gains=norm_gains[0],
        biases=norm_biases[0],
        proj_in=projection_in[0].reshape(width, 3 * head_width),
        in_bias=jnp.concatenate(
            [head_bias[0, 0], jnp.zeros((head_width,), jnp.float32), head_bias[0, 1]]
        ),
        proj_out=projection_out[0],
        residual=residual_bias[0],
        up=up_weight[0],
        up_bias=up_bias[0],
        down=down_weight[0],
        memory=memory_all,
        query_mem=query_memory[0],
        key_mem=key_memory[0],
        value_mem=value_memory[0],
    )
    ordinal = jnp.arange(segment)
    places = jnp.concatenate(
        [(ordinal + head_place * local_count) % segment, segment + jnp.arange(mem_count)]
    )
    allowed = (places[:, None] >= places[None, :])[None]

    positions = jnp.arange(seq_count)
    masks = []
    for micro in range(micro_total):
        if micro == 0:
            item = jnp.zeros((seq_count,), jnp.int32)
        else:
            ends = jnp.cumsum(short_items[micro - 1])
            item = jnp.sum((positions[:, None] >= ends[None, :]).astype(jnp.int32), axis=1)
        own_item = jnp.sum(jnp.where(positions == seq_place, item, 0))
        seen = jnp.logical_and(positions < seq_place, item == own_item).astype(jnp.float32)
        masks.append(jnp.repeat(seen, mem_count)[None, :])
    masks = jnp.stack(masks)

    tick_total = micro_total + sections - 1
    received = jnp.zeros_like(boundary_in[0, 0])
    records = []
    for tick in range(tick_total):
        micro = jnp.clip(tick - section, 0, micro_total - 1)
        local = jnp.where(section == 0, boundary_in[0, min(tick, micro_total - 1)], received)
        records.append(layer_forward(local, params, masks[micro], allowed))
        if tick + 1 < tick_total:
            received = passed_along(records[-1]["output"], "section", 1)
    back_received = jnp.zeros_like(boundary_in[0, 0])
    grads_input = []
    total = None
    for tick in range(tick_total):
        raw = tick - (sections - 1 - section)
        valid = jnp.logical_and(raw >= 0, raw < micro_total)
        micro = jnp.clip(raw, 0, micro_total - 1)
        grad = jnp.where(
            section == sections - 1, boundary_in[0, min(tick, micro_total - 1)], back_received
        )
        record = jax.tree.map(
            lambda *kinds: lax.select_n(section, *kinds),
            *[
                records[min(max(tick - (sections - 1 - place), 0), micro_total - 1) + place]
                for place in range(sections)
            ],
        )
        grad_x, sharded, shared = layer_backward(grad, record, params, masks[micro])
        fresh = jax.tree.map(lambda part: jnp.where(valid, part, 0.0), (sharded, shared))
        total = fresh if total is None else jax.tree.map(jnp.add, total, fresh)
        grads_input.append(grad_x)
        if tick + 1 < tick_total:
            back_received = passed_along(grad_x, "section", -1)
    sharded, shared = total
    grad_in, grad_heads_bias, grad_out, grad_up, grad_up_b, grad_down, grad_mem, grad_value = lax.psum(
        sharded, "seq"
    )
    grad_gains, grad_biases, grad_residual, grad_query, grad_key = lax.psum(shared, ("seq", "head"))
    finished_grads = jnp.stack(
        [grads_input[micro + sections - 1] for micro in range(micro_total)]
    )
    finished_outputs = jnp.stack(
        [records[micro + sections - 1]["output"] for micro in range(micro_total)]
    )
    boundary_out = jnp.where(section == 0, finished_grads, finished_outputs)[None]
    return (
        boundary_out,
        grad_gains[None],
        grad_biases[None],
        grad_in.reshape(projection_in.shape),
        grad_heads_bias[None],
        grad_out[None],
        grad_residual[None],
        grad_up[None],
        grad_up_b[None],
        grad_down[None],
        grad_mem[None],
        grad_query[None],
        grad_key[None],
        grad_value[None],
    )


def barrier_with(pairs, wait_count):
    barrier = pltpu.get_barrier_semaphore()
    for condition, device in pairs:

        @pl.when(condition)
        def _(device=device):
            pl.semaphore_signal(barrier, inc=1, device_id=device, device_id_type=MESH)

    @pl.when(wait_count > 0)
    def _():
        pl.semaphore_wait(barrier, wait_count)


def nn(left, right):
    return mm(left, right)


def lane_tiles(width):
    tile = 256 if width % 256 == 0 else width
    return [(at, tile) for at in range(0, width, tile)]


def rows_at(start, count):
    return pl.ds(pl.multiple_of(start, count), count)


def halves_of(projected):
    small = jnp.log1p(jnp.exp(-jnp.abs(projected)))
    return jnp.concatenate(
        [jnp.maximum(projected, 0.0) + small, jnp.maximum(-projected, 0.0) + small], axis=1
    )


def halves_back(projected, d_halves):
    width = projected.shape[1]
    rising = 1.0 / (1.0 + jnp.exp(-projected))
    falling = 1.0 / (1.0 + jnp.exp(projected))
    return d_halves[:, :width] * rising - d_halves[:, width:] * falling


def turned(values, by):
    return pltpu.roll(values, by % values.shape[1], 1)


GELU_IN = math.sqrt(2.0 / math.pi)


def gelu_parts(pre):
    cubic = 0.044715 * pre * pre
    bent = jnp.tanh(GELU_IN * pre * (1.0 + cubic))
    half = 0.5 * (1.0 + bent)
    slope = half + 0.5 * pre * (1.0 - bent * bent) * GELU_IN * (1.0 + 3.0 * cubic)
    return pre * half, slope


def seen_mask(items, micro, seqs, mem):
    seq = lax.axis_index("seq")
    row_seq = lax.div(lax.broadcasted_iota(jnp.int32, (1, seqs * mem), 1), jnp.int32(mem))
    end = jnp.int32(0)
    own = jnp.int32(0)
    item = jnp.zeros((1, seqs * mem), jnp.int32)
    for piece in range(items.shape[1]):
        end = end + items[jnp.maximum(micro - 1, 0), piece]
        bound = jnp.where(micro == 0, seqs, end)
        own = own + (seq >= bound).astype(jnp.int32)
        item = item + (row_seq >= bound).astype(jnp.int32)
    return jnp.logical_and(row_seq < seq, item == own)


def sender(send, recv):
    def copy(slot, source, target, device):
        return pltpu.make_async_remote_copy(
            src_ref=source,
            dst_ref=target,
            send_sem=send.at[slot],
            recv_sem=recv.at[slot],
            device_id=device,
            device_id_type=MESH,
        )

    return copy


def forward_kernel(
    items, x, gains, biases, w_in, head_bias, w_out, residual, w_up, b_up, w_down, mem_tokens,
    w_query, w_key, w_value,
    rows, qkv, attended, lse, hidden, pre, out_local, out_mem, keys, values, query_proj, weights,
    read, y,
    normed, part, got_part, act, got_out, mem_all, key_block, value_block,
    send, recv, send_k, recv_k, send_v, recv_v,
):
    section, seq, head = (lax.axis_index(name) for name in ("section", "seq", "head"))
    seqs = lax.axis_size("seq")
    micro_total, local, width = x.shape
    segment = 2 * local
    mem = out_mem.shape[1]
    total = segment + mem
    share = w_in.shape[2]
    dv = w_value.shape[1]
    other = 1 - head
    partner = {"head": other}
    copy = sender(send, recv)
    own_rows, other_rows = rows_at(head * local, local), rows_at(other * local, local)
    own_mem = rows_at(head * (mem // 2), mem // 2)
    column_tiles = lane_tiles(width)

    keys[...] = jnp.zeros_like(keys)
    values[...] = jnp.zeros_like(values)
    mem_all[own_mem] = mem_tokens[...]
    barrier_with(
        [(seq >= 0, partner)]
        + [(t < seq, {"seq": t, "head": g}) for t in range(seqs) for g in range(2)]
        + [(section == 1, {"section": 0, "head": g}) for g in range(2)],
        1 + 2 * (seqs - 1 - seq) + 2 * (1 - section),
    )
    per_micro = 3 + 3 * len(column_tiles)

    def slot(micro, number):
        return 1 + micro * per_micro + number

    tokens = copy(0, mem_tokens, mem_all.at[own_mem], partner)
    tokens.start()

    def x_copy(micro):
        return copy(slot(micro, 0), x.at[micro], rows.at[micro, own_rows], partner)

    def y_copy(micro, source_head, target_head):
        return copy(
            slot(micro, 1 + source_head),
            y.at[micro],
            rows.at[micro, rows_at(source_head * local, local)],
            {"section": 1, "head": target_head},
        )

    def y_sent(micro, target_head):
        return pltpu.make_async_remote_copy(
            src_ref=y.at[micro],
            dst_ref=rows.at[micro, own_rows],
            send_sem=send.at[slot(micro, 1 + target_head)],
            recv_sem=recv.at[slot(micro, 1 + head)],
            device_id={"section": 1, "head": target_head},
            device_id_type=MESH,
        )

    @pl.when(section == 0)
    def _():
        for micro in range(micro_total):
            x_copy(micro).start()
            rows[micro, own_rows] = x[micro]

    tokens.wait_recv()
    for micro in range(micro_total):
        rows[micro, segment:] = mem_all[...]

    def key_copy(micro, source, target):
        return pltpu.make_async_remote_copy(
            src_ref=key_block,
            dst_ref=keys.at[micro, rows_at(source * mem, mem)],
            send_sem=send_k.at[micro, target],
            recv_sem=recv_k.at[micro, source],
            device_id={"seq": target},
            device_id_type=MESH,
        )

    def value_copy(micro, source, source_head, target, target_head):
        return pltpu.make_async_remote_copy(
            src_ref=value_block,
            dst_ref=values.at[
                micro, rows_at(source * mem, mem), pl.ds(pl.multiple_of(source_head * dv, 128), dv)
            ],
            send_sem=send_v.at[micro, target, target_head],
            recv_sem=recv_v.at[micro, source, source_head],
            device_id={"seq": target, "head": target_head},
            device_id_type=MESH,
        )

    places = lax.broadcasted_iota(jnp.int32, (total, total), 0)
    allowed = places >= lax.broadcasted_iota(jnp.int32, (total, total), 1)
    lane = lax.broadcasted_iota(jnp.int32, (total, 128), 1)

    def one_micro(micro, carry):
        @pl.when(section == 0)
        def _():
            x_copy(micro).wait_recv()

        @pl.when(section == 1)
        def _():
            for source in range(2):
                y_copy(micro, source, source).wait_recv()

        unit, _ = unit_rows(rows[micro])
        normed[...] = unit * gains[0:1] + biases[0:1]
        for kind in range(3):
            made = nn(normed[...], w_in[kind])
            if kind != 1:
                made = made + head_bias[kind // 2 : kind // 2 + 1]
            qkv[micro, :, kind * share : (kind + 1) * share] = made
        tops = jnp.zeros((total, 128), jnp.float32)
        for place in range(share // HEAD_DIM):
            query, key, value = (
                qkv[micro, :, kind * share + place * HEAD_DIM : kind * share + (place + 1) * HEAD_DIM]
                for kind in range(3)
            )
            scores = jnp.where(allowed, mm_nt(query, key) * SCALE, -1e30)
            top = jnp.max(scores, axis=1, keepdims=True)
            exponent = jnp.exp(scores - top)
            row_total = jnp.sum(exponent, axis=1, keepdims=True)
            attended[micro, :, place * HEAD_DIM : (place + 1) * HEAD_DIM] = (
                nn(exponent, value) / row_total
            )
            tops = jnp.where(lane == place, top + jnp.log(row_total), tops)
        lse[micro] = tops

        def part_copy(index):
            at, tile = column_tiles[index]
            return copy(
                slot(micro, 3 + index),
                part.at[:, at : at + tile],
                got_part.at[micro, :, at : at + tile],
                partner,
            )

        for index, (at, tile) in enumerate(column_tiles):
            part[:, at : at + tile] = nn(attended[micro], w_out[:, at : at + tile])
            part_copy(index).start()
        for index, (at, tile) in enumerate(column_tiles):
            part_copy(index).wait_recv()
            cut = slice(at, at + tile)
            hidden[micro, :, cut] = (
                rows[micro, :, cut] + part[:, cut] + got_part[micro, :, cut] + residual[0:1, cut]
            )
        unit, _ = unit_rows(hidden[micro])
        normed[...] = unit * gains[1:2] + biases[1:2]
        for at, tile in lane_tiles(act.shape[1]):
            cut = slice(at, at + tile)
            made = nn(normed[...], w_up[:, cut]) + b_up[:, cut]
            pre[micro, :, cut] = made
            act[:, cut] = gelu_parts(made)[0]
        for index in range(len(column_tiles)):
            part_copy(index).wait_send()
        count = len(column_tiles)

        def out_copies(index):
            at, tile = column_tiles[index]
            return (
                copy(
                    slot(micro, 3 + count + index),
                    part.at[other_rows, at : at + tile],
                    got_out.at[micro, pl.ds(0, local), at : at + tile],
                    partner,
                ),
                copy(
                    slot(micro, 3 + 2 * count + index),
                    part.at[pl.ds(segment, mem), at : at + tile],
                    got_out.at[micro, pl.ds(local, mem), at : at + tile],
                    partner,
                ),
            )

        for index, (at, tile) in enumerate(column_tiles):
            part[:, at : at + tile] = nn(act[...], w_down[:, at : at + tile])
            for one in reversed(out_copies(index)):
                one.start()
        for index, (at, tile) in enumerate(column_tiles):
            cut = slice(at, at + tile)
            out_copies(index)[1].wait_recv()
            out_mem[micro, :, cut] = (
                part[segment:, cut]
                + got_out[micro, local:, cut]
                + hidden[micro, segment:, cut]
                + residual[1:2, cut]
            )
        key_block[...] = nn(out_mem[micro], w_key[...])
        value_block[...] = nn(out_mem[micro], w_value[...])
        for t in range(seqs):

            @pl.when(t > seq)
            def _(t=t):
                key_copy(micro, seq, t).start()
                for g in range(2):
                    value_copy(micro, seq, head, t, g).start()

        for index, (at, tile) in enumerate(column_tiles):
            cut = slice(at, at + tile)
            out_copies(index)[0].wait_recv()
            out_local[micro, :, cut] = (
                part[own_rows, cut]
                + got_out[micro, :local, cut]
                + hidden[micro, own_rows, cut]
                + residual[1:2, cut]
            )
        query_proj[micro] = nn(out_local[micro], w_query[...])
        query_halves = halves_of(query_proj[micro])
        for t in range(seqs):

            @pl.when(t < seq)
            def _(t=t):
                key_copy(micro, t, t).wait_recv()

        key_halves = halves_of(keys[micro])
        scores = jnp.zeros((local, seqs * mem), jnp.float32)
        for by in (1, 2, 3):
            scores = scores + mm_nt(
                query_halves * turned(query_halves, by), key_halves * turned(key_halves, by)
            )
        scores = jnp.where(seen_mask(items, micro, seqs, mem), scores, 0.0)
        weights[micro] = scores
        for t in range(seqs):

            @pl.when(t < seq)
            def _(t=t):
                for g in range(2):
                    value_copy(micro, t, g, t, g).wait_recv()

        found = nn(scores, values[micro]) / (jnp.sum(scores, axis=1, keepdims=True) + 1.0)
        read[micro] = found
        y[micro] = out_local[micro] + found

        @pl.when(section == 0)
        def _():
            for target in range(2):
                y_sent(micro, target).start()

        for index in range(count):
            for one in out_copies(index):
                one.wait_send()
        for t in range(seqs):

            @pl.when(t > seq)
            def _(t=t):
                key_copy(micro, seq, t).wait_send()
                for g in range(2):
                    value_copy(micro, seq, head, t, g).wait_send()

        return carry

    lax.fori_loop(0, micro_total, one_micro, 0)
    tokens.wait_send()

    @pl.when(section == 0)
    def _():
        for micro in range(micro_total):
            x_copy(micro).wait_send()
            for target in range(2):
                y_sent(micro, target).wait_send()


RECORDS = (
    "rows", "qkv", "attended", "lse", "hidden", "pre", "out_local", "out_mem", "keys", "values",
    "query_proj", "weights", "read",
)


def backward_kernel(
    items, x, gains, biases, w_in, w_out, w_up, w_down, w_query, w_key, w_value, *refs
):
    count = len(RECORDS)
    kept = refs[:count]
    (g_in, g_out, g_up, g_down, g_value, g_whole, g_small, grad_x) = refs[count : count + 8]
    record = dict(zip(RECORDS, refs[count + 8 : 2 * count + 8]))
    (
        d_out, normed, d_pre, d_part, got_mix, d_qkv, got_rows, from_k, from_v, d_keys, d_values,
        mem_part, got_mem, grad_y,
        load, send, recv, send_k, recv_k, send_v, recv_v,
    ) = refs[2 * count + 8 :]
    rows, qkv, attended, lse, hidden, pre = (record[name] for name in RECORDS[:6])
    out_local, out_mem, keys, values = (record[name] for name in RECORDS[6:10])
    query_proj, weights, read = (record[name] for name in RECORDS[10:])

    section, seq, head = (lax.axis_index(name) for name in ("section", "seq", "head"))
    seqs = lax.axis_size("seq")
    micro_total, local, width = x.shape
    segment = 2 * local
    mem = out_mem.shape[0]
    total = segment + mem
    share = w_in.shape[2]
    inner = w_up.shape[1]
    dv = w_value.shape[1]
    other = 1 - head
    partner = {"head": other}
    copy = sender(send, recv)
    own_rows, other_rows = rows_at(head * local, local), rows_at(other * local, local)
    own_mem_rows = rows_at(segment + head * (mem // 2), mem // 2)
    own_mem = rows_at(head * (mem // 2), mem // 2)
    column_tiles = lane_tiles(width)
    inner_tiles = lane_tiles(inner)

    def load_records(micro):
        return [
            pltpu.make_async_copy(kept[i].at[micro], record[RECORDS[i]], load.at[i])
            for i in range(count)
        ]

    for one in load_records(0):
        one.start()
    for ref in (g_in, g_out, g_up, g_down, g_value, g_whole, g_small, from_k, from_v):
        ref[...] = jnp.zeros_like(ref)
    barrier_with(
        [(seq >= 0, partner)]
        + [(t > seq, {"seq": t, "head": g}) for t in range(seqs) for g in range(2)]
        + [(section == 0, {"section": 1})],
        1 + 2 * seq + section,
    )
    per_micro = 3 + 3 * len(column_tiles)

    def slot(micro, number):
        return micro * per_micro + number

    def grad_copy(micro):
        return copy(slot(micro, 0), grad_x.at[micro], grad_y.at[micro], {"section": 0})

    def key_copy(micro, source, target):
        return pltpu.make_async_remote_copy(
            src_ref=d_keys.at[rows_at(target * mem, mem)],
            dst_ref=from_k.at[micro, source],
            send_sem=send_k.at[micro, target],
            recv_sem=recv_k.at[micro, source],
            device_id={"seq": target},
            device_id_type=MESH,
        )

    def value_copy(micro, source, source_head, target, target_head):
        return pltpu.make_async_remote_copy(
            src_ref=d_values.at[
                rows_at(target * mem, mem), pl.ds(pl.multiple_of(target_head * dv, 128), dv)
            ],
            dst_ref=from_v.at[micro, source, source_head],
            send_sem=send_v.at[micro, target, target_head],
            recv_sem=recv_v.at[micro, source, source_head],
            device_id={"seq": target, "head": target_head},
            device_id_type=MESH,
        )

    places = lax.broadcasted_iota(jnp.int32, (total, total), 0)
    allowed = places >= lax.broadcasted_iota(jnp.int32, (total, total), 1)

    def add_small(row, vector):
        for at in range(0, vector.shape[1], 128):
            g_small[row + at // 128 : row + at // 128 + 1] += vector[:, at : at + 128]

    def column_sum(values_in):
        return jnp.sum(values_in, axis=0, keepdims=True)

    def one_micro(micro, carry):
        @pl.when(micro > 0)
        def _():
            for one in load_records(micro):
                one.start()

        for one in load_records(micro):
            one.wait()

        @pl.when(section == 0)
        def _():
            grad_copy(micro).wait_recv()

        @pl.when(section == 1)
        def _():
            grad_y[micro] = x[micro]

        grad = grad_y[micro]
        scores = weights[...]
        denominator = jnp.sum(scores, axis=1, keepdims=True) + 1.0
        d_numer = grad / denominator
        d_denom = -jnp.sum(grad * read[...], axis=1, keepdims=True) / denominator
        d_values[...] = mm_tn(scores, d_numer)
        for t in range(seqs):

            @pl.when(t < seq)
            def _(t=t):
                for g in range(2):
                    value_copy(micro, seq, head, t, g).start()

        d_scores = jnp.where(
            seen_mask(items, micro, seqs, mem), mm_nt(d_numer, values[...]) + d_denom, 0.0
        )
        query_halves, key_halves = halves_of(query_proj[...]), halves_of(keys[...])
        d_key_halves = jnp.zeros_like(key_halves)
        for by in (1, 2, 3):
            d_feats = mm_tn(d_scores, query_halves * turned(query_halves, by))
            d_key_halves += d_feats * turned(key_halves, by) + turned(d_feats * key_halves, -by)
        d_keys[...] = halves_back(keys[...], d_key_halves)
        for t in range(seqs):

            @pl.when(t < seq)
            def _(t=t):
                key_copy(micro, seq, t).start()

        d_query_halves = jnp.zeros_like(query_halves)
        for by in (1, 2, 3):
            d_feats = nn(d_scores, key_halves * turned(key_halves, by))
            d_query_halves += d_feats * turned(query_halves, by) + turned(d_feats * query_halves, -by)
        d_query = halves_back(query_proj[...], d_query_halves)
        d_out[micro, own_rows] = grad + mm_nt(d_query, w_query[...])
        local_copy = copy(
            slot(micro, 1), d_out.at[micro, own_rows], d_out.at[micro, own_rows], partner
        )
        local_copy.start()
        g_whole[0] += mm_tn(out_local[...], d_query)
        for t in range(seqs):

            @pl.when(t > seq)
            def _(t=t):
                key_copy(micro, t, t).wait_recv()
                for g in range(2):
                    value_copy(micro, t, g, t, g).wait_recv()

        d_key_proj = jnp.sum(from_k[micro], axis=0)
        d_value = jnp.sum(from_v[micro], axis=(0, 1))
        mem_part[...] = mm_nt(d_key_proj, w_key[...]) + mm_nt(d_value, w_value[...])
        mem_copy = copy(slot(micro, 2), mem_part, got_mem.at[micro], partner)
        mem_copy.start()
        g_whole[1] += mm_tn(out_mem[...], d_key_proj)
        g_value[...] += mm_tn(out_mem[...], d_value)
        mem_copy.wait_recv()
        d_out[micro, segment:] = mem_part[...] + got_mem[micro]
        local_copy.wait_recv()

        add_small(30, 0.5 * column_sum(d_out[micro]))
        for at, tile in inner_tiles:
            cut = slice(at, at + tile)
            activated, slope = gelu_parts(pre[:, cut])
            made = slope * mm_nt(d_out[micro], w_down[cut])
            pre[:, cut] = activated
            d_pre[:, cut] = made
            add_small(36 + at // 128, column_sum(made))

        def mix_copy(index):
            at, tile = column_tiles[index]
            return copy(
                slot(micro, 3 + index),
                d_part.at[:, at : at + tile],
                got_mix.at[micro, :, at : at + tile],
                partner,
            )

        for index, (at, tile) in enumerate(column_tiles):
            d_part[:, at : at + tile] = mm_nt(d_pre[...], w_up[at : at + tile])
            mix_copy(index).start()
        unit, inverse = unit_rows(hidden[...])
        normed[...] = unit * gains[1:2] + biases[1:2]
        for at, tile in inner_tiles:
            cut = slice(at, at + tile)
            g_down[cut] += mm_tn(pre[:, cut], d_out[micro])
            g_up[:, cut] += mm_tn(normed[...], d_pre[:, cut])
        for index, (at, tile) in enumerate(column_tiles):
            cut = slice(at, at + tile)
            mix_copy(index).wait_recv()
            got_mix[micro, :, cut] += d_part[:, cut]
        unit, inverse = unit_rows(hidden[...])
        d_mixed = got_mix[micro]
        add_small(6, 0.5 * column_sum(d_mixed * unit))
        add_small(18, 0.5 * column_sum(d_mixed))
        hidden[...] = d_out[micro] + unit_rows_back(d_mixed * gains[1:2], unit, inverse)
        add_small(24, 0.5 * column_sum(hidden[...]))
        for index in range(len(column_tiles)):
            mix_copy(index).wait_send()

        d_attended = mm_nt(hidden[...], w_out[...])
        tops = lse[...]
        for place in range(share // HEAD_DIM):
            cut = slice(place * HEAD_DIM, (place + 1) * HEAD_DIM)
            query, key, value = (
                qkv[:, kind * share + place * HEAD_DIM : kind * share + (place + 1) * HEAD_DIM]
                for kind in range(3)
            )
            scores = jnp.where(allowed, mm_nt(query, key) * SCALE, -1e30)
            soft = jnp.exp(scores - tops[:, place : place + 1])
            d_head = d_attended[:, cut]
            inner_dot = jnp.sum(d_head * attended[:, cut], axis=1, keepdims=True)
            d_scores = soft * (mm_nt(d_head, value) - inner_dot) * SCALE
            for kind, made in enumerate(
                (nn(d_scores, key), mm_tn(d_scores, query), mm_tn(soft, d_head))
            ):
                d_qkv[:, kind * share + place * HEAD_DIM : kind * share + (place + 1) * HEAD_DIM] = made
        add_small(48, column_sum(d_qkv[:, :share]))
        add_small(51, column_sum(d_qkv[:, 2 * share :]))

        def rows_copies(index):
            at, tile = column_tiles[index]
            return (
                copy(
                    slot(micro, 3 + len(column_tiles) + index),
                    d_part.at[other_rows, at : at + tile],
                    got_rows.at[micro, pl.ds(0, local), at : at + tile],
                    partner,
                ),
                copy(
                    slot(micro, 3 + 2 * len(column_tiles) + index),
                    d_part.at[pl.ds(segment, mem), at : at + tile],
                    got_rows.at[micro, pl.ds(local, mem), at : at + tile],
                    partner,
                ),
            )

        for index, (at, tile) in enumerate(column_tiles):
            made = mm_nt(d_qkv[:, :share], w_in[0, at : at + tile])
            for kind in (1, 2):
                made = made + mm_nt(
                    d_qkv[:, kind * share : (kind + 1) * share], w_in[kind, at : at + tile]
                )
            d_part[:, at : at + tile] = made
            for one in rows_copies(index):
                one.start()
        unit, inverse = unit_rows(rows[...])
        normed[...] = unit * gains[0:1] + biases[0:1]
        g_out[...] += mm_tn(attended[...], hidden[...])
        for kind in range(3):
            g_in[kind] += mm_tn(normed[...], d_qkv[:, kind * share : (kind + 1) * share])
        for index in range(len(column_tiles)):
            for one in rows_copies(index):
                one.wait_recv()

        def finish(d_normed, at_rows):
            unit, inverse = unit_rows(rows[at_rows])
            add_small(0, column_sum(d_normed * unit))
            add_small(12, column_sum(d_normed))
            return hidden[at_rows] + unit_rows_back(d_normed * gains[0:1], unit, inverse)

        grad_x[micro] = finish(d_part[own_rows] + got_rows[micro, :local], own_rows)

        @pl.when(section == 1)
        def _():
            grad_copy(micro).start()

        mem_rows = rows_at(local + head * (mem // 2), mem // 2)
        d_tokens = finish(d_part[own_mem_rows] + got_rows[micro, mem_rows], own_mem_rows)
        for at in range(0, width, 128):
            row = 56 + (at // 128) * (mem // 2)
            g_small[row : row + mem // 2] += d_tokens[:, at : at + 128]

        for index in range(len(column_tiles)):
            for one in rows_copies(index):
                one.wait_send()
        local_copy.wait_send()
        mem_copy.wait_send()
        for t in range(seqs):

            @pl.when(t < seq)
            def _(t=t):
                key_copy(micro, seq, t).wait_send()
                for g in range(2):
                    value_copy(micro, seq, head, t, g).wait_send()

        return carry

    lax.fori_loop(0, micro_total, one_micro, 0)

    @pl.when(section == 1)
    def _():
        for micro in range(micro_total):
            grad_copy(micro).wait_send()


def ring_kernel(lanes, count, *refs):
    arrays = refs[:count]
    whole = refs[count]
    small_index = count - 1
    sums = refs[count + 1 : 2 * count + 1]
    whole_sum = refs[2 * count + 1]
    held = refs[2 * count + 2 : 3 * count + 3]
    got_whole, got_small, send, recv, local, send_x, recv_x = refs[3 * count + 3 :]
    seqs = lax.axis_size("seq")
    along = seqs // lanes
    seq, head = lax.axis_index("seq"), lax.axis_index("head")
    other = 1 - head
    z, y = seq // lanes, lax.rem(seq, lanes)
    place = y * along + jnp.where(lax.rem(y, 2) == 0, z, along - 1 - z)

    def device(spot):
        row = spot // along
        column = lax.rem(spot, along)
        column = jnp.where(lax.rem(row, 2) == 0, column, along - 1 - column)
        return {"seq": column * lanes + row}

    targets = (device(lax.rem(place + 1, seqs)), device(lax.rem(place + seqs - 1, seqs)))
    partner = {"head": other}
    signs = (1, -1)
    sources = [*arrays[:small_index], got_small, got_whole]
    results = [*sums, whole_sum.at[head]]

    def block(ref, way, spot):
        rows = ref.shape[0] // seqs
        half = rows // 2
        spot = lax.rem(spot + 2 * seqs, seqs)
        return ref.at[pl.ds(pl.multiple_of(spot * rows + way * half, half), half)]

    def copy(source, target, way, index, step):
        return pltpu.make_async_remote_copy(
            src_ref=source,
            dst_ref=target,
            send_sem=send.at[step, way, index],
            recv_sem=recv.at[step, way, index],
            device_id=targets[way],
            device_id_type=MESH,
        )

    def across(source, target, number):
        return pltpu.make_async_remote_copy(
            src_ref=source,
            dst_ref=target,
            send_sem=send_x.at[number],
            recv_sem=recv_x.at[number],
            device_id=partner,
            device_id_type=MESH,
        )

    def hand_over(way, spot, step):
        mine = block(whole_sum.at[head], way, spot)
        return across(mine, mine, 2 + way * seqs + step)

    ways = [(index, way) for index in range(count + 1) for way in range(2)]
    last = seqs - 2
    barrier_with([(place >= 0, target) for target in (*targets, partner)], place * 0 + 3)
    whole_copy = across(whole.at[other], got_whole, 0)
    whole_copy.start()
    small_copy = across(arrays[small_index], got_small, 1)
    small_copy.start()
    for index, way in ways:
        if index == small_index and way == 0:
            small_copy.wait()
            got_small[0:SHARED_ROWS] += arrays[small_index][0:SHARED_ROWS]
            got_small[SHARED_ROWS:] = arrays[small_index][SHARED_ROWS:]
        if index == count and way == 0:
            whole_copy.wait()
            got_whole[...] += whole[head]
        copy(block(sources[index], way, place), held[index].at[way, 0], way, index, 0).start()

    def forward(step, carry):
        for index, way in ways:
            got = held[index].at[way, step - 1]
            copy(got, got, way, index, step - 1).wait_recv()
            got[...] += block(sources[index], way, place - signs[way] * step)[...]
            copy(got, held[index].at[way, step], way, index, step).start()
        return carry

    lax.fori_loop(1, seqs - 1, forward, 0)
    for index, way in ways:
        got = held[index].at[way, last]
        copy(got, got, way, index, last).wait_recv()
        spot = place + signs[way]
        got[...] += block(sources[index], way, spot)[...]
        home = block(results[index], way, spot)
        copy(got, home, way, index, seqs - 1).start()
        pltpu.make_async_copy(got, home, local.at[way, index]).start()
        if index == count:
            across(got, home, 2 + way * seqs).start()

    def onward(step, carry):
        for index, way in ways:
            spot = place - signs[way] * (step - 1)
            got = block(results[index], way, spot)
            copy(got, got, way, index, seqs - 1 + step - 1).wait_recv()
            copy(got, got, way, index, seqs - 1 + step).start()
            if index == count:
                hand_over(way, spot, step).start()
        return carry

    lax.fori_loop(1, seqs - 1, onward, 0)
    for index, way in ways:
        spot = place - signs[way] * last
        got = block(results[index], way, spot)
        copy(got, got, way, index, 2 * seqs - 3).wait_recv()
        if index == count:
            hand_over(way, spot, seqs - 1).start()
        own = held[index].at[way, last]
        home = block(results[index], way, place + signs[way])
        pltpu.make_async_copy(own, home, local.at[way, index]).wait()

    def sent(step, carry):
        for index, way in ways:
            own = held[index].at[way, 0]
            copy(own, own, way, index, step).wait_send()
        return carry

    lax.fori_loop(0, 2 * seqs - 2, sent, 0)

    def crossed(step, carry):
        for way in range(2):
            spot = place - signs[way] * (step - 1)
            theirs = block(whole_sum.at[other], way, spot)
            across(theirs, theirs, 2 + way * seqs + step).wait()
        return carry

    lax.fori_loop(0, seqs, crossed, 0)


def shapes_of(*shapes):
    return tuple(jax.ShapeDtypeStruct(shape, jnp.float32) for shape in shapes)


def buffers(*shapes):
    return [pltpu.VMEM(shape, jnp.float32) for shape in shapes]


def dma(*shape):
    return pltpu.SemaphoreType.DMA(shape)


def params_of(number):
    return pltpu.CompilerParams(
        collective_id=number, has_side_effects=True, vmem_limit_bytes=62 << 20
    )


def shards_of_two(
    boundary_in,
    short_items,
    norm_gains,
    norm_biases,
    projection_in,
    head_bias,
    projection_out,
    residual_bias,
    up_weight,
    up_bias,
    down_weight,
    memory_tokens,
    query_memory,
    key_memory,
    value_memory,
):
    seqs = lax.axis_size("seq")
    x = boundary_in[0]
    micros, local, width = x.shape
    w_in = projection_in[0].transpose(1, 0, 2)
    share = w_in.shape[2]
    inner = up_weight.shape[2]
    half_mem = memory_tokens.shape[1]
    mem = 2 * half_mem
    segment = 2 * local
    total = segment + mem
    dk, dv = key_memory.shape[2], value_memory.shape[2]
    stored = seqs * mem
    tiles = len(lane_tiles(width))
    slots = 3 + 3 * tiles
    record_shapes = dict(
        rows=(total, width),
        qkv=(total, 3 * share),
        attended=(total, share),
        lse=(total, 128),
        hidden=(total, width),
        pre=(total, inner),
        out_local=(local, width),
        out_mem=(mem, width),
        keys=(stored, dk),
        values=(stored, 2 * dv),
        query_proj=(local, dk),
        weights=(local, stored),
        read=(local, width),
    )
    memory_sems = [dma(micros, seqs), dma(micros, seqs), dma(micros, seqs, 2), dma(micros, seqs, 2)]
    weights = (
        norm_gains[0],
        norm_biases[0],
        w_in,
        head_bias[0],
        projection_out[0],
        residual_bias[0],
        up_weight[0],
        up_bias,
        down_weight[0],
        memory_tokens[0],
        query_memory[0],
        key_memory[0],
        value_memory[0],
    )
    *records, y = pl.pallas_call(
        forward_kernel,
        out_shape=shapes_of(
            *((micros, *record_shapes[name]) for name in RECORDS), (micros, local, width)
        ),
        in_specs=[SMEM] + [VMEM] * (1 + len(weights)),
        out_specs=(VMEM,) * (len(RECORDS) + 1),
        scratch_shapes=buffers(
            (total, width),
            (total, width),
            (micros, total, width),
            (total, inner),
            (micros, local + mem, width),
            (mem, width),
            (mem, dk),
            (mem, dv),
        )
        + [dma(1 + micros * slots), dma(1 + micros * slots), *memory_sems],
        compiler_params=params_of(0),
        name="forward",
    )(short_items, x, *weights)
    gradient_shapes = (
        (3, width, share),
        (share, width),
        (width, inner),
        (inner, width),
        (width, dv),
        (2, width, dk),
        (16 * seqs, 128),
    )
    *gradients, grad_x = pl.pallas_call(
        backward_kernel,
        out_shape=shapes_of(*gradient_shapes, (micros, local, width)),
        in_specs=[SMEM] + [VMEM] * 10 + [HBM] * len(RECORDS),
        out_specs=(VMEM,) * 8,
        scratch_shapes=buffers(
            *(record_shapes[name] for name in RECORDS),
            (micros, total, width),
            (total, width),
            (total, inner),
            (total, width),
            (micros, total, width),
            (total, 3 * share),
            (micros, local + mem, width),
            (micros, seqs, mem, dk),
            (micros, seqs, 2, mem, dv),
            (stored, dk),
            (stored, 2 * dv),
            (mem, width),
            (micros, mem, width),
            (micros, local, width),
        )
        + [dma(len(RECORDS)), dma(micros * slots), dma(micros * slots), *memory_sems],
        compiler_params=params_of(1),
        name="backward",
    )(
        short_items,
        x,
        norm_gains[0],
        norm_biases[0],
        w_in,
        projection_out[0],
        up_weight[0],
        down_weight[0],
        query_memory[0],
        key_memory[0],
        value_memory[0],
        *records,
    )
    g_in, g_out, g_up, g_down, g_value, g_whole, g_small = gradients
    arrays = (g_down, g_up, g_in.reshape(3 * width, share), g_out, g_value, g_small)
    count = len(arrays)
    held = [(a.shape[0], a.shape[1]) for a in (*arrays, g_whole[0])]
    g_down, g_up, g_in, g_out, g_value, small, whole = pl.pallas_call(
        functools.partial(ring_kernel, 2, count),
        out_shape=shapes_of(*(a.shape for a in arrays), g_whole.shape),
        in_specs=[VMEM] * (count + 1),
        out_specs=(HBM,) * (count + 1),
        scratch_shapes=buffers(
            *((2, seqs - 1, rows // (2 * seqs), columns) for rows, columns in held),
            (width, dk),
            g_small.shape,
        )
        + [
            dma(2 * seqs - 2, 2, count + 1),
            dma(2 * seqs - 2, 2, count + 1),
            dma(2, count + 1),
            dma(2 + 2 * seqs),
            dma(2 + 2 * seqs),
        ],
        compiler_params=params_of(2),
        name="ring",
    )(*arrays, g_whole)
    section = lax.axis_index("section")
    vectors = small[:36].reshape(3, 1, 2, width)
    return (
        jnp.where(section == 0, grad_x, y)[None],
        vectors[0],
        vectors[1],
        g_in.reshape(3, width, share).transpose(1, 0, 2)[None],
        small[48:54].reshape(1, 2, share),
        g_out[None],
        vectors[2],
        g_up[None],
        small[36:48].reshape(1, inner),
        g_down[None],
        small[56 : 56 + 6 * half_mem]
        .reshape(6, half_mem, 128)
        .transpose(1, 0, 2)
        .reshape(1, half_mem, width),
        whole[0][None],
        whole[1][None],
        g_value[None],
    )


def solution(mesh):
    return jax.shard_map(
        shards_of_two if mesh.shape["head"] == 2 else shards,
        mesh=mesh,
        in_specs=(
            P("section", None, ("seq", "head"), None),
            P(),
            P("section", None, None),
            P("section", None, None),
            P("section", None, None, "head"),
            P("section", None, "head"),
            P("section", "head", None),
            P("section", None, None),
            P("section", None, "head"),
            P("section", "head"),
            P("section", "head", None),
            P("section", "head", None),
            P("section", None, None),
            P("section", None, None),
            P("section", None, "head"),
        ),
        out_specs=(
            P("section", None, ("seq", "head"), None),
            P("section", None, None),
            P("section", None, None),
            P("section", None, None, "head"),
            P("section", None, "head"),
            P("section", "head", None),
            P("section", None, None),
            P("section", None, "head"),
            P("section", "head"),
            P("section", "head", None),
            P("section", "head", None),
            P("section", None, None),
            P("section", None, None),
            P("section", None, "head"),
        ),
        check_vma=False,
    )
```

```python
import functools
import math
from types import SimpleNamespace

import jax
import jax.numpy as jnp
from jax import lax
from jax.experimental import pallas as pl
from jax.experimental.pallas import tpu as pltpu
from jax.sharding import PartitionSpec as P

SECTION, SEQ, HEAD = "section", "seq", "head"
HEAD_DIM = 64
EPSILON = 1e-05
SCALE = 1.0 / math.sqrt(HEAD_DIM)
MESH = pl.DeviceIdType.MESH
VMEM = pl.BlockSpec(memory_space=pltpu.VMEM)
HBM = pl.BlockSpec(memory_space=pltpu.HBM)
SMEM = pl.BlockSpec(memory_space=pltpu.SMEM)
SHARED_ROWS = 36


def mm(left, right, dims=((1,), (0,))):
    return lax.dot_general(
        left, right, (dims, ((), ())), precision=lax.Precision.HIGH, preferred_element_type=jnp.float32
    )


def mm_nt(left, right):
    return mm(left, right, ((1,), (1,)))


def mm_tn(left, right):
    return mm(left, right, ((0,), (0,)))


def unit_rows(rows):
    centred = rows - jnp.mean(rows, axis=-1, keepdims=True)
    inverse = lax.rsqrt(jnp.mean(centred * centred, axis=-1, keepdims=True) + EPSILON)
    return centred * inverse, inverse


def unit_rows_back(d_unit, unit, inverse):
    return inverse * (
        d_unit
        - jnp.mean(d_unit, axis=-1, keepdims=True)
        - unit * jnp.mean(d_unit * unit, axis=-1, keepdims=True)
    )


def features(projected):
    halves = jnp.concatenate([jax.nn.softplus(projected), jax.nn.softplus(-projected)], axis=-1)
    return jnp.concatenate(
        [halves * jnp.roll(halves, rolled_by, axis=-1) for rolled_by in (1, 2, 3)], axis=-1
    )


def gelu_tanh(values_in):
    return jax.nn.gelu(values_in, approximate=True)


def head_sum_rows(rows, share):
    segment = lax.axis_size(HEAD) * share
    turn = lax.axis_index(HEAD) * share
    total = lax.psum(
        jnp.concatenate([jnp.roll(rows[:segment], turn, axis=0), rows[segment:]], axis=0), HEAD
    )
    return jnp.concatenate([jnp.roll(total[:segment], -turn, axis=0), total[segment:]], axis=0)


def head_rows(local):
    gathered = lax.all_gather(local, HEAD, axis=0, tiled=True)
    return jnp.roll(gathered, -lax.axis_index(HEAD) * local.shape[0], axis=0)


def head_scatter(rows):
    share = rows.shape[0] // lax.axis_size(HEAD)
    placed = jnp.roll(rows, lax.axis_index(HEAD) * share, axis=0)
    return lax.psum_scatter(placed, HEAD, scatter_dimension=0, tiled=True)


def heads_of(part):
    return part.reshape(part.shape[0], -1, HEAD_DIM).transpose(1, 0, 2)


def rows_of(part):
    return part.transpose(1, 0, 2).reshape(part.shape[1], -1)


def bmm(left, right, left_dim, right_dim):
    return lax.dot_general(
        left,
        right,
        (((left_dim,), (right_dim,)), ((0,), (0,))),
        precision=lax.Precision.HIGH,
        preferred_element_type=jnp.float32,
    )


def layer_forward(local, params, mask, allowed):
    width = local.shape[1]
    local_count = local.shape[0]
    segment = lax.axis_size(HEAD) * local_count
    rows = jnp.concatenate([head_rows(local), params.memory], axis=0)
    unit_one, inverse_one = unit_rows(rows)
    normed = unit_one * params.gains[0] + params.biases[0]
    projected = mm(normed, params.proj_in) + params.in_bias
    share = projected.shape[1] // 3
    query, key, value = (heads_of(projected[:, i * share : (i + 1) * share]) for i in range(3))
    scores = jnp.where(allowed, bmm(query, key, 2, 2) * SCALE, -1e30)
    row_top = jnp.max(scores, axis=-1, keepdims=True)
    exponent = jnp.exp(scores - row_top)
    soft = exponent / jnp.sum(exponent, axis=-1, keepdims=True)
    attended = rows_of(bmm(soft, value, 2, 1))
    hidden = rows + head_sum_rows(mm(attended, params.proj_out), local_count) + params.residual[0]
    unit_two, inverse_two = unit_rows(hidden)
    mixed = unit_two * params.gains[1] + params.biases[1]
    inner_pre = mm(mixed, params.up) + params.up_bias
    inner_act = gelu_tanh(inner_pre)
    partial = mm(inner_act, params.down)
    out_local = head_scatter(partial[:segment]) + hidden[:local_count] + params.residual[1]
    out_mem = lax.psum(partial[segment:], HEAD) + hidden[segment:] + params.residual[1]
    key_proj = mm(out_mem, params.key_mem)
    values = mm(out_mem, params.value_mem)
    gathered = lax.all_gather(jnp.concatenate([key_proj, values], axis=1), SEQ, axis=0, tiled=True)
    dk = key_proj.shape[1]
    keys_all = gathered[:, :dk]
    values_all = lax.all_gather(gathered[:, dk:], HEAD, axis=1, tiled=True)
    key_feats = features(keys_all)
    query_proj = mm(out_local, params.query_mem)
    query_feats = features(query_proj)
    weights = mask * mm_nt(query_feats, key_feats)
    denominator = jnp.sum(weights, axis=1, keepdims=True) + 1.0
    read = mm(weights, values_all) / denominator
    return SimpleNamespace(
        unit_one=unit_one,
        inverse_one=inverse_one,
        projected=projected,
        attended=attended,
        soft=soft,
        unit_two=unit_two,
        inverse_two=inverse_two,
        inner_pre=inner_pre,
        out_local=out_local,
        out_mem=out_mem,
        keys_all=keys_all,
        values_all=values_all,
        query_proj=query_proj,
        weights=weights,
        denominator=denominator,
        read=read,
        output=out_local + read,
    )


def layer_backward(grad, record, params, mask):
    head_count = lax.axis_size(HEAD)
    seq_count = lax.axis_size(SEQ)
    width = grad.shape[1]
    local_count = grad.shape[0]
    segment = head_count * local_count
    denominator = record.denominator
    d_numer = grad / denominator
    d_denom = -jnp.sum(grad * record.read, axis=1, keepdims=True) / denominator
    d_weights = mask * (mm_nt(d_numer, record.values_all) + d_denom)
    key_feats, keys_back = jax.vjp(features, record.keys_all)
    query_feats, query_back = jax.vjp(features, record.query_proj)
    d_query_proj = query_back(mm(d_weights, key_feats))[0]
    d_keys = keys_back(mm_tn(d_weights, query_feats))[0]
    d_values = mm_tn(record.weights, d_numer)
    d_memory = lax.psum_scatter(
        jnp.concatenate([d_keys, d_values], axis=1), SEQ, scatter_dimension=0, tiled=True
    )
    dk = d_keys.shape[1]
    d_key_proj = d_memory[:, :dk]
    d_value = lax.psum_scatter(
        d_memory[:, dk:], HEAD, scatter_dimension=1, tiled=True
    )
    d_mem = lax.psum(
        mm_nt(d_key_proj, params.key_mem) + mm_nt(d_value, params.value_mem), HEAD
    )
    d_local = grad + mm_nt(d_query_proj, params.query_mem)
    d_result = jnp.concatenate([head_rows(d_local), d_mem], axis=0)
    inner_act, gelu_back = jax.vjp(gelu_tanh, record.inner_pre)
    grad_down = mm_tn(inner_act, d_result)
    d_pre = gelu_back(mm_nt(d_result, params.down))[0]
    gains, biases = params.gains, params.biases
    mixed = record.unit_two * gains[1] + biases[1]
    grad_up = mm_tn(mixed, d_pre)
    d_mixed = head_sum_rows(mm_nt(d_pre, params.up), local_count)
    d_hidden = d_result + unit_rows_back(d_mixed * gains[1], record.unit_two, record.inverse_two)
    grad_out = mm_tn(record.attended, d_hidden)
    d_attended = mm_nt(d_hidden, params.proj_out)
    share = d_attended.shape[1]
    query, key, value = (
        heads_of(record.projected[:, i * share : (i + 1) * share]) for i in range(3)
    )
    soft = record.soft
    d_heads = heads_of(d_attended)
    inner_dot = jnp.sum(d_heads * heads_of(record.attended), axis=-1, keepdims=True)
    d_scores = soft * (bmm(d_heads, value, 2, 2) - inner_dot) * SCALE
    d_projected = jnp.concatenate(
        [
            rows_of(bmm(d_scores, key, 2, 1)),
            rows_of(bmm(d_scores, query, 1, 1)),
            rows_of(bmm(soft, d_heads, 1, 1)),
        ],
        axis=1,
    )
    normed = record.unit_one * gains[0] + biases[0]
    grad_in = mm_tn(normed, d_projected)
    columns = jnp.sum(d_projected, axis=0)
    grad_head_bias = jnp.stack([columns[:share], columns[2 * share :]])
    d_normed_all = mm_nt(d_projected, params.proj_in)
    d_normed = head_scatter(d_normed_all[:segment])
    d_normed_mem = lax.psum_scatter(
        d_normed_all[segment:], HEAD, scatter_dimension=0, tiled=True
    )
    mem_count = d_normed_mem.shape[0]
    own_mem = segment + lax.axis_index(HEAD) * mem_count

    def own(values):
        return jnp.concatenate(
            [values[:local_count], lax.dynamic_slice_in_dim(values, own_mem, mem_count, 0)], axis=0
        )

    d_normed_own = jnp.concatenate([d_normed, d_normed_mem], axis=0)
    unit_own = own(record.unit_one)
    d_rows = own(d_hidden) + unit_rows_back(
        d_normed_own * gains[0], unit_own, own(record.inverse_one)
    )
    part = 1.0 / head_count
    sharded = (
        grad_in,
        grad_head_bias,
        grad_out,
        grad_up,
        jnp.sum(d_pre, axis=0),
        grad_down,
        d_rows[local_count:],
        mm_tn(record.out_mem, d_value),
    )
    shared = (
        jnp.stack(
            [
                jnp.sum(d_normed_own * unit_own, axis=0),
                part * jnp.sum(d_mixed * record.unit_two, axis=0),
            ]
        ),
        jnp.stack([jnp.sum(d_normed_own, axis=0), part * jnp.sum(d_mixed, axis=0)]),
        part * jnp.stack([jnp.sum(d_hidden, axis=0), jnp.sum(d_result, axis=0)]),
        mm_tn(record.out_local, d_query_proj),
        mm_tn(record.out_mem, d_key_proj),
    )
    return (d_rows[:local_count], sharded, shared)


def passed_along(value, axis, steps):
    count = lax.axis_size(axis)
    first, last = (max(0, -steps), min(count, count - steps))
    return lax.ppermute(value, axis, [(source, source + steps) for source in range(first, last)])


def shards(
    boundary_in,
    short_items,
    norm_gains,
    norm_biases,
    projection_in,
    head_bias,
    projection_out,
    residual_bias,
    up_weight,
    up_bias,
    down_weight,
    memory_tokens,
    query_memory,
    key_memory,
    value_memory,
):
    section = lax.axis_index(SECTION)
    sections = lax.axis_size(SECTION)
    head_count = lax.axis_size(HEAD)
    head_place = lax.axis_index(HEAD)
    seq_count = lax.axis_size(SEQ)
    seq_place = lax.axis_index(SEQ)
    micro_total = boundary_in.shape[1]
    local_count = boundary_in.shape[2]
    width = boundary_in.shape[3]
    segment = head_count * local_count
    head_width = projection_in.shape[3]
    memory_all = lax.all_gather(memory_tokens[0], HEAD, axis=0, tiled=True)
    mem_count = memory_all.shape[0]
    params = SimpleNamespace(
        gains=norm_gains[0],
        biases=norm_biases[0],
        proj_in=projection_in[0].reshape(width, 3 * head_width),
        in_bias=jnp.concatenate(
            [head_bias[0, 0], jnp.zeros((head_width,), jnp.float32), head_bias[0, 1]]
        ),
        proj_out=projection_out[0],
        residual=residual_bias[0],
        up=up_weight[0],
        up_bias=up_bias[0],
        down=down_weight[0],
        memory=memory_all,
        query_mem=query_memory[0],
        key_mem=key_memory[0],
        value_mem=value_memory[0],
    )
    ordinal = jnp.arange(segment)
    places = jnp.concatenate(
        [(ordinal + head_place * local_count) % segment, segment + jnp.arange(mem_count)]
    )
    allowed = (places[:, None] >= places[None, :])[None]

    positions = jnp.arange(seq_count)
    masks = []
    for micro in range(micro_total):
        if micro == 0:
            item = jnp.zeros((seq_count,), jnp.int32)
        else:
            ends = jnp.cumsum(short_items[micro - 1])
            item = jnp.sum((positions[:, None] >= ends[None, :]).astype(jnp.int32), axis=1)
        own_item = jnp.sum(jnp.where(positions == seq_place, item, 0))
        seen = jnp.logical_and(positions < seq_place, item == own_item).astype(jnp.float32)
        masks.append(jnp.repeat(seen, mem_count)[None, :])
    masks = jnp.stack(masks)

    tick_total = micro_total + sections - 1
    received = jnp.zeros_like(boundary_in[0, 0])
    records = []
    for tick in range(tick_total):
        micro = jnp.clip(tick - section, 0, micro_total - 1)
        local = jnp.where(section == 0, boundary_in[0, min(tick, micro_total - 1)], received)
        records.append(layer_forward(local, params, masks[micro], allowed))
        if tick + 1 < tick_total:
            received = passed_along(records[-1].output, SECTION, 1)
    back_received = jnp.zeros_like(boundary_in[0, 0])
    grads_input = []
    total = None
    for tick in range(tick_total):
        raw = tick - (sections - 1 - section)
        valid = jnp.logical_and(raw >= 0, raw < micro_total)
        micro = jnp.clip(raw, 0, micro_total - 1)
        grad = jnp.where(
            section == sections - 1, boundary_in[0, min(tick, micro_total - 1)], back_received
        )
        kept = [
            vars(records[min(max(tick - (sections - 1 - place), 0), micro_total - 1) + place])
            for place in range(sections)
        ]
        record = SimpleNamespace(
            **jax.tree.map(lambda *kinds: lax.select_n(section, *kinds), *kept)
        )
        grad_x, sharded, shared = layer_backward(grad, record, params, masks[micro])
        fresh = jax.tree.map(lambda part: jnp.where(valid, part, 0.0), (sharded, shared))
        total = fresh if total is None else jax.tree.map(jnp.add, total, fresh)
        grads_input.append(grad_x)
        if tick + 1 < tick_total:
            back_received = passed_along(grad_x, SECTION, -1)
    sharded, shared = total
    grad_in, grad_heads_bias, grad_out, grad_up, grad_up_b, grad_down, grad_mem, grad_value = lax.psum(
        sharded, SEQ
    )
    grad_gains, grad_biases, grad_residual, grad_query, grad_key = lax.psum(shared, (SEQ, HEAD))
    finished_grads = jnp.stack(
        [grads_input[micro + sections - 1] for micro in range(micro_total)]
    )
    finished_outputs = jnp.stack(
        [records[micro + sections - 1].output for micro in range(micro_total)]
    )
    boundary_out = jnp.where(section == 0, finished_grads, finished_outputs)[None]
    return (
        boundary_out,
        grad_gains[None],
        grad_biases[None],
        grad_in.reshape(projection_in.shape),
        grad_heads_bias[None],
        grad_out[None],
        grad_residual[None],
        grad_up[None],
        grad_up_b[None],
        grad_down[None],
        grad_mem[None],
        grad_query[None],
        grad_key[None],
        grad_value[None],
    )


def barrier_with(pairs, wait_count):
    barrier = pltpu.get_barrier_semaphore()
    for condition, device in pairs:

        @pl.when(condition)
        def _(device=device):
            pl.semaphore_signal(barrier, inc=1, device_id=device, device_id_type=MESH)

    @pl.when(wait_count > 0)
    def _():
        pl.semaphore_wait(barrier, wait_count)


def nn(left, right):
    return mm(left, right)


def lane_tiles(width):
    tile = 256 if width % 256 == 0 else width
    return [(at, tile) for at in range(0, width, tile)]


def rows_at(start, count):
    return pl.ds(pl.multiple_of(start, count), count)


def halves_of(projected):
    small = jnp.log1p(jnp.exp(-jnp.abs(projected)))
    return jnp.concatenate(
        [jnp.maximum(projected, 0.0) + small, jnp.maximum(-projected, 0.0) + small], axis=1
    )


def halves_back(projected, d_halves):
    width = projected.shape[1]
    rising = 1.0 / (1.0 + jnp.exp(-projected))
    falling = 1.0 / (1.0 + jnp.exp(projected))
    return d_halves[:, :width] * rising - d_halves[:, width:] * falling


def turned(values, by):
    return pltpu.roll(values, by % values.shape[1], 1)


GELU_IN = math.sqrt(2.0 / math.pi)


def gelu_parts(pre):
    cubic = 0.044715 * pre * pre
    bent = jnp.tanh(GELU_IN * pre * (1.0 + cubic))
    half = 0.5 * (1.0 + bent)
    slope = half + 0.5 * pre * (1.0 - bent * bent) * GELU_IN * (1.0 + 3.0 * cubic)
    return pre * half, slope


def seen_mask(items, micro, seqs, mem):
    seq = lax.axis_index(SEQ)
    row_seq = lax.div(lax.broadcasted_iota(jnp.int32, (1, seqs * mem), 1), jnp.int32(mem))
    end = jnp.int32(0)
    own = jnp.int32(0)
    item = jnp.zeros((1, seqs * mem), jnp.int32)
    for piece in range(items.shape[1]):
        end = end + items[jnp.maximum(micro - 1, 0), piece]
        bound = jnp.where(micro == 0, seqs, end)
        own = own + (seq >= bound).astype(jnp.int32)
        item = item + (row_seq >= bound).astype(jnp.int32)
    return jnp.logical_and(row_seq < seq, item == own)


WEIGHTS = IN, UP, DOWN, VALUE, QUERY, KEY = tuple(range(6))
COPIES = (1, 2, 3, 3, 3, 1, 1, 1, 3, 3, 3)
(X_IN, Y_OUT, PART, LOCAL, MEMORY, GRAD, D_LOCAL, D_MEMORY, MIX, ROWS, ROWS_MEMORY) = range(11)
COPY_SLOTS = sum(COPIES)
TOKENS, OUT_SHARE = range(2)


def copy_slot(micro, kind, index=0):
    return 2 + micro * COPY_SLOTS + sum(COPIES[:kind]) + index


def column_sum(values_in):
    return jnp.sum(values_in, axis=0, keepdims=True)


SLOTS = 3


def layers_kernel(lanes, *refs):
    refs = list(refs)

    def take(count):
        taken, refs[:] = refs[:count], refs[count:]
        return taken

    items, x, gains, biases, head_bias, residual, b_up, mem_tokens = take(8)
    weights_in = take(len(WEIGHTS))
    (w_out_in,) = take(1)
    down_sum, up_sum, in_sum, out_sum, value_sum, small_sum, whole_sum = take(7)
    y, grad_x = take(2)
    held = take(len(WEIGHTS))
    w_in, w_up, w_down, w_value, w_query, w_key = held
    rows, qkv, attended, lse, hidden, pre = take(6)
    out_local, out_mem, keys, values, query_proj, weights, read = take(7)
    w_out_all, got_attended = take(2)
    (
        normed, d_pre, d_out, part, got_part, got_out, mem_all, key_block, value_block, from_k, from_v,
        mem_part, got_mem, grad_y, wide_scores, wide_soft, wide_query, wide_grad,
        g_small, got_small, got_whole,
    ) = take(21)
    d_keys, d_values = keys, read
    slots = take(9)
    load, store, send, recv, send_k, recv_k, send_v, recv_v = take(8)
    back_sk, back_rk, back_sv, back_rv, send_w, recv_w = take(6)
    send_up, recv_up, send_on, recv_on, send_x, recv_x, free = refs

    section, seq, head = (lax.axis_index(name) for name in (SECTION, SEQ, HEAD))
    seqs = lax.axis_size(SEQ)
    micros, local, width = x.shape
    segment = 2 * local
    mem = out_mem.shape[1]
    half_mem = mem // 2
    total = segment + mem
    share = w_in.shape[2]
    inner = w_up.shape[1]
    heads = share // HEAD_DIM
    dv = w_value.shape[1]
    other = 1 - head
    partner = {HEAD: other}
    own_rows, other_rows = rows_at(head * local, local), rows_at(other * local, local)
    own_mem = rows_at(head * half_mem, half_mem)
    own_mem_rows = rows_at(segment + head * half_mem, half_mem)
    seg_rows, mem_rows = pl.ds(0, segment), pl.ds(segment, mem)
    column_tiles = [(at, width // 3) for at in range(0, width, width // 3)]
    inner_tiles = lane_tiles(inner)

    def copy(slot, source, target, device):
        return pltpu.make_async_remote_copy(
            src_ref=source,
            dst_ref=target,
            send_sem=send.at[slot],
            recv_sem=recv.at[slot],
            device_id=device,
            device_id_type=MESH,
        )

    def weight_copy(name):
        return pltpu.make_async_copy(
            weights_in[name], held[name], load.at[name]
        )

    out_copy = pltpu.make_async_copy(w_out_in, w_out_all.at[head], load.at[len(WEIGHTS)])
    w_out = w_out_all.at[head]

    def each_micro(stage):
        def body(micro, carry):
            stage(micro)
            return carry

        lax.fori_loop(0, micros, body, 0)

    def each_seq(condition, act):
        for t in range(seqs):

            @pl.when(condition(t))
            def _(t=t):
                act(t)

    def later(t):
        return t > seq

    def earlier(t):
        return t < seq

    out_copy.start()
    for name in WEIGHTS:
        weight_copy(name).start()
    keys[...] = jnp.zeros_like(keys)
    values[...] = jnp.zeros_like(values)
    from_k[...] = jnp.zeros_like(from_k)
    from_v[...] = jnp.zeros_like(from_v)
    g_small[...] = jnp.zeros_like(g_small)
    mem_all[own_mem] = mem_tokens[...]
    barrier_with(
        [(seq >= 0, partner)]
        + [(t != seq, {SEQ: t, HEAD: g}) for t in range(seqs) for g in range(2)]
        + [(section == 1, {SECTION: 0, HEAD: g}) for g in range(2)]
        + [(section == 0, {SECTION: 1})],
        1 + 2 * (seqs - 1) + 2 - section,
    )

    tokens = copy(TOKENS, mem_tokens, mem_all.at[own_mem], partner)

    def x_load(micro, target):
        return pltpu.make_async_copy(x.at[micro], target, load.at[len(WEIGHTS) + 1 + micro])

    def x_copy(micro):
        return copy(copy_slot(micro, X_IN), x.at[micro], rows.at[micro, own_rows], partner)

    def y_sent(micro, target_head):
        return pltpu.make_async_remote_copy(
            src_ref=y.at[micro],
            dst_ref=rows.at[micro, own_rows],
            send_sem=send.at[copy_slot(micro, Y_OUT, target_head)],
            recv_sem=recv.at[copy_slot(micro, Y_OUT, head)],
            device_id={SECTION: 1, HEAD: target_head},
            device_id_type=MESH,
        )

    def y_got(micro, source_head):
        here = rows.at[micro, rows_at(source_head * local, local)]
        return copy(copy_slot(micro, Y_OUT, source_head), here, here, partner)

    def tile_copy(kind, micro, index):
        at, tile = column_tiles[index]
        return copy(
            copy_slot(micro, kind, index),
            part.at[micro, :, at : at + tile],
            got_part.at[micro, :, at : at + tile],
            partner,
        )

    def attended_copy(micro, index):
        cut = slice(index * 2 * HEAD_DIM, (index + 1) * 2 * HEAD_DIM)
        return copy(
            copy_slot(micro, PART, index),
            attended.at[micro, :, cut],
            got_attended.at[micro, :, cut],
            partner,
        )

    def local_tile(kind, micro, index):
        at, tile = column_tiles[index]
        return copy(
            copy_slot(micro, kind, index),
            part.at[micro, other_rows, at : at + tile],
            got_out.at[micro, pl.ds(0, local), at : at + tile],
            partner,
        )

    def memory_tile(kind, micro, index):
        at, tile = column_tiles[index]
        return copy(
            copy_slot(micro, kind, index),
            part.at[micro, mem_rows, at : at + tile],
            got_out.at[micro, pl.ds(local, mem), at : at + tile],
            partner,
        )

    def key_copy(micro, source, target):
        return pltpu.make_async_remote_copy(
            src_ref=key_block.at[micro],
            dst_ref=keys.at[micro, rows_at(source * mem, mem)],
            send_sem=send_k.at[micro, target],
            recv_sem=recv_k.at[micro, source],
            device_id={SEQ: target},
            device_id_type=MESH,
        )

    def value_copy(micro, source, source_head, target, target_head):
        return pltpu.make_async_remote_copy(
            src_ref=value_block.at[micro],
            dst_ref=values.at[
                micro, rows_at(source * mem, mem), pl.ds(pl.multiple_of(source_head * dv, 128), dv)
            ],
            send_sem=send_v.at[micro, target, target_head],
            recv_sem=recv_v.at[micro, source, source_head],
            device_id={SEQ: target, HEAD: target_head},
            device_id_type=MESH,
        )

    tokens.start()

    out_share = share // seqs

    def out_piece(half, piece):
        return w_out_all.at[half, rows_at(piece * out_share, out_share)]

    def over_out():
        mine = w_out_in.at[rows_at(seq * out_share, out_share)]
        return copy(OUT_SHARE, mine, out_piece(head, seq), partner)

    def hand_out(source, target):
        return pltpu.make_async_remote_copy(
            src_ref=out_piece(other, source),
            dst_ref=out_piece(other, source),
            send_sem=send_w.at[target],
            recv_sem=recv_w.at[source],
            device_id={SEQ: target},
            device_id_type=MESH,
        )

    over_out().start()

    @pl.when(section == 0)
    def _():
        for micro in range(micros):
            x_copy(micro).start()
            x_load(micro, rows.at[micro, own_rows]).start()

    @pl.when(section == 1)
    def _():
        for micro in range(micros):
            x_load(micro, grad_y.at[micro]).start()

    tokens.wait_recv()
    for micro in range(micros):
        rows[micro, mem_rows] = mem_all[...]
    over_out().wait_recv()
    each_seq(lambda t: t != seq, lambda t: hand_out(seq, t).start())

    causal = lax.broadcasted_iota(jnp.int32, (segment, segment), 0) >= (
        lax.broadcasted_iota(jnp.int32, (segment, segment), 1)
    )
    mem_causal = segment + lax.broadcasted_iota(jnp.int32, (mem, total), 0) >= (
        lax.broadcasted_iota(jnp.int32, (mem, total), 1)
    )
    lane = lax.broadcasted_iota(jnp.int32, (total, 128), 1)

    def lanes_of(kind, place):
        return slice(kind * share + place * HEAD_DIM, kind * share + (place + 1) * HEAD_DIM)

    def attention(micro):
        @pl.when(section == 0)
        def _():
            x_load(micro, rows.at[micro, own_rows]).wait()
            x_copy(micro).wait_recv()

        @pl.when(section == 1)
        def _():
            for source in range(2):
                y_got(micro, source).wait_recv()

        unit, _ = unit_rows(rows[micro])
        normed[micro] = unit * gains[0:1] + biases[0:1]

        @pl.when(micro == 0)
        def _():
            weight_copy(IN).wait()

        for kind in range(3):
            made = nn(normed[micro], w_in[kind])
            if kind != 1:
                made = made + head_bias[kind // 2 : kind // 2 + 1]
            qkv[micro, :, kind * share : (kind + 1) * share] = made
        tops = jnp.zeros((total, 128), jnp.float32)
        for place in range(heads):
            query, key, value = (lanes_of(kind, place) for kind in range(3))
            made_top = []
            for at, allowed, seen in ((seg_rows, causal, seg_rows), (mem_rows, mem_causal, pl.ds(0, total))):
                scores = mm_nt(qkv[micro, at, query], qkv[micro, seen, key]) * SCALE
                scores = jnp.where(allowed, scores, -1e30)
                top = jnp.max(scores, axis=1, keepdims=True)
                exponent = jnp.exp(scores - top)
                row_total = jnp.sum(exponent, axis=1, keepdims=True)
                attended[micro, at, place * HEAD_DIM : (place + 1) * HEAD_DIM] = (
                    nn(exponent, qkv[micro, seen, value]) / row_total
                )
                made_top.append(top + jnp.log(row_total))
            tops = jnp.where(lane == place, jnp.concatenate(made_top, axis=0), tops)
            if place % 2 == 1:
                attended_copy(micro, place // 2).start()
        lse[micro] = tops

    each_micro(attention)
    weight_copy(UP).wait()
    weight_copy(DOWN).wait()
    out_copy.wait()
    each_seq(lambda t: t != seq, lambda t: hand_out(t, t).wait_recv())

    def feed_forward(micro):
        for index in range(heads // 2):
            attended_copy(micro, index).wait()
        for at, tile in column_tiles:
            cut = slice(at, at + tile)
            hidden[micro, :, cut] = (
                rows[micro, :, cut]
                + nn(attended[micro], w_out_all[head, :, cut])
                + nn(got_attended[micro], w_out_all[other, :, cut])
                + residual[0:1, cut]
            )
        unit, _ = unit_rows(hidden[micro])
        normed[micro] = unit * gains[1:2] + biases[1:2]
        for at, tile in inner_tiles:
            cut = slice(at, at + tile)
            made = nn(normed[micro], w_up[:, cut]) + b_up[:, cut]
            pre[micro, :, cut] = made
            d_pre[micro, :, cut] = gelu_parts(made)[0]
        for index, (at, tile) in enumerate(column_tiles):
            part[micro, :, at : at + tile] = nn(d_pre[micro], w_down[:, at : at + tile])
            memory_tile(MEMORY, micro, index).start()
            local_tile(LOCAL, micro, index).start()

    each_micro(feed_forward)
    for name in (KEY, VALUE, QUERY):
        weight_copy(name).wait()

    def memory_write(micro):
        for index, (at, tile) in enumerate(column_tiles):
            cut = slice(at, at + tile)
            memory_tile(MEMORY, micro, index).wait()
            out_mem[micro, :, cut] = (
                part[micro, mem_rows, cut]
                + got_out[micro, local:, cut]
                + hidden[micro, mem_rows, cut]
                + residual[1:2, cut]
            )
        key_block[micro] = nn(out_mem[micro], w_key[...])
        value_block[micro] = nn(out_mem[micro], w_value[...])

        def share_block(t):
            key_copy(micro, seq, t).start()
            for g in range(2):
                value_copy(micro, seq, head, t, g).start()

        each_seq(later, share_block)

    each_micro(memory_write)

    def read_query(micro):
        for index, (at, tile) in enumerate(column_tiles):
            cut = slice(at, at + tile)
            local_tile(LOCAL, micro, index).wait()
            out_local[micro, :, cut] = (
                part[micro, own_rows, cut]
                + got_out[micro, :local, cut]
                + hidden[micro, own_rows, cut]
                + residual[1:2, cut]
            )
        query_proj[micro] = nn(out_local[micro], w_query[...])

    def memory_read(micro):
        read_query(micro)

        def got(t):
            key_copy(micro, t, t).wait_recv()
            for g in range(2):
                value_copy(micro, t, g, t, g).wait_recv()

        query_halves = halves_of(query_proj[micro])
        each_seq(earlier, got)
        key_halves = halves_of(keys[micro])
        scores = jnp.zeros((local, seqs * mem), jnp.float32)
        for by in (1, 2, 3):
            scores = scores + mm_nt(
                query_halves * turned(query_halves, by), key_halves * turned(key_halves, by)
            )
        scores = jnp.where(seen_mask(items, micro, seqs, mem), scores, 0.0)
        weights[micro] = scores
        found = nn(scores, values[micro]) / (jnp.sum(scores, axis=1, keepdims=True) + 1.0)
        read[micro] = found
        y[micro] = out_local[micro] + found

        @pl.when(section == 0)
        def _():
            for target in range(2):
                y_sent(micro, target).start()

    each_micro(memory_read)

    def grad_copy(micro):
        return copy(
            copy_slot(micro, GRAD), grad_x.at[micro], grad_y.at[micro], {SECTION: 0}
        )

    def rows_copy(micro):
        here = d_out.at[micro, own_rows]
        return copy(copy_slot(micro, D_LOCAL), here, here, partner)

    def mem_copy(micro):
        return copy(copy_slot(micro, D_MEMORY), mem_part.at[micro], got_mem.at[micro], partner)

    def back_key(micro, source, target):
        return pltpu.make_async_remote_copy(
            src_ref=d_keys.at[micro, rows_at(target * mem, mem)],
            dst_ref=from_k.at[micro, source],
            send_sem=back_sk.at[micro, target],
            recv_sem=back_rk.at[micro, source],
            device_id={SEQ: target},
            device_id_type=MESH,
        )

    def back_value(micro, source, source_head, target, target_head):
        return pltpu.make_async_remote_copy(
            src_ref=d_values.at[
                micro, rows_at(target * mem, mem), pl.ds(pl.multiple_of(target_head * dv, 128), dv)
            ],
            dst_ref=from_v.at[micro, source, source_head],
            send_sem=back_sv.at[micro, target, target_head],
            recv_sem=back_rv.at[micro, source, source_head],
            device_id={SEQ: target, HEAD: target_head},
            device_id_type=MESH,
        )

    def add_small(row, vector):
        for at in range(0, vector.shape[1], 128):
            g_small[row + at // 128 : row + at // 128 + 1] += vector[:, at : at + 128]

    def read_back(micro):
        @pl.when(section == 0)
        def _():
            grad_copy(micro).wait_recv()

        @pl.when(section == 1)
        def _():
            x_load(micro, grad_y.at[micro]).wait()

        grad = grad_y[micro]
        scores = weights[micro]
        denominator = jnp.sum(scores, axis=1, keepdims=True) + 1.0
        d_numer = grad / denominator
        d_denom = -jnp.sum(grad * read[micro], axis=1, keepdims=True) / denominator
        d_values[micro] = mm_tn(scores, d_numer)

        def send_values(t):
            for g in range(2):
                back_value(micro, seq, head, t, g).start()

        each_seq(earlier, send_values)
        d_scores = jnp.where(
            seen_mask(items, micro, seqs, mem), mm_nt(d_numer, values[micro]) + d_denom, 0.0
        )
        query_halves, key_halves = halves_of(query_proj[micro]), halves_of(keys[micro])
        d_key_halves = jnp.zeros_like(key_halves)
        for by in (1, 2, 3):
            d_feats = mm_tn(d_scores, query_halves * turned(query_halves, by))
            d_key_halves += d_feats * turned(key_halves, by) + turned(d_feats * key_halves, -by)
        d_keys[micro] = halves_back(keys[micro], d_key_halves)
        each_seq(earlier, lambda t: back_key(micro, seq, t).start())
        d_query_halves = jnp.zeros_like(query_halves)
        for by in (1, 2, 3):
            d_feats = nn(d_scores, key_halves * turned(key_halves, by))
            d_query_halves += d_feats * turned(query_halves, by) + turned(d_feats * query_halves, -by)
        query_proj[micro] = halves_back(query_proj[micro], d_query_halves)
        d_out[micro, own_rows] = grad + mm_nt(query_proj[micro], w_query[...])
        rows_copy(micro).start()

    each_micro(read_back)

    def write_back(micro):
        def got(t):
            back_key(micro, t, t).wait_recv()
            for g in range(2):
                back_value(micro, t, g, t, g).wait_recv()

        each_seq(later, got)
        key_block[micro] = jnp.sum(from_k[micro], axis=0)
        value_block[micro] = jnp.sum(from_v[micro], axis=(0, 1))
        mem_part[micro] = mm_nt(key_block[micro], w_key[...]) + mm_nt(
            value_block[micro], w_value[...]
        )
        mem_copy(micro).start()

    def forward_sent(micro):
        def sent(t):
            key_copy(micro, seq, t).wait_send()
            for g in range(2):
                value_copy(micro, seq, head, t, g).wait_send()

        each_seq(later, sent)

    each_micro(forward_sent)
    each_micro(write_back)

    def both(ref):
        return ref[...].reshape(micros * ref.shape[1], ref.shape[2])

    w_query[...] = mm_tn(both(out_local), both(query_proj))
    w_key[...] = mm_tn(both(out_mem), both(key_block))
    w_value[...] = mm_tn(both(out_mem), both(value_block))
    def feed_forward_back(micro):
        mem_copy(micro).wait()
        d_out[micro, mem_rows] = mem_part[micro] + got_mem[micro]
        rows_copy(micro).wait()
        for at, tile in inner_tiles:
            cut = slice(at, at + tile)
            activated, slope = gelu_parts(pre[micro, :, cut])
            made = slope * mm_nt(d_out[micro], w_down[cut])
            pre[micro, :, cut] = activated
            d_pre[micro, :, cut] = made
            add_small(36 + at // 128, column_sum(made))
        for index, (at, tile) in enumerate(column_tiles):
            part[micro, :, at : at + tile] = mm_nt(d_pre[micro], w_up[at : at + tile])
            tile_copy(MIX, micro, index).start()
        add_small(30, 0.5 * column_sum(d_out[micro]))

    each_micro(feed_forward_back)

    def attention_back(micro):
        unit, inverse = unit_rows(hidden[micro])
        for index, (at, tile) in enumerate(column_tiles):
            cut = slice(at, at + tile)
            tile_copy(MIX, micro, index).wait()
            got_part[micro, :, cut] += part[micro, :, cut]
        d_mixed = got_part[micro]
        normed[micro] = unit * gains[1:2] + biases[1:2]
        hidden[micro] = d_out[micro] + unit_rows_back(d_mixed * gains[1:2], unit, inverse)
        add_small(6, 0.5 * column_sum(d_mixed * unit))
        add_small(18, 0.5 * column_sum(d_mixed))
        add_small(24, 0.5 * column_sum(hidden[micro]))
        part[micro, :, :share] = mm_nt(hidden[micro], w_out[...])
        block_rows = lax.div(
            lax.broadcasted_iota(jnp.int32, (mem, share), 1), jnp.int32(HEAD_DIM)
        )
        for place in range(heads):
            query, key, value = (lanes_of(kind, place) for kind in range(3))
            cut = slice(place * HEAD_DIM, (place + 1) * HEAD_DIM)
            wide = pl.ds(place * mem, mem)
            grads = []
            for at, allowed, seen in ((seg_rows, causal, seg_rows), (mem_rows, mem_causal, pl.ds(0, total))):
                scores = mm_nt(qkv[micro, at, query], qkv[micro, seen, key]) * SCALE
                soft = jnp.exp(
                    jnp.where(allowed, scores, -1e30) - lse[micro, at, place : place + 1]
                )
                d_head = part[micro, at, cut]
                inner_dot = jnp.sum(d_head * attended[micro, at, cut], axis=1, keepdims=True)
                d_scores = soft * (mm_nt(d_head, qkv[micro, seen, value]) - inner_dot) * SCALE
                grads.append((soft, d_scores, d_head, nn(d_scores, qkv[micro, seen, key])))
            (soft, d_scores, d_head, d_query), (mem_soft, mem_scores, _, mem_query) = grads
            wide_soft[wide] = mem_soft
            wide_scores[wide] = mem_scores
            mine = block_rows == place
            wide_query[wide] = jnp.where(mine, qkv[micro, mem_rows, :share], 0.0)
            wide_grad[wide] = jnp.where(mine, part[micro, mem_rows, :share], 0.0)
            d_key = mm_tn(d_scores, qkv[micro, seg_rows, query])
            d_value = mm_tn(soft, d_head)
            qkv[micro, seg_rows, query] = d_query
            qkv[micro, mem_rows, query] = mem_query
            qkv[micro, seg_rows, key] = d_key
            qkv[micro, seg_rows, value] = d_value
        qkv[micro, mem_rows, share:] = jnp.zeros((mem, 2 * share), jnp.float32)
        qkv[micro, :, share : 2 * share] += mm_tn(wide_scores[...], wide_query[...])
        qkv[micro, :, 2 * share :] += mm_tn(wide_soft[...], wide_grad[...])
        for index, (at, tile) in enumerate(column_tiles):
            made = mm_nt(qkv[micro, :, :share], w_in[0, at : at + tile])
            for kind in (1, 2):
                made = made + mm_nt(
                    qkv[micro, :, kind * share : (kind + 1) * share], w_in[kind, at : at + tile]
                )
            part[micro, :, at : at + tile] = made
            local_tile(ROWS, micro, index).start()
            memory_tile(ROWS_MEMORY, micro, index).start()
        add_small(48, column_sum(qkv[micro, :, :share]))
        add_small(51, column_sum(qkv[micro, :, 2 * share :]))

    each_micro(attention_back)

    def finish(micro, d_normed, at_rows):
        unit, inverse = unit_rows(rows[micro, at_rows])
        add_small(0, column_sum(d_normed * unit))
        add_small(12, column_sum(d_normed))
        return hidden[micro, at_rows] + unit_rows_back(d_normed * gains[0:1], unit, inverse)

    def rows_back(micro):
        for index in range(len(column_tiles)):
            local_tile(ROWS, micro, index).wait()
            memory_tile(ROWS_MEMORY, micro, index).wait()
        grad_x[micro] = finish(micro, part[micro, own_rows] + got_out[micro, :local], own_rows)

        @pl.when(section == 1)
        def _():
            grad_copy(micro).start()

        mem_half = rows_at(local + head * half_mem, half_mem)
        d_tokens = finish(micro, part[micro, own_mem_rows] + got_out[micro, mem_half], own_mem_rows)
        for at in range(0, width, 128):
            row = 56 + (at // 128) * half_mem
            g_small[row : row + half_mem] += d_tokens[:, at : at + 128]

    along = seqs // lanes
    z, lane_y = seq // lanes, lax.rem(seq, lanes)
    place = lane_y * along + jnp.where(lax.rem(lane_y, 2) == 0, z, along - 1 - z)

    def device(spot):
        row = spot // along
        column = lax.rem(spot, along)
        column = jnp.where(lax.rem(row, 2) == 0, column, along - 1 - column)
        return {SEQ: column * lanes + row}

    targets = (device(lax.rem(place + 1, seqs)), device(lax.rem(place + seqs - 1, seqs)))
    signs = (1, -1)
    kinds = range(w_in.shape[0])
    sources = [w_down, w_value, w_up, w_out, *(w_in.at[kind] for kind in kinds), g_small, got_whole]
    results = [down_sum, value_sum, up_sum, out_sum, *(in_sum.at[kind] for kind in kinds)]
    results += [small_sum, whole_sum.at[head]]
    count = len(sources)
    ways = [(index, way) for index in range(count) for way in range(2)]
    last = seqs - 2

    def block(ref, way, spot):
        size = ref.shape[0] // seqs
        half = size // 2
        spot = lax.rem(spot + 2 * seqs, seqs)
        return ref.at[pl.ds(pl.multiple_of(spot * size + way * half, half), half)]

    def slot_of(index, way, step):
        return slots[index].at[way, lax.rem(step, SLOTS)]

    def up_copy(index, way, step, source):
        turn = lax.rem(step, SLOTS)
        return pltpu.make_async_remote_copy(
            src_ref=source,
            dst_ref=slot_of(index, way, step),
            send_sem=send_up.at[turn, way, index],
            recv_sem=recv_up.at[turn, way, index],
            device_id=targets[way],
            device_id_type=MESH,
        )

    def on_copy(index, way, step, source, target):
        return pltpu.make_async_remote_copy(
            src_ref=source,
            dst_ref=target,
            send_sem=send_on.at[step, way, index],
            recv_sem=recv_on.at[step, way, index],
            device_id=targets[way],
            device_id_type=MESH,
        )

    def over(source, target, number):
        return pltpu.make_async_remote_copy(
            src_ref=source,
            dst_ref=target,
            send_sem=send_x.at[number],
            recv_sem=recv_x.at[number],
            device_id=partner,
            device_id_type=MESH,
        )

    def begin(*indices):
        for index in indices:
            for way in range(2):
                up_copy(index, way, 0, block(sources[index], way, place)).start()

    for at, tile in inner_tiles:
        cut = slice(at, at + tile)
        w_down[cut] = mm_tn(both(pre.at[:, :, cut]), both(d_out))
    begin(0, 1)
    each_micro(rows_back)
    small_copy = over(g_small, got_small, 0)
    small_copy.start()

    def whole_copy(matrix):
        return over((w_query, w_key)[matrix], got_whole, 1)

    for matrix in range(2):

        @pl.when(head == matrix)
        def _(matrix=matrix):
            whole_copy(1 - matrix).start()

    for at, tile in inner_tiles:
        cut = slice(at, at + tile)
        w_up[:, cut] = mm_tn(both(normed), both(d_pre.at[:, :, cut]))
    begin(2)
    w_out_all[head] = mm_tn(both(attended), both(hidden))
    begin(3)
    for micro in range(micros):
        unit, _ = unit_rows(rows[micro])
        normed[micro] = unit * gains[0:1] + biases[0:1]
    for kind in kinds:
        w_in[kind] = mm_tn(both(normed), both(qkv.at[:, :, kind * share : (kind + 1) * share]))
        begin(4 + kind)
    small_copy.wait()
    g_small[0:SHARED_ROWS] += got_small[0:SHARED_ROWS]
    begin(count - 2)
    whole_copy(0).wait()
    for matrix in range(2):

        @pl.when(head == matrix)
        def _(matrix=matrix):
            got_whole[...] += (w_query, w_key)[matrix][...]

    begin(count - 1)

    def sum_up(step, carry):
        @pl.when(step >= SLOTS)
        def _():
            for way in range(2):
                pl.semaphore_wait(free.at[way], 1)

        for index, way in ways:
            got = slot_of(index, way, step - 1)
            up_copy(index, way, step - 1, got).wait_recv()
            got[...] += block(sources[index], way, place - signs[way] * step)[...]
            up_copy(index, way, step, got).start()
        for index, way in ways:
            up_copy(index, way, step - 1, slot_of(index, way, step)).wait_send()

        @pl.when(jnp.logical_and(step >= 2, step + 1 < seqs - 1))
        def _():
            for way in range(2):
                pl.semaphore_signal(
                    free.at[way], inc=1, device_id=targets[1 - way], device_id_type=MESH
                )

        return carry

    lax.fori_loop(1, seqs - 1, sum_up, 0)

    def hand_over(way, spot, step):
        mine = block(whole_sum.at[head], way, spot)
        return over(mine, mine, 2 + way * seqs + step)

    def home(index, way):
        return pltpu.make_async_copy(
            slot_of(index, way, last),
            block(results[index], way, place + signs[way]),
            store.at[way, index],
        )

    for index, way in ways:
        got = slot_of(index, way, last)
        up_copy(index, way, last, got).wait_recv()
        spot = place + signs[way]
        got[...] += block(sources[index], way, spot)[...]
        target = block(results[index], way, spot)
        on_copy(index, way, 0, got, target).start()
        home(index, way).start()
        if index == count - 1:
            over(got, target, 2 + way * seqs).start()

    def pass_on(step, carry):
        for index, way in ways:
            spot = place - signs[way] * (step - 1)
            here = block(results[index], way, spot)
            on_copy(index, way, step - 1, here, here).wait_recv()
            on_copy(index, way, step, here, here).start()
            if index == count - 1:
                hand_over(way, spot, step).start()
        return carry

    lax.fori_loop(1, seqs - 1, pass_on, 0)
    for index, way in ways:
        spot = place - signs[way] * last
        here = block(results[index], way, spot)
        on_copy(index, way, last, here, here).wait_recv()
        if index == count - 1:
            hand_over(way, spot, seqs - 1).start()
        home(index, way).wait()
        up_copy(index, way, last, slot_of(index, way, last)).wait_send()

    def passed(step, carry):
        for index, way in ways:
            own = slot_of(index, way, 0)
            on_copy(index, way, step, own, own).wait_send()
        return carry

    lax.fori_loop(0, seqs - 1, passed, 0)

    def crossed(step, carry):
        for way in range(2):
            theirs = block(whole_sum.at[other], way, place - signs[way] * (step - 1))
            over(theirs, theirs, 2 + way * seqs + step).wait()
        return carry

    lax.fori_loop(0, seqs, crossed, 0)

    tokens.wait_send()
    over_out().wait_send()
    each_seq(lambda t: t != seq, lambda t: hand_out(seq, t).wait_send())

    def all_sent(micro):
        @pl.when(section == 0)
        def _():
            x_copy(micro).wait_send()
            for target in range(2):
                y_sent(micro, target).wait_send()

        @pl.when(section == 1)
        def _():
            grad_copy(micro).wait_send()

        def sent(t):
            back_key(micro, seq, t).wait_send()
            for g in range(2):
                back_value(micro, seq, head, t, g).wait_send()

        each_seq(earlier, sent)

    each_micro(all_sent)


def shapes_of(*shapes):
    return tuple(jax.ShapeDtypeStruct(shape, jnp.float32) for shape in shapes)


def buffers(*shapes):
    return [pltpu.VMEM(shape, jnp.float32) for shape in shapes]


def dma(*shape):
    return pltpu.SemaphoreType.DMA(shape)


def params_of(number):
    return pltpu.CompilerParams(
        collective_id=number, has_side_effects=True, vmem_limit_bytes=62 << 20
    )


def shards_of_two(
    boundary_in,
    short_items,
    norm_gains,
    norm_biases,
    projection_in,
    head_bias,
    projection_out,
    residual_bias,
    up_weight,
    up_bias,
    down_weight,
    memory_tokens,
    query_memory,
    key_memory,
    value_memory,
):
    seqs = lax.axis_size(SEQ)
    x = boundary_in[0]
    micros, local, width = x.shape
    w_in = projection_in[0].transpose(1, 0, 2)
    share = w_in.shape[2]
    inner = up_weight.shape[2]
    half_mem = memory_tokens.shape[1]
    mem = 2 * half_mem
    segment = 2 * local
    total = segment + mem
    dk, dv = key_memory.shape[2], value_memory.shape[2]
    stored = seqs * mem
    records = (
        (total, width),
        (total, 3 * share),
        (total, share),
        (total, 128),
        (total, width),
        (total, inner),
        (local, width),
        (mem, width),
        (stored, dk),
        (stored, 2 * dv),
        (local, dk),
        (local, stored),
        (local, width),
    )
    weights = (
        w_in,
        up_weight[0],
        down_weight[0],
        value_memory[0],
        query_memory[0],
        key_memory[0],
    )
    w_out = projection_out[0]
    few = (norm_gains[0], norm_biases[0], head_bias[0], residual_bias[0], up_bias, memory_tokens[0])
    slots = 2 + micros * COPY_SLOTS
    ring = [w.shape for w in (down_weight[0], value_memory[0], up_weight[0], w_out)]
    ring += [w_in.shape[1:]] * 3 + [(16 * seqs, 128), (width, dk)]
    g_down, g_up, g_in, g_out, g_value, small, whole, y, grad_x = pl.pallas_call(
        functools.partial(layers_kernel, 2),
        out_shape=shapes_of(
            down_weight[0].shape,
            up_weight[0].shape,
            w_in.shape,
            w_out.shape,
            value_memory[0].shape,
            (16 * seqs, 128),
            (2, width, dk),
            (micros, local, width),
            (micros, local, width),
        ),
        in_specs=[SMEM, HBM] + [VMEM] * len(few) + [HBM] * (len(weights) + 1),
        out_specs=(HBM,) * 7 + (VMEM,) * 2,
        scratch_shapes=buffers(
            *(w.shape for w in weights),
            *((micros, *record) for record in records),
            (2, *w_out.shape),
            (micros, total, share),
            (micros, total, width),
            (micros, total, inner),
            (micros, total, width),
            (micros, total, width),
            (micros, total, width),
            (micros, local + mem, width),
            (mem, width),
            (micros, mem, dk),
            (micros, mem, dv),
            (micros, seqs, mem, dk),
            (micros, seqs, 2, mem, dv),
            (micros, mem, width),
            (micros, mem, width),
            (micros, local, width),
            (mem * (share // HEAD_DIM), total),
            (mem * (share // HEAD_DIM), total),
            (mem * (share // HEAD_DIM), share),
            (mem * (share // HEAD_DIM), share),
            (16 * seqs, 128),
            (16 * seqs, 128),
            (width, dk),
            *((2, SLOTS, height // (2 * seqs), columns) for height, columns in ring),
        )
        + [dma(len(weights) + 1 + micros), dma(2, len(ring)), dma(slots), dma(slots)]
        + [dma(micros, seqs), dma(micros, seqs), dma(micros, seqs, 2), dma(micros, seqs, 2)] * 2
        + [dma(seqs), dma(seqs)]
        + [dma(SLOTS, 2, len(ring)), dma(SLOTS, 2, len(ring))]
        + [dma(seqs - 1, 2, len(ring)), dma(seqs - 1, 2, len(ring))]
        + [dma(2 + 2 * seqs), dma(2 + 2 * seqs), pltpu.SemaphoreType.REGULAR((2,))],
        compiler_params=params_of(0),
        name="layers",
    )(short_items, x, *few, *weights, w_out)
    section = lax.axis_index(SECTION)
    vectors = small[:36].reshape(3, 1, 2, width)
    return (
        jnp.where(section == 0, grad_x, y)[None],
        vectors[0],
        vectors[1],
        g_in.transpose(1, 0, 2)[None],
        small[48:54].reshape(1, 2, share),
        g_out[None],
        vectors[2],
        g_up[None],
        small[36:48].reshape(1, inner),
        g_down[None],
        small[56 : 56 + 6 * half_mem]
        .reshape(6, half_mem, 128)
        .transpose(1, 0, 2)
        .reshape(1, half_mem, width),
        whole[0][None],
        whole[1][None],
        g_value[None],
    )


def solution(mesh):
    return jax.shard_map(
        shards_of_two if mesh.shape[HEAD] == 2 else shards,
        mesh=mesh,
        in_specs=(
            P(SECTION, None, (SEQ, HEAD), None),
            P(),
            P(SECTION, None, None),
            P(SECTION, None, None),
            P(SECTION, None, None, HEAD),
            P(SECTION, None, HEAD),
            P(SECTION, HEAD, None),
            P(SECTION, None, None),
            P(SECTION, None, HEAD),
            P(SECTION, HEAD),
            P(SECTION, HEAD, None),
            P(SECTION, HEAD, None),
            P(SECTION, None, None),
            P(SECTION, None, None),
            P(SECTION, None, HEAD),
        ),
        out_specs=(
            P(SECTION, None, (SEQ, HEAD), None),
            P(SECTION, None, None),
            P(SECTION, None, None),
            P(SECTION, None, None, HEAD),
            P(SECTION, None, HEAD),
            P(SECTION, HEAD, None),
            P(SECTION, None, None),
            P(SECTION, None, HEAD),
            P(SECTION, HEAD),
            P(SECTION, HEAD, None),
            P(SECTION, HEAD, None),
            P(SECTION, None, None),
            P(SECTION, None, None),
            P(SECTION, None, HEAD),
        ),
        check_vma=False,
    )
```

```python
import functools
import math
from types import SimpleNamespace

import jax
import jax.numpy as jnp
from jax import lax
from jax.experimental import pallas as pl
from jax.experimental.pallas import tpu as pltpu
from jax.sharding import PartitionSpec as P

SECTION, SEQ, HEAD = "section", "seq", "head"
HEAD_DIM = 64
EPSILON = 1e-05
SCALE = 1.0 / math.sqrt(HEAD_DIM)
MESH = pl.DeviceIdType.MESH
VMEM = pl.BlockSpec(memory_space=pltpu.VMEM)
HBM = pl.BlockSpec(memory_space=pltpu.HBM)
SMEM = pl.BlockSpec(memory_space=pltpu.SMEM)
SHARED_ROWS = 36


def mm(left, right, dims=((1,), (0,))):
    return lax.dot_general(
        left, right, (dims, ((), ())), precision=lax.Precision.HIGH, preferred_element_type=jnp.float32
    )


def mm_nt(left, right):
    return mm(left, right, ((1,), (1,)))


def mm_tn(left, right):
    return mm(left, right, ((0,), (0,)))


def unit_rows(rows):
    centred = rows - jnp.mean(rows, axis=-1, keepdims=True)
    inverse = lax.rsqrt(jnp.mean(centred * centred, axis=-1, keepdims=True) + EPSILON)
    return centred * inverse, inverse


def unit_rows_back(d_unit, unit, inverse):
    return inverse * (
        d_unit
        - jnp.mean(d_unit, axis=-1, keepdims=True)
        - unit * jnp.mean(d_unit * unit, axis=-1, keepdims=True)
    )


def features(projected):
    halves = jnp.concatenate([jax.nn.softplus(projected), jax.nn.softplus(-projected)], axis=-1)
    return jnp.concatenate(
        [halves * jnp.roll(halves, rolled_by, axis=-1) for rolled_by in (1, 2, 3)], axis=-1
    )


def gelu_tanh(values_in):
    return jax.nn.gelu(values_in, approximate=True)


def head_sum_rows(rows, share):
    segment = lax.axis_size(HEAD) * share
    turn = lax.axis_index(HEAD) * share
    total = lax.psum(
        jnp.concatenate([jnp.roll(rows[:segment], turn, axis=0), rows[segment:]], axis=0), HEAD
    )
    return jnp.concatenate([jnp.roll(total[:segment], -turn, axis=0), total[segment:]], axis=0)


def head_rows(local):
    gathered = lax.all_gather(local, HEAD, axis=0, tiled=True)
    return jnp.roll(gathered, -lax.axis_index(HEAD) * local.shape[0], axis=0)


def head_scatter(rows):
    share = rows.shape[0] // lax.axis_size(HEAD)
    placed = jnp.roll(rows, lax.axis_index(HEAD) * share, axis=0)
    return lax.psum_scatter(placed, HEAD, scatter_dimension=0, tiled=True)


def heads_of(part):
    return part.reshape(part.shape[0], -1, HEAD_DIM).transpose(1, 0, 2)


def rows_of(part):
    return part.transpose(1, 0, 2).reshape(part.shape[1], -1)


def bmm(left, right, left_dim, right_dim):
    return lax.dot_general(
        left,
        right,
        (((left_dim,), (right_dim,)), ((0,), (0,))),
        precision=lax.Precision.HIGH,
        preferred_element_type=jnp.float32,
    )


def layer_forward(local, params, mask, allowed):
    width = local.shape[1]
    local_count = local.shape[0]
    segment = lax.axis_size(HEAD) * local_count
    rows = jnp.concatenate([head_rows(local), params.memory], axis=0)
    unit_one, inverse_one = unit_rows(rows)
    normed = unit_one * params.gains[0] + params.biases[0]
    projected = mm(normed, params.proj_in) + params.in_bias
    share = projected.shape[1] // 3
    query, key, value = (heads_of(projected[:, i * share : (i + 1) * share]) for i in range(3))
    scores = jnp.where(allowed, bmm(query, key, 2, 2) * SCALE, -1e30)
    row_top = jnp.max(scores, axis=-1, keepdims=True)
    exponent = jnp.exp(scores - row_top)
    soft = exponent / jnp.sum(exponent, axis=-1, keepdims=True)
    attended = rows_of(bmm(soft, value, 2, 1))
    hidden = rows + head_sum_rows(mm(attended, params.proj_out), local_count) + params.residual[0]
    unit_two, inverse_two = unit_rows(hidden)
    mixed = unit_two * params.gains[1] + params.biases[1]
    inner_pre = mm(mixed, params.up) + params.up_bias
    inner_act = gelu_tanh(inner_pre)
    partial = mm(inner_act, params.down)
    out_local = head_scatter(partial[:segment]) + hidden[:local_count] + params.residual[1]
    out_mem = lax.psum(partial[segment:], HEAD) + hidden[segment:] + params.residual[1]
    key_proj = mm(out_mem, params.key_mem)
    values = mm(out_mem, params.value_mem)
    gathered = lax.all_gather(jnp.concatenate([key_proj, values], axis=1), SEQ, axis=0, tiled=True)
    dk = key_proj.shape[1]
    keys_all = gathered[:, :dk]
    values_all = lax.all_gather(gathered[:, dk:], HEAD, axis=1, tiled=True)
    key_feats = features(keys_all)
    query_proj = mm(out_local, params.query_mem)
    query_feats = features(query_proj)
    weights = mask * mm_nt(query_feats, key_feats)
    denominator = jnp.sum(weights, axis=1, keepdims=True) + 1.0
    read = mm(weights, values_all) / denominator
    return SimpleNamespace(
        unit_one=unit_one,
        inverse_one=inverse_one,
        projected=projected,
        attended=attended,
        soft=soft,
        unit_two=unit_two,
        inverse_two=inverse_two,
        inner_pre=inner_pre,
        out_local=out_local,
        out_mem=out_mem,
        keys_all=keys_all,
        values_all=values_all,
        query_proj=query_proj,
        weights=weights,
        denominator=denominator,
        read=read,
        output=out_local + read,
    )


def layer_backward(grad, record, params, mask):
    head_count = lax.axis_size(HEAD)
    seq_count = lax.axis_size(SEQ)
    width = grad.shape[1]
    local_count = grad.shape[0]
    segment = head_count * local_count
    denominator = record.denominator
    d_numer = grad / denominator
    d_denom = -jnp.sum(grad * record.read, axis=1, keepdims=True) / denominator
    d_weights = mask * (mm_nt(d_numer, record.values_all) + d_denom)
    key_feats, keys_back = jax.vjp(features, record.keys_all)
    query_feats, query_back = jax.vjp(features, record.query_proj)
    d_query_proj = query_back(mm(d_weights, key_feats))[0]
    d_keys = keys_back(mm_tn(d_weights, query_feats))[0]
    d_values = mm_tn(record.weights, d_numer)
    d_memory = lax.psum_scatter(
        jnp.concatenate([d_keys, d_values], axis=1), SEQ, scatter_dimension=0, tiled=True
    )
    dk = d_keys.shape[1]
    d_key_proj = d_memory[:, :dk]
    d_value = lax.psum_scatter(
        d_memory[:, dk:], HEAD, scatter_dimension=1, tiled=True
    )
    d_mem = lax.psum(
        mm_nt(d_key_proj, params.key_mem) + mm_nt(d_value, params.value_mem), HEAD
    )
    d_local = grad + mm_nt(d_query_proj, params.query_mem)
    d_result = jnp.concatenate([head_rows(d_local), d_mem], axis=0)
    inner_act, gelu_back = jax.vjp(gelu_tanh, record.inner_pre)
    grad_down = mm_tn(inner_act, d_result)
    d_pre = gelu_back(mm_nt(d_result, params.down))[0]
    gains, biases = params.gains, params.biases
    mixed = record.unit_two * gains[1] + biases[1]
    grad_up = mm_tn(mixed, d_pre)
    d_mixed = head_sum_rows(mm_nt(d_pre, params.up), local_count)
    d_hidden = d_result + unit_rows_back(d_mixed * gains[1], record.unit_two, record.inverse_two)
    grad_out = mm_tn(record.attended, d_hidden)
    d_attended = mm_nt(d_hidden, params.proj_out)
    share = d_attended.shape[1]
    query, key, value = (
        heads_of(record.projected[:, i * share : (i + 1) * share]) for i in range(3)
    )
    soft = record.soft
    d_heads = heads_of(d_attended)
    inner_dot = jnp.sum(d_heads * heads_of(record.attended), axis=-1, keepdims=True)
    d_scores = soft * (bmm(d_heads, value, 2, 2) - inner_dot) * SCALE
    d_projected = jnp.concatenate(
        [
            rows_of(bmm(d_scores, key, 2, 1)),
            rows_of(bmm(d_scores, query, 1, 1)),
            rows_of(bmm(soft, d_heads, 1, 1)),
        ],
        axis=1,
    )
    normed = record.unit_one * gains[0] + biases[0]
    grad_in = mm_tn(normed, d_projected)
    columns = jnp.sum(d_projected, axis=0)
    grad_head_bias = jnp.stack([columns[:share], columns[2 * share :]])
    d_normed_all = mm_nt(d_projected, params.proj_in)
    d_normed = head_scatter(d_normed_all[:segment])
    d_normed_mem = lax.psum_scatter(
        d_normed_all[segment:], HEAD, scatter_dimension=0, tiled=True
    )
    mem_count = d_normed_mem.shape[0]
    own_mem = segment + lax.axis_index(HEAD) * mem_count

    def own(values):
        return jnp.concatenate(
            [values[:local_count], lax.dynamic_slice_in_dim(values, own_mem, mem_count, 0)], axis=0
        )

    d_normed_own = jnp.concatenate([d_normed, d_normed_mem], axis=0)
    unit_own = own(record.unit_one)
    d_rows = own(d_hidden) + unit_rows_back(
        d_normed_own * gains[0], unit_own, own(record.inverse_one)
    )
    part = 1.0 / head_count
    sharded = (
        grad_in,
        grad_head_bias,
        grad_out,
        grad_up,
        jnp.sum(d_pre, axis=0),
        grad_down,
        d_rows[local_count:],
        mm_tn(record.out_mem, d_value),
    )
    shared = (
        jnp.stack(
            [
                jnp.sum(d_normed_own * unit_own, axis=0),
                part * jnp.sum(d_mixed * record.unit_two, axis=0),
            ]
        ),
        jnp.stack([jnp.sum(d_normed_own, axis=0), part * jnp.sum(d_mixed, axis=0)]),
        part * jnp.stack([jnp.sum(d_hidden, axis=0), jnp.sum(d_result, axis=0)]),
        mm_tn(record.out_local, d_query_proj),
        mm_tn(record.out_mem, d_key_proj),
    )
    return (d_rows[:local_count], sharded, shared)


def passed_along(value, axis, steps):
    count = lax.axis_size(axis)
    first, last = (max(0, -steps), min(count, count - steps))
    return lax.ppermute(value, axis, [(source, source + steps) for source in range(first, last)])


def shards(
    boundary_in,
    short_items,
    norm_gains,
    norm_biases,
    projection_in,
    head_bias,
    projection_out,
    residual_bias,
    up_weight,
    up_bias,
    down_weight,
    memory_tokens,
    query_memory,
    key_memory,
    value_memory,
):
    section = lax.axis_index(SECTION)
    sections = lax.axis_size(SECTION)
    head_count = lax.axis_size(HEAD)
    head_place = lax.axis_index(HEAD)
    seq_count = lax.axis_size(SEQ)
    seq_place = lax.axis_index(SEQ)
    micro_total = boundary_in.shape[1]
    local_count = boundary_in.shape[2]
    width = boundary_in.shape[3]
    segment = head_count * local_count
    head_width = projection_in.shape[3]
    memory_all = lax.all_gather(memory_tokens[0], HEAD, axis=0, tiled=True)
    mem_count = memory_all.shape[0]
    params = SimpleNamespace(
        gains=norm_gains[0],
        biases=norm_biases[0],
        proj_in=projection_in[0].reshape(width, 3 * head_width),
        in_bias=jnp.concatenate(
            [head_bias[0, 0], jnp.zeros((head_width,), jnp.float32), head_bias[0, 1]]
        ),
        proj_out=projection_out[0],
        residual=residual_bias[0],
        up=up_weight[0],
        up_bias=up_bias[0],
        down=down_weight[0],
        memory=memory_all,
        query_mem=query_memory[0],
        key_mem=key_memory[0],
        value_mem=value_memory[0],
    )
    ordinal = jnp.arange(segment)
    places = jnp.concatenate(
        [(ordinal + head_place * local_count) % segment, segment + jnp.arange(mem_count)]
    )
    allowed = (places[:, None] >= places[None, :])[None]

    positions = jnp.arange(seq_count)
    masks = []
    for micro in range(micro_total):
        if micro == 0:
            item = jnp.zeros((seq_count,), jnp.int32)
        else:
            ends = jnp.cumsum(short_items[micro - 1])
            item = jnp.sum((positions[:, None] >= ends[None, :]).astype(jnp.int32), axis=1)
        own_item = jnp.sum(jnp.where(positions == seq_place, item, 0))
        seen = jnp.logical_and(positions < seq_place, item == own_item).astype(jnp.float32)
        masks.append(jnp.repeat(seen, mem_count)[None, :])
    masks = jnp.stack(masks)

    tick_total = micro_total + sections - 1
    received = jnp.zeros_like(boundary_in[0, 0])
    records = []
    for tick in range(tick_total):
        micro = jnp.clip(tick - section, 0, micro_total - 1)
        local = jnp.where(section == 0, boundary_in[0, min(tick, micro_total - 1)], received)
        records.append(layer_forward(local, params, masks[micro], allowed))
        if tick + 1 < tick_total:
            received = passed_along(records[-1].output, SECTION, 1)
    back_received = jnp.zeros_like(boundary_in[0, 0])
    grads_input = []
    total = None
    for tick in range(tick_total):
        raw = tick - (sections - 1 - section)
        valid = jnp.logical_and(raw >= 0, raw < micro_total)
        micro = jnp.clip(raw, 0, micro_total - 1)
        grad = jnp.where(
            section == sections - 1, boundary_in[0, min(tick, micro_total - 1)], back_received
        )
        kept = [
            vars(records[min(max(tick - (sections - 1 - place), 0), micro_total - 1) + place])
            for place in range(sections)
        ]
        record = SimpleNamespace(
            **jax.tree.map(lambda *kinds: lax.select_n(section, *kinds), *kept)
        )
        grad_x, sharded, shared = layer_backward(grad, record, params, masks[micro])
        fresh = jax.tree.map(lambda part: jnp.where(valid, part, 0.0), (sharded, shared))
        total = fresh if total is None else jax.tree.map(jnp.add, total, fresh)
        grads_input.append(grad_x)
        if tick + 1 < tick_total:
            back_received = passed_along(grad_x, SECTION, -1)
    sharded, shared = total
    grad_in, grad_heads_bias, grad_out, grad_up, grad_up_b, grad_down, grad_mem, grad_value = lax.psum(
        sharded, SEQ
    )
    grad_gains, grad_biases, grad_residual, grad_query, grad_key = lax.psum(shared, (SEQ, HEAD))
    finished_grads = jnp.stack(
        [grads_input[micro + sections - 1] for micro in range(micro_total)]
    )
    finished_outputs = jnp.stack(
        [records[micro + sections - 1].output for micro in range(micro_total)]
    )
    boundary_out = jnp.where(section == 0, finished_grads, finished_outputs)[None]
    return (
        boundary_out,
        grad_gains[None],
        grad_biases[None],
        grad_in.reshape(projection_in.shape),
        grad_heads_bias[None],
        grad_out[None],
        grad_residual[None],
        grad_up[None],
        grad_up_b[None],
        grad_down[None],
        grad_mem[None],
        grad_query[None],
        grad_key[None],
        grad_value[None],
    )


def barrier_with(pairs, wait_count):
    barrier = pltpu.get_barrier_semaphore()
    for condition, device in pairs:

        @pl.when(condition)
        def _(device=device):
            pl.semaphore_signal(barrier, inc=1, device_id=device, device_id_type=MESH)

    @pl.when(wait_count > 0)
    def _():
        pl.semaphore_wait(barrier, wait_count)


def nn(left, right):
    return mm(left, right)


def lane_tiles(width):
    tile = 256 if width % 256 == 0 else width
    return [(at, tile) for at in range(0, width, tile)]


def rows_at(start, count):
    return pl.ds(pl.multiple_of(start, count), count)


def halves_of(projected):
    small = jnp.log1p(jnp.exp(-jnp.abs(projected)))
    return jnp.concatenate(
        [jnp.maximum(projected, 0.0) + small, jnp.maximum(-projected, 0.0) + small], axis=1
    )


def halves_back(projected, d_halves):
    width = projected.shape[1]
    rising = 1.0 / (1.0 + jnp.exp(-projected))
    falling = 1.0 / (1.0 + jnp.exp(projected))
    return d_halves[:, :width] * rising - d_halves[:, width:] * falling


def turned(values, by):
    return pltpu.roll(values, by % values.shape[1], 1)


GELU_IN = math.sqrt(2.0 / math.pi)


def gelu_parts(pre):
    cubic = 0.044715 * pre * pre
    bent = jnp.tanh(GELU_IN * pre * (1.0 + cubic))
    half = 0.5 * (1.0 + bent)
    slope = half + 0.5 * pre * (1.0 - bent * bent) * GELU_IN * (1.0 + 3.0 * cubic)
    return pre * half, slope


def seen_mask(items, micro, seqs, mem):
    seq = lax.axis_index(SEQ)
    row_seq = lax.div(lax.broadcasted_iota(jnp.int32, (1, seqs * mem), 1), jnp.int32(mem))
    end = jnp.int32(0)
    own = jnp.int32(0)
    item = jnp.zeros((1, seqs * mem), jnp.int32)
    for piece in range(items.shape[1]):
        end = end + items[jnp.maximum(micro - 1, 0), piece]
        bound = jnp.where(micro == 0, seqs, end)
        own = own + (seq >= bound).astype(jnp.int32)
        item = item + (row_seq >= bound).astype(jnp.int32)
    return jnp.logical_and(row_seq < seq, item == own)


WEIGHTS = IN, UP, DOWN, VALUE, QUERY, KEY = tuple(range(6))
COPIES = (1, 2, 3, 3, 3, 1, 1, 1, 3, 3, 3)
(X_IN, Y_OUT, PART, LOCAL, MEMORY, GRAD, D_LOCAL, D_MEMORY, MIX, ROWS, ROWS_MEMORY) = range(11)
COPY_SLOTS = sum(COPIES)
TOKENS, OUT_SHARE = range(2)


def copy_slot(micro, kind, index=0):
    return 2 + micro * COPY_SLOTS + sum(COPIES[:kind]) + index


def column_sum(values_in):
    return jnp.sum(values_in, axis=0, keepdims=True)


SLOTS = 3
AHEAD = 4


def layers_kernel(lanes, *refs):
    refs = list(refs)

    def take(count):
        taken, refs[:] = refs[:count], refs[count:]
        return taken

    items, x, gains, biases, head_bias, residual, b_up, mem_tokens = take(8)
    weights_in = take(len(WEIGHTS))
    (w_out_in,) = take(1)
    down_sum, up_sum, in_sum, out_sum, value_sum, small_sum, whole_sum = take(7)
    y, grad_x = take(2)
    held = take(len(WEIGHTS))
    w_in, w_up, w_down, w_value, w_query, w_key = held
    rows, qkv, attended, lse, hidden, pre = take(6)
    out_local, out_mem, keys, values, query_proj, weights, read = take(7)
    w_out_all, got_attended = take(2)
    (
        normed, d_pre, d_out, part, got_part, got_out, mem_all, key_block, value_block, from_k, from_v,
        mem_part, got_mem, grad_y, wide_scores, wide_soft, wide_query, wide_grad,
        g_small, got_small, got_whole,
    ) = take(21)
    d_keys, d_values = keys, read
    slots = take(9)
    load, store, send, recv, send_k, recv_k, send_v, recv_v = take(8)
    back_sk, back_rk, back_sv, back_rv, send_w, recv_w = take(6)
    send_up, recv_up, send_on, recv_on, send_x, recv_x, free, go = refs

    section, seq, head = (lax.axis_index(name) for name in (SECTION, SEQ, HEAD))
    seqs = lax.axis_size(SEQ)
    micros, local, width = x.shape
    segment = 2 * local
    mem = out_mem.shape[1]
    half_mem = mem // 2
    total = segment + mem
    share = w_in.shape[2]
    inner = w_up.shape[1]
    heads = share // HEAD_DIM
    dv = w_value.shape[1]
    other = 1 - head
    partner = {HEAD: other}
    own_rows, other_rows = rows_at(head * local, local), rows_at(other * local, local)
    own_mem = rows_at(head * half_mem, half_mem)
    own_mem_rows = rows_at(segment + head * half_mem, half_mem)
    seg_rows, mem_rows = pl.ds(0, segment), pl.ds(segment, mem)
    column_tiles = [(at, width // 3) for at in range(0, width, width // 3)]
    inner_tiles = lane_tiles(inner)

    def copy(slot, source, target, device):
        return pltpu.make_async_remote_copy(
            src_ref=source,
            dst_ref=target,
            send_sem=send.at[slot],
            recv_sem=recv.at[slot],
            device_id=device,
            device_id_type=MESH,
        )

    def weight_copy(name):
        return pltpu.make_async_copy(
            weights_in[name], held[name], load.at[name]
        )

    out_copy = pltpu.make_async_copy(w_out_in, w_out_all.at[head], load.at[len(WEIGHTS)])
    w_out = w_out_all.at[head]

    def each_micro(stage):
        def body(micro, carry):
            stage(micro)
            return carry

        lax.fori_loop(0, micros, body, 0)

    def each_seq(condition, act):
        for t in range(seqs):

            @pl.when(condition(t))
            def _(t=t):
                act(t)

    def later(t):
        return t > seq

    def earlier(t):
        return t < seq

    out_copy.start()
    for name in WEIGHTS:
        weight_copy(name).start()
    keys[...] = jnp.zeros_like(keys)
    values[...] = jnp.zeros_like(values)
    from_k[...] = jnp.zeros_like(from_k)
    from_v[...] = jnp.zeros_like(from_v)
    g_small[...] = jnp.zeros_like(g_small)
    mem_all[own_mem] = mem_tokens[...]
    barrier_with(
        [(seq >= 0, partner)]
        + [(t != seq, {SEQ: t, HEAD: g}) for t in range(seqs) for g in range(2)]
        + [(section == 1, {SECTION: 0, HEAD: g}) for g in range(2)]
        + [(section == 0, {SECTION: 1})],
        1 + 2 * (seqs - 1) + 2 - section,
    )

    tokens = copy(TOKENS, mem_tokens, mem_all.at[own_mem], partner)

    def x_load(micro, target):
        return pltpu.make_async_copy(x.at[micro], target, load.at[len(WEIGHTS) + 1 + micro])

    def x_copy(micro):
        return copy(copy_slot(micro, X_IN), x.at[micro], rows.at[micro, own_rows], partner)

    def y_sent(micro, target_head):
        return pltpu.make_async_remote_copy(
            src_ref=y.at[micro],
            dst_ref=rows.at[micro, own_rows],
            send_sem=send.at[copy_slot(micro, Y_OUT, target_head)],
            recv_sem=recv.at[copy_slot(micro, Y_OUT, head)],
            device_id={SECTION: 1, HEAD: target_head},
            device_id_type=MESH,
        )

    def y_got(micro, source_head):
        here = rows.at[micro, rows_at(source_head * local, local)]
        return copy(copy_slot(micro, Y_OUT, source_head), here, here, partner)

    def tile_copy(kind, micro, index):
        at, tile = column_tiles[index]
        return copy(
            copy_slot(micro, kind, index),
            part.at[micro, :, at : at + tile],
            got_part.at[micro, :, at : at + tile],
            partner,
        )

    def attended_copy(micro, index):
        cut = slice(index * 2 * HEAD_DIM, (index + 1) * 2 * HEAD_DIM)
        return copy(
            copy_slot(micro, PART, index),
            attended.at[micro, :, cut],
            got_attended.at[micro, :, cut],
            partner,
        )

    def local_tile(kind, micro, index):
        at, tile = column_tiles[index]
        return copy(
            copy_slot(micro, kind, index),
            part.at[micro, other_rows, at : at + tile],
            got_out.at[micro, pl.ds(0, local), at : at + tile],
            partner,
        )

    def memory_tile(kind, micro, index):
        at, tile = column_tiles[index]
        return copy(
            copy_slot(micro, kind, index),
            part.at[micro, mem_rows, at : at + tile],
            got_out.at[micro, pl.ds(local, mem), at : at + tile],
            partner,
        )

    def key_copy(micro, source, target):
        return pltpu.make_async_remote_copy(
            src_ref=key_block.at[micro],
            dst_ref=keys.at[micro, rows_at(source * mem, mem)],
            send_sem=send_k.at[micro, target],
            recv_sem=recv_k.at[micro, source],
            device_id={SEQ: target},
            device_id_type=MESH,
        )

    def value_copy(micro, source, source_head, target, target_head):
        return pltpu.make_async_remote_copy(
            src_ref=value_block.at[micro],
            dst_ref=values.at[
                micro, rows_at(source * mem, mem), pl.ds(pl.multiple_of(source_head * dv, 128), dv)
            ],
            send_sem=send_v.at[micro, target, target_head],
            recv_sem=recv_v.at[micro, source, source_head],
            device_id={SEQ: target, HEAD: target_head},
            device_id_type=MESH,
        )

    tokens.start()

    out_share = share // seqs

    def out_piece(half, piece):
        return w_out_all.at[half, rows_at(piece * out_share, out_share)]

    def over_out():
        mine = w_out_in.at[rows_at(seq * out_share, out_share)]
        return copy(OUT_SHARE, mine, out_piece(head, seq), partner)

    def hand_out(source, target):
        return pltpu.make_async_remote_copy(
            src_ref=out_piece(other, source),
            dst_ref=out_piece(other, source),
            send_sem=send_w.at[target],
            recv_sem=recv_w.at[source],
            device_id={SEQ: target},
            device_id_type=MESH,
        )

    @pl.when(section == 0)
    def _():
        over_out().start()

    @pl.when(section == 0)
    def _():
        x_copy(0).start()
        for micro in range(micros):
            x_load(micro, rows.at[micro, own_rows]).start()

    @pl.when(section == 1)
    def _():
        for micro in range(micros):
            x_load(micro, grad_y.at[micro]).start()

    tokens.wait_recv()
    for micro in range(micros):
        rows[micro, mem_rows] = mem_all[...]
    @pl.when(section == 1)
    def _():
        pl.semaphore_wait(go, 1)
        over_out().start()

    over_out().wait_recv()
    each_seq(lambda t: t != seq, lambda t: hand_out(seq, t).start())

    causal = lax.broadcasted_iota(jnp.int32, (segment, segment), 0) >= (
        lax.broadcasted_iota(jnp.int32, (segment, segment), 1)
    )
    mem_causal = segment + lax.broadcasted_iota(jnp.int32, (mem, total), 0) >= (
        lax.broadcasted_iota(jnp.int32, (mem, total), 1)
    )
    lane = lax.broadcasted_iota(jnp.int32, (total, 128), 1)

    def lanes_of(kind, place):
        return slice(kind * share + place * HEAD_DIM, kind * share + (place + 1) * HEAD_DIM)

    def attention(micro):
        @pl.when(section == 0)
        def _():
            x_load(micro, rows.at[micro, own_rows]).wait()
            x_copy(micro).wait_recv()

            @pl.when(micro + 1 < micros)
            def _():
                x_copy(micro + 1).start()

        @pl.when(section == 1)
        def _():
            for source in range(2):
                y_got(micro, source).wait_recv()

        unit, _ = unit_rows(rows[micro])
        normed[micro] = unit * gains[0:1] + biases[0:1]

        @pl.when(micro == 0)
        def _():
            weight_copy(IN).wait()

        for kind in range(3):
            made = nn(normed[micro], w_in[kind])
            if kind != 1:
                made = made + head_bias[kind // 2 : kind // 2 + 1]
            qkv[micro, :, kind * share : (kind + 1) * share] = made
        tops = jnp.zeros((total, 128), jnp.float32)
        for place in range(heads):
            query, key, value = (lanes_of(kind, place) for kind in range(3))
            made_top = []
            for at, allowed, seen in ((seg_rows, causal, seg_rows), (mem_rows, mem_causal, pl.ds(0, total))):
                scores = mm_nt(qkv[micro, at, query], qkv[micro, seen, key]) * SCALE
                scores = jnp.where(allowed, scores, -1e30)
                top = jnp.max(scores, axis=1, keepdims=True)
                exponent = jnp.exp(scores - top)
                row_total = jnp.sum(exponent, axis=1, keepdims=True)
                attended[micro, at, place * HEAD_DIM : (place + 1) * HEAD_DIM] = (
                    nn(exponent, qkv[micro, seen, value]) / row_total
                )
                made_top.append(top + jnp.log(row_total))
            tops = jnp.where(lane == place, jnp.concatenate(made_top, axis=0), tops)
            if place % 2 == 1:
                attended_copy(micro, place // 2).start()
        lse[micro] = tops

    each_micro(attention)
    weight_copy(UP).wait()
    weight_copy(DOWN).wait()
    out_copy.wait()
    each_seq(lambda t: t != seq, lambda t: hand_out(t, t).wait_recv())

    @pl.when(section == 0)
    def _():
        pl.semaphore_signal(go, inc=1, device_id={SECTION: 1}, device_id_type=MESH)


    def feed_forward(micro):
        for index in range(heads // 2):
            attended_copy(micro, index).wait()
        for at, tile in column_tiles:
            cut = slice(at, at + tile)
            hidden[micro, :, cut] = (
                rows[micro, :, cut]
                + nn(attended[micro], w_out_all[head, :, cut])
                + nn(got_attended[micro], w_out_all[other, :, cut])
                + residual[0:1, cut]
            )
        unit, _ = unit_rows(hidden[micro])
        normed[micro] = unit * gains[1:2] + biases[1:2]
        for at, tile in inner_tiles:
            cut = slice(at, at + tile)
            made = nn(normed[micro], w_up[:, cut]) + b_up[:, cut]
            pre[micro, :, cut] = made
            d_pre[micro, :, cut] = gelu_parts(made)[0]
        for index, (at, tile) in enumerate(column_tiles):
            part[micro, :, at : at + tile] = nn(d_pre[micro], w_down[:, at : at + tile])
            memory_tile(MEMORY, micro, index).start()
            local_tile(LOCAL, micro, index).start()

    each_micro(feed_forward)
    for name in (KEY, VALUE, QUERY):
        weight_copy(name).wait()

    def memory_write(micro):
        for index, (at, tile) in enumerate(column_tiles):
            cut = slice(at, at + tile)
            memory_tile(MEMORY, micro, index).wait()
            out_mem[micro, :, cut] = (
                part[micro, mem_rows, cut]
                + got_out[micro, local:, cut]
                + hidden[micro, mem_rows, cut]
                + residual[1:2, cut]
            )
        key_block[micro] = nn(out_mem[micro], w_key[...])
        value_block[micro] = nn(out_mem[micro], w_value[...])

        def share_block(t):
            key_copy(micro, seq, t).start()
            for g in range(2):
                value_copy(micro, seq, head, t, g).start()

        each_seq(later, share_block)

    each_micro(memory_write)

    def read_query(micro):
        for index, (at, tile) in enumerate(column_tiles):
            cut = slice(at, at + tile)
            local_tile(LOCAL, micro, index).wait()
            out_local[micro, :, cut] = (
                part[micro, own_rows, cut]
                + got_out[micro, :local, cut]
                + hidden[micro, own_rows, cut]
                + residual[1:2, cut]
            )
        query_proj[micro] = nn(out_local[micro], w_query[...])

    def memory_read(micro):
        read_query(micro)

        def got(t):
            key_copy(micro, t, t).wait_recv()
            for g in range(2):
                value_copy(micro, t, g, t, g).wait_recv()

        query_halves = halves_of(query_proj[micro])
        each_seq(earlier, got)
        key_halves = halves_of(keys[micro])
        scores = jnp.zeros((local, seqs * mem), jnp.float32)
        for by in (1, 2, 3):
            scores = scores + mm_nt(
                query_halves * turned(query_halves, by), key_halves * turned(key_halves, by)
            )
        scores = jnp.where(seen_mask(items, micro, seqs, mem), scores, 0.0)
        weights[micro] = scores
        found = nn(scores, values[micro]) / (jnp.sum(scores, axis=1, keepdims=True) + 1.0)
        read[micro] = found
        y[micro] = out_local[micro] + found

        @pl.when(section == 0)
        def _():
            for target in range(2):
                y_sent(micro, target).start()

    each_micro(memory_read)

    def grad_copy(micro):
        return copy(
            copy_slot(micro, GRAD), grad_x.at[micro], grad_y.at[micro], {SECTION: 0}
        )

    def rows_copy(micro):
        here = d_out.at[micro, own_rows]
        return copy(copy_slot(micro, D_LOCAL), here, here, partner)

    def mem_copy(micro):
        return copy(copy_slot(micro, D_MEMORY), mem_part.at[micro], got_mem.at[micro], partner)

    def back_key(micro, source, target):
        return pltpu.make_async_remote_copy(
            src_ref=d_keys.at[micro, rows_at(target * mem, mem)],
            dst_ref=from_k.at[micro, source],
            send_sem=back_sk.at[micro, target],
            recv_sem=back_rk.at[micro, source],
            device_id={SEQ: target},
            device_id_type=MESH,
        )

    def back_value(micro, source, source_head, target, target_head):
        return pltpu.make_async_remote_copy(
            src_ref=d_values.at[
                micro, rows_at(target * mem, mem), pl.ds(pl.multiple_of(target_head * dv, 128), dv)
            ],
            dst_ref=from_v.at[micro, source, source_head],
            send_sem=back_sv.at[micro, target, target_head],
            recv_sem=back_rv.at[micro, source, source_head],
            device_id={SEQ: target, HEAD: target_head},
            device_id_type=MESH,
        )

    def add_small(row, vector):
        for at in range(0, vector.shape[1], 128):
            g_small[row + at // 128 : row + at // 128 + 1] += vector[:, at : at + 128]

    def read_back(micro):
        @pl.when(section == 0)
        def _():
            grad_copy(micro).wait_recv()

        @pl.when(section == 1)
        def _():
            x_load(micro, grad_y.at[micro]).wait()

        grad = grad_y[micro]
        scores = weights[micro]
        denominator = jnp.sum(scores, axis=1, keepdims=True) + 1.0
        d_numer = grad / denominator
        d_denom = -jnp.sum(grad * read[micro], axis=1, keepdims=True) / denominator
        d_values[micro] = mm_tn(scores, d_numer)

        def send_values(t):
            for g in range(2):
                back_value(micro, seq, head, t, g).start()

        each_seq(earlier, send_values)
        d_scores = jnp.where(
            seen_mask(items, micro, seqs, mem), mm_nt(d_numer, values[micro]) + d_denom, 0.0
        )
        query_halves, key_halves = halves_of(query_proj[micro]), halves_of(keys[micro])
        d_key_halves = jnp.zeros_like(key_halves)
        for by in (1, 2, 3):
            d_feats = mm_tn(d_scores, query_halves * turned(query_halves, by))
            d_key_halves += d_feats * turned(key_halves, by) + turned(d_feats * key_halves, -by)
        d_keys[micro] = halves_back(keys[micro], d_key_halves)
        each_seq(earlier, lambda t: back_key(micro, seq, t).start())
        d_query_halves = jnp.zeros_like(query_halves)
        for by in (1, 2, 3):
            d_feats = nn(d_scores, key_halves * turned(key_halves, by))
            d_query_halves += d_feats * turned(query_halves, by) + turned(d_feats * query_halves, -by)
        query_proj[micro] = halves_back(query_proj[micro], d_query_halves)
        d_out[micro, own_rows] = grad + mm_nt(query_proj[micro], w_query[...])
        rows_copy(micro).start()

    each_micro(read_back)

    def write_back(micro):
        def got(t):
            back_key(micro, t, t).wait_recv()
            for g in range(2):
                back_value(micro, t, g, t, g).wait_recv()

        each_seq(later, got)
        key_block[micro] = jnp.sum(from_k[micro], axis=0)
        value_block[micro] = jnp.sum(from_v[micro], axis=(0, 1))
        mem_part[micro] = mm_nt(key_block[micro], w_key[...]) + mm_nt(
            value_block[micro], w_value[...]
        )
        mem_copy(micro).start()

    def forward_sent(micro):
        def sent(t):
            key_copy(micro, seq, t).wait_send()
            for g in range(2):
                value_copy(micro, seq, head, t, g).wait_send()

        each_seq(later, sent)

    each_micro(forward_sent)
    each_micro(write_back)

    def both(ref):
        return ref[...].reshape(micros * ref.shape[1], ref.shape[2])

    w_query[...] = mm_tn(both(out_local), both(query_proj))
    w_key[...] = mm_tn(both(out_mem), both(key_block))
    w_value[...] = mm_tn(both(out_mem), both(value_block))
    def feed_forward_back(micro):
        mem_copy(micro).wait()
        d_out[micro, mem_rows] = mem_part[micro] + got_mem[micro]
        rows_copy(micro).wait()
        for at, tile in inner_tiles:
            cut = slice(at, at + tile)
            activated, slope = gelu_parts(pre[micro, :, cut])
            made = slope * mm_nt(d_out[micro], w_down[cut])
            pre[micro, :, cut] = activated
            d_pre[micro, :, cut] = made
            add_small(36 + at // 128, column_sum(made))
        for index, (at, tile) in enumerate(column_tiles):
            part[micro, :, at : at + tile] = mm_nt(d_pre[micro], w_up[at : at + tile])
            tile_copy(MIX, micro, index).start()
        add_small(30, 0.5 * column_sum(d_out[micro]))

    each_micro(feed_forward_back)
    along = seqs // lanes
    z, lane_y = seq // lanes, lax.rem(seq, lanes)
    place = lane_y * along + jnp.where(lax.rem(lane_y, 2) == 0, z, along - 1 - z)

    def device(spot):
        row = spot // along
        column = lax.rem(spot, along)
        column = jnp.where(lax.rem(row, 2) == 0, column, along - 1 - column)
        return {SEQ: column * lanes + row}

    targets = (device(lax.rem(place + 1, seqs)), device(lax.rem(place + seqs - 1, seqs)))
    signs = (1, -1)
    kinds = range(w_in.shape[0])
    sources = [w_down, w_up, w_value, w_out, *(w_in.at[kind] for kind in kinds), g_small, got_whole]
    results = [down_sum, up_sum, value_sum, out_sum, *(in_sum.at[kind] for kind in kinds)]
    results += [small_sum, whole_sum.at[head]]
    count = len(sources)
    ways = [[(index, way) for index in group for way in range(2)] for group in (range(2), range(2, count))]
    last = seqs - 2

    def block(ref, way, spot):
        size = ref.shape[0] // seqs
        half = size // 2
        spot = lax.rem(spot + 2 * seqs, seqs)
        return ref.at[pl.ds(pl.multiple_of(spot * size + way * half, half), half)]

    def slot_of(index, way, step):
        return slots[index].at[way, lax.rem(step, SLOTS)]

    def up_copy(index, way, step, source):
        turn = lax.rem(step, SLOTS)
        return pltpu.make_async_remote_copy(
            src_ref=source,
            dst_ref=slot_of(index, way, step),
            send_sem=send_up.at[turn, way, index],
            recv_sem=recv_up.at[turn, way, index],
            device_id=targets[way],
            device_id_type=MESH,
        )

    def on_copy(index, way, step, source, target):
        return pltpu.make_async_remote_copy(
            src_ref=source,
            dst_ref=target,
            send_sem=send_on.at[step, way, index],
            recv_sem=recv_on.at[step, way, index],
            device_id=targets[way],
            device_id_type=MESH,
        )

    def over(source, target, number):
        return pltpu.make_async_remote_copy(
            src_ref=source,
            dst_ref=target,
            send_sem=send_x.at[number],
            recv_sem=recv_x.at[number],
            device_id=partner,
            device_id_type=MESH,
        )

    def hand_over(way, spot, step):
        mine = block(whole_sum.at[head], way, spot)
        return over(mine, mine, 2 + way * seqs + step)

    def home(index, way):
        return pltpu.make_async_copy(
            slot_of(index, way, last),
            block(results[index], way, place + signs[way]),
            store.at[way, index],
        )

    def sum_up(group, step):
        @pl.when(step >= SLOTS)
        def _():
            for way in range(2):
                pl.semaphore_wait(free.at[group, way], 1)

        for index, way in ways[group]:
            got = slot_of(index, way, step - 1)
            up_copy(index, way, step - 1, got).wait_recv()
            got[...] += block(sources[index], way, place - signs[way] * step)[...]
            up_copy(index, way, step, got).start()
        for index, way in ways[group]:
            up_copy(index, way, step - 1, slot_of(index, way, step)).wait_send()

        @pl.when(jnp.logical_and(step >= 2, step + 1 < seqs - 1))
        def _():
            for way in range(2):
                pl.semaphore_signal(
                    free.at[group, way], inc=1, device_id=targets[1 - way], device_id_type=MESH
                )

    def turn_round(group):
        for index, way in ways[group]:
            got = slot_of(index, way, last)
            up_copy(index, way, last, got).wait_recv()
            spot = place + signs[way]
            got[...] += block(sources[index], way, spot)[...]
            target = block(results[index], way, spot)
            on_copy(index, way, 0, got, target).start()
            home(index, way).start()
            if index == count - 1:
                over(got, target, 2 + way * seqs).start()

    def pass_on(group, step):
        for index, way in ways[group]:
            spot = place - signs[way] * (step - 1)
            here = block(results[index], way, spot)
            on_copy(index, way, step - 1, here, here).wait_recv()

            @pl.when(step < seqs - 1)
            def _(index=index, way=way, here=here):
                on_copy(index, way, step, here, here).start()

            if index == count - 1:
                hand_over(way, spot, step).start()

    def advance(group, step):
        @pl.when(step < seqs - 1)
        def _():
            sum_up(group, step)

        @pl.when(step == seqs - 1)
        def _():
            turn_round(group)

        @pl.when(jnp.logical_and(step >= seqs, step < 2 * seqs - 1))
        def _():
            pass_on(group, step - seqs + 1)

    def begin(*indices):
        for index in indices:
            for way in range(2):
                up_copy(index, way, 0, block(sources[index], way, place)).start()

    for micro in range(micros):
        unit, _ = unit_rows(hidden[micro])
        normed[micro] = unit * gains[1:2] + biases[1:2]
    for at, tile in inner_tiles:
        cut = slice(at, at + tile)
        w_down[cut] = mm_tn(both(pre.at[:, :, cut]), both(d_out))
    begin(0)
    for at, tile in inner_tiles:
        cut = slice(at, at + tile)
        w_up[:, cut] = mm_tn(both(normed), both(d_pre.at[:, :, cut]))
    begin(1, 2)

    def attention_back(micro):
        unit, inverse = unit_rows(hidden[micro])
        for index, (at, tile) in enumerate(column_tiles):
            cut = slice(at, at + tile)
            tile_copy(MIX, micro, index).wait()
            got_part[micro, :, cut] += part[micro, :, cut]
        d_mixed = got_part[micro]
        hidden[micro] = d_out[micro] + unit_rows_back(d_mixed * gains[1:2], unit, inverse)
        add_small(6, 0.5 * column_sum(d_mixed * unit))
        add_small(18, 0.5 * column_sum(d_mixed))
        add_small(24, 0.5 * column_sum(hidden[micro]))
        part[micro, :, :share] = mm_nt(hidden[micro], w_out[...])
        block_rows = lax.div(
            lax.broadcasted_iota(jnp.int32, (mem, share), 1), jnp.int32(HEAD_DIM)
        )
        for place in range(heads):
            query, key, value = (lanes_of(kind, place) for kind in range(3))
            cut = slice(place * HEAD_DIM, (place + 1) * HEAD_DIM)
            wide = pl.ds(place * mem, mem)
            grads = []
            for at, allowed, seen in ((seg_rows, causal, seg_rows), (mem_rows, mem_causal, pl.ds(0, total))):
                scores = mm_nt(qkv[micro, at, query], qkv[micro, seen, key]) * SCALE
                soft = jnp.exp(
                    jnp.where(allowed, scores, -1e30) - lse[micro, at, place : place + 1]
                )
                d_head = part[micro, at, cut]
                inner_dot = jnp.sum(d_head * attended[micro, at, cut], axis=1, keepdims=True)
                d_scores = soft * (mm_nt(d_head, qkv[micro, seen, value]) - inner_dot) * SCALE
                grads.append((soft, d_scores, d_head, nn(d_scores, qkv[micro, seen, key])))
            (soft, d_scores, d_head, d_query), (mem_soft, mem_scores, _, mem_query) = grads
            wide_soft[wide] = mem_soft
            wide_scores[wide] = mem_scores
            mine = block_rows == place
            wide_query[wide] = jnp.where(mine, qkv[micro, mem_rows, :share], 0.0)
            wide_grad[wide] = jnp.where(mine, part[micro, mem_rows, :share], 0.0)
            d_key = mm_tn(d_scores, qkv[micro, seg_rows, query])
            d_value = mm_tn(soft, d_head)
            qkv[micro, seg_rows, query] = d_query
            qkv[micro, mem_rows, query] = mem_query
            qkv[micro, seg_rows, key] = d_key
            qkv[micro, seg_rows, value] = d_value
        qkv[micro, mem_rows, share:] = jnp.zeros((mem, 2 * share), jnp.float32)
        qkv[micro, :, share : 2 * share] += mm_tn(wide_scores[...], wide_query[...])
        qkv[micro, :, 2 * share :] += mm_tn(wide_soft[...], wide_grad[...])
        for index, (at, tile) in enumerate(column_tiles):
            made = mm_nt(qkv[micro, :, :share], w_in[0, at : at + tile])
            for kind in (1, 2):
                made = made + mm_nt(
                    qkv[micro, :, kind * share : (kind + 1) * share], w_in[kind, at : at + tile]
                )
            part[micro, :, at : at + tile] = made
            local_tile(ROWS, micro, index).start()
            memory_tile(ROWS_MEMORY, micro, index).start()
        add_small(48, column_sum(qkv[micro, :, :share]))
        add_small(51, column_sum(qkv[micro, :, 2 * share :]))

    def attention_back_and_ring(micro):
        attention_back(micro)
        sum_up(0, micro + 1)

    each_micro(attention_back_and_ring)

    def finish(micro, d_normed, at_rows):
        unit, inverse = unit_rows(rows[micro, at_rows])
        add_small(0, column_sum(d_normed * unit))
        add_small(12, column_sum(d_normed))
        return hidden[micro, at_rows] + unit_rows_back(d_normed * gains[0:1], unit, inverse)

    def rows_back(micro):
        for index in range(len(column_tiles)):
            local_tile(ROWS, micro, index).wait()
            memory_tile(ROWS_MEMORY, micro, index).wait()
        grad_x[micro] = finish(micro, part[micro, own_rows] + got_out[micro, :local], own_rows)

        @pl.when(section == 1)
        def _():
            grad_copy(micro).start()

        mem_half = rows_at(local + head * half_mem, half_mem)
        d_tokens = finish(micro, part[micro, own_mem_rows] + got_out[micro, mem_half], own_mem_rows)
        for at in range(0, width, 128):
            row = 56 + (at // 128) * half_mem
            g_small[row : row + half_mem] += d_tokens[:, at : at + 128]

    each_micro(rows_back)
    small_copy = over(g_small, got_small, 0)
    small_copy.start()

    def whole_copy(matrix):
        return over((w_query, w_key)[matrix], got_whole, 1)

    for matrix in range(2):

        @pl.when(head == matrix)
        def _(matrix=matrix):
            whole_copy(1 - matrix).start()

    w_out_all[head] = mm_tn(both(attended), both(hidden))
    begin(3)
    sum_up(0, jnp.int32(3))
    for micro in range(micros):
        unit, _ = unit_rows(rows[micro])
        normed[micro] = unit * gains[0:1] + biases[0:1]
    for kind in kinds:
        w_in[kind] = mm_tn(both(normed), both(qkv.at[:, :, kind * share : (kind + 1) * share]))
        begin(4 + kind)
        if kind == 1:
            sum_up(0, jnp.int32(4))
    small_copy.wait()
    g_small[0:SHARED_ROWS] += got_small[0:SHARED_ROWS]
    begin(count - 2)
    whole_copy(0).wait()
    for matrix in range(2):

        @pl.when(head == matrix)
        def _(matrix=matrix):
            got_whole[...] += (w_query, w_key)[matrix][...]

    begin(count - 1)

    def ring_turn(turn, carry):
        advance(0, turn + AHEAD)
        advance(1, turn)
        return carry

    lax.fori_loop(1, 2 * seqs - 1, ring_turn, 0)
    for index, way in ways[0] + ways[1]:
        home(index, way).wait()
        up_copy(index, way, last, slot_of(index, way, last)).wait_send()

    def passed(step, carry):
        for index, way in ways[0] + ways[1]:
            own = slot_of(index, way, 0)
            on_copy(index, way, step, own, own).wait_send()
        return carry

    lax.fori_loop(0, seqs - 1, passed, 0)

    def crossed(step, carry):
        for way in range(2):
            theirs = block(whole_sum.at[other], way, place - signs[way] * (step - 1))
            over(theirs, theirs, 2 + way * seqs + step).wait()
        return carry

    lax.fori_loop(0, seqs, crossed, 0)

    tokens.wait_send()
    over_out().wait_send()
    each_seq(lambda t: t != seq, lambda t: hand_out(seq, t).wait_send())

    def all_sent(micro):
        @pl.when(section == 0)
        def _():
            x_copy(micro).wait_send()
            for target in range(2):
                y_sent(micro, target).wait_send()

        @pl.when(section == 1)
        def _():
            grad_copy(micro).wait_send()

        def sent(t):
            back_key(micro, seq, t).wait_send()
            for g in range(2):
                back_value(micro, seq, head, t, g).wait_send()

        each_seq(earlier, sent)

    each_micro(all_sent)


def shapes_of(*shapes):
    return tuple(jax.ShapeDtypeStruct(shape, jnp.float32) for shape in shapes)


def buffers(*shapes):
    return [pltpu.VMEM(shape, jnp.float32) for shape in shapes]


def dma(*shape):
    return pltpu.SemaphoreType.DMA(shape)


def params_of(number):
    return pltpu.CompilerParams(
        collective_id=number, has_side_effects=True, vmem_limit_bytes=62 << 20
    )


def shards_of_two(
    boundary_in,
    short_items,
    norm_gains,
    norm_biases,
    projection_in,
    head_bias,
    projection_out,
    residual_bias,
    up_weight,
    up_bias,
    down_weight,
    memory_tokens,
    query_memory,
    key_memory,
    value_memory,
):
    seqs = lax.axis_size(SEQ)
    x = boundary_in[0]
    micros, local, width = x.shape
    w_in = projection_in[0].transpose(1, 0, 2)
    share = w_in.shape[2]
    inner = up_weight.shape[2]
    half_mem = memory_tokens.shape[1]
    mem = 2 * half_mem
    segment = 2 * local
    total = segment + mem
    dk, dv = key_memory.shape[2], value_memory.shape[2]
    stored = seqs * mem
    records = (
        (total, width),
        (total, 3 * share),
        (total, share),
        (total, 128),
        (total, width),
        (total, inner),
        (local, width),
        (mem, width),
        (stored, dk),
        (stored, 2 * dv),
        (local, dk),
        (local, stored),
        (local, width),
    )
    weights = (
        w_in,
        up_weight[0],
        down_weight[0],
        value_memory[0],
        query_memory[0],
        key_memory[0],
    )
    w_out = projection_out[0]
    few = (norm_gains[0], norm_biases[0], head_bias[0], residual_bias[0], up_bias, memory_tokens[0])
    slots = 2 + micros * COPY_SLOTS
    ring = [w.shape for w in (down_weight[0], up_weight[0], value_memory[0], w_out)]
    ring += [w_in.shape[1:]] * 3 + [(16 * seqs, 128), (width, dk)]
    g_down, g_up, g_in, g_out, g_value, small, whole, y, grad_x = pl.pallas_call(
        functools.partial(layers_kernel, 2),
        out_shape=shapes_of(
            down_weight[0].shape,
            up_weight[0].shape,
            w_in.shape,
            w_out.shape,
            value_memory[0].shape,
            (16 * seqs, 128),
            (2, width, dk),
            (micros, local, width),
            (micros, local, width),
        ),
        in_specs=[SMEM, HBM] + [VMEM] * len(few) + [HBM] * (len(weights) + 1),
        out_specs=(HBM,) * 7 + (VMEM,) * 2,
        scratch_shapes=buffers(
            *(w.shape for w in weights),
            *((micros, *record) for record in records),
            (2, *w_out.shape),
            (micros, total, share),
            (micros, total, width),
            (micros, total, inner),
            (micros, total, width),
            (micros, total, width),
            (micros, total, width),
            (micros, local + mem, width),
            (mem, width),
            (micros, mem, dk),
            (micros, mem, dv),
            (micros, seqs, mem, dk),
            (micros, seqs, 2, mem, dv),
            (micros, mem, width),
            (micros, mem, width),
            (micros, local, width),
            (mem * (share // HEAD_DIM), total),
            (mem * (share // HEAD_DIM), total),
            (mem * (share // HEAD_DIM), share),
            (mem * (share // HEAD_DIM), share),
            (16 * seqs, 128),
            (16 * seqs, 128),
            (width, dk),
            *((2, SLOTS, height // (2 * seqs), columns) for height, columns in ring),
        )
        + [dma(len(weights) + 1 + micros), dma(2, len(ring)), dma(slots), dma(slots)]
        + [dma(micros, seqs), dma(micros, seqs), dma(micros, seqs, 2), dma(micros, seqs, 2)] * 2
        + [dma(seqs), dma(seqs)]
        + [dma(SLOTS, 2, len(ring)), dma(SLOTS, 2, len(ring))]
        + [dma(seqs - 1, 2, len(ring)), dma(seqs - 1, 2, len(ring))]
        + [dma(2 + 2 * seqs), dma(2 + 2 * seqs), pltpu.SemaphoreType.REGULAR((2, 2)), pltpu.SemaphoreType.REGULAR],
        compiler_params=params_of(0),
        name="layers",
    )(short_items, x, *few, *weights, w_out)
    outs = (
        (1, *x.shape),
        norm_gains.shape,
        norm_biases.shape,
        (1, *w_in.shape),
        head_bias.shape,
        projection_out.shape,
        residual_bias.shape,
        up_weight.shape,
        up_bias.shape,
        down_weight.shape,
        memory_tokens.shape,
        query_memory.shape,
        key_memory.shape,
        value_memory.shape,
    )
    outs = pl.pallas_call(
        finish_kernel,
        out_shape=shapes_of(*outs),
        in_specs=[HBM] * 5 + [VMEM] + [HBM] * 3,
        out_specs=(HBM, VMEM, VMEM, HBM, VMEM, HBM, VMEM, HBM, VMEM, HBM, VMEM, HBM, HBM, HBM),
        scratch_shapes=buffers(
            g_down.shape,
            g_up.shape,
            g_in.shape,
            g_out.shape,
            g_value.shape,
            whole.shape[1:],
            whole.shape[1:],
            y.shape,
        )
        + [dma(8), dma(8)],
        compiler_params=pltpu.CompilerParams(vmem_limit_bytes=62 << 20),
        name="finish",
    )(g_down, g_up, g_in, g_out, g_value, small, whole, y, grad_x)
    return (*outs[:3], outs[3].transpose(0, 2, 1, 3), *outs[4:])


def finish_kernel(
    g_down, g_up, g_in, g_out, g_value, small, whole, y, grad_x,
    rows, gains, biases, proj_in, head_bias, proj_out, residual, up, up_bias, down, tokens, query, key,
    value, *refs
):
    *held, loaded, stored = refs
    pairs = (
        (g_down, down.at[0]),
        (g_up, up.at[0]),
        (g_in, proj_in.at[0]),
        (g_out, proj_out.at[0]),
        (g_value, value.at[0]),
        (whole.at[0], query.at[0]),
        (whole.at[1], key.at[0]),
        (y, rows.at[0]),
    )
    section = lax.axis_index(SECTION)

    def fetch(index, source):
        return pltpu.make_async_copy(source, held[index], loaded.at[index])

    def put(index):
        return pltpu.make_async_copy(held[index], pairs[index][1], stored.at[index])

    last = len(pairs) - 1
    for index in range(last):
        fetch(index, pairs[index][0]).start()

    @pl.when(section == 0)
    def _():
        fetch(last, grad_x).start()

    @pl.when(section != 0)
    def _():
        fetch(last, y).start()

    def spread(target, row, first):
        for at in range(0, target.shape[-1], 128):
            target[0, row : row + 1, at : at + 128] = small[first + at // 128 : first + at // 128 + 1]

    lanes = gains.shape[2] // 128
    for index, target in enumerate((gains, biases, residual)):
        for row in range(2):
            spread(target, row, (2 * index + row) * lanes)
    for at in range(0, up_bias.shape[1], 128):
        first = 6 * lanes + at // 128
        up_bias[:, at : at + 128] = small[first : first + 1]
    for row in range(2):
        spread(head_bias, row, 8 * lanes + row * (head_bias.shape[2] // 128))
    count = tokens.shape[1]
    for at in range(0, tokens.shape[2], 128):
        first = 56 + (at // 128) * count
        tokens[0, :, at : at + 128] = small[first : first + count]
    for index, (source, _) in enumerate(pairs):
        fetch(index, source).wait()
        put(index).start()
    for index in range(len(pairs)):
        put(index).wait()


def solution(mesh):
    return jax.shard_map(
        shards_of_two if mesh.shape[HEAD] == 2 else shards,
        mesh=mesh,
        in_specs=(
            P(SECTION, None, (SEQ, HEAD), None),
            P(),
            P(SECTION, None, None),
            P(SECTION, None, None),
            P(SECTION, None, None, HEAD),
            P(SECTION, None, HEAD),
            P(SECTION, HEAD, None),
            P(SECTION, None, None),
            P(SECTION, None, HEAD),
            P(SECTION, HEAD),
            P(SECTION, HEAD, None),
            P(SECTION, HEAD, None),
            P(SECTION, None, None),
            P(SECTION, None, None),
            P(SECTION, None, HEAD),
        ),
        out_specs=(
            P(SECTION, None, (SEQ, HEAD), None),
            P(SECTION, None, None),
            P(SECTION, None, None),
            P(SECTION, None, None, HEAD),
            P(SECTION, None, HEAD),
            P(SECTION, HEAD, None),
            P(SECTION, None, None),
            P(SECTION, None, HEAD),
            P(SECTION, HEAD),
            P(SECTION, HEAD, None),
            P(SECTION, HEAD, None),
            P(SECTION, None, None),
            P(SECTION, None, None),
            P(SECTION, None, HEAD),
        ),
        check_vma=False,
    )
```

```python
import functools
import math
from types import SimpleNamespace

import jax
import jax.numpy as jnp
from jax import lax
from jax.experimental import pallas as pl
from jax.experimental.pallas import tpu as pltpu
from jax.sharding import PartitionSpec as P

SECTION, SEQ, HEAD = "section", "seq", "head"
HEAD_DIM = 64
EPSILON = 1e-05
SCALE = 1.0 / math.sqrt(HEAD_DIM)
MESH = pl.DeviceIdType.MESH
VMEM = pl.BlockSpec(memory_space=pltpu.VMEM)
HBM = pl.BlockSpec(memory_space=pltpu.HBM)
SMEM = pl.BlockSpec(memory_space=pltpu.SMEM)
SHARED_ROWS = 36


def mm(left, right, dims=((1,), (0,))):
    return lax.dot_general(
        left, right, (dims, ((), ())), precision=lax.Precision.HIGH, preferred_element_type=jnp.float32
    )


def mm_nt(left, right):
    return mm(left, right, ((1,), (1,)))


def mm_tn(left, right):
    return mm(left, right, ((0,), (0,)))


def unit_rows(rows):
    centred = rows - jnp.mean(rows, axis=-1, keepdims=True)
    inverse = lax.rsqrt(jnp.mean(centred * centred, axis=-1, keepdims=True) + EPSILON)
    return centred * inverse, inverse


def unit_rows_back(d_unit, unit, inverse):
    return inverse * (
        d_unit
        - jnp.mean(d_unit, axis=-1, keepdims=True)
        - unit * jnp.mean(d_unit * unit, axis=-1, keepdims=True)
    )


def features(projected):
    halves = jnp.concatenate([jax.nn.softplus(projected), jax.nn.softplus(-projected)], axis=-1)
    return jnp.concatenate(
        [halves * jnp.roll(halves, rolled_by, axis=-1) for rolled_by in (1, 2, 3)], axis=-1
    )


def gelu_tanh(values_in):
    return jax.nn.gelu(values_in, approximate=True)


def head_sum_rows(rows, share):
    segment = lax.axis_size(HEAD) * share
    turn = lax.axis_index(HEAD) * share
    total = lax.psum(
        jnp.concatenate([jnp.roll(rows[:segment], turn, axis=0), rows[segment:]], axis=0), HEAD
    )
    return jnp.concatenate([jnp.roll(total[:segment], -turn, axis=0), total[segment:]], axis=0)


def head_rows(local):
    gathered = lax.all_gather(local, HEAD, axis=0, tiled=True)
    return jnp.roll(gathered, -lax.axis_index(HEAD) * local.shape[0], axis=0)


def head_scatter(rows):
    share = rows.shape[0] // lax.axis_size(HEAD)
    placed = jnp.roll(rows, lax.axis_index(HEAD) * share, axis=0)
    return lax.psum_scatter(placed, HEAD, scatter_dimension=0, tiled=True)


def heads_of(part):
    return part.reshape(part.shape[0], -1, HEAD_DIM).transpose(1, 0, 2)


def rows_of(part):
    return part.transpose(1, 0, 2).reshape(part.shape[1], -1)


def bmm(left, right, left_dim, right_dim):
    return lax.dot_general(
        left,
        right,
        (((left_dim,), (right_dim,)), ((0,), (0,))),
        precision=lax.Precision.HIGH,
        preferred_element_type=jnp.float32,
    )


def layer_forward(local, params, mask, allowed):
    width = local.shape[1]
    local_count = local.shape[0]
    segment = lax.axis_size(HEAD) * local_count
    rows = jnp.concatenate([head_rows(local), params.memory], axis=0)
    unit_one, inverse_one = unit_rows(rows)
    normed = unit_one * params.gains[0] + params.biases[0]
    projected = mm(normed, params.proj_in) + params.in_bias
    share = projected.shape[1] // 3
    query, key, value = (heads_of(projected[:, i * share : (i + 1) * share]) for i in range(3))
    scores = jnp.where(allowed, bmm(query, key, 2, 2) * SCALE, -1e30)
    row_top = jnp.max(scores, axis=-1, keepdims=True)
    exponent = jnp.exp(scores - row_top)
    soft = exponent / jnp.sum(exponent, axis=-1, keepdims=True)
    attended = rows_of(bmm(soft, value, 2, 1))
    hidden = rows + head_sum_rows(mm(attended, params.proj_out), local_count) + params.residual[0]
    unit_two, inverse_two = unit_rows(hidden)
    mixed = unit_two * params.gains[1] + params.biases[1]
    inner_pre = mm(mixed, params.up) + params.up_bias
    inner_act = gelu_tanh(inner_pre)
    partial = mm(inner_act, params.down)
    out_local = head_scatter(partial[:segment]) + hidden[:local_count] + params.residual[1]
    out_mem = lax.psum(partial[segment:], HEAD) + hidden[segment:] + params.residual[1]
    key_proj = mm(out_mem, params.key_mem)
    values = mm(out_mem, params.value_mem)
    gathered = lax.all_gather(jnp.concatenate([key_proj, values], axis=1), SEQ, axis=0, tiled=True)
    dk = key_proj.shape[1]
    keys_all = gathered[:, :dk]
    values_all = lax.all_gather(gathered[:, dk:], HEAD, axis=1, tiled=True)
    key_feats = features(keys_all)
    query_proj = mm(out_local, params.query_mem)
    query_feats = features(query_proj)
    weights = mask * mm_nt(query_feats, key_feats)
    denominator = jnp.sum(weights, axis=1, keepdims=True) + 1.0
    read = mm(weights, values_all) / denominator
    return SimpleNamespace(
        unit_one=unit_one,
        inverse_one=inverse_one,
        projected=projected,
        attended=attended,
        soft=soft,
        unit_two=unit_two,
        inverse_two=inverse_two,
        inner_pre=inner_pre,
        out_local=out_local,
        out_mem=out_mem,
        keys_all=keys_all,
        values_all=values_all,
        query_proj=query_proj,
        weights=weights,
        denominator=denominator,
        read=read,
        output=out_local + read,
    )


def layer_backward(grad, record, params, mask):
    head_count = lax.axis_size(HEAD)
    seq_count = lax.axis_size(SEQ)
    width = grad.shape[1]
    local_count = grad.shape[0]
    segment = head_count * local_count
    denominator = record.denominator
    d_numer = grad / denominator
    d_denom = -jnp.sum(grad * record.read, axis=1, keepdims=True) / denominator
    d_weights = mask * (mm_nt(d_numer, record.values_all) + d_denom)
    key_feats, keys_back = jax.vjp(features, record.keys_all)
    query_feats, query_back = jax.vjp(features, record.query_proj)
    d_query_proj = query_back(mm(d_weights, key_feats))[0]
    d_keys = keys_back(mm_tn(d_weights, query_feats))[0]
    d_values = mm_tn(record.weights, d_numer)
    d_memory = lax.psum_scatter(
        jnp.concatenate([d_keys, d_values], axis=1), SEQ, scatter_dimension=0, tiled=True
    )
    dk = d_keys.shape[1]
    d_key_proj = d_memory[:, :dk]
    d_value = lax.psum_scatter(
        d_memory[:, dk:], HEAD, scatter_dimension=1, tiled=True
    )
    d_mem = lax.psum(
        mm_nt(d_key_proj, params.key_mem) + mm_nt(d_value, params.value_mem), HEAD
    )
    d_local = grad + mm_nt(d_query_proj, params.query_mem)
    d_result = jnp.concatenate([head_rows(d_local), d_mem], axis=0)
    inner_act, gelu_back = jax.vjp(gelu_tanh, record.inner_pre)
    grad_down = mm_tn(inner_act, d_result)
    d_pre = gelu_back(mm_nt(d_result, params.down))[0]
    gains, biases = params.gains, params.biases
    mixed = record.unit_two * gains[1] + biases[1]
    grad_up = mm_tn(mixed, d_pre)
    d_mixed = head_sum_rows(mm_nt(d_pre, params.up), local_count)
    d_hidden = d_result + unit_rows_back(d_mixed * gains[1], record.unit_two, record.inverse_two)
    grad_out = mm_tn(record.attended, d_hidden)
    d_attended = mm_nt(d_hidden, params.proj_out)
    share = d_attended.shape[1]
    query, key, value = (
        heads_of(record.projected[:, i * share : (i + 1) * share]) for i in range(3)
    )
    soft = record.soft
    d_heads = heads_of(d_attended)
    inner_dot = jnp.sum(d_heads * heads_of(record.attended), axis=-1, keepdims=True)
    d_scores = soft * (bmm(d_heads, value, 2, 2) - inner_dot) * SCALE
    d_projected = jnp.concatenate(
        [
            rows_of(bmm(d_scores, key, 2, 1)),
            rows_of(bmm(d_scores, query, 1, 1)),
            rows_of(bmm(soft, d_heads, 1, 1)),
        ],
        axis=1,
    )
    normed = record.unit_one * gains[0] + biases[0]
    grad_in = mm_tn(normed, d_projected)
    columns = jnp.sum(d_projected, axis=0)
    grad_head_bias = jnp.stack([columns[:share], columns[2 * share :]])
    d_normed_all = mm_nt(d_projected, params.proj_in)
    d_normed = head_scatter(d_normed_all[:segment])
    d_normed_mem = lax.psum_scatter(
        d_normed_all[segment:], HEAD, scatter_dimension=0, tiled=True
    )
    mem_count = d_normed_mem.shape[0]
    own_mem = segment + lax.axis_index(HEAD) * mem_count

    def own(values):
        return jnp.concatenate(
            [values[:local_count], lax.dynamic_slice_in_dim(values, own_mem, mem_count, 0)], axis=0
        )

    d_normed_own = jnp.concatenate([d_normed, d_normed_mem], axis=0)
    unit_own = own(record.unit_one)
    d_rows = own(d_hidden) + unit_rows_back(
        d_normed_own * gains[0], unit_own, own(record.inverse_one)
    )
    part = 1.0 / head_count
    sharded = (
        grad_in,
        grad_head_bias,
        grad_out,
        grad_up,
        jnp.sum(d_pre, axis=0),
        grad_down,
        d_rows[local_count:],
        mm_tn(record.out_mem, d_value),
    )
    shared = (
        jnp.stack(
            [
                jnp.sum(d_normed_own * unit_own, axis=0),
                part * jnp.sum(d_mixed * record.unit_two, axis=0),
            ]
        ),
        jnp.stack([jnp.sum(d_normed_own, axis=0), part * jnp.sum(d_mixed, axis=0)]),
        part * jnp.stack([jnp.sum(d_hidden, axis=0), jnp.sum(d_result, axis=0)]),
        mm_tn(record.out_local, d_query_proj),
        mm_tn(record.out_mem, d_key_proj),
    )
    return (d_rows[:local_count], sharded, shared)


def passed_along(value, axis, steps):
    count = lax.axis_size(axis)
    first, last = (max(0, -steps), min(count, count - steps))
    return lax.ppermute(value, axis, [(source, source + steps) for source in range(first, last)])


def shards(
    boundary_in,
    short_items,
    norm_gains,
    norm_biases,
    projection_in,
    head_bias,
    projection_out,
    residual_bias,
    up_weight,
    up_bias,
    down_weight,
    memory_tokens,
    query_memory,
    key_memory,
    value_memory,
):
    section = lax.axis_index(SECTION)
    sections = lax.axis_size(SECTION)
    head_count = lax.axis_size(HEAD)
    head_place = lax.axis_index(HEAD)
    seq_count = lax.axis_size(SEQ)
    seq_place = lax.axis_index(SEQ)
    micro_total = boundary_in.shape[1]
    local_count = boundary_in.shape[2]
    width = boundary_in.shape[3]
    segment = head_count * local_count
    head_width = projection_in.shape[3]
    memory_all = lax.all_gather(memory_tokens[0], HEAD, axis=0, tiled=True)
    mem_count = memory_all.shape[0]
    params = SimpleNamespace(
        gains=norm_gains[0],
        biases=norm_biases[0],
        proj_in=projection_in[0].reshape(width, 3 * head_width),
        in_bias=jnp.concatenate(
            [head_bias[0, 0], jnp.zeros((head_width,), jnp.float32), head_bias[0, 1]]
        ),
        proj_out=projection_out[0],
        residual=residual_bias[0],
        up=up_weight[0],
        up_bias=up_bias[0],
        down=down_weight[0],
        memory=memory_all,
        query_mem=query_memory[0],
        key_mem=key_memory[0],
        value_mem=value_memory[0],
    )
    ordinal = jnp.arange(segment)
    places = jnp.concatenate(
        [(ordinal + head_place * local_count) % segment, segment + jnp.arange(mem_count)]
    )
    allowed = (places[:, None] >= places[None, :])[None]

    positions = jnp.arange(seq_count)
    masks = []
    for micro in range(micro_total):
        if micro == 0:
            item = jnp.zeros((seq_count,), jnp.int32)
        else:
            ends = jnp.cumsum(short_items[micro - 1])
            item = jnp.sum((positions[:, None] >= ends[None, :]).astype(jnp.int32), axis=1)
        own_item = jnp.sum(jnp.where(positions == seq_place, item, 0))
        seen = jnp.logical_and(positions < seq_place, item == own_item).astype(jnp.float32)
        masks.append(jnp.repeat(seen, mem_count)[None, :])
    masks = jnp.stack(masks)

    tick_total = micro_total + sections - 1
    received = jnp.zeros_like(boundary_in[0, 0])
    records = []
    for tick in range(tick_total):
        micro = jnp.clip(tick - section, 0, micro_total - 1)
        local = jnp.where(section == 0, boundary_in[0, min(tick, micro_total - 1)], received)
        records.append(layer_forward(local, params, masks[micro], allowed))
        if tick + 1 < tick_total:
            received = passed_along(records[-1].output, SECTION, 1)
    back_received = jnp.zeros_like(boundary_in[0, 0])
    grads_input = []
    total = None
    for tick in range(tick_total):
        raw = tick - (sections - 1 - section)
        valid = jnp.logical_and(raw >= 0, raw < micro_total)
        micro = jnp.clip(raw, 0, micro_total - 1)
        grad = jnp.where(
            section == sections - 1, boundary_in[0, min(tick, micro_total - 1)], back_received
        )
        kept = [
            vars(records[min(max(tick - (sections - 1 - place), 0), micro_total - 1) + place])
            for place in range(sections)
        ]
        record = SimpleNamespace(
            **jax.tree.map(lambda *kinds: lax.select_n(section, *kinds), *kept)
        )
        grad_x, sharded, shared = layer_backward(grad, record, params, masks[micro])
        fresh = jax.tree.map(lambda part: jnp.where(valid, part, 0.0), (sharded, shared))
        total = fresh if total is None else jax.tree.map(jnp.add, total, fresh)
        grads_input.append(grad_x)
        if tick + 1 < tick_total:
            back_received = passed_along(grad_x, SECTION, -1)
    sharded, shared = total
    grad_in, grad_heads_bias, grad_out, grad_up, grad_up_b, grad_down, grad_mem, grad_value = lax.psum(
        sharded, SEQ
    )
    grad_gains, grad_biases, grad_residual, grad_query, grad_key = lax.psum(shared, (SEQ, HEAD))
    finished_grads = jnp.stack(
        [grads_input[micro + sections - 1] for micro in range(micro_total)]
    )
    finished_outputs = jnp.stack(
        [records[micro + sections - 1].output for micro in range(micro_total)]
    )
    boundary_out = jnp.where(section == 0, finished_grads, finished_outputs)[None]
    return (
        boundary_out,
        grad_gains[None],
        grad_biases[None],
        grad_in.reshape(projection_in.shape),
        grad_heads_bias[None],
        grad_out[None],
        grad_residual[None],
        grad_up[None],
        grad_up_b[None],
        grad_down[None],
        grad_mem[None],
        grad_query[None],
        grad_key[None],
        grad_value[None],
    )


def barrier_with(pairs, wait_count):
    barrier = pltpu.get_barrier_semaphore()
    for condition, device in pairs:

        @pl.when(condition)
        def _(device=device):
            pl.semaphore_signal(barrier, inc=1, device_id=device, device_id_type=MESH)

    @pl.when(wait_count > 0)
    def _():
        pl.semaphore_wait(barrier, wait_count)


def nn(left, right):
    return mm(left, right)


def lane_tiles(width):
    tile = 256 if width % 256 == 0 else width
    return [(at, tile) for at in range(0, width, tile)]


def rows_at(start, count):
    return pl.ds(pl.multiple_of(start, count), count)


def halves_of(projected):
    small = jnp.log1p(jnp.exp(-jnp.abs(projected)))
    return jnp.concatenate(
        [jnp.maximum(projected, 0.0) + small, jnp.maximum(-projected, 0.0) + small], axis=1
    )


def halves_back(projected, d_halves):
    width = projected.shape[1]
    rising = 1.0 / (1.0 + jnp.exp(-projected))
    falling = 1.0 / (1.0 + jnp.exp(projected))
    return d_halves[:, :width] * rising - d_halves[:, width:] * falling


def turned(values, by):
    return pltpu.roll(values, by % values.shape[1], 1)


GELU_IN = math.sqrt(2.0 / math.pi)


def gelu_parts(pre):
    cubic = 0.044715 * pre * pre
    bent = jnp.tanh(GELU_IN * pre * (1.0 + cubic))
    half = 0.5 * (1.0 + bent)
    slope = half + 0.5 * pre * (1.0 - bent * bent) * GELU_IN * (1.0 + 3.0 * cubic)
    return pre * half, slope


def seen_mask(items, micro, seqs, mem):
    seq = lax.axis_index(SEQ)
    row_seq = lax.div(lax.broadcasted_iota(jnp.int32, (1, seqs * mem), 1), jnp.int32(mem))
    end = jnp.int32(0)
    own = jnp.int32(0)
    item = jnp.zeros((1, seqs * mem), jnp.int32)
    for piece in range(items.shape[1]):
        end = end + items[jnp.maximum(micro - 1, 0), piece]
        bound = jnp.where(micro == 0, seqs, end)
        own = own + (seq >= bound).astype(jnp.int32)
        item = item + (row_seq >= bound).astype(jnp.int32)
    return jnp.logical_and(row_seq < seq, item == own)


WEIGHTS = IN, UP, DOWN, VALUE, QUERY, KEY = tuple(range(6))
COPIES = (1, 2, 3, 3, 3, 1, 1, 1, 3, 3, 3)
(X_IN, Y_OUT, PART, LOCAL, MEMORY, GRAD, D_LOCAL, D_MEMORY, MIX, ROWS, ROWS_MEMORY) = range(11)
COPY_SLOTS = sum(COPIES)
TOKENS, OUT_SHARE = range(2)


def copy_slot(micro, kind, index=0):
    return 2 + micro * COPY_SLOTS + sum(COPIES[:kind]) + index


def column_sum(values_in):
    return jnp.sum(values_in, axis=0, keepdims=True)


SLOTS = 3
AHEAD = 7


def layers_kernel(lanes, *refs):
    refs = list(refs)

    def take(count):
        taken, refs[:] = refs[:count], refs[count:]
        return taken

    items, x, gains, biases, head_bias, residual, b_up, mem_tokens = take(8)
    weights_in = take(len(WEIGHTS))
    (w_out_in,) = take(1)
    down_sum, up_sum, in_sum, out_sum, value_sum, small_sum, whole_sum = take(7)
    y, grad_x = take(2)
    held = take(len(WEIGHTS))
    w_in, w_up, w_down, w_value, w_query, w_key = held
    rows, qkv, attended, lse, hidden, pre = take(6)
    out_local, out_mem, keys, values, query_proj, weights, read = take(7)
    w_out_all, got_attended = take(2)
    (
        normed, d_pre, d_out, part, got_part, got_out, mem_all, key_block, value_block, from_k, from_v,
        mem_part, got_mem, grad_y, wide_scores, wide_soft, wide_query, wide_grad,
        g_small, got_small, got_whole,
    ) = take(21)
    d_keys, d_values = keys, read
    slots = take(9)
    load, store, send, recv, send_k, recv_k, send_v, recv_v = take(8)
    back_sk, back_rk, back_sv, back_rv, send_w, recv_w = take(6)
    send_up, recv_up, send_on, recv_on, send_x, recv_x, free, go = refs

    section, seq, head = (lax.axis_index(name) for name in (SECTION, SEQ, HEAD))
    seqs = lax.axis_size(SEQ)
    micros, local, width = x.shape
    segment = 2 * local
    mem = out_mem.shape[1]
    half_mem = mem // 2
    total = segment + mem
    share = w_in.shape[2]
    inner = w_up.shape[1]
    heads = share // HEAD_DIM
    dv = w_value.shape[1]
    other = 1 - head
    partner = {HEAD: other}
    own_rows, other_rows = rows_at(head * local, local), rows_at(other * local, local)
    own_mem = rows_at(head * half_mem, half_mem)
    own_mem_rows = rows_at(segment + head * half_mem, half_mem)
    seg_rows, mem_rows = pl.ds(0, segment), pl.ds(segment, mem)
    column_tiles = [(at, width // 3) for at in range(0, width, width // 3)]
    inner_tiles = lane_tiles(inner)

    def copy(slot, source, target, device):
        return pltpu.make_async_remote_copy(
            src_ref=source,
            dst_ref=target,
            send_sem=send.at[slot],
            recv_sem=recv.at[slot],
            device_id=device,
            device_id_type=MESH,
        )

    def weight_copy(name):
        return pltpu.make_async_copy(
            weights_in[name], held[name], load.at[name]
        )

    out_copy = pltpu.make_async_copy(w_out_in, w_out_all.at[head], load.at[len(WEIGHTS)])
    w_out = w_out_all.at[head]

    def each_micro(stage):
        def body(micro, carry):
            stage(micro)
            return carry

        lax.fori_loop(0, micros, body, 0)

    def each_seq(condition, act):
        for t in range(seqs):

            @pl.when(condition(t))
            def _(t=t):
                act(t)

    def later(t):
        return t > seq

    def earlier(t):
        return t < seq

    out_copy.start()
    for name in WEIGHTS:
        weight_copy(name).start()
    keys[...] = jnp.zeros_like(keys)
    values[...] = jnp.zeros_like(values)
    from_k[...] = jnp.zeros_like(from_k)
    from_v[...] = jnp.zeros_like(from_v)
    g_small[...] = jnp.zeros_like(g_small)
    mem_all[own_mem] = mem_tokens[...]
    barrier_with(
        [(seq >= 0, partner)]
        + [(t != seq, {SEQ: t, HEAD: g}) for t in range(seqs) for g in range(2)]
        + [(section == 1, {SECTION: 0, HEAD: g}) for g in range(2)]
        + [(section == 0, {SECTION: 1})],
        1 + 2 * (seqs - 1) + 2 - section,
    )

    tokens = copy(TOKENS, mem_tokens, mem_all.at[own_mem], partner)

    def x_load(micro, target):
        return pltpu.make_async_copy(x.at[micro], target, load.at[len(WEIGHTS) + 1 + micro])

    def x_copy(micro):
        return copy(copy_slot(micro, X_IN), x.at[micro], rows.at[micro, own_rows], partner)

    def y_sent(micro, target_head):
        return pltpu.make_async_remote_copy(
            src_ref=y.at[micro],
            dst_ref=rows.at[micro, own_rows],
            send_sem=send.at[copy_slot(micro, Y_OUT, target_head)],
            recv_sem=recv.at[copy_slot(micro, Y_OUT, head)],
            device_id={SECTION: 1, HEAD: target_head},
            device_id_type=MESH,
        )

    def y_got(micro, source_head):
        here = rows.at[micro, rows_at(source_head * local, local)]
        return copy(copy_slot(micro, Y_OUT, source_head), here, here, partner)

    def tile_copy(kind, micro, index):
        at, tile = column_tiles[index]
        return copy(
            copy_slot(micro, kind, index),
            part.at[micro, :, at : at + tile],
            got_part.at[micro, :, at : at + tile],
            partner,
        )

    def attended_copy(micro, index):
        cut = slice(index * 2 * HEAD_DIM, (index + 1) * 2 * HEAD_DIM)
        return copy(
            copy_slot(micro, PART, index),
            attended.at[micro, :, cut],
            got_attended.at[micro, :, cut],
            partner,
        )

    def local_tile(kind, micro, index):
        at, tile = column_tiles[index]
        return copy(
            copy_slot(micro, kind, index),
            part.at[micro, other_rows, at : at + tile],
            got_out.at[micro, pl.ds(0, local), at : at + tile],
            partner,
        )

    def memory_tile(kind, micro, index):
        at, tile = column_tiles[index]
        return copy(
            copy_slot(micro, kind, index),
            part.at[micro, mem_rows, at : at + tile],
            got_out.at[micro, pl.ds(local, mem), at : at + tile],
            partner,
        )

    def key_copy(micro, source, target):
        return pltpu.make_async_remote_copy(
            src_ref=key_block.at[micro],
            dst_ref=keys.at[micro, rows_at(source * mem, mem)],
            send_sem=send_k.at[micro, target],
            recv_sem=recv_k.at[micro, source],
            device_id={SEQ: target},
            device_id_type=MESH,
        )

    def value_copy(micro, source, source_head, target, target_head):
        return pltpu.make_async_remote_copy(
            src_ref=value_block.at[micro],
            dst_ref=values.at[
                micro, rows_at(source * mem, mem), pl.ds(pl.multiple_of(source_head * dv, 128), dv)
            ],
            send_sem=send_v.at[micro, target, target_head],
            recv_sem=recv_v.at[micro, source, source_head],
            device_id={SEQ: target, HEAD: target_head},
            device_id_type=MESH,
        )

    tokens.start()

    out_share = share // seqs

    def out_piece(half, piece):
        return w_out_all.at[half, rows_at(piece * out_share, out_share)]

    def over_out():
        mine = w_out_in.at[rows_at(seq * out_share, out_share)]
        return copy(OUT_SHARE, mine, out_piece(head, seq), partner)

    def hand_out(source, target):
        return pltpu.make_async_remote_copy(
            src_ref=out_piece(other, source),
            dst_ref=out_piece(other, source),
            send_sem=send_w.at[target],
            recv_sem=recv_w.at[source],
            device_id={SEQ: target},
            device_id_type=MESH,
        )

    @pl.when(section == 0)
    def _():
        over_out().start()

    @pl.when(section == 0)
    def _():
        x_copy(0).start()
        for micro in range(micros):
            x_load(micro, rows.at[micro, own_rows]).start()

    @pl.when(section == 1)
    def _():
        for micro in range(micros):
            x_load(micro, grad_y.at[micro]).start()

    tokens.wait_recv()
    for micro in range(micros):
        rows[micro, mem_rows] = mem_all[...]
    @pl.when(section == 1)
    def _():
        pl.semaphore_wait(go, 1)
        over_out().start()

    over_out().wait_recv()
    each_seq(lambda t: t != seq, lambda t: hand_out(seq, t).start())

    causal = lax.broadcasted_iota(jnp.int32, (segment, segment), 0) >= (
        lax.broadcasted_iota(jnp.int32, (segment, segment), 1)
    )
    mem_causal = segment + lax.broadcasted_iota(jnp.int32, (mem, total), 0) >= (
        lax.broadcasted_iota(jnp.int32, (mem, total), 1)
    )
    lane = lax.broadcasted_iota(jnp.int32, (total, 128), 1)

    def lanes_of(kind, place):
        return slice(kind * share + place * HEAD_DIM, kind * share + (place + 1) * HEAD_DIM)

    def attention(micro):
        @pl.when(section == 0)
        def _():
            x_load(micro, rows.at[micro, own_rows]).wait()
            x_copy(micro).wait_recv()

            @pl.when(micro + 1 < micros)
            def _():
                x_copy(micro + 1).start()

        @pl.when(section == 1)
        def _():
            for source in range(2):
                y_got(micro, source).wait_recv()

        unit, _ = unit_rows(rows[micro])
        normed[micro] = unit * gains[0:1] + biases[0:1]

        @pl.when(micro == 0)
        def _():
            weight_copy(IN).wait()

        for kind in range(3):
            made = nn(normed[micro], w_in[kind])
            if kind != 1:
                made = made + head_bias[kind // 2 : kind // 2 + 1]
            qkv[micro, :, kind * share : (kind + 1) * share] = made
        tops = jnp.zeros((total, 128), jnp.float32)
        for place in range(heads):
            query, key, value = (lanes_of(kind, place) for kind in range(3))
            made_top = []
            for at, allowed, seen in ((seg_rows, causal, seg_rows), (mem_rows, mem_causal, pl.ds(0, total))):
                scores = mm_nt(qkv[micro, at, query], qkv[micro, seen, key]) * SCALE
                scores = jnp.where(allowed, scores, -1e30)
                top = jnp.max(scores, axis=1, keepdims=True)
                exponent = jnp.exp(scores - top)
                row_total = jnp.sum(exponent, axis=1, keepdims=True)
                attended[micro, at, place * HEAD_DIM : (place + 1) * HEAD_DIM] = (
                    nn(exponent, qkv[micro, seen, value]) / row_total
                )
                made_top.append(top + jnp.log(row_total))
            tops = jnp.where(lane == place, jnp.concatenate(made_top, axis=0), tops)
            if place % 2 == 1:
                attended_copy(micro, place // 2).start()
        lse[micro] = tops

    each_micro(attention)
    weight_copy(UP).wait()
    weight_copy(DOWN).wait()
    out_copy.wait()
    each_seq(lambda t: t != seq, lambda t: hand_out(t, t).wait_recv())

    @pl.when(section == 0)
    def _():
        pl.semaphore_signal(go, inc=1, device_id={SECTION: 1}, device_id_type=MESH)


    def feed_forward(micro):
        for index in range(heads // 2):
            attended_copy(micro, index).wait()
        for at, tile in column_tiles:
            cut = slice(at, at + tile)
            hidden[micro, :, cut] = (
                rows[micro, :, cut]
                + nn(attended[micro], w_out_all[head, :, cut])
                + nn(got_attended[micro], w_out_all[other, :, cut])
                + residual[0:1, cut]
            )
        unit, _ = unit_rows(hidden[micro])
        normed[micro] = unit * gains[1:2] + biases[1:2]
        for at, tile in inner_tiles:
            cut = slice(at, at + tile)
            made = nn(normed[micro], w_up[:, cut]) + b_up[:, cut]
            pre[micro, :, cut] = made
            d_pre[micro, :, cut] = gelu_parts(made)[0]
        for index, (at, tile) in enumerate(column_tiles):
            part[micro, :, at : at + tile] = nn(d_pre[micro], w_down[:, at : at + tile])
            memory_tile(MEMORY, micro, index).start()
            local_tile(LOCAL, micro, index).start()

    each_micro(feed_forward)
    for name in (KEY, VALUE, QUERY):
        weight_copy(name).wait()

    def memory_write(micro):
        for index, (at, tile) in enumerate(column_tiles):
            cut = slice(at, at + tile)
            memory_tile(MEMORY, micro, index).wait()
            out_mem[micro, :, cut] = (
                part[micro, mem_rows, cut]
                + got_out[micro, local:, cut]
                + hidden[micro, mem_rows, cut]
                + residual[1:2, cut]
            )
        key_block[micro] = nn(out_mem[micro], w_key[...])
        value_block[micro] = nn(out_mem[micro], w_value[...])

        def share_block(t):
            key_copy(micro, seq, t).start()
            for g in range(2):
                value_copy(micro, seq, head, t, g).start()

        each_seq(later, share_block)

    each_micro(memory_write)

    def read_query(micro):
        for index, (at, tile) in enumerate(column_tiles):
            cut = slice(at, at + tile)
            local_tile(LOCAL, micro, index).wait()
            out_local[micro, :, cut] = (
                part[micro, own_rows, cut]
                + got_out[micro, :local, cut]
                + hidden[micro, own_rows, cut]
                + residual[1:2, cut]
            )
        query_proj[micro] = nn(out_local[micro], w_query[...])

    def memory_read(micro):
        read_query(micro)

        def got(t):
            key_copy(micro, t, t).wait_recv()
            for g in range(2):
                value_copy(micro, t, g, t, g).wait_recv()

        query_halves = halves_of(query_proj[micro])
        each_seq(earlier, got)
        key_halves = halves_of(keys[micro])
        scores = jnp.zeros((local, seqs * mem), jnp.float32)
        for by in (1, 2, 3):
            scores = scores + mm_nt(
                query_halves * turned(query_halves, by), key_halves * turned(key_halves, by)
            )
        scores = jnp.where(seen_mask(items, micro, seqs, mem), scores, 0.0)
        weights[micro] = scores
        found = nn(scores, values[micro]) / (jnp.sum(scores, axis=1, keepdims=True) + 1.0)
        read[micro] = found
        y[micro] = out_local[micro] + found

        @pl.when(section == 0)
        def _():
            for target in range(2):
                y_sent(micro, target).start()

    each_micro(memory_read)

    def grad_copy(micro):
        return copy(
            copy_slot(micro, GRAD), grad_x.at[micro], grad_y.at[micro], {SECTION: 0}
        )

    def rows_copy(micro):
        here = d_out.at[micro, own_rows]
        return copy(copy_slot(micro, D_LOCAL), here, here, partner)

    def mem_copy(micro):
        return copy(copy_slot(micro, D_MEMORY), mem_part.at[micro], got_mem.at[micro], partner)

    def back_key(micro, source, target):
        return pltpu.make_async_remote_copy(
            src_ref=d_keys.at[micro, rows_at(target * mem, mem)],
            dst_ref=from_k.at[micro, source],
            send_sem=back_sk.at[micro, target],
            recv_sem=back_rk.at[micro, source],
            device_id={SEQ: target},
            device_id_type=MESH,
        )

    def back_value(micro, source, source_head, target, target_head):
        return pltpu.make_async_remote_copy(
            src_ref=d_values.at[
                micro, rows_at(target * mem, mem), pl.ds(pl.multiple_of(target_head * dv, 128), dv)
            ],
            dst_ref=from_v.at[micro, source, source_head],
            send_sem=back_sv.at[micro, target, target_head],
            recv_sem=back_rv.at[micro, source, source_head],
            device_id={SEQ: target, HEAD: target_head},
            device_id_type=MESH,
        )

    def add_small(row, vector):
        for at in range(0, vector.shape[1], 128):
            g_small[row + at // 128 : row + at // 128 + 1] += vector[:, at : at + 128]

    def read_back(micro):
        @pl.when(section == 0)
        def _():
            grad_copy(micro).wait_recv()

        @pl.when(section == 1)
        def _():
            x_load(micro, grad_y.at[micro]).wait()

        grad = grad_y[micro]
        scores = weights[micro]
        denominator = jnp.sum(scores, axis=1, keepdims=True) + 1.0
        d_numer = grad / denominator
        d_denom = -jnp.sum(grad * read[micro], axis=1, keepdims=True) / denominator
        d_values[micro] = mm_tn(scores, d_numer)

        def send_values(t):
            for g in range(2):
                back_value(micro, seq, head, t, g).start()

        each_seq(earlier, send_values)
        d_scores = jnp.where(
            seen_mask(items, micro, seqs, mem), mm_nt(d_numer, values[micro]) + d_denom, 0.0
        )
        query_halves, key_halves = halves_of(query_proj[micro]), halves_of(keys[micro])
        d_key_halves = jnp.zeros_like(key_halves)
        for by in (1, 2, 3):
            d_feats = mm_tn(d_scores, query_halves * turned(query_halves, by))
            d_key_halves += d_feats * turned(key_halves, by) + turned(d_feats * key_halves, -by)
        d_keys[micro] = halves_back(keys[micro], d_key_halves)
        each_seq(earlier, lambda t: back_key(micro, seq, t).start())
        d_query_halves = jnp.zeros_like(query_halves)
        for by in (1, 2, 3):
            d_feats = nn(d_scores, key_halves * turned(key_halves, by))
            d_query_halves += d_feats * turned(query_halves, by) + turned(d_feats * query_halves, -by)
        query_proj[micro] = halves_back(query_proj[micro], d_query_halves)
        d_out[micro, own_rows] = grad + mm_nt(query_proj[micro], w_query[...])
        rows_copy(micro).start()

    each_micro(read_back)

    def write_back(micro):
        def got(t):
            back_key(micro, t, t).wait_recv()
            for g in range(2):
                back_value(micro, t, g, t, g).wait_recv()

        each_seq(later, got)
        key_block[micro] = jnp.sum(from_k[micro], axis=0)
        value_block[micro] = jnp.sum(from_v[micro], axis=(0, 1))
        mem_part[micro] = mm_nt(key_block[micro], w_key[...]) + mm_nt(
            value_block[micro], w_value[...]
        )
        mem_copy(micro).start()

    def forward_sent(micro):
        def sent(t):
            key_copy(micro, seq, t).wait_send()
            for g in range(2):
                value_copy(micro, seq, head, t, g).wait_send()

        each_seq(later, sent)

    each_micro(forward_sent)
    each_micro(write_back)

    def both(ref):
        return ref[...].reshape(micros * ref.shape[1], ref.shape[2])

    w_query[...] = mm_tn(both(out_local), both(query_proj))
    w_key[...] = mm_tn(both(out_mem), both(key_block))
    w_value[...] = mm_tn(both(out_mem), both(value_block))
    def feed_forward_back(micro):
        mem_copy(micro).wait()
        d_out[micro, mem_rows] = mem_part[micro] + got_mem[micro]
        rows_copy(micro).wait()
        for at, tile in inner_tiles:
            cut = slice(at, at + tile)
            activated, slope = gelu_parts(pre[micro, :, cut])
            made = slope * mm_nt(d_out[micro], w_down[cut])
            pre[micro, :, cut] = activated
            d_pre[micro, :, cut] = made
            add_small(36 + at // 128, column_sum(made))
        for index, (at, tile) in enumerate(column_tiles):
            part[micro, :, at : at + tile] = mm_nt(d_pre[micro], w_up[at : at + tile])
            tile_copy(MIX, micro, index).start()
        add_small(30, 0.5 * column_sum(d_out[micro]))

    each_micro(feed_forward_back)
    along = seqs // lanes
    z, lane_y = seq // lanes, lax.rem(seq, lanes)
    place = lane_y * along + jnp.where(lax.rem(lane_y, 2) == 0, z, along - 1 - z)

    def device(spot):
        row = spot // along
        column = lax.rem(spot, along)
        column = jnp.where(lax.rem(row, 2) == 0, column, along - 1 - column)
        return {SEQ: column * lanes + row}

    targets = (device(lax.rem(place + 1, seqs)), device(lax.rem(place + seqs - 1, seqs)))
    signs = (1, -1)
    kinds = range(w_in.shape[0])
    sources = [w_down, w_up, w_value, w_out, *(w_in.at[kind] for kind in kinds), g_small, got_whole]
    results = [down_sum, up_sum, value_sum, out_sum, *(in_sum.at[kind] for kind in kinds)]
    results += [small_sum, whole_sum.at[head]]
    count = len(sources)
    ways = [[(index, way) for index in group for way in range(2)] for group in (range(2), range(2, count))]
    last = seqs - 2

    def block(ref, way, spot):
        size = ref.shape[0] // seqs
        half = size // 2
        spot = lax.rem(spot + 2 * seqs, seqs)
        return ref.at[pl.ds(pl.multiple_of(spot * size + way * half, half), half)]

    def slot_of(index, way, step):
        return slots[index].at[way, lax.rem(step, SLOTS)]

    def up_copy(index, way, step, source):
        turn = lax.rem(step, SLOTS)
        return pltpu.make_async_remote_copy(
            src_ref=source,
            dst_ref=slot_of(index, way, step),
            send_sem=send_up.at[turn, way, index],
            recv_sem=recv_up.at[turn, way, index],
            device_id=targets[way],
            device_id_type=MESH,
        )

    def on_copy(index, way, step, source, target):
        return pltpu.make_async_remote_copy(
            src_ref=source,
            dst_ref=target,
            send_sem=send_on.at[step, way, index],
            recv_sem=recv_on.at[step, way, index],
            device_id=targets[way],
            device_id_type=MESH,
        )

    def over(source, target, number):
        return pltpu.make_async_remote_copy(
            src_ref=source,
            dst_ref=target,
            send_sem=send_x.at[number],
            recv_sem=recv_x.at[number],
            device_id=partner,
            device_id_type=MESH,
        )

    def hand_over(way, spot, step):
        mine = block(whole_sum.at[head], way, spot)
        return over(mine, mine, 2 + way * seqs + step)

    def home(index, way):
        return pltpu.make_async_copy(
            slot_of(index, way, last),
            block(results[index], way, place + signs[way]),
            store.at[way, index],
        )

    def sum_up(group, step):
        @pl.when(step >= SLOTS)
        def _():
            for way in range(2):
                pl.semaphore_wait(free.at[group, way], 1)

        for index, way in ways[group]:
            got = slot_of(index, way, step - 1)
            up_copy(index, way, step - 1, got).wait_recv()
            got[...] += block(sources[index], way, place - signs[way] * step)[...]
            up_copy(index, way, step, got).start()
        for index, way in ways[group]:
            up_copy(index, way, step - 1, slot_of(index, way, step)).wait_send()

        @pl.when(jnp.logical_and(step >= 2, step + 1 < seqs - 1))
        def _():
            for way in range(2):
                pl.semaphore_signal(
                    free.at[group, way], inc=1, device_id=targets[1 - way], device_id_type=MESH
                )

    def turn_round(group):
        for index, way in ways[group]:
            got = slot_of(index, way, last)
            up_copy(index, way, last, got).wait_recv()
            spot = place + signs[way]
            got[...] += block(sources[index], way, spot)[...]
            target = block(results[index], way, spot)
            on_copy(index, way, 0, got, target).start()
            home(index, way).start()
            if index == count - 1:
                over(got, target, 2 + way * seqs).start()

    def pass_on(group, step):
        for index, way in ways[group]:
            spot = place - signs[way] * (step - 1)
            here = block(results[index], way, spot)
            on_copy(index, way, step - 1, here, here).wait_recv()

            @pl.when(step < seqs - 1)
            def _(index=index, way=way, here=here):
                on_copy(index, way, step, here, here).start()

            if index == count - 1:
                hand_over(way, spot, step).start()

    def advance(group, step):
        @pl.when(step < seqs - 1)
        def _():
            sum_up(group, step)

        @pl.when(step == seqs - 1)
        def _():
            turn_round(group)

        @pl.when(jnp.logical_and(step >= seqs, step < 2 * seqs - 1))
        def _():
            pass_on(group, step - seqs + 1)

    def begin(*indices):
        for index in indices:
            for way in range(2):
                up_copy(index, way, 0, block(sources[index], way, place)).start()

    for micro in range(micros):
        unit, _ = unit_rows(hidden[micro])
        normed[micro] = unit * gains[1:2] + biases[1:2]
    for at, tile in inner_tiles:
        cut = slice(at, at + tile)
        w_down[cut] = mm_tn(both(pre.at[:, :, cut]), both(d_out))
    begin(0)
    for at, tile in inner_tiles:
        cut = slice(at, at + tile)
        w_up[:, cut] = mm_tn(both(normed), both(d_pre.at[:, :, cut]))
    begin(1, 2)

    def attention_back(micro):
        unit, inverse = unit_rows(hidden[micro])
        for index, (at, tile) in enumerate(column_tiles):
            cut = slice(at, at + tile)
            tile_copy(MIX, micro, index).wait()
            got_part[micro, :, cut] += part[micro, :, cut]
        d_mixed = got_part[micro]
        hidden[micro] = d_out[micro] + unit_rows_back(d_mixed * gains[1:2], unit, inverse)
        add_small(6, 0.5 * column_sum(d_mixed * unit))
        add_small(18, 0.5 * column_sum(d_mixed))
        add_small(24, 0.5 * column_sum(hidden[micro]))
        part[micro, :, :share] = mm_nt(hidden[micro], w_out[...])
        block_rows = lax.div(
            lax.broadcasted_iota(jnp.int32, (mem, share), 1), jnp.int32(HEAD_DIM)
        )
        for place in range(heads):
            query, key, value = (lanes_of(kind, place) for kind in range(3))
            cut = slice(place * HEAD_DIM, (place + 1) * HEAD_DIM)
            wide = pl.ds(place * mem, mem)
            grads = []
            for at, allowed, seen in ((seg_rows, causal, seg_rows), (mem_rows, mem_causal, pl.ds(0, total))):
                scores = mm_nt(qkv[micro, at, query], qkv[micro, seen, key]) * SCALE
                soft = jnp.exp(
                    jnp.where(allowed, scores, -1e30) - lse[micro, at, place : place + 1]
                )
                d_head = part[micro, at, cut]
                inner_dot = jnp.sum(d_head * attended[micro, at, cut], axis=1, keepdims=True)
                d_scores = soft * (mm_nt(d_head, qkv[micro, seen, value]) - inner_dot) * SCALE
                grads.append((soft, d_scores, d_head, nn(d_scores, qkv[micro, seen, key])))
            (soft, d_scores, d_head, d_query), (mem_soft, mem_scores, _, mem_query) = grads
            wide_soft[wide] = mem_soft
            wide_scores[wide] = mem_scores
            mine = block_rows == place
            wide_query[wide] = jnp.where(mine, qkv[micro, mem_rows, :share], 0.0)
            wide_grad[wide] = jnp.where(mine, part[micro, mem_rows, :share], 0.0)
            d_key = mm_tn(d_scores, qkv[micro, seg_rows, query])
            d_value = mm_tn(soft, d_head)
            qkv[micro, seg_rows, query] = d_query
            qkv[micro, mem_rows, query] = mem_query
            qkv[micro, seg_rows, key] = d_key
            qkv[micro, seg_rows, value] = d_value
            if place == heads // 2:
                sum_up(0, 2 * micro + 1)
        qkv[micro, mem_rows, share:] = jnp.zeros((mem, 2 * share), jnp.float32)
        qkv[micro, :, share : 2 * share] += mm_tn(wide_scores[...], wide_query[...])
        qkv[micro, :, 2 * share :] += mm_tn(wide_soft[...], wide_grad[...])
        for index, (at, tile) in enumerate(column_tiles):
            made = mm_nt(qkv[micro, :, :share], w_in[0, at : at + tile])
            for kind in (1, 2):
                made = made + mm_nt(
                    qkv[micro, :, kind * share : (kind + 1) * share], w_in[kind, at : at + tile]
                )
            part[micro, :, at : at + tile] = made
            local_tile(ROWS, micro, index).start()
            memory_tile(ROWS_MEMORY, micro, index).start()
        add_small(48, column_sum(qkv[micro, :, :share]))
        add_small(51, column_sum(qkv[micro, :, 2 * share :]))

    def attention_back_and_ring(micro):
        attention_back(micro)
        sum_up(0, 2 * micro + 2)

    each_micro(attention_back_and_ring)

    def finish(micro, d_normed, at_rows):
        unit, inverse = unit_rows(rows[micro, at_rows])
        add_small(0, column_sum(d_normed * unit))
        add_small(12, column_sum(d_normed))
        return hidden[micro, at_rows] + unit_rows_back(d_normed * gains[0:1], unit, inverse)

    def rows_back(micro):
        for index in range(len(column_tiles)):
            local_tile(ROWS, micro, index).wait()
            memory_tile(ROWS_MEMORY, micro, index).wait()
        grad_x[micro] = finish(micro, part[micro, own_rows] + got_out[micro, :local], own_rows)

        @pl.when(section == 1)
        def _():
            grad_copy(micro).start()

        mem_half = rows_at(local + head * half_mem, half_mem)
        d_tokens = finish(micro, part[micro, own_mem_rows] + got_out[micro, mem_half], own_mem_rows)
        for at in range(0, width, 128):
            row = 56 + (at // 128) * half_mem
            g_small[row : row + half_mem] += d_tokens[:, at : at + 128]

    each_micro(rows_back)
    small_copy = over(g_small, got_small, 0)
    small_copy.start()

    def whole_copy(matrix):
        return over((w_query, w_key)[matrix], got_whole, 1)

    for matrix in range(2):

        @pl.when(head == matrix)
        def _(matrix=matrix):
            whole_copy(1 - matrix).start()

    sum_up(0, jnp.int32(5))
    w_out_all[head] = mm_tn(both(attended), both(hidden))
    begin(3)
    sum_up(0, jnp.int32(6))
    for micro in range(micros):
        unit, _ = unit_rows(rows[micro])
        normed[micro] = unit * gains[0:1] + biases[0:1]
    for kind in kinds:
        w_in[kind] = mm_tn(both(normed), both(qkv.at[:, :, kind * share : (kind + 1) * share]))
        begin(4 + kind)
        if kind == 1:
            turn_round(0)
    small_copy.wait()
    g_small[0:SHARED_ROWS] += got_small[0:SHARED_ROWS]
    begin(count - 2)
    whole_copy(0).wait()
    for matrix in range(2):

        @pl.when(head == matrix)
        def _(matrix=matrix):
            got_whole[...] += (w_query, w_key)[matrix][...]

    begin(count - 1)

    def ring_turn(turn, carry):
        advance(0, turn + AHEAD)
        advance(1, turn)
        return carry

    lax.fori_loop(1, 2 * seqs - 1, ring_turn, 0)
    for index, way in ways[0] + ways[1]:
        home(index, way).wait()
        up_copy(index, way, last, slot_of(index, way, last)).wait_send()

    def passed(step, carry):
        for index, way in ways[0] + ways[1]:
            own = slot_of(index, way, 0)
            on_copy(index, way, step, own, own).wait_send()
        return carry

    lax.fori_loop(0, seqs - 1, passed, 0)

    def crossed(step, carry):
        for way in range(2):
            theirs = block(whole_sum.at[other], way, place - signs[way] * (step - 1))
            over(theirs, theirs, 2 + way * seqs + step).wait()
        return carry

    lax.fori_loop(0, seqs, crossed, 0)

    tokens.wait_send()
    over_out().wait_send()
    each_seq(lambda t: t != seq, lambda t: hand_out(seq, t).wait_send())

    def all_sent(micro):
        @pl.when(section == 0)
        def _():
            x_copy(micro).wait_send()
            for target in range(2):
                y_sent(micro, target).wait_send()

        @pl.when(section == 1)
        def _():
            grad_copy(micro).wait_send()

        def sent(t):
            back_key(micro, seq, t).wait_send()
            for g in range(2):
                back_value(micro, seq, head, t, g).wait_send()

        each_seq(earlier, sent)

    each_micro(all_sent)


def shapes_of(*shapes):
    return tuple(jax.ShapeDtypeStruct(shape, jnp.float32) for shape in shapes)


def buffers(*shapes):
    return [pltpu.VMEM(shape, jnp.float32) for shape in shapes]


def dma(*shape):
    return pltpu.SemaphoreType.DMA(shape)


def params_of(number):
    return pltpu.CompilerParams(
        collective_id=number, has_side_effects=True, vmem_limit_bytes=63 << 20
    )


def shards_of_two(
    boundary_in,
    short_items,
    norm_gains,
    norm_biases,
    projection_in,
    head_bias,
    projection_out,
    residual_bias,
    up_weight,
    up_bias,
    down_weight,
    memory_tokens,
    query_memory,
    key_memory,
    value_memory,
):
    seqs = lax.axis_size(SEQ)
    x = boundary_in[0]
    micros, local, width = x.shape
    w_in = projection_in[0].transpose(1, 0, 2)
    share = w_in.shape[2]
    inner = up_weight.shape[2]
    half_mem = memory_tokens.shape[1]
    mem = 2 * half_mem
    segment = 2 * local
    total = segment + mem
    dk, dv = key_memory.shape[2], value_memory.shape[2]
    stored = seqs * mem
    records = (
        (total, width),
        (total, 3 * share),
        (total, share),
        (total, 128),
        (total, width),
        (total, inner),
        (local, width),
        (mem, width),
        (stored, dk),
        (stored, 2 * dv),
        (local, dk),
        (local, stored),
        (local, width),
    )
    weights = (
        w_in,
        up_weight[0],
        down_weight[0],
        value_memory[0],
        query_memory[0],
        key_memory[0],
    )
    w_out = projection_out[0]
    few = (norm_gains[0], norm_biases[0], head_bias[0], residual_bias[0], up_bias, memory_tokens[0])
    slots = 2 + micros * COPY_SLOTS
    ring = [w.shape for w in (down_weight[0], up_weight[0], value_memory[0], w_out)]
    ring += [w_in.shape[1:]] * 3 + [(16 * seqs, 128), (width, dk)]
    g_down, g_up, g_in, g_out, g_value, small, whole, y, grad_x = pl.pallas_call(
        functools.partial(layers_kernel, 2),
        out_shape=shapes_of(
            down_weight[0].shape,
            up_weight[0].shape,
            w_in.shape,
            w_out.shape,
            value_memory[0].shape,
            (16 * seqs, 128),
            (2, width, dk),
            (micros, local, width),
            (micros, local, width),
        ),
        in_specs=[SMEM, HBM] + [VMEM] * len(few) + [HBM] * (len(weights) + 1),
        out_specs=(HBM,) * 7 + (VMEM,) * 2,
        scratch_shapes=buffers(
            *(w.shape for w in weights),
            *((micros, *record) for record in records),
            (2, *w_out.shape),
            (micros, total, share),
            (micros, total, width),
            (micros, total, inner),
            (micros, total, width),
            (micros, total, width),
            (micros, total, width),
            (micros, local + mem, width),
            (mem, width),
            (micros, mem, dk),
            (micros, mem, dv),
            (micros, seqs, mem, dk),
            (micros, seqs, 2, mem, dv),
            (micros, mem, width),
            (micros, mem, width),
            (micros, local, width),
            (mem * (share // HEAD_DIM), total),
            (mem * (share // HEAD_DIM), total),
            (mem * (share // HEAD_DIM), share),
            (mem * (share // HEAD_DIM), share),
            (16 * seqs, 128),
            (16 * seqs, 128),
            (width, dk),
            *((2, SLOTS, height // (2 * seqs), columns) for height, columns in ring),
        )
        + [dma(len(weights) + 1 + micros), dma(2, len(ring)), dma(slots), dma(slots)]
        + [dma(micros, seqs), dma(micros, seqs), dma(micros, seqs, 2), dma(micros, seqs, 2)] * 2
        + [dma(seqs), dma(seqs)]
        + [dma(SLOTS, 2, len(ring)), dma(SLOTS, 2, len(ring))]
        + [dma(seqs - 1, 2, len(ring)), dma(seqs - 1, 2, len(ring))]
        + [dma(2 + 2 * seqs), dma(2 + 2 * seqs), pltpu.SemaphoreType.REGULAR((2, 2)), pltpu.SemaphoreType.REGULAR],
        compiler_params=params_of(0),
        name="layers",
    )(short_items, x, *few, *weights, w_out)
    outs = (
        (1, *x.shape),
        norm_gains.shape,
        norm_biases.shape,
        (1, *w_in.shape),
        head_bias.shape,
        projection_out.shape,
        residual_bias.shape,
        up_weight.shape,
        up_bias.shape,
        down_weight.shape,
        memory_tokens.shape,
        query_memory.shape,
        key_memory.shape,
        value_memory.shape,
    )
    outs = pl.pallas_call(
        finish_kernel,
        out_shape=shapes_of(*outs),
        in_specs=[HBM] * 5 + [VMEM] + [HBM] * 3,
        out_specs=(HBM, VMEM, VMEM, HBM, VMEM, HBM, VMEM, HBM, VMEM, HBM, VMEM, HBM, HBM, HBM),
        scratch_shapes=buffers(
            g_down.shape,
            g_up.shape,
            g_in.shape,
            g_out.shape,
            g_value.shape,
            whole.shape[1:],
            whole.shape[1:],
            y.shape,
        )
        + [dma(8), dma(8)],
        compiler_params=pltpu.CompilerParams(vmem_limit_bytes=62 << 20),
        name="finish",
    )(g_down, g_up, g_in, g_out, g_value, small, whole, y, grad_x)
    return (*outs[:3], outs[3].transpose(0, 2, 1, 3), *outs[4:])


def finish_kernel(
    g_down, g_up, g_in, g_out, g_value, small, whole, y, grad_x,
    rows, gains, biases, proj_in, head_bias, proj_out, residual, up, up_bias, down, tokens, query, key,
    value, *refs
):
    *held, loaded, stored = refs
    pairs = (
        (g_down, down.at[0]),
        (g_up, up.at[0]),
        (g_in, proj_in.at[0]),
        (g_out, proj_out.at[0]),
        (g_value, value.at[0]),
        (whole.at[0], query.at[0]),
        (whole.at[1], key.at[0]),
        (y, rows.at[0]),
    )
    section = lax.axis_index(SECTION)

    def fetch(index, source):
        return pltpu.make_async_copy(source, held[index], loaded.at[index])

    def put(index):
        return pltpu.make_async_copy(held[index], pairs[index][1], stored.at[index])

    last = len(pairs) - 1
    for index in range(last):
        fetch(index, pairs[index][0]).start()

    @pl.when(section == 0)
    def _():
        fetch(last, grad_x).start()

    @pl.when(section != 0)
    def _():
        fetch(last, y).start()

    def spread(target, row, first):
        for at in range(0, target.shape[-1], 128):
            target[0, row : row + 1, at : at + 128] = small[first + at // 128 : first + at // 128 + 1]

    lanes = gains.shape[2] // 128
    for index, target in enumerate((gains, biases, residual)):
        for row in range(2):
            spread(target, row, (2 * index + row) * lanes)
    for at in range(0, up_bias.shape[1], 128):
        first = 6 * lanes + at // 128
        up_bias[:, at : at + 128] = small[first : first + 1]
    for row in range(2):
        spread(head_bias, row, 8 * lanes + row * (head_bias.shape[2] // 128))
    count = tokens.shape[1]
    for at in range(0, tokens.shape[2], 128):
        first = 56 + (at // 128) * count
        tokens[0, :, at : at + 128] = small[first : first + count]
    for index, (source, _) in enumerate(pairs):
        fetch(index, source).wait()
        put(index).start()
    for index in range(len(pairs)):
        put(index).wait()


def solution(mesh):
    return jax.shard_map(
        shards_of_two if mesh.shape[HEAD] == 2 else shards,
        mesh=mesh,
        in_specs=(
            P(SECTION, None, (SEQ, HEAD), None),
            P(),
            P(SECTION, None, None),
            P(SECTION, None, None),
            P(SECTION, None, None, HEAD),
            P(SECTION, None, HEAD),
            P(SECTION, HEAD, None),
            P(SECTION, None, None),
            P(SECTION, None, HEAD),
            P(SECTION, HEAD),
            P(SECTION, HEAD, None),
            P(SECTION, HEAD, None),
            P(SECTION, None, None),
            P(SECTION, None, None),
            P(SECTION, None, HEAD),
        ),
        out_specs=(
            P(SECTION, None, (SEQ, HEAD), None),
            P(SECTION, None, None),
            P(SECTION, None, None),
            P(SECTION, None, None, HEAD),
            P(SECTION, None, HEAD),
            P(SECTION, HEAD, None),
            P(SECTION, None, None),
            P(SECTION, None, HEAD),
            P(SECTION, HEAD),
            P(SECTION, HEAD, None),
            P(SECTION, HEAD, None),
            P(SECTION, None, None),
            P(SECTION, None, None),
            P(SECTION, None, HEAD),
        ),
        check_vma=False,
    )
```

```python
import functools
import math
from types import SimpleNamespace

import jax
import jax.numpy as jnp
from jax import lax
from jax.experimental import pallas as pl
from jax.experimental.pallas import tpu as pltpu
from jax.sharding import PartitionSpec as P

SECTION, SEQ, HEAD = "section", "seq", "head"
HEAD_DIM = 64
EPSILON = 1e-05
SCALE = 1.0 / math.sqrt(HEAD_DIM)
MESH = pl.DeviceIdType.MESH
VMEM = pl.BlockSpec(memory_space=pltpu.VMEM)
HBM = pl.BlockSpec(memory_space=pltpu.HBM)
SMEM = pl.BlockSpec(memory_space=pltpu.SMEM)
SHARED_ROWS = 36


def mm(left, right, dims=((1,), (0,))):
    return lax.dot_general(
        left, right, (dims, ((), ())), precision=lax.Precision.HIGH, preferred_element_type=jnp.float32
    )


def mm_nt(left, right):
    return mm(left, right, ((1,), (1,)))


def mm_tn(left, right):
    return mm(left, right, ((0,), (0,)))


def unit_rows(rows):
    centred = rows - jnp.mean(rows, axis=-1, keepdims=True)
    inverse = lax.rsqrt(jnp.mean(centred * centred, axis=-1, keepdims=True) + EPSILON)
    return centred * inverse, inverse


def unit_rows_back(d_unit, unit, inverse):
    return inverse * (
        d_unit
        - jnp.mean(d_unit, axis=-1, keepdims=True)
        - unit * jnp.mean(d_unit * unit, axis=-1, keepdims=True)
    )


def features(projected):
    halves = jnp.concatenate([jax.nn.softplus(projected), jax.nn.softplus(-projected)], axis=-1)
    return jnp.concatenate(
        [halves * jnp.roll(halves, rolled_by, axis=-1) for rolled_by in (1, 2, 3)], axis=-1
    )


def gelu_tanh(values_in):
    return jax.nn.gelu(values_in, approximate=True)


def head_sum_rows(rows, share):
    segment = lax.axis_size(HEAD) * share
    turn = lax.axis_index(HEAD) * share
    total = lax.psum(
        jnp.concatenate([jnp.roll(rows[:segment], turn, axis=0), rows[segment:]], axis=0), HEAD
    )
    return jnp.concatenate([jnp.roll(total[:segment], -turn, axis=0), total[segment:]], axis=0)


def head_rows(local):
    gathered = lax.all_gather(local, HEAD, axis=0, tiled=True)
    return jnp.roll(gathered, -lax.axis_index(HEAD) * local.shape[0], axis=0)


def head_scatter(rows):
    share = rows.shape[0] // lax.axis_size(HEAD)
    placed = jnp.roll(rows, lax.axis_index(HEAD) * share, axis=0)
    return lax.psum_scatter(placed, HEAD, scatter_dimension=0, tiled=True)


def heads_of(part):
    return part.reshape(part.shape[0], -1, HEAD_DIM).transpose(1, 0, 2)


def rows_of(part):
    return part.transpose(1, 0, 2).reshape(part.shape[1], -1)


def bmm(left, right, left_dim, right_dim):
    return lax.dot_general(
        left,
        right,
        (((left_dim,), (right_dim,)), ((0,), (0,))),
        precision=lax.Precision.HIGH,
        preferred_element_type=jnp.float32,
    )


def layer_forward(local, params, mask, allowed):
    width = local.shape[1]
    local_count = local.shape[0]
    segment = lax.axis_size(HEAD) * local_count
    rows = jnp.concatenate([head_rows(local), params.memory], axis=0)
    unit_one, inverse_one = unit_rows(rows)
    normed = unit_one * params.gains[0] + params.biases[0]
    projected = mm(normed, params.proj_in) + params.in_bias
    share = projected.shape[1] // 3
    query, key, value = (heads_of(projected[:, i * share : (i + 1) * share]) for i in range(3))
    scores = jnp.where(allowed, bmm(query, key, 2, 2) * SCALE, -1e30)
    row_top = jnp.max(scores, axis=-1, keepdims=True)
    exponent = jnp.exp(scores - row_top)
    soft = exponent / jnp.sum(exponent, axis=-1, keepdims=True)
    attended = rows_of(bmm(soft, value, 2, 1))
    hidden = rows + head_sum_rows(mm(attended, params.proj_out), local_count) + params.residual[0]
    unit_two, inverse_two = unit_rows(hidden)
    mixed = unit_two * params.gains[1] + params.biases[1]
    inner_pre = mm(mixed, params.up) + params.up_bias
    inner_act = gelu_tanh(inner_pre)
    partial = mm(inner_act, params.down)
    out_local = head_scatter(partial[:segment]) + hidden[:local_count] + params.residual[1]
    out_mem = lax.psum(partial[segment:], HEAD) + hidden[segment:] + params.residual[1]
    key_proj = mm(out_mem, params.key_mem)
    values = mm(out_mem, params.value_mem)
    gathered = lax.all_gather(jnp.concatenate([key_proj, values], axis=1), SEQ, axis=0, tiled=True)
    dk = key_proj.shape[1]
    keys_all = gathered[:, :dk]
    values_all = lax.all_gather(gathered[:, dk:], HEAD, axis=1, tiled=True)
    key_feats = features(keys_all)
    query_proj = mm(out_local, params.query_mem)
    query_feats = features(query_proj)
    weights = mask * mm_nt(query_feats, key_feats)
    denominator = jnp.sum(weights, axis=1, keepdims=True) + 1.0
    read = mm(weights, values_all) / denominator
    return SimpleNamespace(
        unit_one=unit_one,
        inverse_one=inverse_one,
        projected=projected,
        attended=attended,
        soft=soft,
        unit_two=unit_two,
        inverse_two=inverse_two,
        inner_pre=inner_pre,
        out_local=out_local,
        out_mem=out_mem,
        keys_all=keys_all,
        values_all=values_all,
        query_proj=query_proj,
        weights=weights,
        denominator=denominator,
        read=read,
        output=out_local + read,
    )


def layer_backward(grad, record, params, mask):
    head_count = lax.axis_size(HEAD)
    seq_count = lax.axis_size(SEQ)
    width = grad.shape[1]
    local_count = grad.shape[0]
    segment = head_count * local_count
    denominator = record.denominator
    d_numer = grad / denominator
    d_denom = -jnp.sum(grad * record.read, axis=1, keepdims=True) / denominator
    d_weights = mask * (mm_nt(d_numer, record.values_all) + d_denom)
    key_feats, keys_back = jax.vjp(features, record.keys_all)
    query_feats, query_back = jax.vjp(features, record.query_proj)
    d_query_proj = query_back(mm(d_weights, key_feats))[0]
    d_keys = keys_back(mm_tn(d_weights, query_feats))[0]
    d_values = mm_tn(record.weights, d_numer)
    d_memory = lax.psum_scatter(
        jnp.concatenate([d_keys, d_values], axis=1), SEQ, scatter_dimension=0, tiled=True
    )
    dk = d_keys.shape[1]
    d_key_proj = d_memory[:, :dk]
    d_value = lax.psum_scatter(
        d_memory[:, dk:], HEAD, scatter_dimension=1, tiled=True
    )
    d_mem = lax.psum(
        mm_nt(d_key_proj, params.key_mem) + mm_nt(d_value, params.value_mem), HEAD
    )
    d_local = grad + mm_nt(d_query_proj, params.query_mem)
    d_result = jnp.concatenate([head_rows(d_local), d_mem], axis=0)
    inner_act, gelu_back = jax.vjp(gelu_tanh, record.inner_pre)
    grad_down = mm_tn(inner_act, d_result)
    d_pre = gelu_back(mm_nt(d_result, params.down))[0]
    gains, biases = params.gains, params.biases
    mixed = record.unit_two * gains[1] + biases[1]
    grad_up = mm_tn(mixed, d_pre)
    d_mixed = head_sum_rows(mm_nt(d_pre, params.up), local_count)
    d_hidden = d_result + unit_rows_back(d_mixed * gains[1], record.unit_two, record.inverse_two)
    grad_out = mm_tn(record.attended, d_hidden)
    d_attended = mm_nt(d_hidden, params.proj_out)
    share = d_attended.shape[1]
    query, key, value = (
        heads_of(record.projected[:, i * share : (i + 1) * share]) for i in range(3)
    )
    soft = record.soft
    d_heads = heads_of(d_attended)
    inner_dot = jnp.sum(d_heads * heads_of(record.attended), axis=-1, keepdims=True)
    d_scores = soft * (bmm(d_heads, value, 2, 2) - inner_dot) * SCALE
    d_projected = jnp.concatenate(
        [
            rows_of(bmm(d_scores, key, 2, 1)),
            rows_of(bmm(d_scores, query, 1, 1)),
            rows_of(bmm(soft, d_heads, 1, 1)),
        ],
        axis=1,
    )
    normed = record.unit_one * gains[0] + biases[0]
    grad_in = mm_tn(normed, d_projected)
    columns = jnp.sum(d_projected, axis=0)
    grad_head_bias = jnp.stack([columns[:share], columns[2 * share :]])
    d_normed_all = mm_nt(d_projected, params.proj_in)
    d_normed = head_scatter(d_normed_all[:segment])
    d_normed_mem = lax.psum_scatter(
        d_normed_all[segment:], HEAD, scatter_dimension=0, tiled=True
    )
    mem_count = d_normed_mem.shape[0]
    own_mem = segment + lax.axis_index(HEAD) * mem_count

    def own(values):
        return jnp.concatenate(
            [values[:local_count], lax.dynamic_slice_in_dim(values, own_mem, mem_count, 0)], axis=0
        )

    d_normed_own = jnp.concatenate([d_normed, d_normed_mem], axis=0)
    unit_own = own(record.unit_one)
    d_rows = own(d_hidden) + unit_rows_back(
        d_normed_own * gains[0], unit_own, own(record.inverse_one)
    )
    part = 1.0 / head_count
    sharded = (
        grad_in,
        grad_head_bias,
        grad_out,
        grad_up,
        jnp.sum(d_pre, axis=0),
        grad_down,
        d_rows[local_count:],
        mm_tn(record.out_mem, d_value),
    )
    shared = (
        jnp.stack(
            [
                jnp.sum(d_normed_own * unit_own, axis=0),
                part * jnp.sum(d_mixed * record.unit_two, axis=0),
            ]
        ),
        jnp.stack([jnp.sum(d_normed_own, axis=0), part * jnp.sum(d_mixed, axis=0)]),
        part * jnp.stack([jnp.sum(d_hidden, axis=0), jnp.sum(d_result, axis=0)]),
        mm_tn(record.out_local, d_query_proj),
        mm_tn(record.out_mem, d_key_proj),
    )
    return (d_rows[:local_count], sharded, shared)


def passed_along(value, axis, steps):
    count = lax.axis_size(axis)
    first, last = (max(0, -steps), min(count, count - steps))
    return lax.ppermute(value, axis, [(source, source + steps) for source in range(first, last)])


def shards(
    boundary_in,
    short_items,
    norm_gains,
    norm_biases,
    projection_in,
    head_bias,
    projection_out,
    residual_bias,
    up_weight,
    up_bias,
    down_weight,
    memory_tokens,
    query_memory,
    key_memory,
    value_memory,
):
    section = lax.axis_index(SECTION)
    sections = lax.axis_size(SECTION)
    head_count = lax.axis_size(HEAD)
    head_place = lax.axis_index(HEAD)
    seq_count = lax.axis_size(SEQ)
    seq_place = lax.axis_index(SEQ)
    micro_total = boundary_in.shape[1]
    local_count = boundary_in.shape[2]
    width = boundary_in.shape[3]
    segment = head_count * local_count
    head_width = projection_in.shape[3]
    memory_all = lax.all_gather(memory_tokens[0], HEAD, axis=0, tiled=True)
    mem_count = memory_all.shape[0]
    params = SimpleNamespace(
        gains=norm_gains[0],
        biases=norm_biases[0],
        proj_in=projection_in[0].reshape(width, 3 * head_width),
        in_bias=jnp.concatenate(
            [head_bias[0, 0], jnp.zeros((head_width,), jnp.float32), head_bias[0, 1]]
        ),
        proj_out=projection_out[0],
        residual=residual_bias[0],
        up=up_weight[0],
        up_bias=up_bias[0],
        down=down_weight[0],
        memory=memory_all,
        query_mem=query_memory[0],
        key_mem=key_memory[0],
        value_mem=value_memory[0],
    )
    ordinal = jnp.arange(segment)
    places = jnp.concatenate(
        [(ordinal + head_place * local_count) % segment, segment + jnp.arange(mem_count)]
    )
    allowed = (places[:, None] >= places[None, :])[None]

    positions = jnp.arange(seq_count)
    masks = []
    for micro in range(micro_total):
        if micro == 0:
            item = jnp.zeros((seq_count,), jnp.int32)
        else:
            ends = jnp.cumsum(short_items[micro - 1])
            item = jnp.sum((positions[:, None] >= ends[None, :]).astype(jnp.int32), axis=1)
        own_item = jnp.sum(jnp.where(positions == seq_place, item, 0))
        seen = jnp.logical_and(positions < seq_place, item == own_item).astype(jnp.float32)
        masks.append(jnp.repeat(seen, mem_count)[None, :])
    masks = jnp.stack(masks)

    tick_total = micro_total + sections - 1
    received = jnp.zeros_like(boundary_in[0, 0])
    records = []
    for tick in range(tick_total):
        micro = jnp.clip(tick - section, 0, micro_total - 1)
        local = jnp.where(section == 0, boundary_in[0, min(tick, micro_total - 1)], received)
        records.append(layer_forward(local, params, masks[micro], allowed))
        if tick + 1 < tick_total:
            received = passed_along(records[-1].output, SECTION, 1)
    back_received = jnp.zeros_like(boundary_in[0, 0])
    grads_input = []
    total = None
    for tick in range(tick_total):
        raw = tick - (sections - 1 - section)
        valid = jnp.logical_and(raw >= 0, raw < micro_total)
        micro = jnp.clip(raw, 0, micro_total - 1)
        grad = jnp.where(
            section == sections - 1, boundary_in[0, min(tick, micro_total - 1)], back_received
        )
        kept = [
            vars(records[min(max(tick - (sections - 1 - place), 0), micro_total - 1) + place])
            for place in range(sections)
        ]
        record = SimpleNamespace(
            **jax.tree.map(lambda *kinds: lax.select_n(section, *kinds), *kept)
        )
        grad_x, sharded, shared = layer_backward(grad, record, params, masks[micro])
        fresh = jax.tree.map(lambda part: jnp.where(valid, part, 0.0), (sharded, shared))
        total = fresh if total is None else jax.tree.map(jnp.add, total, fresh)
        grads_input.append(grad_x)
        if tick + 1 < tick_total:
            back_received = passed_along(grad_x, SECTION, -1)
    sharded, shared = total
    grad_in, grad_heads_bias, grad_out, grad_up, grad_up_b, grad_down, grad_mem, grad_value = lax.psum(
        sharded, SEQ
    )
    grad_gains, grad_biases, grad_residual, grad_query, grad_key = lax.psum(shared, (SEQ, HEAD))
    finished_grads = jnp.stack(
        [grads_input[micro + sections - 1] for micro in range(micro_total)]
    )
    finished_outputs = jnp.stack(
        [records[micro + sections - 1].output for micro in range(micro_total)]
    )
    boundary_out = jnp.where(section == 0, finished_grads, finished_outputs)[None]
    return (
        boundary_out,
        grad_gains[None],
        grad_biases[None],
        grad_in.reshape(projection_in.shape),
        grad_heads_bias[None],
        grad_out[None],
        grad_residual[None],
        grad_up[None],
        grad_up_b[None],
        grad_down[None],
        grad_mem[None],
        grad_query[None],
        grad_key[None],
        grad_value[None],
    )


def barrier_with(pairs, wait_count):
    barrier = pltpu.get_barrier_semaphore()
    for condition, device in pairs:

        @pl.when(condition)
        def _(device=device):
            pl.semaphore_signal(barrier, inc=1, device_id=device, device_id_type=MESH)

    @pl.when(wait_count > 0)
    def _():
        pl.semaphore_wait(barrier, wait_count)


def nn(left, right):
    return mm(left, right)


def lane_tiles(width):
    tile = 256 if width % 256 == 0 else width
    return [(at, tile) for at in range(0, width, tile)]


def rows_at(start, count):
    return pl.ds(pl.multiple_of(start, count), count)


def halves_of(projected):
    small = jnp.log1p(jnp.exp(-jnp.abs(projected)))
    return jnp.concatenate(
        [jnp.maximum(projected, 0.0) + small, jnp.maximum(-projected, 0.0) + small], axis=1
    )


def halves_back(projected, d_halves):
    width = projected.shape[1]
    rising = 1.0 / (1.0 + jnp.exp(-projected))
    falling = 1.0 / (1.0 + jnp.exp(projected))
    return d_halves[:, :width] * rising - d_halves[:, width:] * falling


def turned(values, by):
    return pltpu.roll(values, by % values.shape[1], 1)


GELU_IN = math.sqrt(2.0 / math.pi)


def gelu_parts(pre):
    cubic = 0.044715 * pre * pre
    bent = jnp.tanh(GELU_IN * pre * (1.0 + cubic))
    half = 0.5 * (1.0 + bent)
    slope = half + 0.5 * pre * (1.0 - bent * bent) * GELU_IN * (1.0 + 3.0 * cubic)
    return pre * half, slope


def seen_mask(items, micro, seqs, mem):
    seq = lax.axis_index(SEQ)
    row_seq = lax.div(lax.broadcasted_iota(jnp.int32, (1, seqs * mem), 1), jnp.int32(mem))
    end = jnp.int32(0)
    own = jnp.int32(0)
    item = jnp.zeros((1, seqs * mem), jnp.int32)
    for piece in range(items.shape[1]):
        end = end + items[jnp.maximum(micro - 1, 0), piece]
        bound = jnp.where(micro == 0, seqs, end)
        own = own + (seq >= bound).astype(jnp.int32)
        item = item + (row_seq >= bound).astype(jnp.int32)
    return jnp.logical_and(row_seq < seq, item == own)


WEIGHTS = IN, UP, DOWN, VALUE, QUERY, KEY = tuple(range(6))
COPIES = (1, 2, 3, 3, 3, 1, 1, 1, 3, 3, 3)
(X_IN, Y_OUT, PART, LOCAL, MEMORY, GRAD, D_LOCAL, D_MEMORY, MIX, ROWS, ROWS_MEMORY) = range(11)
COPY_SLOTS = sum(COPIES)
TOKENS, OUT_SHARE = range(2)


def copy_slot(micro, kind, index=0):
    return 2 + micro * COPY_SLOTS + sum(COPIES[:kind]) + index


def column_sum(values_in):
    return jnp.sum(values_in, axis=0, keepdims=True)


SLOTS = 3
AHEAD = (3, 9)


def layers_kernel(lanes, *refs):
    refs = list(refs)

    def take(count):
        taken, refs[:] = refs[:count], refs[count:]
        return taken

    items, x, gains, biases, head_bias, residual, b_up, mem_tokens = take(8)
    weights_in = take(len(WEIGHTS))
    (w_out_in,) = take(1)
    down_sum, up_sum, in_sum, out_sum, value_sum, key_sum, small_sum, half_sum = take(8)
    y, grad_x = take(2)
    held = take(len(WEIGHTS))
    w_in, w_up, w_down, w_value, w_query, w_key = held
    rows, qkv, attended, lse, hidden, pre = take(6)
    out_local, out_mem, keys, values, query_proj, weights, read = take(7)
    w_out_all, got_attended = take(2)
    (
        normed, d_pre, d_out, part, got_part, got_out, mem_all, key_block, value_block, from_k, from_v,
        mem_part, got_mem, grad_y, wide_scores, wide_soft, wide_query, wide_grad,
        g_small, got_small, got_half, got_key, all_mem, all_value, all_key,
    ) = take(25)
    d_keys, d_values = keys, read
    slots = take(8)
    load, store, send, recv, send_w, recv_w, send_up, recv_up, send_x, recv_x, send_f, recv_f, free, go = refs

    section, seq, head = (lax.axis_index(name) for name in (SECTION, SEQ, HEAD))
    seqs = lax.axis_size(SEQ)
    micros, local, width = x.shape
    segment = 2 * local
    mem = out_mem.shape[1]
    half_mem = mem // 2
    total = segment + mem
    share = w_in.shape[2]
    inner = w_up.shape[1]
    heads = share // HEAD_DIM
    dv = w_value.shape[1]
    other = 1 - head
    partner = {HEAD: other}
    own_rows, other_rows = rows_at(head * local, local), rows_at(other * local, local)
    own_mem = rows_at(head * half_mem, half_mem)
    own_mem_rows = rows_at(segment + head * half_mem, half_mem)
    seg_rows, mem_rows = pl.ds(0, segment), pl.ds(segment, mem)
    column_tiles = [(at, width // 3) for at in range(0, width, width // 3)]
    inner_tiles = lane_tiles(inner)

    def key_slot(micro, place):
        return 2 + micros * COPY_SLOTS + micro * 3 * seqs + place

    def value_slot(micro, place, of_head):
        return key_slot(micro, seqs + 2 * place + of_head)

    def copy(slot, source, target, device):
        return pltpu.make_async_remote_copy(
            src_ref=source,
            dst_ref=target,
            send_sem=send.at[slot],
            recv_sem=recv.at[slot],
            device_id=device,
            device_id_type=MESH,
        )

    def weight_copy(name):
        return pltpu.make_async_copy(
            weights_in[name], held[name], load.at[name]
        )

    out_copy = pltpu.make_async_copy(w_out_in, w_out_all.at[head], load.at[len(WEIGHTS)])
    w_out = w_out_all.at[head]

    def each_micro(stage):
        def body(micro, carry):
            stage(micro)
            return carry

        lax.fori_loop(0, micros, body, 0)

    def each_seq(condition, act):
        for t in range(seqs):

            @pl.when(condition(t))
            def _(t=t):
                act(t)

    def later(t):
        return t > seq

    def earlier(t):
        return t < seq

    out_copy.start()
    for name in WEIGHTS:
        weight_copy(name).start()
    keys[...] = jnp.zeros_like(keys)
    values[...] = jnp.zeros_like(values)
    from_k[...] = jnp.zeros_like(from_k)
    from_v[...] = jnp.zeros_like(from_v)
    g_small[...] = jnp.zeros_like(g_small)
    mem_all[own_mem] = mem_tokens[...]
    barrier_with(
        [(seq >= 0, partner)]
        + [(t != seq, {SEQ: t, HEAD: g}) for t in range(seqs) for g in range(2)]
        + [(section == 1, {SECTION: 0, HEAD: g}) for g in range(2)]
        + [(section == 0, {SECTION: 1})],
        1 + 2 * (seqs - 1) + 2 - section,
    )

    tokens = copy(TOKENS, mem_tokens, mem_all.at[own_mem], partner)

    def x_load(micro, target):
        return pltpu.make_async_copy(x.at[micro], target, load.at[len(WEIGHTS) + 1 + micro])

    def x_copy(micro):
        return copy(copy_slot(micro, X_IN), x.at[micro], rows.at[micro, own_rows], partner)

    def y_sent(micro, target_head):
        return pltpu.make_async_remote_copy(
            src_ref=y.at[micro],
            dst_ref=rows.at[micro, own_rows],
            send_sem=send.at[copy_slot(micro, Y_OUT, target_head)],
            recv_sem=recv.at[copy_slot(micro, Y_OUT, head)],
            device_id={SECTION: 1, HEAD: target_head},
            device_id_type=MESH,
        )

    def y_got(micro, source_head):
        here = rows.at[micro, rows_at(source_head * local, local)]
        return copy(copy_slot(micro, Y_OUT, source_head), here, here, partner)

    def tile_copy(kind, micro, index):
        at, tile = column_tiles[index]
        return copy(
            copy_slot(micro, kind, index),
            part.at[micro, :, at : at + tile],
            got_part.at[micro, :, at : at + tile],
            partner,
        )

    def attended_copy(micro, index):
        cut = slice(index * 2 * HEAD_DIM, (index + 1) * 2 * HEAD_DIM)
        return copy(
            copy_slot(micro, PART, index),
            attended.at[micro, :, cut],
            got_attended.at[micro, :, cut],
            partner,
        )

    def local_tile(kind, micro, index):
        at, tile = column_tiles[index]
        return copy(
            copy_slot(micro, kind, index),
            part.at[micro, other_rows, at : at + tile],
            got_out.at[micro, pl.ds(0, local), at : at + tile],
            partner,
        )

    def memory_tile(kind, micro, index):
        at, tile = column_tiles[index]
        return copy(
            copy_slot(micro, kind, index),
            part.at[micro, mem_rows, at : at + tile],
            got_out.at[micro, pl.ds(local, mem), at : at + tile],
            partner,
        )

    def key_copy(micro, source, target):
        return pltpu.make_async_remote_copy(
            src_ref=key_block.at[micro],
            dst_ref=keys.at[micro, rows_at(source * mem, mem)],
            send_sem=send.at[key_slot(micro, target)],
            recv_sem=recv.at[key_slot(micro, source)],
            device_id={SEQ: target},
            device_id_type=MESH,
        )

    def value_copy(micro, source, source_head, target, target_head):
        return pltpu.make_async_remote_copy(
            src_ref=value_block.at[micro],
            dst_ref=values.at[
                micro, rows_at(source * mem, mem), pl.ds(pl.multiple_of(source_head * dv, 128), dv)
            ],
            send_sem=send.at[value_slot(micro, target, target_head)],
            recv_sem=recv.at[value_slot(micro, source, source_head)],
            device_id={SEQ: target, HEAD: target_head},
            device_id_type=MESH,
        )

    tokens.start()

    out_share = share // seqs

    def out_piece(half, piece):
        return w_out_all.at[half, rows_at(piece * out_share, out_share)]

    def over_out():
        mine = w_out_in.at[rows_at(seq * out_share, out_share)]
        return copy(OUT_SHARE, mine, out_piece(head, seq), partner)

    def hand_out(source, target):
        return pltpu.make_async_remote_copy(
            src_ref=out_piece(other, source),
            dst_ref=out_piece(other, source),
            send_sem=send_w.at[target],
            recv_sem=recv_w.at[source],
            device_id={SEQ: target},
            device_id_type=MESH,
        )

    @pl.when(section == 0)
    def _():
        over_out().start()

    @pl.when(section == 0)
    def _():
        x_copy(0).start()
        for micro in range(micros):
            x_load(micro, rows.at[micro, own_rows]).start()

    @pl.when(section == 1)
    def _():
        for micro in range(micros):
            x_load(micro, grad_y.at[micro]).start()

    tokens.wait_recv()
    for micro in range(micros):
        rows[micro, mem_rows] = mem_all[...]
    @pl.when(section == 1)
    def _():
        pl.semaphore_wait(go, 1)
        over_out().start()

    over_out().wait_recv()
    each_seq(lambda t: t != seq, lambda t: hand_out(seq, t).start())

    causal = lax.broadcasted_iota(jnp.int32, (segment, segment), 0) >= (
        lax.broadcasted_iota(jnp.int32, (segment, segment), 1)
    )
    mem_causal = segment + lax.broadcasted_iota(jnp.int32, (mem, total), 0) >= (
        lax.broadcasted_iota(jnp.int32, (mem, total), 1)
    )
    lane = lax.broadcasted_iota(jnp.int32, (total, 128), 1)

    def lanes_of(kind, place):
        return slice(kind * share + place * HEAD_DIM, kind * share + (place + 1) * HEAD_DIM)

    def attention(micro):
        @pl.when(section == 0)
        def _():
            x_load(micro, rows.at[micro, own_rows]).wait()
            x_copy(micro).wait_recv()

            @pl.when(micro + 1 < micros)
            def _():
                x_copy(micro + 1).start()

        @pl.when(section == 1)
        def _():
            for source in range(2):
                y_got(micro, source).wait_recv()

        unit, _ = unit_rows(rows[micro])
        normed[micro] = unit * gains[0:1] + biases[0:1]

        @pl.when(micro == 0)
        def _():
            weight_copy(IN).wait()

        for kind in range(3):
            made = nn(normed[micro], w_in[kind])
            if kind != 1:
                made = made + head_bias[kind // 2 : kind // 2 + 1]
            qkv[micro, :, kind * share : (kind + 1) * share] = made
        tops = jnp.zeros((total, 128), jnp.float32)
        for place in range(heads):
            query, key, value = (lanes_of(kind, place) for kind in range(3))
            made_top = []
            for at, allowed, seen in ((seg_rows, causal, seg_rows), (mem_rows, mem_causal, pl.ds(0, total))):
                scores = mm_nt(qkv[micro, at, query], qkv[micro, seen, key]) * SCALE
                scores = jnp.where(allowed, scores, -1e30)
                top = jnp.max(scores, axis=1, keepdims=True)
                exponent = jnp.exp(scores - top)
                row_total = jnp.sum(exponent, axis=1, keepdims=True)
                attended[micro, at, place * HEAD_DIM : (place + 1) * HEAD_DIM] = (
                    nn(exponent, qkv[micro, seen, value]) / row_total
                )
                made_top.append(top + jnp.log(row_total))
            tops = jnp.where(lane == place, jnp.concatenate(made_top, axis=0), tops)
            if place % 2 == 1:
                attended_copy(micro, place // 2).start()
        lse[micro] = tops

    each_micro(attention)
    weight_copy(UP).wait()
    weight_copy(DOWN).wait()
    out_copy.wait()
    each_seq(lambda t: t != seq, lambda t: hand_out(t, t).wait_recv())

    @pl.when(section == 0)
    def _():
        pl.semaphore_signal(go, inc=1, device_id={SECTION: 1}, device_id_type=MESH)


    def feed_forward(micro):
        for index in range(heads // 2):
            attended_copy(micro, index).wait()
        for at, tile in column_tiles:
            cut = slice(at, at + tile)
            hidden[micro, :, cut] = (
                rows[micro, :, cut]
                + nn(attended[micro], w_out_all[head, :, cut])
                + nn(got_attended[micro], w_out_all[other, :, cut])
                + residual[0:1, cut]
            )
        unit, _ = unit_rows(hidden[micro])
        normed[micro] = unit * gains[1:2] + biases[1:2]
        for at, tile in inner_tiles:
            cut = slice(at, at + tile)
            made = nn(normed[micro], w_up[:, cut]) + b_up[:, cut]
            pre[micro, :, cut] = made
            d_pre[micro, :, cut] = gelu_parts(made)[0]
        for index, (at, tile) in enumerate(column_tiles):
            part[micro, :, at : at + tile] = nn(d_pre[micro], w_down[:, at : at + tile])
            memory_tile(MEMORY, micro, index).start()
            local_tile(LOCAL, micro, index).start()

    each_micro(feed_forward)
    for name in (KEY, VALUE, QUERY):
        weight_copy(name).wait()

    def memory_write(micro):
        for index, (at, tile) in enumerate(column_tiles):
            cut = slice(at, at + tile)
            memory_tile(MEMORY, micro, index).wait()
            out_mem[micro, :, cut] = (
                part[micro, mem_rows, cut]
                + got_out[micro, local:, cut]
                + hidden[micro, mem_rows, cut]
                + residual[1:2, cut]
            )
        key_block[micro] = nn(out_mem[micro], w_key[...])
        value_block[micro] = nn(out_mem[micro], w_value[...])

        def share_block(t):
            key_copy(micro, seq, t).start()
            for g in range(2):
                value_copy(micro, seq, head, t, g).start()

        each_seq(later, share_block)

    each_micro(memory_write)

    def read_query(micro):
        for index, (at, tile) in enumerate(column_tiles):
            cut = slice(at, at + tile)
            local_tile(LOCAL, micro, index).wait()
            out_local[micro, :, cut] = (
                part[micro, own_rows, cut]
                + got_out[micro, :local, cut]
                + hidden[micro, own_rows, cut]
                + residual[1:2, cut]
            )
        query_proj[micro] = nn(out_local[micro], w_query[...])

    def memory_read(micro):
        read_query(micro)

        def got(t):
            key_copy(micro, t, t).wait_recv()
            for g in range(2):
                value_copy(micro, t, g, t, g).wait_recv()

        query_halves = halves_of(query_proj[micro])
        each_seq(earlier, got)
        key_halves = halves_of(keys[micro])
        scores = jnp.zeros((local, seqs * mem), jnp.float32)
        for by in (1, 2, 3):
            scores = scores + mm_nt(
                query_halves * turned(query_halves, by), key_halves * turned(key_halves, by)
            )
        scores = jnp.where(seen_mask(items, micro, seqs, mem), scores, 0.0)
        weights[micro] = scores
        found = nn(scores, values[micro]) / (jnp.sum(scores, axis=1, keepdims=True) + 1.0)
        read[micro] = found
        y[micro] = out_local[micro] + found

        @pl.when(section == 0)
        def _():
            for target in range(2):
                y_sent(micro, target).start()

    each_micro(memory_read)

    def grad_copy(micro):
        return copy(
            copy_slot(micro, GRAD), grad_x.at[micro], grad_y.at[micro], {SECTION: 0}
        )

    def rows_copy(micro):
        here = d_out.at[micro, own_rows]
        return copy(copy_slot(micro, D_LOCAL), here, here, partner)

    def mem_copy(micro):
        return copy(copy_slot(micro, D_MEMORY), mem_part.at[micro], got_mem.at[micro], partner)

    def back_key(micro, source, target):
        return pltpu.make_async_remote_copy(
            src_ref=d_keys.at[micro, rows_at(target * mem, mem)],
            dst_ref=from_k.at[micro, source],
            send_sem=send.at[key_slot(micro, target)],
            recv_sem=recv.at[key_slot(micro, source)],
            device_id={SEQ: target},
            device_id_type=MESH,
        )

    def back_value(micro, source, source_head, target, target_head):
        return pltpu.make_async_remote_copy(
            src_ref=d_values.at[
                micro, rows_at(target * mem, mem), pl.ds(pl.multiple_of(target_head * dv, 128), dv)
            ],
            dst_ref=from_v.at[micro, source, source_head],
            send_sem=send.at[value_slot(micro, target, target_head)],
            recv_sem=recv.at[value_slot(micro, source, source_head)],
            device_id={SEQ: target, HEAD: target_head},
            device_id_type=MESH,
        )

    factors = ((out_mem, all_mem), (value_block, all_value), (key_block, all_key))

    def factor_copy(kind, source, target):
        own, everyone = factors[kind]
        return pltpu.make_async_remote_copy(
            src_ref=own,
            dst_ref=everyone.at[:, rows_at(source * mem, mem)],
            send_sem=send_f.at[kind, target],
            recv_sem=recv_f.at[kind, source],
            device_id={SEQ: target},
            device_id_type=MESH,
        )

    def others(t):
        return t != seq

    def spread_factor(kind):
        own, everyone = factors[kind]
        everyone[:, rows_at(seq * mem, mem)] = own[...]
        each_seq(others, lambda t: factor_copy(kind, seq, t).start())

    spread_factor(0)

    def key_half_copy(micro):
        return pltpu.make_async_remote_copy(
            src_ref=key_block.at[micro],
            dst_ref=got_key.at[micro],
            send_sem=send_x.at[micro],
            recv_sem=recv_x.at[micro],
            device_id=partner,
            device_id_type=MESH,
        )

    def add_small(row, vector):
        for at in range(0, vector.shape[1], 128):
            g_small[row + at // 128 : row + at // 128 + 1] += vector[:, at : at + 128]

    def read_back(micro):
        @pl.when(section == 0)
        def _():
            grad_copy(micro).wait_recv()

        @pl.when(section == 1)
        def _():
            x_load(micro, grad_y.at[micro]).wait()

        grad = grad_y[micro]
        scores = weights[micro]
        denominator = jnp.sum(scores, axis=1, keepdims=True) + 1.0
        d_numer = grad / denominator
        d_denom = -jnp.sum(grad * read[micro], axis=1, keepdims=True) / denominator
        d_values[micro] = mm_tn(scores, d_numer)

        def send_values(t):
            for g in range(2):
                back_value(micro, seq, head, t, g).start()

        each_seq(earlier, send_values)
        d_scores = jnp.where(
            seen_mask(items, micro, seqs, mem), mm_nt(d_numer, values[micro]) + d_denom, 0.0
        )
        query_halves, key_halves = halves_of(query_proj[micro]), halves_of(keys[micro])
        d_key_halves = jnp.zeros_like(key_halves)
        for by in (1, 2, 3):
            d_feats = mm_tn(d_scores, query_halves * turned(query_halves, by))
            d_key_halves += d_feats * turned(key_halves, by) + turned(d_feats * key_halves, -by)
        d_keys[micro] = halves_back(keys[micro], d_key_halves)
        each_seq(earlier, lambda t: back_key(micro, seq, t).start())
        d_query_halves = jnp.zeros_like(query_halves)
        for by in (1, 2, 3):
            d_feats = nn(d_scores, key_halves * turned(key_halves, by))
            d_query_halves += d_feats * turned(query_halves, by) + turned(d_feats * query_halves, -by)
        query_proj[micro] = halves_back(query_proj[micro], d_query_halves)
        d_out[micro, own_rows] = grad + mm_nt(query_proj[micro], w_query[...])
        rows_copy(micro).start()

    each_micro(read_back)

    def write_back(micro):
        def got(t):
            back_key(micro, t, t).wait_recv()
            for g in range(2):
                back_value(micro, t, g, t, g).wait_recv()

        each_seq(later, got)
        key_block[micro] = jnp.sum(from_k[micro], axis=0)
        value_block[micro] = jnp.sum(from_v[micro], axis=(0, 1))
        mem_part[micro] = mm_nt(key_block[micro], w_key[...]) + mm_nt(
            value_block[micro], w_value[...]
        )
        mem_copy(micro).start()
        key_half_copy(micro).start()

    def forward_sent(micro):
        def sent(t):
            key_copy(micro, seq, t).wait_send()
            for g in range(2):
                value_copy(micro, seq, head, t, g).wait_send()

        each_seq(later, sent)

    each_micro(forward_sent)
    each_micro(write_back)

    def both(ref):
        return ref[...].reshape(micros * ref.shape[1], ref.shape[2])

    w_query[...] = mm_tn(both(out_local), both(query_proj))
    spread_factor(1)
    for micro in range(micros):
        key_half_copy(micro).wait()
        key_block[micro] += got_key[micro]
    spread_factor(2)
    def feed_forward_back(micro):
        mem_copy(micro).wait()
        d_out[micro, mem_rows] = mem_part[micro] + got_mem[micro]
        rows_copy(micro).wait()
        for at, tile in inner_tiles:
            cut = slice(at, at + tile)
            activated, slope = gelu_parts(pre[micro, :, cut])
            made = slope * mm_nt(d_out[micro], w_down[cut])
            pre[micro, :, cut] = activated
            d_pre[micro, :, cut] = made
            add_small(36 + at // 128, column_sum(made))
        for index, (at, tile) in enumerate(column_tiles):
            part[micro, :, at : at + tile] = mm_nt(d_pre[micro], w_up[at : at + tile])
            tile_copy(MIX, micro, index).start()
        add_small(30, 0.5 * column_sum(d_out[micro]))

    each_micro(feed_forward_back)
    along = seqs // lanes
    z, lane_y = seq // lanes, lax.rem(seq, lanes)
    place = lane_y * along + jnp.where(lax.rem(lane_y, 2) == 0, z, along - 1 - z)

    def device(spot):
        row = spot // along
        column = lax.rem(spot, along)
        column = jnp.where(lax.rem(row, 2) == 0, column, along - 1 - column)
        return {SEQ: column * lanes + row}

    targets = (device(lax.rem(place + 1, seqs)), device(lax.rem(place + seqs - 1, seqs)))
    signs = (1, -1)
    kinds = range(w_in.shape[0])
    sources = [w_down, w_up, w_out, *(w_in.at[kind] for kind in kinds), g_small, got_half]
    results = [down_sum, up_sum, out_sum, *(in_sum.at[kind] for kind in kinds)]
    results += [small_sum, half_sum.at[head]]
    count = len(sources)
    ways = [[(index, way) for index in group for way in range(2)] for group in (range(2), range(2, count))]
    last = seqs - 2

    def block(ref, way, spot):
        size = ref.shape[0] // seqs
        half = size // 2
        spot = lax.rem(spot + 2 * seqs, seqs)
        return ref.at[pl.ds(pl.multiple_of(spot * size + way * half, half), half)]

    def slot_of(index, way, step):
        return slots[index].at[way, lax.rem(step, SLOTS)]

    def up_copy(index, way, step, source):
        turn = lax.rem(step, SLOTS)
        return pltpu.make_async_remote_copy(
            src_ref=source,
            dst_ref=slot_of(index, way, step),
            send_sem=send_up.at[turn, way, index],
            recv_sem=recv_up.at[turn, way, index],
            device_id=targets[way],
            device_id_type=MESH,
        )

    def on_copy(index, way, step, source, target):
        return pltpu.make_async_remote_copy(
            src_ref=source,
            dst_ref=target,
            send_sem=send.at[(step * 2 + way) * count + index],
            recv_sem=recv.at[(step * 2 + way) * count + index],
            device_id=targets[way],
            device_id_type=MESH,
        )

    def over(source, target, number):
        return pltpu.make_async_remote_copy(
            src_ref=source,
            dst_ref=target,
            send_sem=send_x.at[number],
            recv_sem=recv_x.at[number],
            device_id=partner,
            device_id_type=MESH,
        )

    def hand_over(way, spot, step):
        mine = block(half_sum.at[head], way, spot)
        return over(mine, mine, 2 + way * seqs + step)

    def home(index, way):
        return pltpu.make_async_copy(
            slot_of(index, way, last),
            block(results[index], way, place + signs[way]),
            store.at[way, index],
        )

    def sum_up(group, step):
        @pl.when(step >= SLOTS)
        def _():
            for way in range(2):
                pl.semaphore_wait(free.at[group, way], 1)

        for index, way in ways[group]:
            got = slot_of(index, way, step - 1)
            up_copy(index, way, step - 1, got).wait_recv()
            got[...] += block(sources[index], way, place - signs[way] * step)[...]
            up_copy(index, way, step, got).start()
        for index, way in ways[group]:
            up_copy(index, way, step - 1, slot_of(index, way, step)).wait_send()

        @pl.when(jnp.logical_and(step >= 2, step + 1 < seqs - 1))
        def _():
            for way in range(2):
                pl.semaphore_signal(
                    free.at[group, way], inc=1, device_id=targets[1 - way], device_id_type=MESH
                )

    def turn_round(group):
        for index, way in ways[group]:
            got = slot_of(index, way, last)
            up_copy(index, way, last, got).wait_recv()
            spot = place + signs[way]
            got[...] += block(sources[index], way, spot)[...]
            target = block(results[index], way, spot)
            on_copy(index, way, 0, got, target).start()
            home(index, way).start()
            if index == count - 1:
                over(got, target, 2 + way * seqs).start()

    def pass_on(group, step):
        for index, way in ways[group]:
            spot = place - signs[way] * (step - 1)
            here = block(results[index], way, spot)
            on_copy(index, way, step - 1, here, here).wait_recv()

            @pl.when(step < seqs - 1)
            def _(index=index, way=way, here=here):
                on_copy(index, way, step, here, here).start()

            if index == count - 1:
                hand_over(way, spot, step).start()

    def advance(group, step):
        @pl.when(step < seqs - 1)
        def _():
            sum_up(group, step)

        @pl.when(step == seqs - 1)
        def _():
            turn_round(group)

        @pl.when(jnp.logical_and(step >= seqs, step < 2 * seqs - 1))
        def _():
            pass_on(group, step - seqs + 1)

    def begin(*indices):
        for index in indices:
            for way in range(2):
                up_copy(index, way, 0, block(sources[index], way, place)).start()

    for micro in range(micros):
        unit, _ = unit_rows(hidden[micro])
        normed[micro] = unit * gains[1:2] + biases[1:2]
    for at, tile in inner_tiles:
        cut = slice(at, at + tile)
        w_down[cut] = mm_tn(both(pre.at[:, :, cut]), both(d_out))
    begin(0)
    for at, tile in inner_tiles:
        cut = slice(at, at + tile)
        w_up[:, cut] = mm_tn(both(normed), both(d_pre.at[:, :, cut]))
    begin(1)

    def attention_back(micro):
        unit, inverse = unit_rows(hidden[micro])
        for index, (at, tile) in enumerate(column_tiles):
            cut = slice(at, at + tile)
            tile_copy(MIX, micro, index).wait()
            got_part[micro, :, cut] += part[micro, :, cut]
        d_mixed = got_part[micro]
        hidden[micro] = d_out[micro] + unit_rows_back(d_mixed * gains[1:2], unit, inverse)
        add_small(6, 0.5 * column_sum(d_mixed * unit))
        add_small(18, 0.5 * column_sum(d_mixed))
        add_small(24, 0.5 * column_sum(hidden[micro]))
        part[micro, :, :share] = mm_nt(hidden[micro], w_out[...])
        block_rows = lax.div(
            lax.broadcasted_iota(jnp.int32, (mem, share), 1), jnp.int32(HEAD_DIM)
        )
        for place in range(heads):
            query, key, value = (lanes_of(kind, place) for kind in range(3))
            cut = slice(place * HEAD_DIM, (place + 1) * HEAD_DIM)
            wide = pl.ds(place * mem, mem)
            grads = []
            for at, allowed, seen in ((seg_rows, causal, seg_rows), (mem_rows, mem_causal, pl.ds(0, total))):
                scores = mm_nt(qkv[micro, at, query], qkv[micro, seen, key]) * SCALE
                soft = jnp.exp(
                    jnp.where(allowed, scores, -1e30) - lse[micro, at, place : place + 1]
                )
                d_head = part[micro, at, cut]
                inner_dot = jnp.sum(d_head * attended[micro, at, cut], axis=1, keepdims=True)
                d_scores = soft * (mm_nt(d_head, qkv[micro, seen, value]) - inner_dot) * SCALE
                grads.append((soft, d_scores, d_head, nn(d_scores, qkv[micro, seen, key])))
            (soft, d_scores, d_head, d_query), (mem_soft, mem_scores, _, mem_query) = grads
            wide_soft[wide] = mem_soft
            wide_scores[wide] = mem_scores
            mine = block_rows == place
            wide_query[wide] = jnp.where(mine, qkv[micro, mem_rows, :share], 0.0)
            wide_grad[wide] = jnp.where(mine, part[micro, mem_rows, :share], 0.0)
            d_key = mm_tn(d_scores, qkv[micro, seg_rows, query])
            d_value = mm_tn(soft, d_head)
            qkv[micro, seg_rows, query] = d_query
            qkv[micro, mem_rows, query] = mem_query
            qkv[micro, seg_rows, key] = d_key
            qkv[micro, seg_rows, value] = d_value
            if place % 2 == 1 and place + 1 < heads:

                @pl.when(section == 1)
                def _(place=place):
                    sum_up(0, 3 * micro + (place + 1) // 2)

        qkv[micro, mem_rows, share:] = jnp.zeros((mem, 2 * share), jnp.float32)
        qkv[micro, :, share : 2 * share] += mm_tn(wide_scores[...], wide_query[...])
        qkv[micro, :, 2 * share :] += mm_tn(wide_soft[...], wide_grad[...])
        for index, (at, tile) in enumerate(column_tiles):
            made = mm_nt(qkv[micro, :, :share], w_in[0, at : at + tile])
            for kind in (1, 2):
                made = made + mm_nt(
                    qkv[micro, :, kind * share : (kind + 1) * share], w_in[kind, at : at + tile]
                )
            part[micro, :, at : at + tile] = made
            local_tile(ROWS, micro, index).start()
            memory_tile(ROWS_MEMORY, micro, index).start()
        add_small(48, column_sum(qkv[micro, :, :share]))
        add_small(51, column_sum(qkv[micro, :, 2 * share :]))

    def attention_back_and_ring(micro):
        attention_back(micro)
        sum_up(0, jnp.where(section == 1, 3 * micro + 3, micro + 1))

    each_micro(attention_back_and_ring)

    def finish(micro, d_normed, at_rows):
        unit, inverse = unit_rows(rows[micro, at_rows])
        add_small(0, column_sum(d_normed * unit))
        add_small(12, column_sum(d_normed))
        return hidden[micro, at_rows] + unit_rows_back(d_normed * gains[0:1], unit, inverse)

    def rows_back(micro):
        for index in range(len(column_tiles)):
            local_tile(ROWS, micro, index).wait()
            memory_tile(ROWS_MEMORY, micro, index).wait()
        grad_x[micro] = finish(micro, part[micro, own_rows] + got_out[micro, :local], own_rows)

        @pl.when(section == 1)
        def _():
            grad_copy(micro).start()

        mem_half = rows_at(local + head * half_mem, half_mem)
        d_tokens = finish(micro, part[micro, own_mem_rows] + got_out[micro, mem_half], own_mem_rows)
        for at in range(0, width, 128):
            row = 56 + (at // 128) * half_mem
            g_small[row : row + half_mem] += d_tokens[:, at : at + 128]

    each_micro(rows_back)
    small_copy = over(g_small, got_small, 0)
    small_copy.start()

    half = width // 2
    half_copy = over(w_query.at[rows_at(other * half, half)], got_half, 1)
    half_copy.start()

    tokens.wait_send()
    over_out().wait_send()
    each_seq(lambda t: t != seq, lambda t: hand_out(seq, t).wait_send())

    def all_sent(micro):
        @pl.when(section == 0)
        def _():
            x_copy(micro).wait_send()
            for target in range(2):
                y_sent(micro, target).wait_send()

        @pl.when(section == 1)
        def _():
            grad_copy(micro).wait_send()

        def sent(t):
            back_key(micro, seq, t).wait_send()
            for g in range(2):
                back_value(micro, seq, head, t, g).wait_send()

        each_seq(earlier, sent)

    each_micro(all_sent)

    @pl.when(section == 1)
    def _():
        turn_round(0)

    w_out_all[head] = mm_tn(both(attended), both(hidden))
    begin(2)

    @pl.when(section == 1)
    def _():
        pass_on(0, jnp.int32(1))

    @pl.when(section == 0)
    def _():
        sum_up(0, jnp.int32(3))

    for micro in range(micros):
        unit, _ = unit_rows(rows[micro])
        normed[micro] = unit * gains[0:1] + biases[0:1]
    for kind in kinds:
        w_in[kind] = mm_tn(both(normed), both(qkv.at[:, :, kind * share : (kind + 1) * share]))
        begin(3 + kind)
        if kind == 1:

            @pl.when(section == 1)
            def _():
                pass_on(0, jnp.int32(2))

    small_copy.wait()
    g_small[0:SHARED_ROWS] += got_small[0:SHARED_ROWS]
    begin(count - 2)
    half_copy.wait()
    got_half[...] += w_query[rows_at(head * half, half)]
    begin(count - 1)
    for kind in range(3):
        each_seq(others, lambda t, kind=kind: factor_copy(kind, t, t).wait_recv())
    w_key[...] = mm_tn(both(all_mem), both(all_key))
    w_value[...] = mm_tn(both(all_mem), both(all_value))
    value_out = pltpu.make_async_copy(w_value, value_sum, load.at[0])
    key_out = pltpu.make_async_copy(w_key, key_sum, load.at[1])
    value_out.start()
    key_out.start()

    def ring_turn(turn, carry):
        advance(0, turn + jnp.where(section == 1, AHEAD[1], AHEAD[0]))
        advance(1, turn)
        return carry

    lax.fori_loop(1, 2 * seqs - 1, ring_turn, 0)
    value_out.wait()
    key_out.wait()
    for kind in range(3):
        each_seq(others, lambda t, kind=kind: factor_copy(kind, seq, t).wait_send())
    for index, way in ways[0] + ways[1]:
        home(index, way).wait()
        up_copy(index, way, last, slot_of(index, way, last)).wait_send()

    def passed(step, carry):
        for index, way in ways[0] + ways[1]:
            own = slot_of(index, way, 0)
            on_copy(index, way, step, own, own).wait_send()
        return carry

    lax.fori_loop(0, seqs - 1, passed, 0)

    def crossed(step, carry):
        for way in range(2):
            theirs = block(half_sum.at[other], way, place - signs[way] * (step - 1))
            over(theirs, theirs, 2 + way * seqs + step).wait()
        return carry

    lax.fori_loop(0, seqs, crossed, 0)


def shapes_of(*shapes):
    return tuple(jax.ShapeDtypeStruct(shape, jnp.float32) for shape in shapes)


def buffers(*shapes):
    return [pltpu.VMEM(shape, jnp.float32) for shape in shapes]


def dma(*shape):
    return pltpu.SemaphoreType.DMA(shape)


def params_of(number):
    return pltpu.CompilerParams(
        collective_id=number, has_side_effects=True, vmem_limit_bytes=63 << 20
    )


def shards_of_two(
    boundary_in,
    short_items,
    norm_gains,
    norm_biases,
    projection_in,
    head_bias,
    projection_out,
    residual_bias,
    up_weight,
    up_bias,
    down_weight,
    memory_tokens,
    query_memory,
    key_memory,
    value_memory,
):
    seqs = lax.axis_size(SEQ)
    x = boundary_in[0]
    micros, local, width = x.shape
    w_in = projection_in[0].transpose(1, 0, 2)
    share = w_in.shape[2]
    inner = up_weight.shape[2]
    half_mem = memory_tokens.shape[1]
    mem = 2 * half_mem
    segment = 2 * local
    total = segment + mem
    dk, dv = key_memory.shape[2], value_memory.shape[2]
    stored = seqs * mem
    records = (
        (total, width),
        (total, 3 * share),
        (total, share),
        (total, 128),
        (total, width),
        (total, inner),
        (local, width),
        (mem, width),
        (stored, dk),
        (stored, 2 * dv),
        (local, dk),
        (local, stored),
        (local, width),
    )
    weights = (
        w_in,
        up_weight[0],
        down_weight[0],
        value_memory[0],
        query_memory[0],
        key_memory[0],
    )
    w_out = projection_out[0]
    few = (norm_gains[0], norm_biases[0], head_bias[0], residual_bias[0], up_bias, memory_tokens[0])
    ring = [w.shape for w in (down_weight[0], up_weight[0], w_out)]
    ring += [w_in.shape[1:]] * 3 + [(16 * seqs, 128), (width // 2, dk)]
    slots = max(2 + micros * (COPY_SLOTS + 3 * seqs), 2 * (seqs - 1) * len(ring))
    g_down, g_up, g_in, g_out, g_value, g_key, small, g_query, y, grad_x = pl.pallas_call(
        functools.partial(layers_kernel, 2),
        out_shape=shapes_of(
            down_weight[0].shape,
            up_weight[0].shape,
            w_in.shape,
            w_out.shape,
            value_memory[0].shape,
            key_memory[0].shape,
            (16 * seqs, 128),
            (2, width // 2, dk),
            (micros, local, width),
            (micros, local, width),
        ),
        in_specs=[SMEM, HBM] + [VMEM] * len(few) + [HBM] * (len(weights) + 1),
        out_specs=(HBM,) * 8 + (VMEM,) * 2,
        scratch_shapes=buffers(
            *(w.shape for w in weights),
            *((micros, *record) for record in records),
            (2, *w_out.shape),
            (micros, total, share),
            (micros, total, width),
            (micros, total, inner),
            (micros, total, width),
            (micros, total, width),
            (micros, total, width),
            (micros, local + mem, width),
            (mem, width),
            (micros, mem, dk),
            (micros, mem, dv),
            (micros, seqs, mem, dk),
            (micros, seqs, 2, mem, dv),
            (micros, mem, width),
            (micros, mem, width),
            (micros, local, width),
            (mem * (share // HEAD_DIM), total),
            (mem * (share // HEAD_DIM), total),
            (mem * (share // HEAD_DIM), share),
            (mem * (share // HEAD_DIM), share),
            (16 * seqs, 128),
            (16 * seqs, 128),
            (width // 2, dk),
            (micros, mem, dk),
            (micros, stored, width),
            (micros, stored, dv),
            (micros, stored, dk),
            *((2, SLOTS, height // (2 * seqs), columns) for height, columns in ring),
        )
        + [dma(len(weights) + 1 + micros), dma(2, len(ring)), dma(slots), dma(slots)]
        + [dma(seqs), dma(seqs)]
        + [dma(SLOTS, 2, len(ring)), dma(SLOTS, 2, len(ring))]
        + [dma(2 + 2 * seqs), dma(2 + 2 * seqs), dma(3, seqs), dma(3, seqs), pltpu.SemaphoreType.REGULAR((2, 2)), pltpu.SemaphoreType.REGULAR],
        compiler_params=params_of(0),
        name="layers",
    )(short_items, x, *few, *weights, w_out)
    outs = (
        (1, *x.shape),
        norm_gains.shape,
        norm_biases.shape,
        (1, *w_in.shape),
        head_bias.shape,
        projection_out.shape,
        residual_bias.shape,
        up_weight.shape,
        up_bias.shape,
        down_weight.shape,
        memory_tokens.shape,
        query_memory.shape,
        key_memory.shape,
        value_memory.shape,
    )
    outs = pl.pallas_call(
        finish_kernel,
        out_shape=shapes_of(*outs),
        in_specs=[HBM] * 5 + [VMEM] + [HBM] * 4,
        out_specs=(HBM, VMEM, VMEM, HBM, VMEM, HBM, VMEM, HBM, VMEM, HBM, VMEM, HBM, HBM, HBM),
        scratch_shapes=buffers(
            g_down.shape,
            g_up.shape,
            g_in.shape,
            g_out.shape,
            g_value.shape,
            g_key.shape,
            g_key.shape,
            y.shape,
        )
        + [dma(8), dma(8)],
        compiler_params=pltpu.CompilerParams(vmem_limit_bytes=62 << 20),
        name="finish",
    )(g_down, g_up, g_in, g_out, g_value, small, g_query.reshape(width, dk), g_key, y, grad_x)
    return (*outs[:3], outs[3].transpose(0, 2, 1, 3), *outs[4:])


def finish_kernel(
    g_down, g_up, g_in, g_out, g_value, small, g_query, g_key, y, grad_x,
    rows, gains, biases, proj_in, head_bias, proj_out, residual, up, up_bias, down, tokens, query, key,
    value, *refs
):
    *held, loaded, stored = refs
    pairs = (
        (g_down, down.at[0]),
        (g_up, up.at[0]),
        (g_in, proj_in.at[0]),
        (g_out, proj_out.at[0]),
        (g_value, value.at[0]),
        (g_query, query.at[0]),
        (g_key, key.at[0]),
        (y, rows.at[0]),
    )
    section = lax.axis_index(SECTION)

    def fetch(index, source):
        return pltpu.make_async_copy(source, held[index], loaded.at[index])

    def put(index):
        return pltpu.make_async_copy(held[index], pairs[index][1], stored.at[index])

    last = len(pairs) - 1
    for index in range(last):
        fetch(index, pairs[index][0]).start()

    @pl.when(section == 0)
    def _():
        fetch(last, grad_x).start()

    @pl.when(section != 0)
    def _():
        fetch(last, y).start()

    def spread(target, row, first):
        for at in range(0, target.shape[-1], 128):
            target[0, row : row + 1, at : at + 128] = small[first + at // 128 : first + at // 128 + 1]

    lanes = gains.shape[2] // 128
    for index, target in enumerate((gains, biases, residual)):
        for row in range(2):
            spread(target, row, (2 * index + row) * lanes)
    for at in range(0, up_bias.shape[1], 128):
        first = 6 * lanes + at // 128
        up_bias[:, at : at + 128] = small[first : first + 1]
    for row in range(2):
        spread(head_bias, row, 8 * lanes + row * (head_bias.shape[2] // 128))
    count = tokens.shape[1]
    for at in range(0, tokens.shape[2], 128):
        first = 56 + (at // 128) * count
        tokens[0, :, at : at + 128] = small[first : first + count]
    for index, (source, _) in enumerate(pairs):
        fetch(index, source).wait()
        put(index).start()
    for index in range(len(pairs)):
        put(index).wait()


def solution(mesh):
    return jax.shard_map(
        shards_of_two if mesh.shape[HEAD] == 2 else shards,
        mesh=mesh,
        in_specs=(
            P(SECTION, None, (SEQ, HEAD), None),
            P(),
            P(SECTION, None, None),
            P(SECTION, None, None),
            P(SECTION, None, None, HEAD),
            P(SECTION, None, HEAD),
            P(SECTION, HEAD, None),
            P(SECTION, None, None),
            P(SECTION, None, HEAD),
            P(SECTION, HEAD),
            P(SECTION, HEAD, None),
            P(SECTION, HEAD, None),
            P(SECTION, None, None),
            P(SECTION, None, None),
            P(SECTION, None, HEAD),
        ),
        out_specs=(
            P(SECTION, None, (SEQ, HEAD), None),
            P(SECTION, None, None),
            P(SECTION, None, None),
            P(SECTION, None, None, HEAD),
            P(SECTION, None, HEAD),
            P(SECTION, HEAD, None),
            P(SECTION, None, None),
            P(SECTION, None, HEAD),
            P(SECTION, HEAD),
            P(SECTION, HEAD, None),
            P(SECTION, HEAD, None),
            P(SECTION, None, None),
            P(SECTION, None, None),
            P(SECTION, None, HEAD),
        ),
        check_vma=False,
    )
```

```python
import functools
import math
from types import SimpleNamespace

import jax
import jax.numpy as jnp
from jax import lax
from jax.experimental import pallas as pl
from jax.experimental.pallas import tpu as pltpu
from jax.sharding import PartitionSpec as P

SECTION, SEQ, HEAD = "section", "seq", "head"
HEAD_DIM = 64
EPSILON = 1e-05
SCALE = 1.0 / math.sqrt(HEAD_DIM)
MESH = pl.DeviceIdType.MESH
VMEM = pl.BlockSpec(memory_space=pltpu.VMEM)
HBM = pl.BlockSpec(memory_space=pltpu.HBM)
SMEM = pl.BlockSpec(memory_space=pltpu.SMEM)
SHARED_ROWS = 36


def mm(left, right, dims=((1,), (0,))):
    return lax.dot_general(
        left, right, (dims, ((), ())), precision=lax.Precision.HIGH, preferred_element_type=jnp.float32
    )


def mm_nt(left, right):
    return mm(left, right, ((1,), (1,)))


def mm_tn(left, right):
    return mm(left, right, ((0,), (0,)))


def unit_rows(rows):
    centred = rows - jnp.mean(rows, axis=-1, keepdims=True)
    inverse = lax.rsqrt(jnp.mean(centred * centred, axis=-1, keepdims=True) + EPSILON)
    return centred * inverse, inverse


def unit_rows_back(d_unit, unit, inverse):
    return inverse * (
        d_unit
        - jnp.mean(d_unit, axis=-1, keepdims=True)
        - unit * jnp.mean(d_unit * unit, axis=-1, keepdims=True)
    )


def features(projected):
    halves = jnp.concatenate([jax.nn.softplus(projected), jax.nn.softplus(-projected)], axis=-1)
    return jnp.concatenate(
        [halves * jnp.roll(halves, rolled_by, axis=-1) for rolled_by in (1, 2, 3)], axis=-1
    )


def gelu_tanh(values_in):
    return jax.nn.gelu(values_in, approximate=True)


def head_sum_rows(rows, share):
    segment = lax.axis_size(HEAD) * share
    turn = lax.axis_index(HEAD) * share
    total = lax.psum(
        jnp.concatenate([jnp.roll(rows[:segment], turn, axis=0), rows[segment:]], axis=0), HEAD
    )
    return jnp.concatenate([jnp.roll(total[:segment], -turn, axis=0), total[segment:]], axis=0)


def head_rows(local):
    gathered = lax.all_gather(local, HEAD, axis=0, tiled=True)
    return jnp.roll(gathered, -lax.axis_index(HEAD) * local.shape[0], axis=0)


def head_scatter(rows):
    share = rows.shape[0] // lax.axis_size(HEAD)
    placed = jnp.roll(rows, lax.axis_index(HEAD) * share, axis=0)
    return lax.psum_scatter(placed, HEAD, scatter_dimension=0, tiled=True)


def heads_of(part):
    return part.reshape(part.shape[0], -1, HEAD_DIM).transpose(1, 0, 2)


def rows_of(part):
    return part.transpose(1, 0, 2).reshape(part.shape[1], -1)


def bmm(left, right, left_dim, right_dim):
    return lax.dot_general(
        left,
        right,
        (((left_dim,), (right_dim,)), ((0,), (0,))),
        precision=lax.Precision.HIGH,
        preferred_element_type=jnp.float32,
    )


def layer_forward(local, params, mask, allowed):
    width = local.shape[1]
    local_count = local.shape[0]
    segment = lax.axis_size(HEAD) * local_count
    rows = jnp.concatenate([head_rows(local), params.memory], axis=0)
    unit_one, inverse_one = unit_rows(rows)
    normed = unit_one * params.gains[0] + params.biases[0]
    projected = mm(normed, params.proj_in) + params.in_bias
    share = projected.shape[1] // 3
    query, key, value = (heads_of(projected[:, i * share : (i + 1) * share]) for i in range(3))
    scores = jnp.where(allowed, bmm(query, key, 2, 2) * SCALE, -1e30)
    row_top = jnp.max(scores, axis=-1, keepdims=True)
    exponent = jnp.exp(scores - row_top)
    soft = exponent / jnp.sum(exponent, axis=-1, keepdims=True)
    attended = rows_of(bmm(soft, value, 2, 1))
    hidden = rows + head_sum_rows(mm(attended, params.proj_out), local_count) + params.residual[0]
    unit_two, inverse_two = unit_rows(hidden)
    mixed = unit_two * params.gains[1] + params.biases[1]
    inner_pre = mm(mixed, params.up) + params.up_bias
    inner_act = gelu_tanh(inner_pre)
    partial = mm(inner_act, params.down)
    out_local = head_scatter(partial[:segment]) + hidden[:local_count] + params.residual[1]
    out_mem = lax.psum(partial[segment:], HEAD) + hidden[segment:] + params.residual[1]
    key_proj = mm(out_mem, params.key_mem)
    values = mm(out_mem, params.value_mem)
    gathered = lax.all_gather(jnp.concatenate([key_proj, values], axis=1), SEQ, axis=0, tiled=True)
    dk = key_proj.shape[1]
    keys_all = gathered[:, :dk]
    values_all = lax.all_gather(gathered[:, dk:], HEAD, axis=1, tiled=True)
    key_feats = features(keys_all)
    query_proj = mm(out_local, params.query_mem)
    query_feats = features(query_proj)
    weights = mask * mm_nt(query_feats, key_feats)
    denominator = jnp.sum(weights, axis=1, keepdims=True) + 1.0
    read = mm(weights, values_all) / denominator
    return SimpleNamespace(
        unit_one=unit_one,
        inverse_one=inverse_one,
        projected=projected,
        attended=attended,
        soft=soft,
        unit_two=unit_two,
        inverse_two=inverse_two,
        inner_pre=inner_pre,
        out_local=out_local,
        out_mem=out_mem,
        keys_all=keys_all,
        values_all=values_all,
        query_proj=query_proj,
        weights=weights,
        denominator=denominator,
        read=read,
        output=out_local + read,
    )


def layer_backward(grad, record, params, mask):
    head_count = lax.axis_size(HEAD)
    seq_count = lax.axis_size(SEQ)
    width = grad.shape[1]
    local_count = grad.shape[0]
    segment = head_count * local_count
    denominator = record.denominator
    d_numer = grad / denominator
    d_denom = -jnp.sum(grad * record.read, axis=1, keepdims=True) / denominator
    d_weights = mask * (mm_nt(d_numer, record.values_all) + d_denom)
    key_feats, keys_back = jax.vjp(features, record.keys_all)
    query_feats, query_back = jax.vjp(features, record.query_proj)
    d_query_proj = query_back(mm(d_weights, key_feats))[0]
    d_keys = keys_back(mm_tn(d_weights, query_feats))[0]
    d_values = mm_tn(record.weights, d_numer)
    d_memory = lax.psum_scatter(
        jnp.concatenate([d_keys, d_values], axis=1), SEQ, scatter_dimension=0, tiled=True
    )
    dk = d_keys.shape[1]
    d_key_proj = d_memory[:, :dk]
    d_value = lax.psum_scatter(
        d_memory[:, dk:], HEAD, scatter_dimension=1, tiled=True
    )
    d_mem = lax.psum(
        mm_nt(d_key_proj, params.key_mem) + mm_nt(d_value, params.value_mem), HEAD
    )
    d_local = grad + mm_nt(d_query_proj, params.query_mem)
    d_result = jnp.concatenate([head_rows(d_local), d_mem], axis=0)
    inner_act, gelu_back = jax.vjp(gelu_tanh, record.inner_pre)
    grad_down = mm_tn(inner_act, d_result)
    d_pre = gelu_back(mm_nt(d_result, params.down))[0]
    gains, biases = params.gains, params.biases
    mixed = record.unit_two * gains[1] + biases[1]
    grad_up = mm_tn(mixed, d_pre)
    d_mixed = head_sum_rows(mm_nt(d_pre, params.up), local_count)
    d_hidden = d_result + unit_rows_back(d_mixed * gains[1], record.unit_two, record.inverse_two)
    grad_out = mm_tn(record.attended, d_hidden)
    d_attended = mm_nt(d_hidden, params.proj_out)
    share = d_attended.shape[1]
    query, key, value = (
        heads_of(record.projected[:, i * share : (i + 1) * share]) for i in range(3)
    )
    soft = record.soft
    d_heads = heads_of(d_attended)
    inner_dot = jnp.sum(d_heads * heads_of(record.attended), axis=-1, keepdims=True)
    d_scores = soft * (bmm(d_heads, value, 2, 2) - inner_dot) * SCALE
    d_projected = jnp.concatenate(
        [
            rows_of(bmm(d_scores, key, 2, 1)),
            rows_of(bmm(d_scores, query, 1, 1)),
            rows_of(bmm(soft, d_heads, 1, 1)),
        ],
        axis=1,
    )
    normed = record.unit_one * gains[0] + biases[0]
    grad_in = mm_tn(normed, d_projected)
    columns = jnp.sum(d_projected, axis=0)
    grad_head_bias = jnp.stack([columns[:share], columns[2 * share :]])
    d_normed_all = mm_nt(d_projected, params.proj_in)
    d_normed = head_scatter(d_normed_all[:segment])
    d_normed_mem = lax.psum_scatter(
        d_normed_all[segment:], HEAD, scatter_dimension=0, tiled=True
    )
    mem_count = d_normed_mem.shape[0]
    own_mem = segment + lax.axis_index(HEAD) * mem_count

    def own(values):
        return jnp.concatenate(
            [values[:local_count], lax.dynamic_slice_in_dim(values, own_mem, mem_count, 0)], axis=0
        )

    d_normed_own = jnp.concatenate([d_normed, d_normed_mem], axis=0)
    unit_own = own(record.unit_one)
    d_rows = own(d_hidden) + unit_rows_back(
        d_normed_own * gains[0], unit_own, own(record.inverse_one)
    )
    part = 1.0 / head_count
    sharded = (
        grad_in,
        grad_head_bias,
        grad_out,
        grad_up,
        jnp.sum(d_pre, axis=0),
        grad_down,
        d_rows[local_count:],
        mm_tn(record.out_mem, d_value),
    )
    shared = (
        jnp.stack(
            [
                jnp.sum(d_normed_own * unit_own, axis=0),
                part * jnp.sum(d_mixed * record.unit_two, axis=0),
            ]
        ),
        jnp.stack([jnp.sum(d_normed_own, axis=0), part * jnp.sum(d_mixed, axis=0)]),
        part * jnp.stack([jnp.sum(d_hidden, axis=0), jnp.sum(d_result, axis=0)]),
        mm_tn(record.out_local, d_query_proj),
        mm_tn(record.out_mem, d_key_proj),
    )
    return (d_rows[:local_count], sharded, shared)


def passed_along(value, axis, steps):
    count = lax.axis_size(axis)
    first, last = (max(0, -steps), min(count, count - steps))
    return lax.ppermute(value, axis, [(source, source + steps) for source in range(first, last)])


def shards(
    boundary_in,
    short_items,
    norm_gains,
    norm_biases,
    projection_in,
    head_bias,
    projection_out,
    residual_bias,
    up_weight,
    up_bias,
    down_weight,
    memory_tokens,
    query_memory,
    key_memory,
    value_memory,
):
    section = lax.axis_index(SECTION)
    sections = lax.axis_size(SECTION)
    head_count = lax.axis_size(HEAD)
    head_place = lax.axis_index(HEAD)
    seq_count = lax.axis_size(SEQ)
    seq_place = lax.axis_index(SEQ)
    micro_total = boundary_in.shape[1]
    local_count = boundary_in.shape[2]
    width = boundary_in.shape[3]
    segment = head_count * local_count
    head_width = projection_in.shape[3]
    memory_all = lax.all_gather(memory_tokens[0], HEAD, axis=0, tiled=True)
    mem_count = memory_all.shape[0]
    params = SimpleNamespace(
        gains=norm_gains[0],
        biases=norm_biases[0],
        proj_in=projection_in[0].reshape(width, 3 * head_width),
        in_bias=jnp.concatenate(
            [head_bias[0, 0], jnp.zeros((head_width,), jnp.float32), head_bias[0, 1]]
        ),
        proj_out=projection_out[0],
        residual=residual_bias[0],
        up=up_weight[0],
        up_bias=up_bias[0],
        down=down_weight[0],
        memory=memory_all,
        query_mem=query_memory[0],
        key_mem=key_memory[0],
        value_mem=value_memory[0],
    )
    ordinal = jnp.arange(segment)
    places = jnp.concatenate(
        [(ordinal + head_place * local_count) % segment, segment + jnp.arange(mem_count)]
    )
    allowed = (places[:, None] >= places[None, :])[None]

    positions = jnp.arange(seq_count)
    masks = []
    for micro in range(micro_total):
        if micro == 0:
            item = jnp.zeros((seq_count,), jnp.int32)
        else:
            ends = jnp.cumsum(short_items[micro - 1])
            item = jnp.sum((positions[:, None] >= ends[None, :]).astype(jnp.int32), axis=1)
        own_item = jnp.sum(jnp.where(positions == seq_place, item, 0))
        seen = jnp.logical_and(positions < seq_place, item == own_item).astype(jnp.float32)
        masks.append(jnp.repeat(seen, mem_count)[None, :])
    masks = jnp.stack(masks)

    tick_total = micro_total + sections - 1
    received = jnp.zeros_like(boundary_in[0, 0])
    records = []
    for tick in range(tick_total):
        micro = jnp.clip(tick - section, 0, micro_total - 1)
        local = jnp.where(section == 0, boundary_in[0, min(tick, micro_total - 1)], received)
        records.append(layer_forward(local, params, masks[micro], allowed))
        if tick + 1 < tick_total:
            received = passed_along(records[-1].output, SECTION, 1)
    back_received = jnp.zeros_like(boundary_in[0, 0])
    grads_input = []
    total = None
    for tick in range(tick_total):
        raw = tick - (sections - 1 - section)
        valid = jnp.logical_and(raw >= 0, raw < micro_total)
        micro = jnp.clip(raw, 0, micro_total - 1)
        grad = jnp.where(
            section == sections - 1, boundary_in[0, min(tick, micro_total - 1)], back_received
        )
        kept = [
            vars(records[min(max(tick - (sections - 1 - place), 0), micro_total - 1) + place])
            for place in range(sections)
        ]
        record = SimpleNamespace(
            **jax.tree.map(lambda *kinds: lax.select_n(section, *kinds), *kept)
        )
        grad_x, sharded, shared = layer_backward(grad, record, params, masks[micro])
        fresh = jax.tree.map(lambda part: jnp.where(valid, part, 0.0), (sharded, shared))
        total = fresh if total is None else jax.tree.map(jnp.add, total, fresh)
        grads_input.append(grad_x)
        if tick + 1 < tick_total:
            back_received = passed_along(grad_x, SECTION, -1)
    sharded, shared = total
    grad_in, grad_heads_bias, grad_out, grad_up, grad_up_b, grad_down, grad_mem, grad_value = lax.psum(
        sharded, SEQ
    )
    grad_gains, grad_biases, grad_residual, grad_query, grad_key = lax.psum(shared, (SEQ, HEAD))
    finished_grads = jnp.stack(
        [grads_input[micro + sections - 1] for micro in range(micro_total)]
    )
    finished_outputs = jnp.stack(
        [records[micro + sections - 1].output for micro in range(micro_total)]
    )
    boundary_out = jnp.where(section == 0, finished_grads, finished_outputs)[None]
    return (
        boundary_out,
        grad_gains[None],
        grad_biases[None],
        grad_in.reshape(projection_in.shape),
        grad_heads_bias[None],
        grad_out[None],
        grad_residual[None],
        grad_up[None],
        grad_up_b[None],
        grad_down[None],
        grad_mem[None],
        grad_query[None],
        grad_key[None],
        grad_value[None],
    )


def barrier_with(pairs, wait_count):
    barrier = pltpu.get_barrier_semaphore()
    for condition, device in pairs:

        @pl.when(condition)
        def _(device=device):
            pl.semaphore_signal(barrier, inc=1, device_id=device, device_id_type=MESH)

    @pl.when(wait_count > 0)
    def _():
        pl.semaphore_wait(barrier, wait_count)


def nn(left, right):
    return mm(left, right)


def lane_tiles(width):
    tile = 256 if width % 256 == 0 else width
    return [(at, tile) for at in range(0, width, tile)]


def rows_at(start, count):
    return pl.ds(pl.multiple_of(start, count), count)


def halves_of(projected):
    small = jnp.log1p(jnp.exp(-jnp.abs(projected)))
    return jnp.concatenate(
        [jnp.maximum(projected, 0.0) + small, jnp.maximum(-projected, 0.0) + small], axis=1
    )


def halves_back(projected, d_halves):
    width = projected.shape[1]
    rising = 1.0 / (1.0 + jnp.exp(-projected))
    falling = 1.0 / (1.0 + jnp.exp(projected))
    return d_halves[:, :width] * rising - d_halves[:, width:] * falling


def turned(values, by):
    return pltpu.roll(values, by % values.shape[1], 1)


GELU_IN = math.sqrt(2.0 / math.pi)


def gelu_parts(pre):
    cubic = 0.044715 * pre * pre
    bent = jnp.tanh(GELU_IN * pre * (1.0 + cubic))
    half = 0.5 * (1.0 + bent)
    slope = half + 0.5 * pre * (1.0 - bent * bent) * GELU_IN * (1.0 + 3.0 * cubic)
    return pre * half, slope


def seen_mask(items, micro, seqs, mem):
    seq = lax.axis_index(SEQ)
    row_seq = lax.div(lax.broadcasted_iota(jnp.int32, (1, seqs * mem), 1), jnp.int32(mem))
    end = jnp.int32(0)
    own = jnp.int32(0)
    item = jnp.zeros((1, seqs * mem), jnp.int32)
    for piece in range(items.shape[1]):
        end = end + items[jnp.maximum(micro - 1, 0), piece]
        bound = jnp.where(micro == 0, seqs, end)
        own = own + (seq >= bound).astype(jnp.int32)
        item = item + (row_seq >= bound).astype(jnp.int32)
    return jnp.logical_and(row_seq < seq, item == own)


WEIGHTS = IN, UP, DOWN, VALUE, QUERY, KEY = tuple(range(6))
COPIES = (1, 2, 3, 3, 3, 1, 1, 1, 3, 3, 3)
(X_IN, Y_OUT, PART, LOCAL, MEMORY, GRAD, D_LOCAL, D_MEMORY, MIX, ROWS, ROWS_MEMORY) = range(11)
COPY_SLOTS = sum(COPIES)
TOKENS, OUT_SHARE = range(2)


def copy_slot(micro, kind, index=0):
    return 2 + micro * COPY_SLOTS + sum(COPIES[:kind]) + index


def column_sum(values_in):
    return jnp.sum(values_in, axis=0, keepdims=True)


SLOTS = 3
AHEAD = (3, 7)


def layers_kernel(lanes, *refs):
    refs = list(refs)

    def take(count):
        taken, refs[:] = refs[:count], refs[count:]
        return taken

    items, x, gains, biases, head_bias, residual, b_up, mem_tokens = take(8)
    weights_in = take(len(WEIGHTS))
    (w_out_in,) = take(1)
    down_sum, up_sum, in_sum, out_sum, value_sum, key_sum, small_sum, half_sum = take(8)
    y, grad_x = take(2)
    held = take(len(WEIGHTS))
    w_in, w_up, w_down, w_value, w_query, w_key = held
    rows, qkv, attended, lse, hidden, pre = take(6)
    out_local, out_mem, keys, values, query_proj, weights, read = take(7)
    w_out_all, got_attended = take(2)
    (
        normed, d_pre, d_out, part, got_part, got_out, mem_all, key_block, value_block, from_k, from_v,
        mem_part, got_mem, grad_y, wide_scores, wide_soft, wide_query, wide_grad,
        g_small, got_small, got_half, got_key, all_mem, all_value, all_key,
    ) = take(25)
    d_keys, d_values = keys, read
    slots = take(8)
    load, store, send, recv, send_w, recv_w, send_up, recv_up, send_x, recv_x, send_f, recv_f, free, go = refs

    section, seq, head = (lax.axis_index(name) for name in (SECTION, SEQ, HEAD))
    seqs = lax.axis_size(SEQ)
    micros, local, width = x.shape
    segment = 2 * local
    mem = out_mem.shape[1]
    half_mem = mem // 2
    total = segment + mem
    share = w_in.shape[2]
    inner = w_up.shape[1]
    heads = share // HEAD_DIM
    dv = w_value.shape[1]
    other = 1 - head
    partner = {HEAD: other}
    own_rows, other_rows = rows_at(head * local, local), rows_at(other * local, local)
    own_mem = rows_at(head * half_mem, half_mem)
    own_mem_rows = rows_at(segment + head * half_mem, half_mem)
    seg_rows, mem_rows = pl.ds(0, segment), pl.ds(segment, mem)
    column_tiles = [(at, width // 3) for at in range(0, width, width // 3)]
    inner_tiles = lane_tiles(inner)

    def key_slot(micro, place):
        return 2 + micros * COPY_SLOTS + micro * 3 * seqs + place

    def value_slot(micro, place, of_head):
        return key_slot(micro, seqs + 2 * place + of_head)

    def copy(slot, source, target, device):
        return pltpu.make_async_remote_copy(
            src_ref=source,
            dst_ref=target,
            send_sem=send.at[slot],
            recv_sem=recv.at[slot],
            device_id=device,
            device_id_type=MESH,
        )

    def weight_copy(name):
        return pltpu.make_async_copy(
            weights_in[name], held[name], load.at[name]
        )

    out_copy = pltpu.make_async_copy(w_out_in, w_out_all.at[head], load.at[len(WEIGHTS)])
    w_out = w_out_all.at[head]

    def each_micro(stage):
        def body(micro, carry):
            stage(micro)
            return carry

        lax.fori_loop(0, micros, body, 0)

    def each_seq(condition, act):
        for t in range(seqs):

            @pl.when(condition(t))
            def _(t=t):
                act(t)

    def later(t):
        return t > seq

    def earlier(t):
        return t < seq

    out_copy.start()
    for name in WEIGHTS:
        weight_copy(name).start()
    keys[...] = jnp.zeros_like(keys)
    values[...] = jnp.zeros_like(values)
    from_k[...] = jnp.zeros_like(from_k)
    from_v[...] = jnp.zeros_like(from_v)
    g_small[...] = jnp.zeros_like(g_small)
    mem_all[own_mem] = mem_tokens[...]
    barrier_with(
        [(seq >= 0, partner)]
        + [(t != seq, {SEQ: t, HEAD: g}) for t in range(seqs) for g in range(2)]
        + [(section == 1, {SECTION: 0, HEAD: g}) for g in range(2)]
        + [(section == 0, {SECTION: 1})],
        1 + 2 * (seqs - 1) + 2 - section,
    )

    tokens = copy(TOKENS, mem_tokens, mem_all.at[own_mem], partner)

    def x_load(micro, target):
        return pltpu.make_async_copy(x.at[micro], target, load.at[len(WEIGHTS) + 1 + micro])

    def x_copy(micro):
        return copy(copy_slot(micro, X_IN), x.at[micro], rows.at[micro, own_rows], partner)

    def y_sent(micro, target_head):
        return pltpu.make_async_remote_copy(
            src_ref=y.at[micro],
            dst_ref=rows.at[micro, own_rows],
            send_sem=send.at[copy_slot(micro, Y_OUT, target_head)],
            recv_sem=recv.at[copy_slot(micro, Y_OUT, head)],
            device_id={SECTION: 1, HEAD: target_head},
            device_id_type=MESH,
        )

    def y_got(micro, source_head):
        here = rows.at[micro, rows_at(source_head * local, local)]
        return copy(copy_slot(micro, Y_OUT, source_head), here, here, partner)

    def tile_copy(kind, micro, index):
        at, tile = column_tiles[index]
        return copy(
            copy_slot(micro, kind, index),
            part.at[micro, :, at : at + tile],
            got_part.at[micro, :, at : at + tile],
            partner,
        )

    def attended_copy(micro, index):
        cut = slice(index * 2 * HEAD_DIM, (index + 1) * 2 * HEAD_DIM)
        return copy(
            copy_slot(micro, PART, index),
            attended.at[micro, :, cut],
            got_attended.at[micro, :, cut],
            partner,
        )

    def local_tile(kind, micro, index):
        at, tile = column_tiles[index]
        return copy(
            copy_slot(micro, kind, index),
            part.at[micro, other_rows, at : at + tile],
            got_out.at[micro, pl.ds(0, local), at : at + tile],
            partner,
        )

    def memory_tile(kind, micro, index):
        at, tile = column_tiles[index]
        return copy(
            copy_slot(micro, kind, index),
            part.at[micro, mem_rows, at : at + tile],
            got_out.at[micro, pl.ds(local, mem), at : at + tile],
            partner,
        )

    def key_copy(micro, source, target):
        return pltpu.make_async_remote_copy(
            src_ref=key_block.at[micro],
            dst_ref=keys.at[micro, rows_at(source * mem, mem)],
            send_sem=send.at[key_slot(micro, target)],
            recv_sem=recv.at[key_slot(micro, source)],
            device_id={SEQ: target},
            device_id_type=MESH,
        )

    def value_copy(micro, source, source_head, target, target_head):
        return pltpu.make_async_remote_copy(
            src_ref=value_block.at[micro],
            dst_ref=values.at[
                micro, rows_at(source * mem, mem), pl.ds(pl.multiple_of(source_head * dv, 128), dv)
            ],
            send_sem=send.at[value_slot(micro, target, target_head)],
            recv_sem=recv.at[value_slot(micro, source, source_head)],
            device_id={SEQ: target, HEAD: target_head},
            device_id_type=MESH,
        )

    tokens.start()

    out_share = share // seqs

    def out_piece(half, piece):
        return w_out_all.at[half, rows_at(piece * out_share, out_share)]

    def over_out():
        mine = w_out_in.at[rows_at(seq * out_share, out_share)]
        return copy(OUT_SHARE, mine, out_piece(head, seq), partner)

    def hand_out(source, target):
        return pltpu.make_async_remote_copy(
            src_ref=out_piece(other, source),
            dst_ref=out_piece(other, source),
            send_sem=send_w.at[target],
            recv_sem=recv_w.at[source],
            device_id={SEQ: target},
            device_id_type=MESH,
        )

    @pl.when(section == 0)
    def _():
        over_out().start()

    @pl.when(section == 0)
    def _():
        x_copy(0).start()
        for micro in range(micros):
            x_load(micro, rows.at[micro, own_rows]).start()

    @pl.when(section == 1)
    def _():
        for micro in range(micros):
            x_load(micro, grad_y.at[micro]).start()

    tokens.wait_recv()
    for micro in range(micros):
        rows[micro, mem_rows] = mem_all[...]
    @pl.when(section == 1)
    def _():
        pl.semaphore_wait(go, 1)
        over_out().start()

    over_out().wait_recv()
    each_seq(lambda t: t != seq, lambda t: hand_out(seq, t).start())

    causal = lax.broadcasted_iota(jnp.int32, (segment, segment), 0) >= (
        lax.broadcasted_iota(jnp.int32, (segment, segment), 1)
    )
    mem_causal = segment + lax.broadcasted_iota(jnp.int32, (mem, total), 0) >= (
        lax.broadcasted_iota(jnp.int32, (mem, total), 1)
    )
    lane = lax.broadcasted_iota(jnp.int32, (total, 128), 1)

    def lanes_of(kind, place):
        return slice(kind * share + place * HEAD_DIM, kind * share + (place + 1) * HEAD_DIM)

    def attention(micro):
        @pl.when(section == 0)
        def _():
            x_load(micro, rows.at[micro, own_rows]).wait()
            x_copy(micro).wait_recv()

            @pl.when(micro + 1 < micros)
            def _():
                x_copy(micro + 1).start()

        @pl.when(section == 1)
        def _():
            for source in range(2):
                y_got(micro, source).wait_recv()

        unit, _ = unit_rows(rows[micro])
        normed[micro] = unit * gains[0:1] + biases[0:1]

        @pl.when(micro == 0)
        def _():
            weight_copy(IN).wait()

        for kind in range(3):
            made = nn(normed[micro], w_in[kind])
            if kind != 1:
                made = made + head_bias[kind // 2 : kind // 2 + 1]
            qkv[micro, :, kind * share : (kind + 1) * share] = made
        tops = jnp.zeros((total, 128), jnp.float32)
        for place in range(heads):
            query, key, value = (lanes_of(kind, place) for kind in range(3))
            made_top = []
            for at, allowed, seen in ((seg_rows, causal, seg_rows), (mem_rows, mem_causal, pl.ds(0, total))):
                scores = mm_nt(qkv[micro, at, query], qkv[micro, seen, key]) * SCALE
                scores = jnp.where(allowed, scores, -1e30)
                top = jnp.max(scores, axis=1, keepdims=True)
                exponent = jnp.exp(scores - top)
                row_total = jnp.sum(exponent, axis=1, keepdims=True)
                attended[micro, at, place * HEAD_DIM : (place + 1) * HEAD_DIM] = (
                    nn(exponent, qkv[micro, seen, value]) / row_total
                )
                made_top.append(top + jnp.log(row_total))
            tops = jnp.where(lane == place, jnp.concatenate(made_top, axis=0), tops)
            if place % 2 == 1:
                attended_copy(micro, place // 2).start()
        lse[micro] = tops

    each_micro(attention)
    weight_copy(UP).wait()
    weight_copy(DOWN).wait()
    out_copy.wait()
    each_seq(lambda t: t != seq, lambda t: hand_out(t, t).wait_recv())

    @pl.when(section == 0)
    def _():
        pl.semaphore_signal(go, inc=1, device_id={SECTION: 1}, device_id_type=MESH)


    def feed_forward(micro):
        for index in range(heads // 2):
            attended_copy(micro, index).wait()
        for at, tile in column_tiles:
            cut = slice(at, at + tile)
            hidden[micro, :, cut] = (
                rows[micro, :, cut]
                + nn(attended[micro], w_out_all[head, :, cut])
                + nn(got_attended[micro], w_out_all[other, :, cut])
                + residual[0:1, cut]
            )
        unit, _ = unit_rows(hidden[micro])
        normed[micro] = unit * gains[1:2] + biases[1:2]
        for at, tile in inner_tiles:
            cut = slice(at, at + tile)
            made = nn(normed[micro], w_up[:, cut]) + b_up[:, cut]
            pre[micro, :, cut] = made
            d_pre[micro, :, cut] = gelu_parts(made)[0]
        for index, (at, tile) in enumerate(column_tiles):
            part[micro, :, at : at + tile] = nn(d_pre[micro], w_down[:, at : at + tile])
            memory_tile(MEMORY, micro, index).start()
            local_tile(LOCAL, micro, index).start()

    each_micro(feed_forward)
    for name in (KEY, VALUE, QUERY):
        weight_copy(name).wait()

    def memory_write(micro):
        for index, (at, tile) in enumerate(column_tiles):
            cut = slice(at, at + tile)
            memory_tile(MEMORY, micro, index).wait()
            out_mem[micro, :, cut] = (
                part[micro, mem_rows, cut]
                + got_out[micro, local:, cut]
                + hidden[micro, mem_rows, cut]
                + residual[1:2, cut]
            )
        key_block[micro] = nn(out_mem[micro], w_key[...])
        value_block[micro] = nn(out_mem[micro], w_value[...])

        def share_block(t):
            key_copy(micro, seq, t).start()
            for g in range(2):
                value_copy(micro, seq, head, t, g).start()

        each_seq(later, share_block)

    each_micro(memory_write)

    def read_query(micro):
        for index, (at, tile) in enumerate(column_tiles):
            cut = slice(at, at + tile)
            local_tile(LOCAL, micro, index).wait()
            out_local[micro, :, cut] = (
                part[micro, own_rows, cut]
                + got_out[micro, :local, cut]
                + hidden[micro, own_rows, cut]
                + residual[1:2, cut]
            )
        query_proj[micro] = nn(out_local[micro], w_query[...])

    def memory_read(micro):
        read_query(micro)

        def got(t):
            key_copy(micro, t, t).wait_recv()
            for g in range(2):
                value_copy(micro, t, g, t, g).wait_recv()

        query_halves = halves_of(query_proj[micro])
        each_seq(earlier, got)
        key_halves = halves_of(keys[micro])
        scores = jnp.zeros((local, seqs * mem), jnp.float32)
        for by in (1, 2, 3):
            scores = scores + mm_nt(
                query_halves * turned(query_halves, by), key_halves * turned(key_halves, by)
            )
        scores = jnp.where(seen_mask(items, micro, seqs, mem), scores, 0.0)
        weights[micro] = scores
        found = nn(scores, values[micro]) / (jnp.sum(scores, axis=1, keepdims=True) + 1.0)
        read[micro] = found
        y[micro] = out_local[micro] + found

        @pl.when(section == 0)
        def _():
            for target in range(2):
                y_sent(micro, target).start()

    each_micro(memory_read)

    def grad_copy(micro):
        return copy(
            copy_slot(micro, GRAD), grad_x.at[micro], grad_y.at[micro], {SECTION: 0}
        )

    def rows_copy(micro):
        here = d_out.at[micro, own_rows]
        return copy(copy_slot(micro, D_LOCAL), here, here, partner)

    def mem_copy(micro):
        return copy(copy_slot(micro, D_MEMORY), mem_part.at[micro], got_mem.at[micro], partner)

    def back_key(micro, source, target):
        return pltpu.make_async_remote_copy(
            src_ref=d_keys.at[micro, rows_at(target * mem, mem)],
            dst_ref=from_k.at[micro, source],
            send_sem=send.at[key_slot(micro, target)],
            recv_sem=recv.at[key_slot(micro, source)],
            device_id={SEQ: target},
            device_id_type=MESH,
        )

    def back_value(micro, source, source_head, target, target_head):
        return pltpu.make_async_remote_copy(
            src_ref=d_values.at[
                micro, rows_at(target * mem, mem), pl.ds(pl.multiple_of(target_head * dv, 128), dv)
            ],
            dst_ref=from_v.at[micro, source, source_head],
            send_sem=send.at[value_slot(micro, target, target_head)],
            recv_sem=recv.at[value_slot(micro, source, source_head)],
            device_id={SEQ: target, HEAD: target_head},
            device_id_type=MESH,
        )

    factors = ((out_mem, all_mem), (value_block, all_value), (key_block, all_key))

    def factor_copy(kind, source, target):
        own, everyone = factors[kind]
        return pltpu.make_async_remote_copy(
            src_ref=own,
            dst_ref=everyone.at[:, rows_at(source * mem, mem)],
            send_sem=send_f.at[kind, target],
            recv_sem=recv_f.at[kind, source],
            device_id={SEQ: target},
            device_id_type=MESH,
        )

    def others(t):
        return t != seq

    def spread_factor(kind):
        own, everyone = factors[kind]
        everyone[:, rows_at(seq * mem, mem)] = own[...]
        each_seq(others, lambda t: factor_copy(kind, seq, t).start())

    spread_factor(0)

    def key_half_copy(micro):
        return pltpu.make_async_remote_copy(
            src_ref=key_block.at[micro],
            dst_ref=got_key.at[micro],
            send_sem=send_x.at[micro],
            recv_sem=recv_x.at[micro],
            device_id=partner,
            device_id_type=MESH,
        )

    def add_small(row, vector):
        for at in range(0, vector.shape[1], 128):
            g_small[row + at // 128 : row + at // 128 + 1] += vector[:, at : at + 128]

    def read_back(micro):
        @pl.when(section == 0)
        def _():
            grad_copy(micro).wait_recv()

        @pl.when(section == 1)
        def _():
            x_load(micro, grad_y.at[micro]).wait()

        grad = grad_y[micro]
        scores = weights[micro]
        denominator = jnp.sum(scores, axis=1, keepdims=True) + 1.0
        d_numer = grad / denominator
        d_denom = -jnp.sum(grad * read[micro], axis=1, keepdims=True) / denominator
        d_values[micro] = mm_tn(scores, d_numer)

        def send_values(t):
            for g in range(2):
                back_value(micro, seq, head, t, g).start()

        each_seq(earlier, send_values)
        d_scores = jnp.where(
            seen_mask(items, micro, seqs, mem), mm_nt(d_numer, values[micro]) + d_denom, 0.0
        )
        query_halves, key_halves = halves_of(query_proj[micro]), halves_of(keys[micro])
        d_key_halves = jnp.zeros_like(key_halves)
        for by in (1, 2, 3):
            d_feats = mm_tn(d_scores, query_halves * turned(query_halves, by))
            d_key_halves += d_feats * turned(key_halves, by) + turned(d_feats * key_halves, -by)
        d_keys[micro] = halves_back(keys[micro], d_key_halves)
        each_seq(earlier, lambda t: back_key(micro, seq, t).start())
        d_query_halves = jnp.zeros_like(query_halves)
        for by in (1, 2, 3):
            d_feats = nn(d_scores, key_halves * turned(key_halves, by))
            d_query_halves += d_feats * turned(query_halves, by) + turned(d_feats * query_halves, -by)
        query_proj[micro] = halves_back(query_proj[micro], d_query_halves)
        d_out[micro, own_rows] = grad + mm_nt(query_proj[micro], w_query[...])
        rows_copy(micro).start()

    each_micro(read_back)

    def write_back(micro):
        def got(t):
            back_key(micro, t, t).wait_recv()
            for g in range(2):
                back_value(micro, t, g, t, g).wait_recv()

        each_seq(later, got)
        key_block[micro] = jnp.sum(from_k[micro], axis=0)
        value_block[micro] = jnp.sum(from_v[micro], axis=(0, 1))
        mem_part[micro] = mm_nt(key_block[micro], w_key[...]) + mm_nt(
            value_block[micro], w_value[...]
        )
        mem_copy(micro).start()
        key_half_copy(micro).start()

    def forward_sent(micro):
        def sent(t):
            key_copy(micro, seq, t).wait_send()
            for g in range(2):
                value_copy(micro, seq, head, t, g).wait_send()

        each_seq(later, sent)

    each_micro(forward_sent)
    each_micro(write_back)

    def both(ref):
        return ref[...].reshape(micros * ref.shape[1], ref.shape[2])

    w_query[...] = mm_tn(both(out_local), both(query_proj))
    spread_factor(1)
    for micro in range(micros):
        key_half_copy(micro).wait()
        key_block[micro] += got_key[micro]
    spread_factor(2)
    def feed_forward_back(micro):
        mem_copy(micro).wait()
        d_out[micro, mem_rows] = mem_part[micro] + got_mem[micro]
        rows_copy(micro).wait()
        for at, tile in inner_tiles:
            cut = slice(at, at + tile)
            activated, slope = gelu_parts(pre[micro, :, cut])
            made = slope * mm_nt(d_out[micro], w_down[cut])
            pre[micro, :, cut] = activated
            d_pre[micro, :, cut] = made
            add_small(36 + at // 128, column_sum(made))
        for index, (at, tile) in enumerate(column_tiles):
            part[micro, :, at : at + tile] = mm_nt(d_pre[micro], w_up[at : at + tile])
            tile_copy(MIX, micro, index).start()
        add_small(30, 0.5 * column_sum(d_out[micro]))

    each_micro(feed_forward_back)
    along = seqs // lanes
    z, lane_y = seq // lanes, lax.rem(seq, lanes)
    place = lane_y * along + jnp.where(lax.rem(lane_y, 2) == 0, z, along - 1 - z)

    def device(spot):
        row = spot // along
        column = lax.rem(spot, along)
        column = jnp.where(lax.rem(row, 2) == 0, column, along - 1 - column)
        return {SEQ: column * lanes + row}

    targets = (device(lax.rem(place + 1, seqs)), device(lax.rem(place + seqs - 1, seqs)))
    signs = (1, -1)
    kinds = range(w_in.shape[0])
    sources = [w_down, w_up, w_out, *(w_in.at[kind] for kind in kinds), g_small, got_half]
    results = [down_sum, up_sum, out_sum, *(in_sum.at[kind] for kind in kinds)]
    results += [small_sum, half_sum.at[head]]
    count = len(sources)
    ways = [[(index, way) for index in group for way in range(2)] for group in (range(2), range(2, count))]
    last = seqs - 2

    def block(ref, way, spot):
        size = ref.shape[0] // seqs
        half = size // 2
        spot = lax.rem(spot + 2 * seqs, seqs)
        return ref.at[pl.ds(pl.multiple_of(spot * size + way * half, half), half)]

    def slot_of(index, way, step):
        return slots[index].at[way, lax.rem(step, SLOTS)]

    def up_copy(index, way, step, source):
        turn = lax.rem(step, SLOTS)
        return pltpu.make_async_remote_copy(
            src_ref=source,
            dst_ref=slot_of(index, way, step),
            send_sem=send_up.at[turn, way, index],
            recv_sem=recv_up.at[turn, way, index],
            device_id=targets[way],
            device_id_type=MESH,
        )

    def on_copy(index, way, step, source, target):
        return pltpu.make_async_remote_copy(
            src_ref=source,
            dst_ref=target,
            send_sem=send.at[(step * 2 + way) * count + index],
            recv_sem=recv.at[(step * 2 + way) * count + index],
            device_id=targets[way],
            device_id_type=MESH,
        )

    def over(source, target, number):
        return pltpu.make_async_remote_copy(
            src_ref=source,
            dst_ref=target,
            send_sem=send_x.at[number],
            recv_sem=recv_x.at[number],
            device_id=partner,
            device_id_type=MESH,
        )

    def hand_over(way, spot, step):
        mine = block(half_sum.at[head], way, spot)
        return over(mine, mine, 2 + way * seqs + step)

    def home(index, way):
        return pltpu.make_async_copy(
            slot_of(index, way, last),
            block(results[index], way, place + signs[way]),
            store.at[way, index],
        )

    def sum_up(group, step):
        @pl.when(step >= SLOTS)
        def _():
            for way in range(2):
                pl.semaphore_wait(free.at[group, way], 1)

        for index, way in ways[group]:
            got = slot_of(index, way, step - 1)
            up_copy(index, way, step - 1, got).wait_recv()
            got[...] += block(sources[index], way, place - signs[way] * step)[...]
            up_copy(index, way, step, got).start()
        for index, way in ways[group]:
            up_copy(index, way, step - 1, slot_of(index, way, step)).wait_send()

        @pl.when(jnp.logical_and(step >= 2, step + 1 < seqs - 1))
        def _():
            for way in range(2):
                pl.semaphore_signal(
                    free.at[group, way], inc=1, device_id=targets[1 - way], device_id_type=MESH
                )

    def turn_round(group):
        for index, way in ways[group]:
            got = slot_of(index, way, last)
            up_copy(index, way, last, got).wait_recv()
            spot = place + signs[way]
            got[...] += block(sources[index], way, spot)[...]
            target = block(results[index], way, spot)
            on_copy(index, way, 0, got, target).start()
            home(index, way).start()
            if index == count - 1:
                over(got, target, 2 + way * seqs).start()

    def pass_on(group, step):
        for index, way in ways[group]:
            spot = place - signs[way] * (step - 1)
            here = block(results[index], way, spot)
            on_copy(index, way, step - 1, here, here).wait_recv()

            @pl.when(step < seqs - 1)
            def _(index=index, way=way, here=here):
                on_copy(index, way, step, here, here).start()

            if index == count - 1:
                hand_over(way, spot, step).start()

    def advance(group, step):
        @pl.when(step < seqs - 1)
        def _():
            sum_up(group, step)

        @pl.when(step == seqs - 1)
        def _():
            turn_round(group)

        @pl.when(jnp.logical_and(step >= seqs, step < 2 * seqs - 1))
        def _():
            pass_on(group, step - seqs + 1)

    def begin(*indices):
        for index in indices:
            for way in range(2):
                up_copy(index, way, 0, block(sources[index], way, place)).start()

    for micro in range(micros):
        unit, _ = unit_rows(hidden[micro])
        normed[micro] = unit * gains[1:2] + biases[1:2]
    for at, tile in inner_tiles:
        cut = slice(at, at + tile)
        w_down[cut] = mm_tn(both(pre.at[:, :, cut]), both(d_out))
    begin(0)
    for at, tile in inner_tiles:
        cut = slice(at, at + tile)
        w_up[:, cut] = mm_tn(both(normed), both(d_pre.at[:, :, cut]))
    begin(1)

    def attention_back(micro):
        unit, inverse = unit_rows(hidden[micro])
        for index, (at, tile) in enumerate(column_tiles):
            cut = slice(at, at + tile)
            tile_copy(MIX, micro, index).wait()
            got_part[micro, :, cut] += part[micro, :, cut]
        d_mixed = got_part[micro]
        hidden[micro] = d_out[micro] + unit_rows_back(d_mixed * gains[1:2], unit, inverse)
        add_small(6, 0.5 * column_sum(d_mixed * unit))
        add_small(18, 0.5 * column_sum(d_mixed))
        add_small(24, 0.5 * column_sum(hidden[micro]))
        part[micro, :, :share] = mm_nt(hidden[micro], w_out[...])
        block_rows = lax.div(
            lax.broadcasted_iota(jnp.int32, (mem, share), 1), jnp.int32(HEAD_DIM)
        )
        for place in range(heads):
            query, key, value = (lanes_of(kind, place) for kind in range(3))
            cut = slice(place * HEAD_DIM, (place + 1) * HEAD_DIM)
            wide = pl.ds(place * mem, mem)
            grads = []
            for at, allowed, seen in ((seg_rows, causal, seg_rows), (mem_rows, mem_causal, pl.ds(0, total))):
                scores = mm_nt(qkv[micro, at, query], qkv[micro, seen, key]) * SCALE
                soft = jnp.exp(
                    jnp.where(allowed, scores, -1e30) - lse[micro, at, place : place + 1]
                )
                d_head = part[micro, at, cut]
                inner_dot = jnp.sum(d_head * attended[micro, at, cut], axis=1, keepdims=True)
                d_scores = soft * (mm_nt(d_head, qkv[micro, seen, value]) - inner_dot) * SCALE
                grads.append((soft, d_scores, d_head, nn(d_scores, qkv[micro, seen, key])))
            (soft, d_scores, d_head, d_query), (mem_soft, mem_scores, _, mem_query) = grads
            wide_soft[wide] = mem_soft
            wide_scores[wide] = mem_scores
            mine = block_rows == place
            wide_query[wide] = jnp.where(mine, qkv[micro, mem_rows, :share], 0.0)
            wide_grad[wide] = jnp.where(mine, part[micro, mem_rows, :share], 0.0)
            d_key = mm_tn(d_scores, qkv[micro, seg_rows, query])
            d_value = mm_tn(soft, d_head)
            qkv[micro, seg_rows, query] = d_query
            qkv[micro, mem_rows, query] = mem_query
            qkv[micro, seg_rows, key] = d_key
            qkv[micro, seg_rows, value] = d_value
            if place == heads // 2:

                @pl.when(section == 1)
                def _():
                    sum_up(0, 2 * micro + 1)

        qkv[micro, mem_rows, share:] = jnp.zeros((mem, 2 * share), jnp.float32)
        qkv[micro, :, share : 2 * share] += mm_tn(wide_scores[...], wide_query[...])
        qkv[micro, :, 2 * share :] += mm_tn(wide_soft[...], wide_grad[...])
        for index, (at, tile) in enumerate(column_tiles):
            made = mm_nt(qkv[micro, :, :share], w_in[0, at : at + tile])
            for kind in (1, 2):
                made = made + mm_nt(
                    qkv[micro, :, kind * share : (kind + 1) * share], w_in[kind, at : at + tile]
                )
            part[micro, :, at : at + tile] = made
            local_tile(ROWS, micro, index).start()
            memory_tile(ROWS_MEMORY, micro, index).start()
        add_small(48, column_sum(qkv[micro, :, :share]))
        add_small(51, column_sum(qkv[micro, :, 2 * share :]))

    def attention_back_and_ring(micro):
        attention_back(micro)
        sum_up(0, jnp.where(section == 1, 2 * micro + 2, micro + 1))

    each_micro(attention_back_and_ring)

    def finish(micro, d_normed, at_rows):
        unit, inverse = unit_rows(rows[micro, at_rows])
        add_small(0, column_sum(d_normed * unit))
        add_small(12, column_sum(d_normed))
        return hidden[micro, at_rows] + unit_rows_back(d_normed * gains[0:1], unit, inverse)

    def rows_back(micro):
        for index in range(len(column_tiles)):
            local_tile(ROWS, micro, index).wait()
            memory_tile(ROWS_MEMORY, micro, index).wait()
        grad_x[micro] = finish(micro, part[micro, own_rows] + got_out[micro, :local], own_rows)

        @pl.when(section == 1)
        def _():
            grad_copy(micro).start()

        mem_half = rows_at(local + head * half_mem, half_mem)
        d_tokens = finish(micro, part[micro, own_mem_rows] + got_out[micro, mem_half], own_mem_rows)
        for at in range(0, width, 128):
            row = 56 + (at // 128) * half_mem
            g_small[row : row + half_mem] += d_tokens[:, at : at + 128]

    each_micro(rows_back)
    small_copy = over(g_small, got_small, 0)
    small_copy.start()

    half = width // 2
    half_copy = over(w_query.at[rows_at(other * half, half)], got_half, 1)
    half_copy.start()

    tokens.wait_send()
    over_out().wait_send()
    each_seq(lambda t: t != seq, lambda t: hand_out(seq, t).wait_send())

    def all_sent(micro):
        @pl.when(section == 0)
        def _():
            x_copy(micro).wait_send()
            for target in range(2):
                y_sent(micro, target).wait_send()

        @pl.when(section == 1)
        def _():
            grad_copy(micro).wait_send()

        def sent(t):
            back_key(micro, seq, t).wait_send()
            for g in range(2):
                back_value(micro, seq, head, t, g).wait_send()

        each_seq(earlier, sent)

    each_micro(all_sent)

    @pl.when(section == 1)
    def _():
        sum_up(0, jnp.int32(5))

    w_out_all[head] = mm_tn(both(attended), both(hidden))
    begin(2)

    @pl.when(section == 1)
    def _():
        sum_up(0, jnp.int32(6))

    @pl.when(section == 0)
    def _():
        sum_up(0, jnp.int32(3))

    for micro in range(micros):
        unit, _ = unit_rows(rows[micro])
        normed[micro] = unit * gains[0:1] + biases[0:1]
    for kind in kinds:
        w_in[kind] = mm_tn(both(normed), both(qkv.at[:, :, kind * share : (kind + 1) * share]))
        begin(3 + kind)
        if kind == 1:

            @pl.when(section == 1)
            def _():
                turn_round(0)

    small_copy.wait()
    g_small[0:SHARED_ROWS] += got_small[0:SHARED_ROWS]
    begin(count - 2)
    half_copy.wait()
    got_half[...] += w_query[rows_at(head * half, half)]
    begin(count - 1)
    for kind in range(3):
        each_seq(others, lambda t, kind=kind: factor_copy(kind, t, t).wait_recv())
    w_key[...] = mm_tn(both(all_mem), both(all_key))
    w_value[...] = mm_tn(both(all_mem), both(all_value))
    value_out = pltpu.make_async_copy(w_value, value_sum, load.at[0])
    key_out = pltpu.make_async_copy(w_key, key_sum, load.at[1])
    value_out.start()
    key_out.start()

    def ring_turn(turn, carry):
        advance(0, turn + jnp.where(section == 1, AHEAD[1], AHEAD[0]))
        advance(1, turn)
        return carry

    lax.fori_loop(1, 2 * seqs - 1, ring_turn, 0)
    value_out.wait()
    key_out.wait()
    for kind in range(3):
        each_seq(others, lambda t, kind=kind: factor_copy(kind, seq, t).wait_send())
    for index, way in ways[0] + ways[1]:
        home(index, way).wait()
        up_copy(index, way, last, slot_of(index, way, last)).wait_send()

    def passed(step, carry):
        for index, way in ways[0] + ways[1]:
            own = slot_of(index, way, 0)
            on_copy(index, way, step, own, own).wait_send()
        return carry

    lax.fori_loop(0, seqs - 1, passed, 0)

    def crossed(step, carry):
        for way in range(2):
            theirs = block(half_sum.at[other], way, place - signs[way] * (step - 1))
            over(theirs, theirs, 2 + way * seqs + step).wait()
        return carry

    lax.fori_loop(0, seqs, crossed, 0)


def shapes_of(*shapes):
    return tuple(jax.ShapeDtypeStruct(shape, jnp.float32) for shape in shapes)


def buffers(*shapes):
    return [pltpu.VMEM(shape, jnp.float32) for shape in shapes]


def dma(*shape):
    return pltpu.SemaphoreType.DMA(shape)


def params_of(number):
    return pltpu.CompilerParams(
        collective_id=number, has_side_effects=True, vmem_limit_bytes=63 << 20
    )


def shards_of_two(
    boundary_in,
    short_items,
    norm_gains,
    norm_biases,
    projection_in,
    head_bias,
    projection_out,
    residual_bias,
    up_weight,
    up_bias,
    down_weight,
    memory_tokens,
    query_memory,
    key_memory,
    value_memory,
):
    seqs = lax.axis_size(SEQ)
    x = boundary_in[0]
    micros, local, width = x.shape
    w_in = projection_in[0].transpose(1, 0, 2)
    share = w_in.shape[2]
    inner = up_weight.shape[2]
    half_mem = memory_tokens.shape[1]
    mem = 2 * half_mem
    segment = 2 * local
    total = segment + mem
    dk, dv = key_memory.shape[2], value_memory.shape[2]
    stored = seqs * mem
    records = (
        (total, width),
        (total, 3 * share),
        (total, share),
        (total, 128),
        (total, width),
        (total, inner),
        (local, width),
        (mem, width),
        (stored, dk),
        (stored, 2 * dv),
        (local, dk),
        (local, stored),
        (local, width),
    )
    weights = (
        w_in,
        up_weight[0],
        down_weight[0],
        value_memory[0],
        query_memory[0],
        key_memory[0],
    )
    w_out = projection_out[0]
    few = (norm_gains[0], norm_biases[0], head_bias[0], residual_bias[0], up_bias, memory_tokens[0])
    ring = [w.shape for w in (down_weight[0], up_weight[0], w_out)]
    ring += [w_in.shape[1:]] * 3 + [(16 * seqs, 128), (width // 2, dk)]
    slots = max(2 + micros * (COPY_SLOTS + 3 * seqs), 2 * (seqs - 1) * len(ring))
    g_down, g_up, g_in, g_out, g_value, g_key, small, g_query, y, grad_x = pl.pallas_call(
        functools.partial(layers_kernel, 2),
        out_shape=shapes_of(
            down_weight[0].shape,
            up_weight[0].shape,
            w_in.shape,
            w_out.shape,
            value_memory[0].shape,
            key_memory[0].shape,
            (16 * seqs, 128),
            (2, width // 2, dk),
            (micros, local, width),
            (micros, local, width),
        ),
        in_specs=[SMEM, HBM] + [VMEM] * len(few) + [HBM] * (len(weights) + 1),
        out_specs=(HBM,) * 8 + (VMEM,) * 2,
        scratch_shapes=buffers(
            *(w.shape for w in weights),
            *((micros, *record) for record in records),
            (2, *w_out.shape),
            (micros, total, share),
            (micros, total, width),
            (micros, total, inner),
            (micros, total, width),
            (micros, total, width),
            (micros, total, width),
            (micros, local + mem, width),
            (mem, width),
            (micros, mem, dk),
            (micros, mem, dv),
            (micros, seqs, mem, dk),
            (micros, seqs, 2, mem, dv),
            (micros, mem, width),
            (micros, mem, width),
            (micros, local, width),
            (mem * (share // HEAD_DIM), total),
            (mem * (share // HEAD_DIM), total),
            (mem * (share // HEAD_DIM), share),
            (mem * (share // HEAD_DIM), share),
            (16 * seqs, 128),
            (16 * seqs, 128),
            (width // 2, dk),
            (micros, mem, dk),
            (micros, stored, width),
            (micros, stored, dv),
            (micros, stored, dk),
            *((2, SLOTS, height // (2 * seqs), columns) for height, columns in ring),
        )
        + [dma(len(weights) + 1 + micros), dma(2, len(ring)), dma(slots), dma(slots)]
        + [dma(seqs), dma(seqs)]
        + [dma(SLOTS, 2, len(ring)), dma(SLOTS, 2, len(ring))]
        + [dma(2 + 2 * seqs), dma(2 + 2 * seqs), dma(3, seqs), dma(3, seqs), pltpu.SemaphoreType.REGULAR((2, 2)), pltpu.SemaphoreType.REGULAR],
        compiler_params=params_of(0),
        name="layers",
    )(short_items, x, *few, *weights, w_out)
    outs = (
        (1, *x.shape),
        norm_gains.shape,
        norm_biases.shape,
        (1, *w_in.shape),
        head_bias.shape,
        projection_out.shape,
        residual_bias.shape,
        up_weight.shape,
        up_bias.shape,
        down_weight.shape,
        memory_tokens.shape,
        query_memory.shape,
        key_memory.shape,
        value_memory.shape,
    )
    outs = pl.pallas_call(
        finish_kernel,
        out_shape=shapes_of(*outs),
        in_specs=[HBM] * 5 + [VMEM] + [HBM] * 4,
        out_specs=(HBM, VMEM, VMEM, HBM, VMEM, HBM, VMEM, HBM, VMEM, HBM, VMEM, HBM, HBM, HBM),
        scratch_shapes=buffers(
            g_down.shape,
            g_up.shape,
            g_in.shape,
            g_out.shape,
            g_value.shape,
            g_key.shape,
            g_key.shape,
            y.shape,
        )
        + [dma(8), dma(8)],
        compiler_params=pltpu.CompilerParams(vmem_limit_bytes=62 << 20),
        name="finish",
    )(g_down, g_up, g_in, g_out, g_value, small, g_query.reshape(width, dk), g_key, y, grad_x)
    return (*outs[:3], outs[3].transpose(0, 2, 1, 3), *outs[4:])


def finish_kernel(
    g_down, g_up, g_in, g_out, g_value, small, g_query, g_key, y, grad_x,
    rows, gains, biases, proj_in, head_bias, proj_out, residual, up, up_bias, down, tokens, query, key,
    value, *refs
):
    *held, loaded, stored = refs
    pairs = (
        (g_down, down.at[0]),
        (g_up, up.at[0]),
        (g_in, proj_in.at[0]),
        (g_out, proj_out.at[0]),
        (g_value, value.at[0]),
        (g_query, query.at[0]),
        (g_key, key.at[0]),
        (y, rows.at[0]),
    )
    section = lax.axis_index(SECTION)

    def fetch(index, source):
        return pltpu.make_async_copy(source, held[index], loaded.at[index])

    def put(index):
        return pltpu.make_async_copy(held[index], pairs[index][1], stored.at[index])

    last = len(pairs) - 1
    for index in range(last):
        fetch(index, pairs[index][0]).start()

    @pl.when(section == 0)
    def _():
        fetch(last, grad_x).start()

    @pl.when(section != 0)
    def _():
        fetch(last, y).start()

    def spread(target, row, first):
        for at in range(0, target.shape[-1], 128):
            target[0, row : row + 1, at : at + 128] = small[first + at // 128 : first + at // 128 + 1]

    lanes = gains.shape[2] // 128
    for index, target in enumerate((gains, biases, residual)):
        for row in range(2):
            spread(target, row, (2 * index + row) * lanes)
    for at in range(0, up_bias.shape[1], 128):
        first = 6 * lanes + at // 128
        up_bias[:, at : at + 128] = small[first : first + 1]
    for row in range(2):
        spread(head_bias, row, 8 * lanes + row * (head_bias.shape[2] // 128))
    count = tokens.shape[1]
    for at in range(0, tokens.shape[2], 128):
        first = 56 + (at // 128) * count
        tokens[0, :, at : at + 128] = small[first : first + count]
    for index, (source, _) in enumerate(pairs):
        fetch(index, source).wait()
        put(index).start()
    for index in range(len(pairs)):
        put(index).wait()


def solution(mesh):
    return jax.shard_map(
        shards_of_two if mesh.shape[HEAD] == 2 else shards,
        mesh=mesh,
        in_specs=(
            P(SECTION, None, (SEQ, HEAD), None),
            P(),
            P(SECTION, None, None),
            P(SECTION, None, None),
            P(SECTION, None, None, HEAD),
            P(SECTION, None, HEAD),
            P(SECTION, HEAD, None),
            P(SECTION, None, None),
            P(SECTION, None, HEAD),
            P(SECTION, HEAD),
            P(SECTION, HEAD, None),
            P(SECTION, HEAD, None),
            P(SECTION, None, None),
            P(SECTION, None, None),
            P(SECTION, None, HEAD),
        ),
        out_specs=(
            P(SECTION, None, (SEQ, HEAD), None),
            P(SECTION, None, None),
            P(SECTION, None, None),
            P(SECTION, None, None, HEAD),
            P(SECTION, None, HEAD),
            P(SECTION, HEAD, None),
            P(SECTION, None, None),
            P(SECTION, None, HEAD),
            P(SECTION, HEAD),
            P(SECTION, HEAD, None),
            P(SECTION, HEAD, None),
            P(SECTION, None, None),
            P(SECTION, None, None),
            P(SECTION, None, HEAD),
        ),
        check_vma=False,
    )
```
